32 devices in a mesh: gx: 4 (over z), gy: 4 (over x, core), gz: 2 (over y).
Axes of the slice: x: 2, y: 2, z: 4, core: 2. Of those that a mesh axis runs over, the one named last changes fastest.
Arguments:
- populations: float32 [19, 16, 128, 512], P(None, 'gx', 'gy', 'gz'), may hold values from 0.02 to 0.09
- stretch: float32 [6, 16, 128, 512], P(None, 'gx', 'gy', 'gz'), may hold values from -2.5 to 2.5
- mass: float32 [16, 128, 512], P('gx', 'gy', 'gz'), may hold values from 0 to 1
- flags: int32 [16, 128, 512], P('gx', 'gy', 'gz'), may hold values from 0 to 2
- conv_source: int32 [32768], P(('gx', 'gy', 'gz')), may hold values from 0 to 32767, as said below
- conv_kind: int32 [32768], P(('gx', 'gy', 'gz')), may hold values from 0 to 1
- conv_direction: int32 [32768], P(('gx', 'gy', 'gz')), may hold values from 1 to 18
Outputs:
- new_populations: float32 [19, 16, 128, 512], P(None, 'gx', 'gy', 'gz')
- new_stretch: float32 [6, 16, 128, 512], P(None, 'gx', 'gy', 'gz')
- new_mass: float32 [16, 128, 512], P('gx', 'gy', 'gz')
The draws below stay inside these ranges and needn't reach their ends.
Inputs may be any that keep to these rules, and one draw needn't show every extreme that they name: `conv_source`: the 1024 sources of one brick are distinct cells of that brick. Every brick lists, for each direction i = 1..18, a conversion with direction i whose source lies on the brick's boundary so that its neighbour x + c_i lies in another brick.
All inputs are finite; a program needn't handle non-finite values.
Results may differ from the reference program's by a relative error of at most 0.0003.
Values sent between devices are 32-bit elements; how exact they have to be, the bound alone decides.
No kernel may reach another device: no remote copies, remote signals or barrier semaphores. Data moves between devices by JAX's collectives and lax.ppermute only.
A program may use at most 64 MiB of HBM per device.

```python
import jax
import jax.numpy as jnp

BX = 4
BY = 32
BZ = 256
CONV_DEV = 1024
NX = 16
NY = 128
NZ = 512
BRICKS = 32
CONV_TOTAL = 32768
N_GY = 4
N_GZ = 2


velocity_set = ((0, 0, 0), (1, 0, 0), (-1, 0, 0), (0, 1, 0), (0, -1, 0), (0, 0, 1), (0, 0, -1), (1, 1, 0), (-1, -1, 0), (1, -1, 0), (-1, 1, 0), (1, 0, 1), (-1, 0, -1), (1, 0, -1), (-1, 0, 1), (0, 1, 1), (0, -1, -1), (0, 1, -1), (0, -1, 1))


def edge_value(sign, extent, free):
    if sign > 0:
        return jnp.int32(extent - 1)
    if sign < 0:
        return jnp.int32(0)
    return free


def conversion_lists(key):
    keys = jax.random.split(jax.random.fold_in(key, 11), BRICKS)
    cells = BX * BY * BZ

    def one_brick(brick_key):
        key_x, key_y, key_perm, key_dir = jax.random.split(brick_key, 4)
        free_x = jax.random.randint(key_x, (18,), 0, BX).astype(jnp.int32)
        free_y = jax.random.randint(key_y, (18,), 0, BY).astype(jnp.int32)
        forced = []
        flat_slot = 0
        for index in range(1, 19):
            step_x, step_y, step_z = velocity_set[index]
            pick = index - 1
            if step_z == 0:
                cell_z = jnp.int32(1 + flat_slot)
                flat_slot = flat_slot + 1
                cell_x = edge_value(step_x, BX, free_x[pick])
                cell_y = edge_value(step_y, BY, free_y[pick])
            else:
                cell_z = edge_value(step_z, BZ, jnp.int32(0))
                if step_x == 0 and step_y == 0:
                    cell_x = free_x[pick]
                    cell_y = jnp.int32(1)
                elif step_y == 0:
                    cell_x = edge_value(step_x, BX, jnp.int32(0))
                    cell_y = jnp.int32(2)
                else:
                    cell_y = edge_value(step_y, BY, jnp.int32(0))
                    if index == 15:
                        cell_x = jnp.int32(BX - 1)
                    elif index == 16:
                        cell_x = jnp.int32(0)
                    else:
                        cell_x = free_x[pick]
            forced.append(cell_x * (BY * BZ) + cell_y * BZ + cell_z)
        forced = jnp.stack(forced).astype(jnp.int32)
        marked = jnp.zeros((cells,), jnp.int32).at[forced].set(1)
        order = jax.random.permutation(key_perm, cells).astype(jnp.int32)
        ranked = jnp.argsort(marked[order], stable=True)
        others = order[ranked[:CONV_DEV - 18]]
        sources = jnp.concatenate([forced, others.astype(jnp.int32)])
        headings = jnp.concatenate([jnp.arange(1, 19, dtype=jnp.int32), jax.random.randint(key_dir, (CONV_DEV - 18,), 1, 19).astype(jnp.int32)])
        return (sources, headings)
    sources, headings = jax.vmap(one_brick)(keys)
    return (sources.reshape(-1).astype(jnp.int32), headings.reshape(-1).astype(jnp.int32))


def draw_conv_source(key, part):
    return conversion_lists(key)[0]


def draw_conv_direction(key, part):
    return conversion_lists(key)[1]


def set_ends(entries, stream_key, least, largest):
    dims = entries.shape
    spot = [jax.random.randint(jax.random.fold_in(stream_key, axis), (), 0, dims[axis]) for axis in range(len(dims))]
    entries = entries.at[tuple(spot)].set(least)
    longest = dims.index(max(dims))
    spot[longest] = (spot[longest] + 1) % dims[longest]
    return entries.at[tuple(spot)].set(largest)


def block_scale(stream_key, shape, cuts, low, high):
    factor_of, own = 1.0, jax.random.fold_in(stream_key, 6)
    for axis_at, blocks in cuts:
        draws = jnp.exp(jax.random.uniform(jax.random.fold_in(own, axis_at), (blocks,), jnp.float32, low / len(cuts), high / len(cuts)))
        factor_of = factor_of * jnp.repeat(draws, shape[axis_at] // blocks).reshape([-1 if axis == axis_at else 1 for axis in range(len(shape))])
    return factor_of


def centred(rng, dims, scale, limit, shards=(), kind=jnp.bfloat16):
    gain = block_scale(rng, dims, shards, -0.22, 0.18) if shards else 1.0
    values = jax.random.normal(rng, dims, jnp.float32) * scale * gain
    return jnp.minimum(jnp.maximum(values, -limit), limit).astype(kind)


def setup_inputs(seed: int = 0) -> dict:
    arg_keys = jax.random.split(jax.random.key(seed), 8)
    return {
        "populations": jnp.clip(0.02 + 0.07000000402331352 * jax.random.uniform(arg_keys[0], (19, NX, NY, NZ), jnp.float32) ** block_scale(arg_keys[0], (19, NX, NY, NZ), ((1, 4), (2, 4), (3, 2)), -0.2, 0.2), 0.02, 0.09),
        "stretch": centred(arg_keys[1], (6, NX, NY, NZ), 0.3, 2.5, ((1, 4), (2, 4), (3, 2)), jnp.float32),
        "mass": jnp.clip(1.0 * jax.random.uniform(arg_keys[2], (NX, NY, NZ), jnp.float32) ** block_scale(arg_keys[2], (NX, NY, NZ), ((0, 4), (1, 4), (2, 2)), -0.2, 0.2), 0.0, 1.0),
        "flags": set_ends(jax.random.randint(arg_keys[3], (NX, NY, NZ), 0, 3), jax.random.fold_in(arg_keys[3], 1), 0, 2).astype(jnp.int32),
        "conv_source": draw_conv_source(jax.random.fold_in(arg_keys[7], 71), 0),
        "conv_kind": set_ends(jax.random.randint(arg_keys[5], (CONV_TOTAL,), 0, 2), jax.random.fold_in(arg_keys[5], 1), 0, 1).astype(jnp.int32),
        "conv_direction": draw_conv_direction(jax.random.fold_in(arg_keys[7], 71), 0),
    }


velocity_set = ((0, 0, 0), (1, 0, 0), (-1, 0, 0), (0, 1, 0), (0, -1, 0), (0, 0, 1), (0, 0, -1), (1, 1, 0), (-1, -1, 0), (1, -1, 0), (-1, 1, 0), (1, 0, 1), (-1, 0, -1), (1, 0, -1), (-1, 0, 1), (0, 1, 1), (0, -1, -1), (0, 1, -1), (0, -1, 1))
opposite_of = (0, 2, 1, 4, 3, 6, 5, 8, 7, 10, 9, 12, 11, 14, 13, 16, 15, 18, 17)
lattice_weights = (1.0 / 3.0,) + (1.0 / 18.0,) * 6 + (1.0 / 36.0,) * 12
symmetric_slot = ((0, 3, 4), (3, 1, 5), (4, 5, 2))
tensor_pairs = ((0, 0), (1, 1), (2, 2), (0, 1), (0, 2), (1, 2))
relax_time = 0.8
polymer_time = 8.0
polymer_coeff = 0.05
unit_steps = ((1, 0, 0), (0, 1, 0), (0, 0, 1))


def window(array, start, offset, span):
    return array[..., start + offset[0]:start + offset[0] + span[0], start + offset[1]:start + offset[1] + span[1], start + offset[2]:start + offset[2] + span[2]]


def along(index, vector):
    total = None
    for comp in range(3):
        sign = velocity_set[index][comp]
        if sign != 0:
            term = vector[comp] if sign > 0 else -vector[comp]
            total = term if total is None else total + term
    return total


def moments(pops):
    density = pops[0]
    for index in range(1, 19):
        density = density + pops[index]
    moving = []
    for comp in range(3):
        total = jnp.zeros_like(density)
        for index in range(19):
            sign = velocity_set[index][comp]
            if sign == 1:
                total = total + pops[index]
            elif sign == -1:
                total = total - pops[index]
        moving.append(total / density)
    return density, jnp.stack(moving)


def polymer(fields, margin, keep, size):
    start = margin - keep
    span = tuple(extent + 2 * keep for extent in size)

    def deriv(comp, axis_num):
        upper = window(fields[comp], start, unit_steps[axis_num], span)
        lower = window(fields[comp], start, tuple(-step for step in unit_steps[axis_num]), span)
        return 0.5 * (upper - lower)

    grad = [[deriv(row, col) for col in range(3)] for row in range(3)]
    parts = [window(fields[3 + slot], start, (0, 0, 0), span) for slot in range(6)]

    def tensor(row, col):
        value = parts[symmetric_slot[row][col]]
        return value + 1.0 if row == col else value

    force = []
    for row in range(3):
        total = deriv(3 + symmetric_slot[row][0], 0) + deriv(3 + symmetric_slot[row][1], 1) + deriv(3 + symmetric_slot[row][2], 2)
        force.append(polymer_coeff * total)
    updated = []
    for row, col in tensor_pairs:
        term = grad[row][0] * tensor(0, col) + tensor(row, 0) * grad[col][0]
        for inner in (1, 2):
            term = term + grad[row][inner] * tensor(inner, col) + tensor(row, inner) * grad[col][inner]
        old = parts[symmetric_slot[row][col]]
        updated.append(old + term - old / polymer_time)
    return jnp.stack(force), jnp.stack(updated)


def equilibrium(index, density, shift, squared):
    proj = along(index, shift)
    if proj is None:
        return lattice_weights[index] * density * (1.0 - 1.5 * squared)
    return lattice_weights[index] * density * (1.0 + 3.0 * proj + 4.5 * proj * proj - 1.5 * squared)


def collide(pops, density, velocity, force):
    shift = velocity + 0.5 * force / density
    squared = shift[0] * shift[0] + shift[1] * shift[1] + shift[2] * shift[2]
    shift_force = shift[0] * force[0] + shift[1] * force[1] + shift[2] * force[2]
    factor = 1.0 - 0.5 / relax_time
    posts = []
    for index in range(19):
        equal = equilibrium(index, density, shift, squared)
        proj = along(index, shift)
        push = along(index, force)
        if proj is None:
            source = factor * lattice_weights[index] * (-3.0 * shift_force)
        else:
            source = factor * lattice_weights[index] * (3.0 * (push - shift_force) + 9.0 * proj * push)
        posts.append(pops[index] - (pops[index] - equal) / relax_time + source)
    return jnp.stack(posts), shift


def stream(post_ext, gas_ext, shift, size):
    squared = shift[0] * shift[0] + shift[1] * shift[1] + shift[2] * shift[2]
    result = [window(post_ext[0], 1, (0, 0, 0), size)]
    change = jnp.zeros(size, jnp.float32)
    for index in range(1, 19):
        back = tuple(-step for step in velocity_set[index])
        incoming = window(post_ext[index], 1, back, size)
        from_gas = window(gas_ext, 1, back, size)
        leaving = window(post_ext[opposite_of[index]], 1, (0, 0, 0), size)
        rebuilt = equilibrium(index, 1.0, shift, squared) + equilibrium(opposite_of[index], 1.0, shift, squared) - leaving
        result.append(jnp.where(from_gas > 0.5, rebuilt, incoming))
        change = change + (1.0 - from_gas) * (incoming - leaving)
    return jnp.stack(result), change


def global_index(brick, cell):
    brick_x = brick // (N_GY * N_GZ)
    brick_y = (brick // N_GZ) % N_GY
    brick_z = brick % N_GZ
    cell_x = cell // (BY * BZ)
    cell_y = (cell // BZ) % BY
    cell_z = cell % BZ
    return (((brick_x * BX + cell_x) * NY + brick_y * BY + cell_y) * NZ + brick_z * BZ + cell_z).astype(jnp.int32)


def reference(populations, stretch, mass, flags, conv_source, conv_kind, conv_direction):
    size = populations.shape[1:]
    gas = (flags == 0).astype(jnp.float32)
    stacked = jnp.concatenate([populations, stretch, gas[None]], 0)
    extended = jnp.pad(stacked, ((0, 0), (2, 2), (2, 2), (2, 2)), mode="wrap")
    density, velocity = moments(extended[:19])
    fields = jnp.concatenate([velocity, extended[19:25]], 0)
    force, updated = polymer(fields, 2, 1, size)
    inner = tuple(extent + 2 for extent in size)
    post, shift = collide(window(extended[:19], 1, (0, 0, 0), inner), window(density, 1, (0, 0, 0), inner), window(velocity, 1, (0, 0, 0), inner), force)
    new_pops, change = stream(post, window(extended[25], 1, (0, 0, 0), inner), window(shift, 1, (0, 0, 0), size), size)
    new_stretch = window(updated, 1, (0, 0, 0), size)
    new_density = new_pops[0]
    for index in range(1, 19):
        new_density = new_density + new_pops[index]
    read = mass + (flags == 1).astype(jnp.float32) * change
    owner = (jnp.arange(conv_source.shape[0]) // CONV_DEV).astype(jnp.int32)
    sources = global_index(owner, conv_source)
    flat_mass = read.reshape(-1)
    flat_density = new_density.reshape(-1)
    level = conv_kind.astype(jnp.float32) * flat_density[sources]
    excess = flat_mass[sources] - level
    flat_mass = flat_mass.at[sources].set(level)
    cells = flat_mass.shape[0]
    excess_field = jnp.zeros((cells,), jnp.float32).at[sources].set(excess).reshape(size)
    heading_field = jnp.zeros((cells,), jnp.float32).at[sources].set(conv_direction.astype(jnp.float32)).reshape(size)
    arrived = jnp.zeros(size, jnp.float32)
    for index in range(1, 19):
        moved_heading = jnp.roll(heading_field, velocity_set[index], axis=(0, 1, 2))
        moved_excess = jnp.roll(excess_field, velocity_set[index], axis=(0, 1, 2))
        arrived = arrived + jnp.where(moved_heading == float(index), moved_excess, 0.0)
    return new_pops, new_stretch, flat_mass.reshape(size) + arrived
```

```python
import jax
import jax.numpy as jnp
from jax import lax
from jax.experimental import pallas as pl
from jax.experimental.pallas import tpu as pltpu
from jax.sharding import PartitionSpec as P

velocity_set = (
    (0, 0, 0),
    (1, 0, 0),
    (-1, 0, 0),
    (0, 1, 0),
    (0, -1, 0),
    (0, 0, 1),
    (0, 0, -1),
    (1, 1, 0),
    (-1, -1, 0),
    (1, -1, 0),
    (-1, 1, 0),
    (1, 0, 1),
    (-1, 0, -1),
    (1, 0, -1),
    (-1, 0, 1),
    (0, 1, 1),
    (0, -1, -1),
    (0, 1, -1),
    (0, -1, 1),
)
opposite_of = (0, 2, 1, 4, 3, 6, 5, 8, 7, 10, 9, 12, 11, 14, 13, 16, 15, 18, 17)
lattice_weights = (1.0 / 3.0,) + (1.0 / 18.0,) * 6 + (1.0 / 36.0,) * 12
symmetric_slot = ((0, 3, 4), (3, 1, 5), (4, 5, 2))
tensor_pairs = ((0, 0), (1, 1), (2, 2), (0, 1), (0, 2), (1, 2))
relax_time = 0.8
polymer_time = 8.0
polymer_coeff = 0.05


def moving(axis, sign):
    return tuple(index for index in range(19) if velocity_set[index][axis] == sign)


x_up, x_down = (moving(0, 1), moving(0, -1))
y_up, y_down = (moving(1, 1), moving(1, -1))
z_up, z_down = (moving(2, 1), moving(2, -1))
pairs = tuple(range(1, 19, 2))
gas_slot = 5
edge_slot = 6
lanes = 128
tall = 8


def iota(shape, dim):
    return lax.broadcasted_iota(jnp.int32, shape, dim)


def wide(tile, width):
    return jnp.concatenate([tile] * (width // tile.shape[1]), axis=1)


def rows_of(load, chunk, chunks, step, edge):
    low = chunk * tall
    if step == 0:
        return load(low, low + tall)
    if step == 1 and chunk > 0:
        return load(low - 1, low + tall - 1)
    if step == -1 and chunk < chunks - 1:
        return load(low + 1, low + tall + 1)
    rows = load(low, low + tall)
    at = iota(rows.shape, 0)
    if step == 1:
        return jnp.where(at == 0, edge(), pltpu.roll(rows, 1, 0))
    return jnp.where(at == tall - 1, edge(), pltpu.roll(rows, tall - 1, 0))


def columns_of(rows, halo, lane, step):
    width = rows.shape[1]
    at = iota(rows.shape, 1)
    if step == 1:
        edge = wide(pltpu.roll(halo, (lanes - lane) % lanes, 1), width)
        return jnp.where(at == 0, edge, pltpu.roll(rows, 1, 1))
    edge = wide(pltpu.roll(halo, lanes - 1 - lane, 1), width)
    return jnp.where(at == width - 1, edge, pltpu.roll(rows, width - 1, 1))


def packed(high, low):
    at = iota(high[0].shape, 1)
    tile = jnp.zeros_like(high[0])
    for slot, part in enumerate(high):
        tile = jnp.where(at == slot, pltpu.roll(part, slot + 1, 1), tile)
    for place, part in enumerate(low):
        slot = len(high) + place
        tile = jnp.where(at == slot, pltpu.roll(part, slot, 1), tile)
    return tile


def along(index, vector):
    total = None
    for comp in range(3):
        sign = velocity_set[index][comp]
        if sign != 0:
            term = vector[comp] if sign > 0 else -vector[comp]
            total = term if total is None else total + term
    return total


def conversions(source, kind, heading, code, *, columns):
    count = source.shape[1]
    value = (heading[...] + 32 * kind[...]).astype(jnp.float32)
    row, column = (source[...] // columns, source[...] % columns)
    by_row = jnp.where(iota((code.shape[0], count), 0) == row, value, 0.0).astype(jnp.bfloat16)
    by_column = jnp.where(iota((columns, count), 0) == column, 1.0, 0.0).astype(jnp.bfloat16)
    code[...] = lax.dot_general(
        by_row, by_column, (((1,), (1,)), ((), ())), preferred_element_type=jnp.float32
    )


def moments(pops, stretch, flags, flow, face_z, up_y, down_y, up_x, down_x):
    bx, by, bz = flags.shape

    def plane(x, carry):
        for chunk in range(by // tall):
            rows = pl.ds(chunk * tall, tall)
            part = [pops[index, x, rows, :] for index in range(19)]
            density = part[0]
            for index in range(1, 19):
                density = density + part[index]
            inverse = 1.0 / density
            for comp in range(3):
                total = None
                for index in pairs:
                    sign = velocity_set[index][comp]
                    if sign != 0:
                        term = part[index] - part[index + 1]
                        term = term if sign > 0 else -term
                        total = term if total is None else total + term
                flow[comp, x, rows, :] = total * inverse
            flow[3, x, rows, :] = density
            flow[4, x, rows, :] = inverse
        return carry

    lax.fori_loop(0, bx, plane, 0)

    def faces(x, carry):
        sent = [(stretch, symmetric_slot[comp][1]) for comp in range(3)] + [
            (flow, comp) for comp in range(3)
        ]
        for slot, (ref, field) in enumerate(sent):
            up_y[x, slot : slot + 1, :] = ref[field, x, by - 1 : by, :]
            down_y[x, slot : slot + 1, :] = ref[field, x, 0:1, :]
        up_y[x, 6:8, :] = jnp.zeros((2, bz), jnp.float32)
        down_y[x, 6:8, :] = jnp.zeros((2, bz), jnp.float32)
        sent = [(stretch, symmetric_slot[comp][2]) for comp in range(3)] + sent[3:]
        face_z[x] = packed(
            [ref[field, x, :, bz - lanes : bz] for ref, field in sent],
            [ref[field, x, :, 0:lanes] for ref, field in sent],
        )
        return carry

    lax.fori_loop(0, bx, faces, 0)
    for comp in range(3):
        up_x[comp] = flow[comp, bx - 1]
        down_x[comp] = flow[comp, 0]
    up_x[3] = jnp.where(flags[bx - 1] == 0, 1.0, 0.0)
    down_x[3] = jnp.where(flags[0] == 0, 1.0, 0.0)


def beside(ref, field, x, step, halo, slot):
    last = ref.shape[1] - 1
    inside = jnp.clip(x + step, 0, last)
    beyond = x == (0 if step < 0 else last)
    return lambda low, high: jnp.where(
        beyond, halo[slot, low:high, :], ref[field, inside, low:high, :]
    )


def differences(ref, field, slots, x, chunk, chunks, below, above, y_below, y_above, z_halo):
    slot_x, slot_y, slot_z = slots
    low, high = (chunk * tall, chunk * tall + tall)

    def load(first, stop):
        return ref[field, x, first:stop, :]

    result = [None, None, None]
    if slot_x is not None:
        after = beside(ref, field, x, 1, above, slot_x)(low, high)
        before = beside(ref, field, x, -1, below, slot_x)(low, high)
        result[0] = after - before
    if slot_y is not None:
        after = rows_of(load, chunk, chunks, -1, lambda: y_above[x, slot_y : slot_y + 1, :])
        before = rows_of(load, chunk, chunks, 1, lambda: y_below[x, slot_y : slot_y + 1, :])
        result[1] = after - before
    if slot_z is not None:
        rows, halo = (load(low, high), z_halo[x, low:high, :])
        after = columns_of(rows, halo, 6 + slot_z, -1)
        before = columns_of(rows, halo, slot_z, 1)
        result[2] = after - before
    return result


def collide(
    pops,
    stretch,
    flags,
    flow,
    below,
    above,
    y_below,
    y_above,
    z_halo,
    post,
    shift,
    up_x,
    down_x,
    up_y,
    down_y,
    face_z,
):
    bx, by, bz = flags.shape
    chunks = by // tall
    halos = (below, above, y_below, y_above, z_halo)
    factor = 1.0 - 0.5 / relax_time
    rate = 1.0 / relax_time

    def plane(x, carry):
        for chunk in range(chunks):
            rows = pl.ds(chunk * tall, tall)
            terms = [[], [], []]
            for field in range(6):
                slots = [None, None, None]
                for comp in range(3):
                    for axis in range(3):
                        if symmetric_slot[comp][axis] == field:
                            slots[axis] = comp
                found = differences(stretch, field, slots, x, chunk, chunks, *halos)
                for axis in range(3):
                    if slots[axis] is not None:
                        terms[slots[axis]].append(found[axis])
            force = [0.5 * polymer_coeff * (part[0] + part[1] + part[2]) for part in terms]
            density, half = (flow[3, x, rows, :], 0.5 * flow[4, x, rows, :])
            moved = [flow[comp, x, rows, :] + half * force[comp] for comp in range(3)]
            for comp in range(3):
                shift[comp, x, rows, :] = moved[comp]
            squared = moved[0] * moved[0] + moved[1] * moved[1] + moved[2] * moved[2]
            work = moved[0] * force[0] + moved[1] * force[1] + moved[2] * force[2]
            weight = rate * density
            common = weight - 1.5 * weight * squared - 3.0 * factor * work
            odd = [3.0 * weight * moved[comp] + 3.0 * factor * force[comp] for comp in range(3)]
            even = [4.5 * weight * moved[comp] + 9.0 * factor * force[comp] for comp in range(3)]
            keep = 1.0 - rate
            post[0, x, rows, :] = keep * pops[0, x, rows, :] + lattice_weights[0] * common
            for index in pairs:
                both = common + along(index, moved) * along(index, even)
                differ = along(index, odd)
                scale = lattice_weights[index]
                post[index, x, rows, :] = keep * pops[index, x, rows, :] + scale * (both + differ)
                post[index + 1, x, rows, :] = keep * pops[index + 1, x, rows, :] + scale * (
                    both - differ
                )
        return carry

    lax.fori_loop(0, bx, plane, 0)

    def faces(x, carry):
        for slot in range(5):
            up_y[x, slot : slot + 1, :] = post[y_up[slot], x, by - 1 : by, :]
            down_y[x, slot : slot + 1, :] = post[y_down[slot], x, 0:1, :]
        gas = jnp.where(flags[x] == 0, 1.0, 0.0)
        up_y[x, 5:6, :] = gas[by - 1 : by, :]
        down_y[x, 5:6, :] = gas[0:1, :]
        up_y[x, 6:8, :] = jnp.zeros((2, bz), jnp.float32)
        down_y[x, 6:8, :] = jnp.zeros((2, bz), jnp.float32)
        face_z[x] = packed(
            [post[index, x, :, bz - lanes : bz] for index in z_up] + [gas[:, bz - lanes : bz]],
            [post[index, x, :, 0:lanes] for index in z_down] + [gas[:, 0:lanes]],
        )
        return carry

    lax.fori_loop(0, bx, faces, 0)
    for slot in range(5):
        up_x[slot] = post[x_up[slot], bx - 1]
        down_x[slot] = post[x_down[slot], 0]


def restretch(stretch, flow, below, above, y_below, y_above, z_halo, updated):
    bx, by, bz = stretch.shape[1:]
    chunks = by // tall

    def plane(x, carry):
        for chunk in range(chunks):
            rows = pl.ds(chunk * tall, tall)
            grad = [
                differences(
                    flow,
                    comp,
                    (comp, 3 + comp, 3 + comp),
                    x,
                    chunk,
                    chunks,
                    below,
                    above,
                    y_below,
                    y_above,
                    z_halo,
                )
                for comp in range(3)
            ]
            part = [stretch[slot, x, rows, :] for slot in range(6)]
            full = [part[slot] + 1.0 if slot < 3 else part[slot] for slot in range(6)]

            def product(row, col):
                total = grad[row][0] * full[symmetric_slot[0][col]]
                for inner in (1, 2):
                    total = total + grad[row][inner] * full[symmetric_slot[inner][col]]
                return total

            for slot, (row, col) in enumerate(tensor_pairs):
                old = (1.0 - 1.0 / polymer_time) * part[slot]
                if row == col:
                    updated[slot, x, rows, :] = old + product(row, col)
                else:
                    updated[slot, x, rows, :] = old + 0.5 * (product(row, col) + product(col, row))
        return carry

    lax.fori_loop(0, bx, plane, 0)


def forward_rows(up_y, down_y, z_halo, up_out, down_out):
    bx, by = z_halo.shape[:2]
    bz = up_y.shape[2]
    for x in range(bx):
        up_out[x] = up_y[x]
        down_out[x] = down_y[x]
        up_out[x, edge_slot : edge_slot + 1, :] = wide(z_halo[x, by - 1 : by, :], bz)
        down_out[x, edge_slot : edge_slot + 1, :] = wide(z_halo[x, 0:1, :], bz)


up_edges = ((0, y_up.index(7)), (0, gas_slot), (1, y_down.index(9)), (1, gas_slot))
down_edges = ((0, y_up.index(10)), (0, gas_slot), (1, y_down.index(8)), (1, gas_slot))


def forward_edges(y_below, y_above, z_halo, up_out, down_out):
    bx, by = z_halo.shape[:2]
    halves = y_below.shape[2] // lanes
    sides = (y_below, y_above)
    for out, x, edges in ((up_out, bx - 1, up_edges), (down_out, 0, down_edges)):
        for place, (side, slot) in enumerate(edges):
            for half in range(halves):
                at = half * 4 + place
                out[at : at + 1, :] = sides[side][
                    x, slot : slot + 1, half * lanes : half * lanes + lanes
                ]
        out[4 * halves :, :] = z_halo[x]


def stream(
    post,
    shift,
    mass,
    flags,
    code,
    gas_below,
    gas_above,
    below,
    above,
    y_below,
    y_above,
    z_halo,
    edges_below,
    edges_above,
    fresh,
    settled,
    spread,
    row_up,
    row_down,
    out_z,
    gas,
    low_rows,
    high_rows,
    columns,
    excess,
    heading,
):
    bx, by, bz = flags.shape
    chunks = by // tall
    halves = bz // lanes

    gas[0] = gas_below[3]
    gas[bx + 1] = gas_above[3]
    for x in range(bx):
        gas[x + 1] = jnp.where(flags[x] == 0, 1.0, 0.0)
        low_rows[x + 1] = y_below[x]
        high_rows[x + 1] = y_above[x]
        columns[x + 1] = z_halo[x]
    for ref, at, edges in ((edges_below, 0, up_edges), (edges_above, bx + 1, down_edges)):
        for place, (side, slot) in enumerate(edges):
            line = jnp.concatenate(
                [ref[half * 4 + place : half * 4 + place + 1, :] for half in range(halves)], axis=1
            )
            (low_rows, high_rows)[side][at, slot : slot + 1, :] = line
        columns[at] = ref[4 * halves :, :]

    def moved(load, index, source, chunk, slot, lane):
        step_y, step_z = velocity_set[index][1:]
        edges = low_rows if step_y == 1 else high_rows
        rows = rows_of(
            load, chunk, chunks, step_y, lambda: edges[source, slot : slot + 1, :]
        )
        if step_z == 0:
            return rows
        halo = rows_of(
            lambda low, high: columns[source, low:high, :],
            chunk,
            chunks,
            step_y,
            lambda: edges[source, edge_slot : edge_slot + 1, 0:lanes],
        )
        return columns_of(rows, halo, lane, step_z)

    def plane(x, carry):
        for chunk in range(chunks):
            rows = pl.ds(chunk * tall, tall)
            speed = [shift[comp, x, rows, :] for comp in range(3)]
            squared = speed[0] * speed[0] + speed[1] * speed[1] + speed[2] * speed[2]
            rest = 1.0 - 1.5 * squared
            total = post[0, x, rows, :]
            fresh[0, x, rows, :] = total
            change = jnp.zeros((tall, bz), jnp.float32)
            for first in pairs:
                proj = along(first, speed)
                equal = 2.0 * lattice_weights[first] * (rest + 4.5 * proj * proj)
                for index in (first, first + 1):
                    step_x, step_y, step_z = velocity_set[index]
                    source = x + 1 - step_x
                    if step_x == 0:
                        load = lambda low, high: post[index, x, low:high, :]
                    elif step_x == 1:
                        load = beside(post, index, x, -1, below, x_up.index(index))
                    else:
                        load = beside(post, index, x, 1, above, x_down.index(index))
                    slot, lane, gas_lane = (None, None, None)
                    if step_y != 0:
                        slot = (y_up if step_y == 1 else y_down).index(index)
                    if step_z == 1:
                        lane, gas_lane = (z_up.index(index), gas_slot)
                    elif step_z == -1:
                        lane, gas_lane = (6 + z_down.index(index), 6 + gas_slot)
                    arriving = moved(load, index, source, chunk, slot, lane)
                    from_gas = moved(
                        lambda low, high: gas[source, low:high, :],
                        index,
                        source,
                        chunk,
                        gas_slot,
                        gas_lane,
                    )
                    leaving = post[opposite_of[index], x, rows, :]
                    open_side = from_gas > 0.5
                    value = jnp.where(open_side, equal - leaving, arriving)
                    fresh[index, x, rows, :] = value
                    total = total + value
                    change = change + jnp.where(open_side, 0.0, arriving - leaving)
            read = mass[x, rows, :] + jnp.where(flags[x, rows, :] == 1, change, 0.0)
            mark = code[x, rows, :]
            liquid = mark >= 32.0
            converts = mark > 0.0
            level = jnp.where(liquid, total, 0.0)
            excess[x, rows, :] = jnp.where(converts, read - level, 0.0)
            heading[x, rows, :] = jnp.where(liquid, mark - 32.0, mark)
            settled[x, rows, :] = jnp.where(converts, level, read)
        return carry

    lax.fori_loop(0, bx, plane, 0)

    row_at, lane_at = (iota((by, bz), 0), iota((by, bz), 1))
    line_at = iota((1, bz), 1)
    tile_lane, line_lane = (iota((by, lanes), 1), iota((1, lanes), 1))

    def rows_up(rows):
        return jnp.where(row_at == 0, 0.0, pltpu.roll(rows, 1, 0))

    def rows_down(rows):
        return jnp.where(row_at == by - 1, 0.0, pltpu.roll(rows, by - 1, 0))

    def over(rows, at, step):
        if step == 1:
            return jnp.where(at == 0, 0.0, pltpu.roll(rows, 1, 1))
        return jnp.where(at == bz - 1, 0.0, pltpu.roll(rows, bz - 1, 1))

    def summed(parts):
        total = parts[0]
        for part in parts[1:]:
            total = total + part
        return total

    tile = jnp.zeros((by, lanes), jnp.float32)
    line_up = jnp.zeros((1, lanes), jnp.float32)
    line_down = jnp.zeros((1, lanes), jnp.float32)
    row_up[...] = jnp.zeros(row_up.shape, jnp.float32)
    row_down[...] = jnp.zeros(row_down.shape, jnp.float32)
    for target in range(bx + 2):
        groups = {}
        for index in range(1, 19):
            step_x, step_y, step_z = velocity_set[index]
            x = target - 1 - step_x
            if 0 <= x < bx:
                part = jnp.where(heading[x] == float(index), excess[x], 0.0)
                groups.setdefault((step_y, step_z), []).append(part)
        groups = {key: summed(parts) for key, parts in groups.items()}
        total = jnp.zeros((by, bz), jnp.float32)
        line = {1: jnp.zeros((1, bz), jnp.float32), -1: jnp.zeros((1, bz), jnp.float32)}
        for step_z in (0, 1, -1):
            group = jnp.zeros((by, bz), jnp.float32)
            ends = {}
            if (0, step_z) in groups:
                group = group + groups[(0, step_z)]
            if (1, step_z) in groups:
                group = group + rows_up(groups[(1, step_z)])
                ends[1] = groups[(1, step_z)][by - 1 : by, :]
            if (-1, step_z) in groups:
                group = group + rows_down(groups[(-1, step_z)])
                ends[-1] = groups[(-1, step_z)][0:1, :]
            if step_z == 0:
                total = total + group
                for side in ends:
                    line[side] = line[side] + ends[side]
                continue
            total = total + over(group, lane_at, step_z)
            for side in ends:
                line[side] = line[side] + over(ends[side], line_at, step_z)
            if step_z == 1:
                spot, cut, roll = (target, slice(bz - lanes, bz), target + 1)
            else:
                spot, cut, roll = (8 + target, slice(0, lanes), 8 + target)
            tile = jnp.where(tile_lane == spot, pltpu.roll(group[:, cut], roll, 1), tile)
            if 1 in ends:
                line_up = jnp.where(
                    line_lane == spot, pltpu.roll(ends[1][:, cut], roll, 1), line_up
                )
            if -1 in ends:
                line_down = jnp.where(
                    line_lane == spot, pltpu.roll(ends[-1][:, cut], roll, 1), line_down
                )
        spread[target] = total
        row_up[target : target + 1, :] = line[1]
        row_down[target : target + 1, :] = line[-1]
    out_z[0:by, :] = tile
    out_z[by:, :] = jnp.zeros((tall, lanes), jnp.float32)
    out_z[by : by + 1, :] = line_up
    out_z[by + 1 : by + 2, :] = line_down


def add_corners(row_up, row_down, z_halo, up_out, down_out):
    by = z_halo.shape[0] - tall
    bz = row_up.shape[1]
    lane, sub = (iota((tall, lanes), 1), iota((tall, lanes), 0))
    at = iota((tall, bz), 1)
    for place, (ref, out) in enumerate(((row_up, up_out), (row_down, down_out))):
        line = jnp.broadcast_to(z_halo[by + place : by + place + 1, :], (tall, lanes))
        first = jnp.sum(jnp.where(lane == sub, line, 0.0), axis=1, keepdims=True)
        last = jnp.sum(jnp.where(lane == sub + 8, line, 0.0), axis=1, keepdims=True)
        out[...] = ref[...] + jnp.where(at == 0, first, 0.0) + jnp.where(at == bz - 1, last, 0.0)


def with_edges(total, target, z_halo, y_below, y_above):
    by, bz = total.shape
    row_at, lane_at = (iota((by, bz), 0), iota((by, bz), 1))
    total = total + jnp.where(lane_at == 0, z_halo[0:by, target : target + 1], 0.0)
    total = total + jnp.where(lane_at == bz - 1, z_halo[0:by, 8 + target : 9 + target], 0.0)
    total = total + jnp.where(row_at == 0, y_below[target : target + 1, :], 0.0)
    return total + jnp.where(row_at == by - 1, y_above[target : target + 1, :], 0.0)


def add_faces(spread, z_halo, y_below, y_above, up_out, down_out):
    last = spread.shape[0] - 1
    up_out[...] = with_edges(spread[last], last, z_halo, y_below, y_above)
    down_out[...] = with_edges(spread[0], 0, z_halo, y_below, y_above)


def add_all(settled, spread, z_halo, y_below, y_above, below, above, new_mass):
    bx = settled.shape[0]
    for x in range(bx):
        total = with_edges(spread[x + 1], x + 1, z_halo, y_below, y_above)
        if x == 0:
            total = total + below[...]
        if x == bx - 1:
            total = total + above[...]
        new_mass[x] = settled[x] + total


def passed(array, axis, step):
    devices = lax.axis_size(axis)
    return lax.ppermute(array, axis, [(i, (i + step) % devices) for i in range(devices)])


def both_ways(tile, lower):
    before = passed(tile, "gz", 1)
    if lax.axis_size("gz") == 2:
        return before
    after = passed(tile, "gz", -1)
    return jnp.where(iota(tile.shape, tile.ndim - 1) < lower, before, after)


def call(body, outs, scratch=(), cost=(0, 0)):
    return pl.pallas_call(
        body,
        out_shape=[jax.ShapeDtypeStruct(shape, jnp.float32) for shape in outs],
        scratch_shapes=[pltpu.VMEM(shape, jnp.float32) for shape in scratch],
        compiler_params=pltpu.CompilerParams(vmem_limit_bytes=40 * 1024 * 1024),
        cost_estimate=pl.CostEstimate(flops=cost[0], bytes_accessed=cost[1], transcendentals=0),
    )


def shards(populations, stretch, mass, flags, conv_source, conv_kind, conv_direction):
    bx, by, bz = flags.shape
    cells = bx * by * bz
    box, face, tile = ((bx, by, bz), (by, bz), (bx, by, lanes))
    rows = (bx, 8, bz)

    own = [symmetric_slot[comp][0] for comp in range(3)]
    stretch_up = jnp.concatenate([stretch[slot : slot + 1, bx - 1] for slot in own])
    stretch_down = jnp.concatenate([stretch[slot : slot + 1, 0] for slot in own])
    stretch_below = passed(stretch_up, "gx", 1)
    stretch_above = passed(stretch_down, "gx", -1)

    flow, face_z, up_y, down_y, up_x, down_x = call(
        moments,
        [(5, *box), tile, rows, rows, (4, *face), (4, *face)],
        cost=(60 * cells, 150 * cells),
    )(populations, stretch, flags)
    z_first = both_ways(face_z, 6)
    y_below, y_above = (passed(up_y, "gy", 1), passed(down_y, "gy", -1))
    flow_below, flow_above = (passed(up_x, "gx", 1), passed(down_x, "gx", -1))

    entries = conv_source.shape[0]
    (code,) = call(
        lambda *refs: conversions(*refs, columns=bz), [(bx * by, bz)], cost=(40 * cells, 4 * cells)
    )(*(array.reshape(1, entries) for array in (conv_source, conv_kind, conv_direction)))
    code = code.reshape(box)

    post, shift, up_x, down_x, up_y, down_y, face_z = call(
        collide,
        [(19, *box), (3, *box), (5, *face), (5, *face), rows, rows, tile],
        cost=(250 * cells, 250 * cells),
    )(
        populations,
        stretch,
        flags,
        flow,
        stretch_below,
        stretch_above,
        y_below,
        y_above,
        z_first,
    )
    post_below, post_above = (passed(up_x, "gx", 1), passed(down_x, "gx", -1))
    z_halo = both_ways(face_z, 6)
    up_y, down_y = call(forward_rows, [rows, rows])(up_y, down_y, z_halo)
    post_y_below, post_y_above = (passed(up_y, "gy", 1), passed(down_y, "gy", -1))
    edges = (4 * (bz // lanes) + by, lanes)
    up_x, down_x = call(forward_edges, [edges, edges])(post_y_below, post_y_above, z_halo)
    edges_below, edges_above = (passed(up_x, "gx", 1), passed(down_x, "gx", -1))

    (new_stretch,) = call(restretch, [(6, *box)], cost=(150 * cells, 80 * cells))(
        stretch, flow, flow_below, flow_above, y_below, y_above, z_first
    )

    line = (8, bz)
    fresh, settled, spread, row_up, row_down, out_z = call(
        stream,
        [(19, *box), box, (bx + 2, *face), line, line, (by + 8, lanes)],
        scratch=[
            (bx + 2, *face),
            (bx + 2, 8, bz),
            (bx + 2, 8, bz),
            (bx + 2, by, lanes),
            box,
            box,
        ],
        cost=(400 * cells, 250 * cells),
    )(
        post,
        shift,
        mass,
        flags,
        code,
        flow_below,
        flow_above,
        post_below,
        post_above,
        post_y_below,
        post_y_above,
        z_halo,
        edges_below,
        edges_above,
    )
    z_last = both_ways(out_z, 8)
    row_up, row_down = call(add_corners, [line, line])(row_up, row_down, z_last)
    last_below, last_above = (passed(row_up, "gy", 1), passed(row_down, "gy", -1))
    up_x, down_x = call(add_faces, [face, face])(spread, z_last, last_below, last_above)
    below, above = (passed(up_x, "gx", 1), passed(down_x, "gx", -1))
    (new_mass,) = call(add_all, [box])(
        settled, spread, z_last, last_below, last_above, below, above
    )
    return (fresh, new_stretch, new_mass)


def solution(mesh):
    return jax.shard_map(
        shards,
        mesh=mesh,
        in_specs=(
            P(None, "gx", "gy", "gz"),
            P(None, "gx", "gy", "gz"),
            P("gx", "gy", "gz"),
            P("gx", "gy", "gz"),
            P(("gx", "gy", "gz")),
            P(("gx", "gy", "gz")),
            P(("gx", "gy", "gz")),
        ),
        out_specs=(P(None, "gx", "gy", "gz"), P(None, "gx", "gy", "gz"), P("gx", "gy", "gz")),
        check_vma=False,
    )
```

```python
import jax
import jax.numpy as jnp
from jax import lax
from jax.experimental import pallas as pl
from jax.experimental.pallas import tpu as pltpu
from jax.sharding import PartitionSpec as P

velocity_set = (
    (0, 0, 0),
    (1, 0, 0),
    (-1, 0, 0),
    (0, 1, 0),
    (0, -1, 0),
    (0, 0, 1),
    (0, 0, -1),
    (1, 1, 0),
    (-1, -1, 0),
    (1, -1, 0),
    (-1, 1, 0),
    (1, 0, 1),
    (-1, 0, -1),
    (1, 0, -1),
    (-1, 0, 1),
    (0, 1, 1),
    (0, -1, -1),
    (0, 1, -1),
    (0, -1, 1),
)
opposite_of = (0, 2, 1, 4, 3, 6, 5, 8, 7, 10, 9, 12, 11, 14, 13, 16, 15, 18, 17)
lattice_weights = (1.0 / 3.0,) + (1.0 / 18.0,) * 6 + (1.0 / 36.0,) * 12
symmetric_slot = ((0, 3, 4), (3, 1, 5), (4, 5, 2))
tensor_pairs = ((0, 0), (1, 1), (2, 2), (0, 1), (0, 2), (1, 2))
relax_time = 0.8
polymer_time = 8.0
polymer_coeff = 0.05


def moving(axis, sign):
    return tuple(index for index in range(19) if velocity_set[index][axis] == sign)


x_up, x_down = (moving(0, 1), moving(0, -1))
y_up, y_down = (moving(1, 1), moving(1, -1))
z_up, z_down = (moving(2, 1), moving(2, -1))
pairs = tuple(range(1, 19, 2))
gas_slot = 5
edge_slot = 6
lanes = 128
tall = 8


def iota(shape, dim):
    return lax.broadcasted_iota(jnp.int32, shape, dim)


def wide(tile, width):
    return jnp.concatenate([tile] * (width // tile.shape[1]), axis=1)


def rows_of(load, chunk, chunks, step, edge):
    low = chunk * tall
    if step == 0:
        return load(low, low + tall)
    if step == 1 and chunk > 0:
        return load(low - 1, low + tall - 1)
    if step == -1 and chunk < chunks - 1:
        return load(low + 1, low + tall + 1)
    rows = load(low, low + tall)
    at = iota(rows.shape, 0)
    if step == 1:
        return jnp.where(at == 0, edge(), pltpu.roll(rows, 1, 0))
    return jnp.where(at == tall - 1, edge(), pltpu.roll(rows, tall - 1, 0))


def columns_of(rows, halo, lane, step):
    width = rows.shape[1]
    at = iota(rows.shape, 1)
    if step == 1:
        edge = wide(pltpu.roll(halo, (lanes - lane) % lanes, 1), width)
        return jnp.where(at == 0, edge, pltpu.roll(rows, 1, 1))
    edge = wide(pltpu.roll(halo, lanes - 1 - lane, 1), width)
    return jnp.where(at == width - 1, edge, pltpu.roll(rows, width - 1, 1))


def packed(high, low):
    at = iota(high[0].shape, 1)
    tile = jnp.zeros_like(high[0])
    for slot, part in enumerate(high):
        tile = jnp.where(at == slot, pltpu.roll(part, slot + 1, 1), tile)
    for place, part in enumerate(low):
        slot = len(high) + place
        tile = jnp.where(at == slot, pltpu.roll(part, slot, 1), tile)
    return tile


def along(index, vector):
    total = None
    for comp in range(3):
        sign = velocity_set[index][comp]
        if sign != 0:
            term = vector[comp] if sign > 0 else -vector[comp]
            total = term if total is None else total + term
    return total


def conversions(source, kind, heading, code, *, columns):
    count = source.shape[1]
    value = (heading[...] + 32 * kind[...]).astype(jnp.float32)
    row, column = (source[...] // columns, source[...] % columns)
    by_row = jnp.where(iota((code.shape[0], count), 0) == row, value, 0.0).astype(jnp.bfloat16)
    by_column = jnp.where(iota((columns, count), 0) == column, 1.0, 0.0).astype(jnp.bfloat16)
    code[...] = lax.dot_general(
        by_row, by_column, (((1,), (1,)), ((), ())), preferred_element_type=jnp.float32
    )


def moments(pops_in, stretch_in, flags_in, pops, stretch, flags, flow, sent, up_x, down_x, sems):
    bx, by, bz = flags.shape
    copies = []
    for x in range(bx):
        copies.append(
            (
                pltpu.make_async_copy(pops_in.at[:, x], pops.at[:, x], sems.at[0, x]),
                pltpu.make_async_copy(stretch_in.at[:, x], stretch.at[:, x], sems.at[1, x]),
            )
        )
    marks = pltpu.make_async_copy(flags_in, flags, sems.at[2, 0])
    for pair in copies:
        for copy in pair:
            copy.start()
    marks.start()

    def plane(x):
        for chunk in range(by // tall):
            rows = pl.ds(chunk * tall, tall)
            part = [pops[index, x, rows, :] for index in range(19)]
            density = part[0]
            for index in range(1, 19):
                density = density + part[index]
            inverse = 1.0 / density
            for comp in range(3):
                total = None
                for index in pairs:
                    sign = velocity_set[index][comp]
                    if sign != 0:
                        term = part[index] - part[index + 1]
                        term = term if sign > 0 else -term
                        total = term if total is None else total + term
                flow[comp, x, rows, :] = total * inverse
            flow[3, x, rows, :] = density
            flow[4, x, rows, :] = inverse
        pack_face(
            sent,
            x,
            [(stretch, symmetric_slot[comp][1]) for comp in range(3)]
            + [(flow, comp) for comp in range(3)],
            [(stretch, symmetric_slot[comp][1]) for comp in range(3)]
            + [(flow, comp) for comp in range(3)],
        )
        fields = [(stretch, symmetric_slot[comp][2]) for comp in range(3)] + [
            (flow, comp) for comp in range(3)
        ]
        return packed(
            [ref[field, x, :, bz - lanes : bz] for ref, field in fields],
            [ref[field, x, :, 0:lanes] for ref, field in fields],
        )

    tiles = []
    for x in range(bx):
        for copy in copies[x]:
            copy.wait()
        tiles.append(plane(x))
    pack_columns(sent, tiles)
    for comp in range(3):
        up_x[comp] = stretch[symmetric_slot[comp][0], bx - 1]
        down_x[comp] = stretch[symmetric_slot[comp][0], 0]
    marks.wait()


def pack_face(sent, x, high, low):
    by = high[0][0].shape[2]
    for place, (ref, field) in enumerate(high):
        sent[8 * x + place : 8 * x + place + 1, :] = ref[field, x, by - 1 : by, :]
    base = 8 * sent_planes(sent)
    for place, (ref, field) in enumerate(low):
        sent[base + 8 * x + place : base + 8 * x + place + 1, :] = ref[field, x, 0:1, :]


def sent_planes(sent):
    return (sent.shape[0] - 8) // 16


def pack_columns(sent, tiles):
    rows = jnp.concatenate(tiles, axis=0)
    cells = rows.shape[0]
    turned = rows.T
    base = sent.shape[0] - 8
    sent[base:, 0:cells] = turned[0:8, :]
    sent[base:, lanes : lanes + cells] = turned[8:16, :]


def turned_columns(ref, at, lower, upper, cells):
    slot = iota((16, cells), 0)
    parts = [
        jnp.concatenate([ref[which, at:, 0:cells], ref[which, at:, lanes : lanes + cells]], axis=0)
        for which in (lower, upper)
    ]
    rows = jnp.where(slot < 6, parts[0], parts[1])
    rows = jnp.concatenate([rows, jnp.zeros((lanes - 16, cells), jnp.float32)], axis=0)
    return rows.T


def unpack(found, y_below, y_above, z_halo):
    bx, by = z_halo.shape[:2]
    base = 16 * bx
    ring = ring_places()
    z_halo[...] = turned_columns(found, base, ring[2], ring[3], bx * by).reshape(z_halo.shape)
    corners = (
        turned_columns(found, base, ring[4], ring[5], bx * by),
        turned_columns(found, base, ring[6], ring[7], bx * by),
    )
    for x in range(bx):
        y_below[x] = found[ring[0], 8 * x : 8 * x + 8, :]
        y_above[x] = found[ring[1], 8 * (bx + x) : 8 * (bx + x) + 8, :]
        last = x * by + by - 1
        y_below[x, edge_slot : edge_slot + 1, 0:lanes] = corners[0][last : last + 1, :]
        y_above[x, edge_slot : edge_slot + 1, 0:lanes] = corners[1][x * by : x * by + 1, :]


def beside(ref, field, x, step, halo, slot):
    last = ref.shape[1] - 1
    inside = jnp.clip(x + step, 0, last)
    beyond = x == (0 if step < 0 else last)
    return lambda low, high: jnp.where(
        beyond, halo[slot, low:high, :], ref[field, inside, low:high, :]
    )


def differences(ref, field, slots, x, chunk, chunks, below, above, y_below, y_above, z_halo):
    slot_x, slot_y, slot_z = slots
    low, high = (chunk * tall, chunk * tall + tall)

    def load(first, stop):
        return ref[field, x, first:stop, :]

    result = [None, None, None]
    if slot_x is not None:
        after = beside(ref, field, x, 1, above, slot_x)(low, high)
        before = beside(ref, field, x, -1, below, slot_x)(low, high)
        result[0] = after - before
    if slot_y is not None:
        after = rows_of(load, chunk, chunks, -1, lambda: y_above[x, slot_y : slot_y + 1, :])
        before = rows_of(load, chunk, chunks, 1, lambda: y_below[x, slot_y : slot_y + 1, :])
        result[1] = after - before
    if slot_z is not None:
        rows, halo = (load(low, high), z_halo[x, low:high, :])
        after = columns_of(rows, halo, 6 + slot_z, -1)
        before = columns_of(rows, halo, slot_z, 1)
        result[2] = after - before
    return result


def collide(
    pops,
    stretch,
    flags,
    flow,
    below,
    above,
    y_below,
    y_above,
    z_halo,
    post,
    shift,
    sent,
    up_x,
    down_x,
    gas,
):
    bx, by, bz = flags.shape
    chunks = by // tall
    halos = (below, above, y_below, y_above, z_halo)
    factor = 1.0 - 0.5 / relax_time
    rate = 1.0 / relax_time

    def plane(x, carry):
        for chunk in range(chunks):
            rows = pl.ds(chunk * tall, tall)
            terms = [[], [], []]
            for field in range(6):
                slots = [None, None, None]
                for comp in range(3):
                    for axis in range(3):
                        if symmetric_slot[comp][axis] == field:
                            slots[axis] = comp
                found = differences(stretch, field, slots, x, chunk, chunks, *halos)
                for axis in range(3):
                    if slots[axis] is not None:
                        terms[slots[axis]].append(found[axis])
            force = [0.5 * polymer_coeff * (part[0] + part[1] + part[2]) for part in terms]
            density, half = (flow[3, x, rows, :], 0.5 * flow[4, x, rows, :])
            moved = [flow[comp, x, rows, :] + half * force[comp] for comp in range(3)]
            for comp in range(3):
                shift[comp, x, rows, :] = moved[comp]
            squared = moved[0] * moved[0] + moved[1] * moved[1] + moved[2] * moved[2]
            work = moved[0] * force[0] + moved[1] * force[1] + moved[2] * force[2]
            weight = rate * density
            common = weight - 1.5 * weight * squared - 3.0 * factor * work
            odd = [3.0 * weight * moved[comp] + 3.0 * factor * force[comp] for comp in range(3)]
            even = [4.5 * weight * moved[comp] + 9.0 * factor * force[comp] for comp in range(3)]
            keep = 1.0 - rate
            post[0, x, rows, :] = keep * pops[0, x, rows, :] + lattice_weights[0] * common
            for index in pairs:
                both = common + along(index, moved) * along(index, even)
                differ = along(index, odd)
                scale = lattice_weights[index]
                post[index, x, rows, :] = keep * pops[index, x, rows, :] + scale * (both + differ)
                post[index + 1, x, rows, :] = keep * pops[index + 1, x, rows, :] + scale * (
                    both - differ
                )
        return carry

    lax.fori_loop(0, bx, plane, 0)

    tiles = []
    for x in range(bx):
        gas[0, x] = jnp.where(flags[x] == 0, 1.0, 0.0)
        pack_face(
            sent,
            x,
            [(post, index) for index in y_up] + [(gas, 0)],
            [(post, index) for index in y_down] + [(gas, 0)],
        )
        tiles.append(
            packed(
                [post[index, x, :, bz - lanes : bz] for index in z_up]
                + [gas[0, x, :, bz - lanes : bz]],
                [post[index, x, :, 0:lanes] for index in z_down] + [gas[0, x, :, 0:lanes]],
            )
        )
    pack_columns(sent, tiles)
    for slot in range(5):
        up_x[slot] = post[x_up[slot], bx - 1]
        down_x[slot] = post[x_down[slot], 0]
    for comp in range(3):
        up_x[5 + comp] = flow[comp, bx - 1]
        down_x[5 + comp] = flow[comp, 0]
    up_x[8] = gas[0, bx - 1]
    down_x[8] = gas[0, 0]


def restretch(stretch, flow, below, above, y_below, y_above, z_halo, updated):
    bx, by, bz = stretch.shape[1:]
    chunks = by // tall

    def plane(x, carry):
        for chunk in range(chunks):
            rows = pl.ds(chunk * tall, tall)
            grad = [
                differences(
                    flow,
                    comp,
                    (5 + comp, 3 + comp, 3 + comp),
                    x,
                    chunk,
                    chunks,
                    below,
                    above,
                    y_below,
                    y_above,
                    z_halo,
                )
                for comp in range(3)
            ]
            part = [stretch[slot, x, rows, :] for slot in range(6)]
            full = [part[slot] + 1.0 if slot < 3 else part[slot] for slot in range(6)]

            def product(row, col):
                total = grad[row][0] * full[symmetric_slot[0][col]]
                for inner in (1, 2):
                    total = total + grad[row][inner] * full[symmetric_slot[inner][col]]
                return total

            for slot, (row, col) in enumerate(tensor_pairs):
                old = (1.0 - 1.0 / polymer_time) * part[slot]
                if row == col:
                    updated[slot, x, rows, :] = old + product(row, col)
                else:
                    updated[slot, x, rows, :] = old + 0.5 * (product(row, col) + product(col, row))
        return carry

    lax.fori_loop(0, bx, plane, 0)


up_edges = ((0, y_up.index(7)), (0, gas_slot), (1, y_down.index(9)), (1, gas_slot))
down_edges = ((0, y_up.index(10)), (0, gas_slot), (1, y_down.index(8)), (1, gas_slot))


def forward_edges(y_below, y_above, z_halo, up_out, down_out):
    bx, by = z_halo.shape[:2]
    halves = y_below.shape[2] // lanes
    sides = (y_below, y_above)
    for out, x, edges in ((up_out, bx - 1, up_edges), (down_out, 0, down_edges)):
        for place, (side, slot) in enumerate(edges):
            for half in range(halves):
                at = half * 4 + place
                out[at : at + 1, :] = sides[side][
                    x, slot : slot + 1, half * lanes : half * lanes + lanes
                ]
        out[4 * halves :, :] = z_halo[x]


def stream(
    post,
    shift,
    mass,
    flags,
    code,
    below,
    above,
    y_below,
    y_above,
    z_halo,
    edges_below,
    edges_above,
    fresh,
    settled,
    spread,
    sent,
    gas,
    low_rows,
    high_rows,
    columns,
    excess,
    heading,
):
    bx, by, bz = flags.shape
    chunks = by // tall
    halves = bz // lanes

    gas[0] = below[8]
    gas[bx + 1] = above[8]
    for x in range(bx):
        gas[x + 1] = jnp.where(flags[x] == 0, 1.0, 0.0)
        low_rows[x + 1] = y_below[x]
        high_rows[x + 1] = y_above[x]
        columns[x + 1] = z_halo[x]
    for ref, at, edges in ((edges_below, 0, up_edges), (edges_above, bx + 1, down_edges)):
        for place, (side, slot) in enumerate(edges):
            line = jnp.concatenate(
                [ref[half * 4 + place : half * 4 + place + 1, :] for half in range(halves)], axis=1
            )
            (low_rows, high_rows)[side][at, slot : slot + 1, :] = line
        columns[at] = ref[4 * halves :, :]

    def moved(load, index, source, chunk, slot, lane):
        step_y, step_z = velocity_set[index][1:]
        edges = low_rows if step_y == 1 else high_rows
        rows = rows_of(
            load, chunk, chunks, step_y, lambda: edges[source, slot : slot + 1, :]
        )
        if step_z == 0:
            return rows
        halo = rows_of(
            lambda low, high: columns[source, low:high, :],
            chunk,
            chunks,
            step_y,
            lambda: edges[source, edge_slot : edge_slot + 1, 0:lanes],
        )
        return columns_of(rows, halo, lane, step_z)

    def plane(x, carry):
        for chunk in range(chunks):
            rows = pl.ds(chunk * tall, tall)
            speed = [shift[comp, x, rows, :] for comp in range(3)]
            squared = speed[0] * speed[0] + speed[1] * speed[1] + speed[2] * speed[2]
            rest = 1.0 - 1.5 * squared
            total = post[0, x, rows, :]
            fresh[0, x, rows, :] = total
            change = jnp.zeros((tall, bz), jnp.float32)
            for first in pairs:
                proj = along(first, speed)
                equal = 2.0 * lattice_weights[first] * (rest + 4.5 * proj * proj)
                for index in (first, first + 1):
                    step_x, step_y, step_z = velocity_set[index]
                    source = x + 1 - step_x
                    if step_x == 0:
                        load = lambda low, high: post[index, x, low:high, :]
                    elif step_x == 1:
                        load = beside(post, index, x, -1, below, x_up.index(index))
                    else:
                        load = beside(post, index, x, 1, above, x_down.index(index))
                    slot, lane, gas_lane = (None, None, None)
                    if step_y != 0:
                        slot = (y_up if step_y == 1 else y_down).index(index)
                    if step_z == 1:
                        lane, gas_lane = (z_up.index(index), gas_slot)
                    elif step_z == -1:
                        lane, gas_lane = (6 + z_down.index(index), 6 + gas_slot)
                    arriving = moved(load, index, source, chunk, slot, lane)
                    from_gas = moved(
                        lambda low, high: gas[source, low:high, :],
                        index,
                        source,
                        chunk,
                        gas_slot,
                        gas_lane,
                    )
                    leaving = post[opposite_of[index], x, rows, :]
                    open_side = from_gas > 0.5
                    value = jnp.where(open_side, equal - leaving, arriving)
                    fresh[index, x, rows, :] = value
                    total = total + value
                    change = change + jnp.where(open_side, 0.0, arriving - leaving)
            read = mass[x, rows, :] + jnp.where(flags[x, rows, :] == 1, change, 0.0)
            mark = code[x, rows, :]
            liquid = mark >= 32.0
            converts = mark > 0.0
            level = jnp.where(liquid, total, 0.0)
            excess[x, rows, :] = jnp.where(converts, read - level, 0.0)
            heading[x, rows, :] = jnp.where(liquid, mark - 32.0, mark)
            settled[x, rows, :] = jnp.where(converts, level, read)
        return carry

    lax.fori_loop(0, bx, plane, 0)

    row_at, lane_at = (iota((by, bz), 0), iota((by, bz), 1))
    line_at = iota((1, bz), 1)
    tile_lane, line_lane = (iota((by, lanes), 1), iota((1, lanes), 1))

    def rows_up(rows):
        return jnp.where(row_at == 0, 0.0, pltpu.roll(rows, 1, 0))

    def rows_down(rows):
        return jnp.where(row_at == by - 1, 0.0, pltpu.roll(rows, by - 1, 0))

    def over(rows, at, step):
        if step == 1:
            return jnp.where(at == 0, 0.0, pltpu.roll(rows, 1, 1))
        return jnp.where(at == bz - 1, 0.0, pltpu.roll(rows, bz - 1, 1))

    def summed(parts):
        total = parts[0]
        for part in parts[1:]:
            total = total + part
        return total

    tile = jnp.zeros((by, lanes), jnp.float32)
    line_up = jnp.zeros((1, lanes), jnp.float32)
    line_down = jnp.zeros((1, lanes), jnp.float32)
    sent[...] = jnp.zeros(sent.shape, jnp.float32)
    for target in range(bx + 2):
        groups = {}
        for index in range(1, 19):
            step_x, step_y, step_z = velocity_set[index]
            x = target - 1 - step_x
            if 0 <= x < bx:
                part = jnp.where(heading[x] == float(index), excess[x], 0.0)
                groups.setdefault((step_y, step_z), []).append(part)
        groups = {key: summed(parts) for key, parts in groups.items()}
        total = jnp.zeros((by, bz), jnp.float32)
        line = {1: jnp.zeros((1, bz), jnp.float32), -1: jnp.zeros((1, bz), jnp.float32)}
        for step_z in (0, 1, -1):
            group = jnp.zeros((by, bz), jnp.float32)
            ends = {}
            if (0, step_z) in groups:
                group = group + groups[(0, step_z)]
            if (1, step_z) in groups:
                group = group + rows_up(groups[(1, step_z)])
                ends[1] = groups[(1, step_z)][by - 1 : by, :]
            if (-1, step_z) in groups:
                group = group + rows_down(groups[(-1, step_z)])
                ends[-1] = groups[(-1, step_z)][0:1, :]
            if step_z == 0:
                total = total + group
                for side in ends:
                    line[side] = line[side] + ends[side]
                continue
            total = total + over(group, lane_at, step_z)
            for side in ends:
                line[side] = line[side] + over(ends[side], line_at, step_z)
            if step_z == 1:
                spot, cut, roll = (target, slice(bz - lanes, bz), target + 1)
            else:
                spot, cut, roll = (8 + target, slice(0, lanes), 8 + target)
            tile = jnp.where(tile_lane == spot, pltpu.roll(group[:, cut], roll, 1), tile)
            if 1 in ends:
                line_up = jnp.where(
                    line_lane == spot, pltpu.roll(ends[1][:, cut], roll, 1), line_up
                )
            if -1 in ends:
                line_down = jnp.where(
                    line_lane == spot, pltpu.roll(ends[-1][:, cut], roll, 1), line_down
                )
        spread[target] = total
        sent[target : target + 1, :] = line[1]
        sent[8 + target : 9 + target, :] = line[-1]
    rest = jnp.zeros((lanes - by - 2, lanes), jnp.float32)
    turned = jnp.concatenate([tile, line_up, line_down, rest], axis=0).T
    sent[16:24, 0:lanes] = turned[0:8, :]
    sent[16:24, lanes : 2 * lanes] = turned[8:16, :]


def collect(found, spread, z_halo, y_below, y_above, up_out, down_out):
    by = z_halo.shape[0]
    ring = ring_places()
    tile = turned_columns(found, 16, ring[2], ring[3], lanes)[0:by, :]
    row_at = iota(tile.shape, 0)
    low = turned_columns(found, 16, ring[4], ring[5], lanes)[by : by + 1, :]
    high = turned_columns(found, 16, ring[6], ring[7], lanes)[by + 1 : by + 2, :]
    tile = tile + jnp.where(row_at == 0, low, 0.0) + jnp.where(row_at == by - 1, high, 0.0)
    z_halo[...] = tile
    y_below[...] = found[ring[0], 0:8, :]
    y_above[...] = found[ring[1], 8:16, :]
    last = spread.shape[0] - 1
    up_out[...] = with_edges(spread[last], last, z_halo, y_below, y_above)
    down_out[...] = with_edges(spread[0], 0, z_halo, y_below, y_above)


def with_edges(total, target, z_halo, y_below, y_above):
    by, bz = total.shape
    row_at, lane_at = (iota((by, bz), 0), iota((by, bz), 1))
    total = total + jnp.where(lane_at == 0, z_halo[0:by, target : target + 1], 0.0)
    total = total + jnp.where(lane_at == bz - 1, z_halo[0:by, 8 + target : 9 + target], 0.0)
    total = total + jnp.where(row_at == 0, y_below[target : target + 1, :], 0.0)
    return total + jnp.where(row_at == by - 1, y_above[target : target + 1, :], 0.0)


def add_all(settled, spread, z_halo, y_below, y_above, below, above, new_mass):
    bx = settled.shape[0]
    for x in range(bx):
        total = with_edges(spread[x + 1], x + 1, z_halo, y_below, y_above)
        if x == 0:
            total = total + below[...]
        if x == bx - 1:
            total = total + above[...]
        new_mass[x] = settled[x] + total


def passed(array, axis, step):
    devices = lax.axis_size(axis)
    return lax.ppermute(array, axis, [(i, (i + step) % devices) for i in range(devices)])


def ring_places():
    (many_y, many_z) = (lax.axis_size("gy"), lax.axis_size("gz"))
    (y, z) = (lax.axis_index("gy"), lax.axis_index("gz"))
    y_low, y_high = (lax.rem(y + many_y - 1, many_y), lax.rem(y + 1, many_y))
    z_low, z_high = (lax.rem(z + many_z - 1, many_z), lax.rem(z + 1, many_z))
    places = (
        (y_low, z),
        (y_high, z),
        (y, z_low),
        (y, z_high),
        (y_low, z_low),
        (y_low, z_high),
        (y_high, z_low),
        (y_high, z_high),
    )
    return [row * many_z + column for row, column in places]


def gathered(array):
    return lax.all_gather(array, ("gy", "gz"))


remote = pl.BlockSpec(memory_space=pltpu.HBM)


def call(body, outs, specs=None, scratch=(), cost=(0, 0)):
    extra = {} if specs is None else {"in_specs": specs}
    return pl.pallas_call(
        body,
        out_shape=[
            shape
            if isinstance(shape, jax.ShapeDtypeStruct)
            else jax.ShapeDtypeStruct(shape, jnp.float32)
            for shape in outs
        ],
        scratch_shapes=[
            pltpu.VMEM(shape, jnp.float32) if isinstance(shape, tuple) else shape
            for shape in scratch
        ],
        compiler_params=pltpu.CompilerParams(vmem_limit_bytes=40 * 1024 * 1024),
        cost_estimate=pl.CostEstimate(flops=cost[0], bytes_accessed=cost[1], transcendentals=0),
        **extra,
    )


def shards(populations, stretch, mass, flags, conv_source, conv_kind, conv_direction):
    bx, by, bz = flags.shape
    cells = bx * by * bz
    box, face, tile = ((bx, by, bz), (by, bz), (bx, by, lanes))
    rows = (bx, 8, bz)
    message = (16 * bx + 8, bz)

    pops, stretch, flags, flow, sent, up_x, down_x = call(
        moments,
        [
            (19, *box),
            (6, *box),
            jax.ShapeDtypeStruct(box, jnp.int32),
            (5, *box),
            message,
            (3, *face),
            (3, *face),
        ],
        specs=[remote] * 3,
        scratch=[pltpu.SemaphoreType.DMA((3, bx))],
        cost=(60 * cells, 150 * cells),
    )(*(pltpu.with_memory_space_constraint(array, pltpu.HBM) for array in (populations, stretch, flags)))
    found = gathered(sent)
    below, above = (passed(up_x, "gx", 1), passed(down_x, "gx", -1))

    entries = conv_source.shape[0]
    (code,) = call(
        lambda *refs: conversions(*refs, columns=bz), [(bx * by, bz)], cost=(40 * cells, 4 * cells)
    )(*(array.reshape(1, entries) for array in (conv_source, conv_kind, conv_direction)))
    code = code.reshape(box)

    y_below, y_above, z_first = call(unpack, [rows, rows, tile])(found)
    post, shift, sent, up_x, down_x = call(
        collide,
        [(19, *box), (3, *box), message, (9, *face), (9, *face)],
        scratch=[(1, *box)],
        cost=(250 * cells, 250 * cells),
    )(pops, stretch, flags, flow, below, above, y_below, y_above, z_first)
    found = gathered(sent)
    below, above = (passed(up_x, "gx", 1), passed(down_x, "gx", -1))
    post_y_below, post_y_above, z_halo = call(
        unpack, [rows, rows, tile]
    )(found)
    edges = (4 * (bz // lanes) + by, lanes)
    up_x, down_x = call(forward_edges, [edges, edges])(post_y_below, post_y_above, z_halo)
    edges_below, edges_above = (passed(up_x, "gx", 1), passed(down_x, "gx", -1))

    fresh, settled, spread, sent = call(
        stream,
        [(19, *box), box, (bx + 2, *face), (24, bz)],
        scratch=[
            (bx + 2, *face),
            (bx + 2, 8, bz),
            (bx + 2, 8, bz),
            (bx + 2, by, lanes),
            box,
            box,
        ],
        cost=(400 * cells, 250 * cells),
    )(
        post,
        shift,
        mass,
        flags,
        code,
        below,
        above,
        post_y_below,
        post_y_above,
        z_halo,
        edges_below,
        edges_above,
    )
    found = gathered(sent)
    (new_stretch,) = call(restretch, [(6, *box)], cost=(150 * cells, 80 * cells))(
        stretch, flow, below, above, y_below, y_above, z_first
    )
    z_last, last_below, last_above, up_x, down_x = call(
        collect,
        [(by, lanes), (8, bz), (8, bz), face, face],
    )(found, spread)
    below, above = (passed(up_x, "gx", 1), passed(down_x, "gx", -1))
    (new_mass,) = call(add_all, [box])(
        settled, spread, z_last, last_below, last_above, below, above
    )
    return (fresh, new_stretch, new_mass)


def solution(mesh):
    return jax.shard_map(
        shards,
        mesh=mesh,
        in_specs=(
            P(None, "gx", "gy", "gz"),
            P(None, "gx", "gy", "gz"),
            P("gx", "gy", "gz"),
            P("gx", "gy", "gz"),
            P(("gx", "gy", "gz")),
            P(("gx", "gy", "gz")),
            P(("gx", "gy", "gz")),
        ),
        out_specs=(P(None, "gx", "gy", "gz"), P(None, "gx", "gy", "gz"), P("gx", "gy", "gz")),
        check_vma=False,
    )
```

```python
import jax
import jax.numpy as jnp
from jax import lax
from jax.experimental import pallas as pl
from jax.experimental.pallas import tpu as pltpu
from jax.sharding import PartitionSpec as P

velocity_set = (
    (0, 0, 0),
    (1, 0, 0),
    (-1, 0, 0),
    (0, 1, 0),
    (0, -1, 0),
    (0, 0, 1),
    (0, 0, -1),
    (1, 1, 0),
    (-1, -1, 0),
    (1, -1, 0),
    (-1, 1, 0),
    (1, 0, 1),
    (-1, 0, -1),
    (1, 0, -1),
    (-1, 0, 1),
    (0, 1, 1),
    (0, -1, -1),
    (0, 1, -1),
    (0, -1, 1),
)
opposite_of = (0, 2, 1, 4, 3, 6, 5, 8, 7, 10, 9, 12, 11, 14, 13, 16, 15, 18, 17)
lattice_weights = (1.0 / 3.0,) + (1.0 / 18.0,) * 6 + (1.0 / 36.0,) * 12
symmetric_slot = ((0, 3, 4), (3, 1, 5), (4, 5, 2))
tensor_pairs = ((0, 0), (1, 1), (2, 2), (0, 1), (0, 2), (1, 2))
relax_time = 0.8
polymer_time = 8.0
polymer_coeff = 0.05


def moving(axis, sign):
    return tuple(index for index in range(19) if velocity_set[index][axis] == sign)


x_up, x_down = (moving(0, 1), moving(0, -1))
y_up, y_down = (moving(1, 1), moving(1, -1))
z_up, z_down = (moving(2, 1), moving(2, -1))
pairs = tuple(range(1, 19, 2))
gas_slot = 5
edge_slot = 6
lanes = 128
tall = 8


def iota(shape, dim):
    return lax.broadcasted_iota(jnp.int32, shape, dim)


def wide(tile, width):
    return jnp.concatenate([tile] * (width // tile.shape[1]), axis=1)


def rows_of(load, chunk, chunks, step, edge):
    low = chunk * tall
    if step == 0:
        return load(low, low + tall)
    if step == 1 and chunk > 0:
        return load(low - 1, low + tall - 1)
    if step == -1 and chunk < chunks - 1:
        return load(low + 1, low + tall + 1)
    rows = load(low, low + tall)
    at = iota(rows.shape, 0)
    if step == 1:
        return jnp.where(at == 0, edge(), pltpu.roll(rows, 1, 0))
    return jnp.where(at == tall - 1, edge(), pltpu.roll(rows, tall - 1, 0))


def columns_of(rows, halo, lane, step):
    width = rows.shape[1]
    at = iota(rows.shape, 1)
    if step == 1:
        edge = wide(pltpu.roll(halo, (lanes - lane) % lanes, 1), width)
        return jnp.where(at == 0, edge, pltpu.roll(rows, 1, 1))
    edge = wide(pltpu.roll(halo, lanes - 1 - lane, 1), width)
    return jnp.where(at == width - 1, edge, pltpu.roll(rows, width - 1, 1))


def packed(high, low):
    at = iota(high[0].shape, 1)
    tile = jnp.zeros_like(high[0])
    for slot, part in enumerate(high):
        tile = jnp.where(at == slot, pltpu.roll(part, slot + 1, 1), tile)
    for place, part in enumerate(low):
        slot = len(high) + place
        tile = jnp.where(at == slot, pltpu.roll(part, slot, 1), tile)
    return tile


def along(index, vector):
    total = None
    for comp in range(3):
        sign = velocity_set[index][comp]
        if sign != 0:
            term = vector[comp] if sign > 0 else -vector[comp]
            total = term if total is None else total + term
    return total


def conversions(source, kind, heading, code, *, columns):
    count = source.shape[1]
    value = (heading[...] + 32 * kind[...]).astype(jnp.float32)
    row, column = (source[...] // columns, source[...] % columns)
    by_row = jnp.where(iota((code.shape[0], count), 0) == row, value, 0.0).astype(jnp.bfloat16)
    by_column = jnp.where(iota((columns, count), 0) == column, 1.0, 0.0).astype(jnp.bfloat16)
    code[...] = lax.dot_general(
        by_row, by_column, (((1,), (1,)), ((), ())), preferred_element_type=jnp.float32
    )


def odd(axis):
    return lax.rem(lax.axis_index(axis), 2) == 1


def select(chosen, first, second):
    return jnp.where(chosen, first[...], second[...])


def swap_rows(first, second, x, high, low, flip):
    for place, ((top, top_field), (bottom, bottom_field)) in enumerate(zip(high, low)):
        by = top.shape[2]
        up = top[top_field, x, by - 1 : by, :]
        down = bottom[bottom_field, x, 0:1, :]
        first[x, place : place + 1, :] = jnp.where(flip, down, up)
        second[x, place : place + 1, :] = jnp.where(flip, up, down)
    for place in range(len(high), 8):
        first[x, place : place + 1, :] = jnp.zeros((1, first.shape[2]), jnp.float32)
        second[x, place : place + 1, :] = jnp.zeros((1, first.shape[2]), jnp.float32)


def column_rows(tiles):
    return jnp.concatenate(tiles, axis=0).T[0:16, :]


def row_columns(rows):
    rest = jnp.zeros((lanes - rows.shape[0], rows.shape[1]), jnp.float32)
    return jnp.concatenate([rows, rest], axis=0).T


def moments(
    pops_in,
    stretch_in,
    flags_in,
    pops,
    stretch,
    flags,
    flow,
    columns,
    y_first,
    y_second,
    x_first,
    x_second,
    v_first,
    v_second,
    sems,
):
    bx, by, bz = flags.shape
    flip_x, flip_y = (odd("gx"), odd("gy"))
    copies = []
    for x in range(bx):
        copies.append(
            (
                pltpu.make_async_copy(pops_in.at[:, x], pops.at[:, x], sems.at[0, x]),
                pltpu.make_async_copy(stretch_in.at[:, x], stretch.at[:, x], sems.at[1, x]),
            )
        )
    marks = pltpu.make_async_copy(flags_in, flags, sems.at[2, 0])
    for pair in copies:
        for copy in pair:
            copy.start()
    marks.start()
    along_y = [(stretch, symmetric_slot[comp][1]) for comp in range(3)]
    along_z = [(stretch, symmetric_slot[comp][2]) for comp in range(3)]
    speed = [(flow, comp) for comp in range(3)]

    def plane(x):
        for chunk in range(by // tall):
            rows = pl.ds(chunk * tall, tall)
            part = [pops[index, x, rows, :] for index in range(19)]
            density = part[0]
            for index in range(1, 19):
                density = density + part[index]
            inverse = 1.0 / density
            for comp in range(3):
                total = None
                for index in pairs:
                    sign = velocity_set[index][comp]
                    if sign != 0:
                        term = part[index] - part[index + 1]
                        term = term if sign > 0 else -term
                        total = term if total is None else total + term
                flow[comp, x, rows, :] = total * inverse
            flow[3, x, rows, :] = density
            flow[4, x, rows, :] = inverse
        swap_rows(y_first, y_second, x, along_y + speed, along_y + speed, flip_y)
        return packed(
            [ref[field, x, :, bz - lanes : bz] for ref, field in along_z + speed],
            [ref[field, x, :, 0:lanes] for ref, field in along_z + speed],
        )

    tiles = []
    for x in range(bx):
        for copy in copies[x]:
            copy.wait()
        tiles.append(plane(x))
    columns[...] = column_rows(tiles)
    marks.wait()
    gas = [jnp.where(flags[x] == 0, 1.0, 0.0) for x in (bx - 1, 0)]
    for out, last in ((x_first, flip_x), (x_second, jnp.logical_not(flip_x))):
        for comp in range(3):
            slot = symmetric_slot[comp][0]
            out[comp] = jnp.where(last, stretch[slot, 0], stretch[slot, bx - 1])
    for out, last in ((v_first, flip_x), (v_second, jnp.logical_not(flip_x))):
        for comp in range(3):
            out[comp] = jnp.where(last, flow[comp, 0], flow[comp, bx - 1])
        out[3] = jnp.where(last, gas[1], gas[0])


def beside(ref, field, x, step, halo, slot):
    last = ref.shape[1] - 1
    inside = jnp.clip(x + step, 0, last)
    beyond = x == (0 if step < 0 else last)
    return lambda low, high: jnp.where(
        beyond, halo[slot, low:high, :], ref[field, inside, low:high, :]
    )


def differences(ref, field, slots, x, chunk, chunks, below, above, y_below, y_above, z_halo):
    slot_x, slot_y, slot_z = slots
    low, high = (chunk * tall, chunk * tall + tall)

    def load(first, stop):
        return ref[field, x, first:stop, :]

    result = [None, None, None]
    if slot_x is not None:
        after = beside(ref, field, x, 1, above, slot_x)(low, high)
        before = beside(ref, field, x, -1, below, slot_x)(low, high)
        result[0] = after - before
    if slot_y is not None:
        after = rows_of(load, chunk, chunks, -1, lambda: y_above[x, slot_y : slot_y + 1, :])
        before = rows_of(load, chunk, chunks, 1, lambda: y_below[x, slot_y : slot_y + 1, :])
        result[1] = after - before
    if slot_z is not None:
        rows, halo = (load(low, high), z_halo[x, low:high, :])
        after = columns_of(rows, halo, 6 + slot_z, -1)
        before = columns_of(rows, halo, slot_z, 1)
        result[2] = after - before
    return result


def collide(
    pops,
    stretch,
    flags,
    flow,
    x_first,
    x_second,
    y_first,
    y_second,
    z_rows,
    post,
    shift,
    columns,
    ahead,
    behind,
    up_first,
    up_second,
    below,
    above,
    y_below,
    y_above,
    z_halo,
    gas,
):
    bx, by, bz = flags.shape
    chunks = by // tall
    halos = (below, above, y_below, y_above, z_halo)
    flip_x, flip_y = (odd("gx"), odd("gy"))
    below[...] = select(flip_x, x_first, x_second)
    above[...] = select(flip_x, x_second, x_first)
    y_below[...] = select(flip_y, y_first, y_second)
    y_above[...] = select(flip_y, y_second, y_first)
    z_halo[...] = row_columns(z_rows[...]).reshape(z_halo.shape)
    factor = 1.0 - 0.5 / relax_time
    rate = 1.0 / relax_time

    def plane(x, carry):
        for chunk in range(chunks):
            rows = pl.ds(chunk * tall, tall)
            terms = [[], [], []]
            for field in range(6):
                slots = [None, None, None]
                for comp in range(3):
                    for axis in range(3):
                        if symmetric_slot[comp][axis] == field:
                            slots[axis] = comp
                found = differences(stretch, field, slots, x, chunk, chunks, *halos)
                for axis in range(3):
                    if slots[axis] is not None:
                        terms[slots[axis]].append(found[axis])
            force = [0.5 * polymer_coeff * (part[0] + part[1] + part[2]) for part in terms]
            density, half = (flow[3, x, rows, :], 0.5 * flow[4, x, rows, :])
            moved = [flow[comp, x, rows, :] + half * force[comp] for comp in range(3)]
            for comp in range(3):
                shift[comp, x, rows, :] = moved[comp]
            squared = moved[0] * moved[0] + moved[1] * moved[1] + moved[2] * moved[2]
            work = moved[0] * force[0] + moved[1] * force[1] + moved[2] * force[2]
            weight = rate * density
            common = weight - 1.5 * weight * squared - 3.0 * factor * work
            odd = [3.0 * weight * moved[comp] + 3.0 * factor * force[comp] for comp in range(3)]
            even = [4.5 * weight * moved[comp] + 9.0 * factor * force[comp] for comp in range(3)]
            keep = 1.0 - rate
            post[0, x, rows, :] = keep * pops[0, x, rows, :] + lattice_weights[0] * common
            for index in pairs:
                both = common + along(index, moved) * along(index, even)
                differ = along(index, odd)
                scale = lattice_weights[index]
                post[index, x, rows, :] = keep * pops[index, x, rows, :] + scale * (both + differ)
                post[index + 1, x, rows, :] = keep * pops[index + 1, x, rows, :] + scale * (
                    both - differ
                )
        return carry

    lax.fori_loop(0, bx, plane, 0)

    tiles = []
    for x in range(bx):
        gas[0, x] = jnp.where(flags[x] == 0, 1.0, 0.0)
        swap_rows(
            up_first,
            up_second,
            x,
            [(post, index) for index in y_up] + [(gas, 0)],
            [(post, index) for index in y_down] + [(gas, 0)],
            flip_y,
        )
        tiles.append(
            packed(
                [post[index, x, :, bz - lanes : bz] for index in z_up]
                + [gas[0, x, :, bz - lanes : bz]],
                [post[index, x, :, 0:lanes] for index in z_down] + [gas[0, x, :, 0:lanes]],
            )
        )
    columns[...] = column_rows(tiles)
    for slot in range(5):
        up, down = (post[x_up[slot], bx - 1], post[x_down[slot], 0])
        ahead[slot] = jnp.where(flip_x, down, up)
        behind[slot] = jnp.where(flip_x, up, down)


def restretch(
    stretch,
    flow,
    x_first,
    x_second,
    y_first,
    y_second,
    z_rows,
    updated,
    below,
    above,
    y_below,
    y_above,
    z_halo,
):
    bx, by, bz = stretch.shape[1:]
    chunks = by // tall
    flip_x, flip_y = (odd("gx"), odd("gy"))
    for comp in range(3):
        below[comp] = jnp.where(flip_x, x_first[comp], x_second[comp])
        above[comp] = jnp.where(flip_x, x_second[comp], x_first[comp])
    y_below[...] = select(flip_y, y_first, y_second)
    y_above[...] = select(flip_y, y_second, y_first)
    z_halo[...] = row_columns(z_rows[...]).reshape(z_halo.shape)

    def plane(x, carry):
        for chunk in range(chunks):
            rows = pl.ds(chunk * tall, tall)
            grad = [
                differences(
                    flow,
                    comp,
                    (comp, 3 + comp, 3 + comp),
                    x,
                    chunk,
                    chunks,
                    below,
                    above,
                    y_below,
                    y_above,
                    z_halo,
                )
                for comp in range(3)
            ]
            part = [stretch[slot, x, rows, :] for slot in range(6)]
            full = [part[slot] + 1.0 if slot < 3 else part[slot] for slot in range(6)]

            def product(row, col):
                total = grad[row][0] * full[symmetric_slot[0][col]]
                for inner in (1, 2):
                    total = total + grad[row][inner] * full[symmetric_slot[inner][col]]
                return total

            for slot, (row, col) in enumerate(tensor_pairs):
                old = (1.0 - 1.0 / polymer_time) * part[slot]
                if row == col:
                    updated[slot, x, rows, :] = old + product(row, col)
                else:
                    updated[slot, x, rows, :] = old + 0.5 * (product(row, col) + product(col, row))
        return carry

    lax.fori_loop(0, bx, plane, 0)


def forward_rows(first, second, z_rows, first_out, second_out):
    bx, by = (first.shape[0], z_rows.shape[1] // first.shape[0])
    bz = first.shape[2]
    flip = odd("gy")
    tile = row_columns(z_rows[...])
    for x in range(bx):
        first_out[x] = first[x]
        second_out[x] = second[x]
        up = tile[x * by + by - 1 : x * by + by, :]
        down = tile[x * by : x * by + 1, :]
        first_out[x, edge_slot : edge_slot + 1, :] = wide(jnp.where(flip, down, up), bz)
        second_out[x, edge_slot : edge_slot + 1, :] = wide(jnp.where(flip, up, down), bz)


up_edges = ((0, y_up.index(7)), (0, gas_slot), (1, y_down.index(9)), (1, gas_slot))
down_edges = ((0, y_up.index(10)), (0, gas_slot), (1, y_down.index(8)), (1, gas_slot))


def forward_edges(y_first, y_second, z_rows, first_out, second_out):
    bx, bz = (y_first.shape[0], y_first.shape[2])
    halves = bz // lanes
    flip_x, flip_y = (odd("gx"), odd("gy"))
    for half in range(halves):
        cut = slice(half * lanes, half * lanes + lanes)
        for place in range(4):
            found = []
            for x, edges in ((bx - 1, up_edges), (0, down_edges)):
                side, slot = edges[place]
                one = y_first[x, slot : slot + 1, cut]
                two = y_second[x, slot : slot + 1, cut]
                found.append(jnp.where(flip_y, one, two) if side == 0 else jnp.where(flip_y, two, one))
            at = half * 4 + place
            first_out[at : at + 1, :] = jnp.where(flip_x, found[1], found[0])
            second_out[at : at + 1, :] = jnp.where(flip_x, found[0], found[1])
    first_out[4 * halves :, :] = z_rows[...]
    second_out[4 * halves :, :] = z_rows[...]


def stream(
    post,
    shift,
    mass,
    flags,
    code,
    v_first,
    v_second,
    x_first,
    x_second,
    y_first,
    y_second,
    z_rows,
    edges_first,
    edges_second,
    fresh,
    settled,
    spread,
    lines,
    out_z,
    below,
    above,
    gas,
    low_rows,
    high_rows,
    columns,
    excess,
    heading,
):
    bx, by, bz = flags.shape
    chunks = by // tall
    halves = bz // lanes
    flip_x, flip_y = (odd("gx"), odd("gy"))

    below[...] = select(flip_x, x_first, x_second)
    above[...] = select(flip_x, x_second, x_first)
    gas[0] = jnp.where(flip_x, v_first[3], v_second[3])
    gas[bx + 1] = jnp.where(flip_x, v_second[3], v_first[3])
    tile = row_columns(z_rows[...])
    for x in range(bx):
        gas[x + 1] = jnp.where(flags[x] == 0, 1.0, 0.0)
        low_rows[x + 1] = jnp.where(flip_y, y_first[x], y_second[x])
        high_rows[x + 1] = jnp.where(flip_y, y_second[x], y_first[x])
        columns[x + 1] = tile[x * by : x * by + by, :]
    edges_below = select(flip_x, edges_first, edges_second)
    edges_above = select(flip_x, edges_second, edges_first)
    for found, at, x, edges in (
        (edges_below, 0, bx - 1, up_edges),
        (edges_above, bx + 1, 0, down_edges),
    ):
        for place, (side, slot) in enumerate(edges):
            line = jnp.concatenate(
                [found[half * 4 + place : half * 4 + place + 1, :] for half in range(halves)],
                axis=1,
            )
            (low_rows, high_rows)[side][at, slot : slot + 1, :] = line
        columns[at] = row_columns(found[4 * halves :, :])[x * by : x * by + by, :]

    def moved(load, index, source, chunk, slot, lane):
        step_y, step_z = velocity_set[index][1:]
        edges = low_rows if step_y == 1 else high_rows
        rows = rows_of(
            load, chunk, chunks, step_y, lambda: edges[source, slot : slot + 1, :]
        )
        if step_z == 0:
            return rows
        halo = rows_of(
            lambda low, high: columns[source, low:high, :],
            chunk,
            chunks,
            step_y,
            lambda: edges[source, edge_slot : edge_slot + 1, 0:lanes],
        )
        return columns_of(rows, halo, lane, step_z)

    def plane(x, carry):
        for chunk in range(chunks):
            rows = pl.ds(chunk * tall, tall)
            speed = [shift[comp, x, rows, :] for comp in range(3)]
            squared = speed[0] * speed[0] + speed[1] * speed[1] + speed[2] * speed[2]
            rest = 1.0 - 1.5 * squared
            total = post[0, x, rows, :]
            fresh[0, x, rows, :] = total
            change = jnp.zeros((tall, bz), jnp.float32)
            for first in pairs:
                proj = along(first, speed)
                equal = 2.0 * lattice_weights[first] * (rest + 4.5 * proj * proj)
                for index in (first, first + 1):
                    step_x, step_y, step_z = velocity_set[index]
                    source = x + 1 - step_x
                    if step_x == 0:
                        load = lambda low, high: post[index, x, low:high, :]
                    elif step_x == 1:
                        load = beside(post, index, x, -1, below, x_up.index(index))
                    else:
                        load = beside(post, index, x, 1, above, x_down.index(index))
                    slot, lane, gas_lane = (None, None, None)
                    if step_y != 0:
                        slot = (y_up if step_y == 1 else y_down).index(index)
                    if step_z == 1:
                        lane, gas_lane = (z_up.index(index), gas_slot)
                    elif step_z == -1:
                        lane, gas_lane = (6 + z_down.index(index), 6 + gas_slot)
                    arriving = moved(load, index, source, chunk, slot, lane)
                    from_gas = moved(
                        lambda low, high: gas[source, low:high, :],
                        index,
                        source,
                        chunk,
                        gas_slot,
                        gas_lane,
                    )
                    leaving = post[opposite_of[index], x, rows, :]
                    open_side = from_gas > 0.5
                    value = jnp.where(open_side, equal - leaving, arriving)
                    fresh[index, x, rows, :] = value
                    total = total + value
                    change = change + jnp.where(open_side, 0.0, arriving - leaving)
            read = mass[x, rows, :] + jnp.where(flags[x, rows, :] == 1, change, 0.0)
            mark = code[x, rows, :]
            liquid = mark >= 32.0
            converts = mark > 0.0
            level = jnp.where(liquid, total, 0.0)
            excess[x, rows, :] = jnp.where(converts, read - level, 0.0)
            heading[x, rows, :] = jnp.where(liquid, mark - 32.0, mark)
            settled[x, rows, :] = jnp.where(converts, level, read)
        return carry

    lax.fori_loop(0, bx, plane, 0)

    row_at, lane_at = (iota((by, bz), 0), iota((by, bz), 1))
    line_at = iota((1, bz), 1)
    tile_lane, line_lane = (iota((by, lanes), 1), iota((1, lanes), 1))

    def rows_up(rows):
        return jnp.where(row_at == 0, 0.0, pltpu.roll(rows, 1, 0))

    def rows_down(rows):
        return jnp.where(row_at == by - 1, 0.0, pltpu.roll(rows, by - 1, 0))

    def over(rows, at, step):
        if step == 1:
            return jnp.where(at == 0, 0.0, pltpu.roll(rows, 1, 1))
        return jnp.where(at == bz - 1, 0.0, pltpu.roll(rows, bz - 1, 1))

    def summed(parts):
        total = parts[0]
        for part in parts[1:]:
            total = total + part
        return total

    tile = jnp.zeros((by, lanes), jnp.float32)
    line_up = jnp.zeros((1, lanes), jnp.float32)
    line_down = jnp.zeros((1, lanes), jnp.float32)
    lines[...] = jnp.zeros(lines.shape, jnp.float32)
    for target in range(bx + 2):
        groups = {}
        for index in range(1, 19):
            step_x, step_y, step_z = velocity_set[index]
            x = target - 1 - step_x
            if 0 <= x < bx:
                part = jnp.where(heading[x] == float(index), excess[x], 0.0)
                groups.setdefault((step_y, step_z), []).append(part)
        groups = {key: summed(parts) for key, parts in groups.items()}
        total = jnp.zeros((by, bz), jnp.float32)
        line = {1: jnp.zeros((1, bz), jnp.float32), -1: jnp.zeros((1, bz), jnp.float32)}
        for step_z in (0, 1, -1):
            group = jnp.zeros((by, bz), jnp.float32)
            ends = {}
            if (0, step_z) in groups:
                group = group + groups[(0, step_z)]
            if (1, step_z) in groups:
                group = group + rows_up(groups[(1, step_z)])
                ends[1] = groups[(1, step_z)][by - 1 : by, :]
            if (-1, step_z) in groups:
                group = group + rows_down(groups[(-1, step_z)])
                ends[-1] = groups[(-1, step_z)][0:1, :]
            if step_z == 0:
                total = total + group
                for side in ends:
                    line[side] = line[side] + ends[side]
                continue
            total = total + over(group, lane_at, step_z)
            for side in ends:
                line[side] = line[side] + over(ends[side], line_at, step_z)
            if step_z == 1:
                spot, cut, roll = (target, slice(bz - lanes, bz), target + 1)
            else:
                spot, cut, roll = (8 + target, slice(0, lanes), 8 + target)
            tile = jnp.where(tile_lane == spot, pltpu.roll(group[:, cut], roll, 1), tile)
            if 1 in ends:
                line_up = jnp.where(
                    line_lane == spot, pltpu.roll(ends[1][:, cut], roll, 1), line_up
                )
            if -1 in ends:
                line_down = jnp.where(
                    line_lane == spot, pltpu.roll(ends[-1][:, cut], roll, 1), line_down
                )
        spread[target] = total
        lines[target : target + 1, :] = line[1]
        lines[8 + target : 9 + target, :] = line[-1]
    rest = jnp.zeros((lanes - by - 2, lanes), jnp.float32)
    out_z[...] = column_rows([tile, line_up, line_down, rest])


def add_corners(lines, z_rows, first, second, *, by):
    bz = lines.shape[1]
    at = iota((8, bz), 1)
    flip = odd("gy")
    found = []
    for side in range(2):
        corner = z_rows[:, by + side : by + side + 1]
        line = lines[8 * side : 8 * side + 8, :] + jnp.where(at == 0, corner[0:8, :], 0.0)
        found.append(line + jnp.where(at == bz - 1, corner[8:16, :], 0.0))
    first[...] = jnp.where(flip, found[1], found[0])
    second[...] = jnp.where(flip, found[0], found[1])


def with_edges(total, target, tile, y_below, y_above):
    by, bz = total.shape
    row_at, lane_at = (iota((by, bz), 0), iota((by, bz), 1))
    total = total + jnp.where(lane_at == 0, tile[0:by, target : target + 1], 0.0)
    total = total + jnp.where(lane_at == bz - 1, tile[0:by, 8 + target : 9 + target], 0.0)
    total = total + jnp.where(row_at == 0, y_below[target : target + 1, :], 0.0)
    return total + jnp.where(row_at == by - 1, y_above[target : target + 1, :], 0.0)


def add_faces(spread, z_rows, y_first, y_second, first, second):
    last = spread.shape[0] - 1
    flip_x, flip_y = (odd("gx"), odd("gy"))
    tile = row_columns(z_rows[...])
    y_below, y_above = (select(flip_y, y_first, y_second), select(flip_y, y_second, y_first))
    up = with_edges(spread[last], last, tile, y_below, y_above)
    down = with_edges(spread[0], 0, tile, y_below, y_above)
    first[...] = jnp.where(flip_x, down, up)
    second[...] = jnp.where(flip_x, up, down)


def add_all(settled, spread, z_rows, y_first, y_second, x_first, x_second, new_mass):
    bx = settled.shape[0]
    flip_x, flip_y = (odd("gx"), odd("gy"))
    tile = row_columns(z_rows[...])
    y_below, y_above = (select(flip_y, y_first, y_second), select(flip_y, y_second, y_first))
    for x in range(bx):
        total = with_edges(spread[x + 1], x + 1, tile, y_below, y_above)
        if x == 0:
            total = total + select(flip_x, x_first, x_second)
        if x == bx - 1:
            total = total + select(flip_x, x_second, x_first)
        new_mass[x] = settled[x] + total


def swapped(first, second, axis):
    devices = lax.axis_size(axis)
    ahead = [(i, (i + 1) % devices if i % 2 == 0 else i - 1) for i in range(devices)]
    behind = [(i, (i - 1) % devices if i % 2 == 0 else (i + 1) % devices) for i in range(devices)]
    return lax.ppermute(first, axis, ahead), lax.ppermute(second, axis, behind)


def both_ways(rows, lower):
    devices = lax.axis_size("gz")
    before = lax.ppermute(rows, "gz", [(i, (i + 1) % devices) for i in range(devices)])
    if devices == 2:
        return before
    after = lax.ppermute(rows, "gz", [(i, (i - 1) % devices) for i in range(devices)])
    return jnp.where(iota(rows.shape, 0) < lower, before, after)


remote = pl.BlockSpec(memory_space=pltpu.HBM)


def call(body, outs, specs=None, scratch=(), cost=(0, 0)):
    extra = {} if specs is None else {"in_specs": specs}
    return pl.pallas_call(
        body,
        out_shape=[
            shape
            if isinstance(shape, jax.ShapeDtypeStruct)
            else jax.ShapeDtypeStruct(shape, jnp.float32)
            for shape in outs
        ],
        scratch_shapes=[
            pltpu.VMEM(shape, jnp.float32) if isinstance(shape, tuple) else shape
            for shape in scratch
        ],
        compiler_params=pltpu.CompilerParams(vmem_limit_bytes=40 * 1024 * 1024),
        cost_estimate=pl.CostEstimate(flops=cost[0], bytes_accessed=cost[1], transcendentals=0),
        **extra,
    )


def shards(populations, stretch, mass, flags, conv_source, conv_kind, conv_direction):
    bx, by, bz = flags.shape
    cells = bx * by * bz
    box, face, tile = ((bx, by, bz), (by, bz), (bx, by, lanes))
    rows, columns = ((bx, 8, bz), (16, bx * by))

    pops, stretch, flags, flow, z_out, y_one, y_two, x_one, x_two, v_one, v_two = call(
        moments,
        [
            (19, *box),
            (6, *box),
            jax.ShapeDtypeStruct(box, jnp.int32),
            (5, *box),
            columns,
            rows,
            rows,
            (3, *face),
            (3, *face),
            (4, *face),
            (4, *face),
        ],
        specs=[remote] * 3,
        scratch=[pltpu.SemaphoreType.DMA((3, bx))],
        cost=(60 * cells, 150 * cells),
    )(
        *(
            pltpu.with_memory_space_constraint(array, pltpu.HBM)
            for array in (populations, stretch, flags)
        )
    )
    stretch_x = swapped(x_one, x_two, "gx")
    z_first = both_ways(z_out, 6)
    y_first = swapped(y_one, y_two, "gy")
    flow_x = swapped(v_one, v_two, "gx")

    entries = conv_source.shape[0]
    (code,) = call(
        lambda *refs: conversions(*refs, columns=bz), [(bx * by, bz)], cost=(40 * cells, 4 * cells)
    )(*(array.reshape(1, entries) for array in (conv_source, conv_kind, conv_direction)))
    code = code.reshape(box)

    post, shift, z_out, x_one, x_two, y_one, y_two = call(
        collide,
        [(19, *box), (3, *box), columns, (5, *face), (5, *face), rows, rows],
        scratch=[(3, *face), (3, *face), rows, rows, tile, (1, *box)],
        cost=(250 * cells, 250 * cells),
    )(pops, stretch, flags, flow, *stretch_x, *y_first, z_first)
    post_x = swapped(x_one, x_two, "gx")
    z_post = both_ways(z_out, 6)
    y_one, y_two = call(forward_rows, [rows, rows])(y_one, y_two, z_post)
    post_y = swapped(y_one, y_two, "gy")
    edges = (4 * (bz // lanes) + 16, lanes)
    x_one, x_two = call(forward_edges, [edges, edges])(*post_y, z_post)
    edges_x = swapped(x_one, x_two, "gx")

    (new_stretch,) = call(
        restretch,
        [(6, *box)],
        scratch=[(3, *face), (3, *face), rows, rows, tile],
        cost=(150 * cells, 80 * cells),
    )(stretch, flow, *flow_x, *y_first, z_first)

    fresh, settled, spread, lines, z_out = call(
        stream,
        [(19, *box), box, (bx + 2, *face), (16, bz), columns],
        scratch=[
            (5, *face),
            (5, *face),
            (bx + 2, *face),
            (bx + 2, 8, bz),
            (bx + 2, 8, bz),
            (bx + 2, by, lanes),
            box,
            box,
        ],
        cost=(400 * cells, 250 * cells),
    )(post, shift, mass, flags, code, *flow_x, *post_x, *post_y, z_post, *edges_x)
    z_last = both_ways(z_out, 8)
    y_one, y_two = call(lambda *refs: add_corners(*refs, by=by), [(8, bz), (8, bz)])(
        lines, z_last
    )
    last_y = swapped(y_one, y_two, "gy")
    x_one, x_two = call(add_faces, [face, face])(spread, z_last, *last_y)
    last_x = swapped(x_one, x_two, "gx")
    (new_mass,) = call(add_all, [box])(settled, spread, z_last, *last_y, *last_x)
    return (fresh, new_stretch, new_mass)


def solution(mesh):
    return jax.shard_map(
        shards,
        mesh=mesh,
        in_specs=(
            P(None, "gx", "gy", "gz"),
            P(None, "gx", "gy", "gz"),
            P("gx", "gy", "gz"),
            P("gx", "gy", "gz"),
            P(("gx", "gy", "gz")),
            P(("gx", "gy", "gz")),
            P(("gx", "gy", "gz")),
        ),
        out_specs=(P(None, "gx", "gy", "gz"), P(None, "gx", "gy", "gz"), P("gx", "gy", "gz")),
        check_vma=False,
    )
```

```python
import jax
import jax.numpy as jnp
from jax import lax
from jax.experimental import pallas as pl
from jax.experimental.pallas import tpu as pltpu
from jax.sharding import PartitionSpec as P

velocity_set = (
    (0, 0, 0),
    (1, 0, 0),
    (-1, 0, 0),
    (0, 1, 0),
    (0, -1, 0),
    (0, 0, 1),
    (0, 0, -1),
    (1, 1, 0),
    (-1, -1, 0),
    (1, -1, 0),
    (-1, 1, 0),
    (1, 0, 1),
    (-1, 0, -1),
    (1, 0, -1),
    (-1, 0, 1),
    (0, 1, 1),
    (0, -1, -1),
    (0, 1, -1),
    (0, -1, 1),
)
opposite_of = (0, 2, 1, 4, 3, 6, 5, 8, 7, 10, 9, 12, 11, 14, 13, 16, 15, 18, 17)
lattice_weights = (1.0 / 3.0,) + (1.0 / 18.0,) * 6 + (1.0 / 36.0,) * 12
symmetric_slot = ((0, 3, 4), (3, 1, 5), (4, 5, 2))
tensor_pairs = ((0, 0), (1, 1), (2, 2), (0, 1), (0, 2), (1, 2))
relax_time = 0.8
polymer_time = 8.0
polymer_coeff = 0.05


def moving(axis, sign):
    return tuple(index for index in range(19) if velocity_set[index][axis] == sign)


x_up, x_down = (moving(0, 1), moving(0, -1))
y_up, y_down = (moving(1, 1), moving(1, -1))
z_up, z_down = (moving(2, 1), moving(2, -1))
pairs = tuple(range(1, 19, 2))
gas_slot = 5
edge_slot = 6
lanes = 128
tall = 8


def iota(shape, dim):
    return lax.broadcasted_iota(jnp.int32, shape, dim)


def wide(tile, width):
    return jnp.concatenate([tile] * (width // tile.shape[1]), axis=1)


def rows_of(load, chunk, chunks, step, edge):
    low = chunk * tall
    if step == 0:
        return load(low, low + tall)
    if step == 1 and chunk > 0:
        return load(low - 1, low + tall - 1)
    if step == -1 and chunk < chunks - 1:
        return load(low + 1, low + tall + 1)
    rows = load(low, low + tall)
    at = iota(rows.shape, 0)
    if step == 1:
        return jnp.where(at == 0, edge(), pltpu.roll(rows, 1, 0))
    return jnp.where(at == tall - 1, edge(), pltpu.roll(rows, tall - 1, 0))


def columns_of(rows, halo, lane, step):
    width = rows.shape[1]
    at = iota(rows.shape, 1)
    if step == 1:
        edge = wide(pltpu.roll(halo, (lanes - lane) % lanes, 1), width)
        return jnp.where(at == 0, edge, pltpu.roll(rows, 1, 1))
    edge = wide(pltpu.roll(halo, lanes - 1 - lane, 1), width)
    return jnp.where(at == width - 1, edge, pltpu.roll(rows, width - 1, 1))


def packed(high, low):
    at = iota(high[0].shape, 1)
    tile = jnp.zeros_like(high[0])
    for slot, part in enumerate(high):
        tile = jnp.where(at == slot, pltpu.roll(part, slot + 1, 1), tile)
    for place, part in enumerate(low):
        slot = len(high) + place
        tile = jnp.where(at == slot, pltpu.roll(part, slot, 1), tile)
    return tile


def along(index, vector):
    total = None
    for comp in range(3):
        sign = velocity_set[index][comp]
        if sign != 0:
            term = vector[comp] if sign > 0 else -vector[comp]
            total = term if total is None else total + term
    return total


def conversions(source, kind, heading, code, *, columns):
    count = source.shape[1]
    value = (heading[...] + 32 * kind[...]).astype(jnp.float32)
    row, column = (source[...] // columns, source[...] % columns)
    by_row = jnp.where(iota((code.shape[0], count), 0) == row, value, 0.0).astype(jnp.bfloat16)
    by_column = jnp.where(iota((columns, count), 0) == column, 1.0, 0.0).astype(jnp.bfloat16)
    code[...] = lax.dot_general(
        by_row, by_column, (((1,), (1,)), ((), ())), preferred_element_type=jnp.float32
    )


def odd(axis):
    return lax.rem(lax.axis_index(axis), 2) == 1


def select(chosen, first, second):
    return jnp.where(chosen, first[...], second[...])


def swap_rows(first, second, x, high, low, flip):
    for place, ((top, top_field), (bottom, bottom_field)) in enumerate(zip(high, low)):
        by = top.shape[2]
        up = top[top_field, x, by - 1 : by, :]
        down = bottom[bottom_field, x, 0:1, :]
        first[x, place : place + 1, :] = jnp.where(flip, down, up)
        second[x, place : place + 1, :] = jnp.where(flip, up, down)
    for place in range(len(high), 8):
        first[x, place : place + 1, :] = jnp.zeros((1, first.shape[2]), jnp.float32)
        second[x, place : place + 1, :] = jnp.zeros((1, first.shape[2]), jnp.float32)


def column_rows(tiles):
    return jnp.concatenate(tiles, axis=0).T[0:16, :]


def row_columns(rows):
    rest = jnp.zeros((lanes - rows.shape[0], rows.shape[1]), jnp.float32)
    return jnp.concatenate([rows, rest], axis=0).T


def moments(
    pops_in,
    stretch_in,
    flags_in,
    pops,
    stretch,
    flags,
    flow,
    columns,
    y_first,
    y_second,
    x_first,
    x_second,
    sems,
):
    bx, by, bz = flags.shape
    flip_x, flip_y = (odd("gx"), odd("gy"))
    copies = []
    for x in range(bx):
        copies.append(
            (
                pltpu.make_async_copy(pops_in.at[:, x], pops.at[:, x], sems.at[0, x]),
                pltpu.make_async_copy(stretch_in.at[:, x], stretch.at[:, x], sems.at[1, x]),
            )
        )
    marks = pltpu.make_async_copy(flags_in, flags, sems.at[2, 0])
    for pair in copies:
        for copy in pair:
            copy.start()
    marks.start()
    along_y = [(stretch, symmetric_slot[comp][1]) for comp in range(3)]
    along_z = [(stretch, symmetric_slot[comp][2]) for comp in range(3)]
    speed = [(flow, comp) for comp in range(3)]

    def plane(x):
        for chunk in range(by // tall):
            rows = pl.ds(chunk * tall, tall)
            part = [pops[index, x, rows, :] for index in range(19)]
            density = part[0]
            for index in range(1, 19):
                density = density + part[index]
            inverse = 1.0 / density
            for comp in range(3):
                total = None
                for index in pairs:
                    sign = velocity_set[index][comp]
                    if sign != 0:
                        term = part[index] - part[index + 1]
                        term = term if sign > 0 else -term
                        total = term if total is None else total + term
                flow[comp, x, rows, :] = total * inverse
            flow[3, x, rows, :] = density
            flow[4, x, rows, :] = inverse
        swap_rows(y_first, y_second, x, along_y + speed, along_y + speed, flip_y)
        return packed(
            [ref[field, x, :, bz - lanes : bz] for ref, field in along_z + speed],
            [ref[field, x, :, 0:lanes] for ref, field in along_z + speed],
        )

    tiles = []
    for x in range(bx):
        for copy in copies[x]:
            copy.wait()
        tiles.append(plane(x))
    columns[...] = column_rows(tiles)
    marks.wait()
    for out, last in ((x_first, flip_x), (x_second, jnp.logical_not(flip_x))):
        for comp in range(3):
            slot = symmetric_slot[comp][0]
            out[comp] = jnp.where(last, stretch[slot, 0], stretch[slot, bx - 1])
            out[3 + comp] = jnp.where(last, flow[comp, 0], flow[comp, bx - 1])


def beside(ref, field, x, step, halo, slot):
    last = ref.shape[1] - 1
    inside = jnp.clip(x + step, 0, last)
    beyond = x == (0 if step < 0 else last)
    return lambda low, high: jnp.where(
        beyond, halo[slot, low:high, :], ref[field, inside, low:high, :]
    )


def differences(ref, field, slots, x, chunk, chunks, below, above, y_below, y_above, z_halo):
    slot_x, slot_y, slot_z = slots
    low, high = (chunk * tall, chunk * tall + tall)

    def load(first, stop):
        return ref[field, x, first:stop, :]

    result = [None, None, None]
    if slot_x is not None:
        after = beside(ref, field, x, 1, above, slot_x)(low, high)
        before = beside(ref, field, x, -1, below, slot_x)(low, high)
        result[0] = after - before
    if slot_y is not None:
        after = rows_of(load, chunk, chunks, -1, lambda: y_above[x, slot_y : slot_y + 1, :])
        before = rows_of(load, chunk, chunks, 1, lambda: y_below[x, slot_y : slot_y + 1, :])
        result[1] = after - before
    if slot_z is not None:
        rows, halo = (load(low, high), z_halo[x, low:high, :])
        after = columns_of(rows, halo, 6 + slot_z, -1)
        before = columns_of(rows, halo, slot_z, 1)
        result[2] = after - before
    return result


def collide(
    pops,
    stretch,
    flags,
    flow,
    x_first,
    x_second,
    y_first,
    y_second,
    z_rows,
    post,
    shift,
    columns,
    ahead,
    behind,
    up_first,
    up_second,
    below,
    above,
    y_below,
    y_above,
    z_halo,
    gas,
):
    bx, by, bz = flags.shape
    chunks = by // tall
    halos = (below, above, y_below, y_above, z_halo)
    flip_x, flip_y = (odd("gx"), odd("gy"))
    below[...] = select(flip_x, x_first, x_second)
    above[...] = select(flip_x, x_second, x_first)
    y_below[...] = select(flip_y, y_first, y_second)
    y_above[...] = select(flip_y, y_second, y_first)
    z_halo[...] = row_columns(z_rows[...]).reshape(z_halo.shape)
    factor = 1.0 - 0.5 / relax_time
    rate = 1.0 / relax_time

    def plane(x, carry):
        for chunk in range(chunks):
            rows = pl.ds(chunk * tall, tall)
            terms = [[], [], []]
            for field in range(6):
                slots = [None, None, None]
                for comp in range(3):
                    for axis in range(3):
                        if symmetric_slot[comp][axis] == field:
                            slots[axis] = comp
                found = differences(stretch, field, slots, x, chunk, chunks, *halos)
                for axis in range(3):
                    if slots[axis] is not None:
                        terms[slots[axis]].append(found[axis])
            force = [0.5 * polymer_coeff * (part[0] + part[1] + part[2]) for part in terms]
            density, half = (flow[3, x, rows, :], 0.5 * flow[4, x, rows, :])
            moved = [flow[comp, x, rows, :] + half * force[comp] for comp in range(3)]
            for comp in range(3):
                shift[comp, x, rows, :] = moved[comp]
            squared = moved[0] * moved[0] + moved[1] * moved[1] + moved[2] * moved[2]
            work = moved[0] * force[0] + moved[1] * force[1] + moved[2] * force[2]
            weight = rate * density
            common = weight - 1.5 * weight * squared - 3.0 * factor * work
            odd = [3.0 * weight * moved[comp] + 3.0 * factor * force[comp] for comp in range(3)]
            even = [4.5 * weight * moved[comp] + 9.0 * factor * force[comp] for comp in range(3)]
            keep = 1.0 - rate
            post[0, x, rows, :] = keep * pops[0, x, rows, :] + lattice_weights[0] * common
            for index in pairs:
                both = common + along(index, moved) * along(index, even)
                differ = along(index, odd)
                scale = lattice_weights[index]
                post[index, x, rows, :] = keep * pops[index, x, rows, :] + scale * (both + differ)
                post[index + 1, x, rows, :] = keep * pops[index + 1, x, rows, :] + scale * (
                    both - differ
                )
        return carry

    lax.fori_loop(0, bx, plane, 0)

    tiles = []
    for x in range(bx):
        gas[0, x] = jnp.where(flags[x] == 0, 1.0, 0.0)
        swap_rows(
            up_first,
            up_second,
            x,
            [(post, index) for index in y_up] + [(gas, 0)],
            [(post, index) for index in y_down] + [(gas, 0)],
            flip_y,
        )
        tiles.append(
            packed(
                [post[index, x, :, bz - lanes : bz] for index in z_up]
                + [gas[0, x, :, bz - lanes : bz]],
                [post[index, x, :, 0:lanes] for index in z_down] + [gas[0, x, :, 0:lanes]],
            )
        )
    columns[...] = column_rows(tiles)
    for slot in range(5):
        up, down = (post[x_up[slot], bx - 1], post[x_down[slot], 0])
        ahead[slot] = jnp.where(flip_x, down, up)
        behind[slot] = jnp.where(flip_x, up, down)
    ahead[5] = jnp.where(flip_x, gas[0, 0], gas[0, bx - 1])
    behind[5] = jnp.where(flip_x, gas[0, bx - 1], gas[0, 0])


def restretch(
    stretch,
    flow,
    x_first,
    x_second,
    y_first,
    y_second,
    z_rows,
    inner,
    outer,
    updated,
    fresh,
    below,
    above,
    y_below,
    y_above,
    z_halo,
    sems,
):
    bx, by, bz = stretch.shape[1:]
    copies = [
        pltpu.make_async_copy(inner, fresh.at[:, 1 : bx - 1], sems.at[0]),
        pltpu.make_async_copy(outer.at[:, 0], fresh.at[:, 0], sems.at[1]),
        pltpu.make_async_copy(outer.at[:, 1], fresh.at[:, bx - 1], sems.at[2]),
    ]
    for copy in copies:
        copy.start()
    chunks = by // tall
    flip_x, flip_y = (odd("gx"), odd("gy"))
    below[...] = select(flip_x, x_first, x_second)
    above[...] = select(flip_x, x_second, x_first)
    y_below[...] = select(flip_y, y_first, y_second)
    y_above[...] = select(flip_y, y_second, y_first)
    z_halo[...] = row_columns(z_rows[...]).reshape(z_halo.shape)

    def plane(x, carry):
        for chunk in range(chunks):
            rows = pl.ds(chunk * tall, tall)
            grad = [
                differences(
                    flow,
                    comp,
                    (3 + comp, 3 + comp, 3 + comp),
                    x,
                    chunk,
                    chunks,
                    below,
                    above,
                    y_below,
                    y_above,
                    z_halo,
                )
                for comp in range(3)
            ]
            part = [stretch[slot, x, rows, :] for slot in range(6)]
            full = [part[slot] + 1.0 if slot < 3 else part[slot] for slot in range(6)]

            def product(row, col):
                total = grad[row][0] * full[symmetric_slot[0][col]]
                for inner in (1, 2):
                    total = total + grad[row][inner] * full[symmetric_slot[inner][col]]
                return total

            for slot, (row, col) in enumerate(tensor_pairs):
                old = (1.0 - 1.0 / polymer_time) * part[slot]
                if row == col:
                    updated[slot, x, rows, :] = old + product(row, col)
                else:
                    updated[slot, x, rows, :] = old + 0.5 * (product(row, col) + product(col, row))
        return carry

    lax.fori_loop(0, bx, plane, 0)
    for copy in copies:
        copy.wait()


up_edges = ((0, y_up.index(7)), (0, gas_slot), (1, y_down.index(9)), (1, gas_slot))
down_edges = ((0, y_up.index(10)), (0, gas_slot), (1, y_down.index(8)), (1, gas_slot))


def forward_edges(y_first, y_second, z_rows, first_out, second_out, corner):
    bx, bz = (y_first.shape[0], y_first.shape[2])
    halves = bz // lanes
    flip_x, flip_y = (odd("gx"), odd("gy"))
    for half in range(halves):
        cut = slice(half * lanes, half * lanes + lanes)
        for place in range(4):
            found = []
            for x, edges in ((bx - 1, up_edges), (0, down_edges)):
                side, slot = edges[place]
                one = y_first[x, slot : slot + 1, cut]
                two = y_second[x, slot : slot + 1, cut]
                found.append(jnp.where(flip_y, one, two) if side == 0 else jnp.where(flip_y, two, one))
            at = half * 4 + place
            first_out[at : at + 1, :] = jnp.where(flip_x, found[1], found[0])
            second_out[at : at + 1, :] = jnp.where(flip_x, found[0], found[1])
    first_out[4 * halves :, :] = z_rows[...]
    second_out[4 * halves :, :] = z_rows[...]
    corner[...] = z_rows[...]


def own_halos(
    flags, y_first, y_second, z_rows, corner_first, corner_second, gas, low_rows, high_rows, columns
):
    bx, by = flags.shape[:2]
    flip = odd("gy")
    tile = row_columns(z_rows[...])
    corner_below = row_columns(select(flip, corner_first, corner_second))
    corner_above = row_columns(select(flip, corner_second, corner_first))
    for x in range(bx):
        gas[x + 1] = jnp.where(flags[x] == 0, 1.0, 0.0)
        low_rows[x + 1] = jnp.where(flip, y_first[x], y_second[x])
        high_rows[x + 1] = jnp.where(flip, y_second[x], y_first[x])
        columns[x + 1] = tile[x * by : x * by + by, :]
        end = x * by + by - 1
        low_rows[x + 1, edge_slot : edge_slot + 1, 0:lanes] = corner_below[end : end + 1, :]
        high_rows[x + 1, edge_slot : edge_slot + 1, 0:lanes] = corner_above[
            x * by : x * by + 1, :
        ]


def stream_plane(
    x,
    post,
    shift,
    mass,
    flags,
    code,
    gas,
    low_rows,
    high_rows,
    columns,
    below,
    above,
    fresh,
    settled,
    excess,
    heading,
    place,
    kept,
):
    bx, by, bz = flags.shape
    chunks = by // tall

    def reader(index):
        step = velocity_set[index][0]
        source = x - step
        if isinstance(x, int) and source < 0:
            return lambda low, high: below[x_up.index(index), low:high, :]
        if isinstance(x, int) and source >= bx:
            return lambda low, high: above[x_down.index(index), low:high, :]
        return lambda low, high: post[index, source, low:high, :]

    def moved(load, index, chunk, slot, lane):
        step_x, step_y, step_z = velocity_set[index]
        source = x + 1 - step_x
        edges = low_rows if step_y == 1 else high_rows
        rows = rows_of(load, chunk, chunks, step_y, lambda: edges[source, slot : slot + 1, :])
        if step_z == 0:
            return rows
        halo = rows_of(
            lambda low, high: columns[source, low:high, :],
            chunk,
            chunks,
            step_y,
            lambda: edges[source, edge_slot : edge_slot + 1, 0:lanes],
        )
        return columns_of(rows, halo, lane, step_z)

    for chunk in range(chunks):
        rows = pl.ds(chunk * tall, tall)
        speed = [shift[comp, x, rows, :] for comp in range(3)]
        squared = speed[0] * speed[0] + speed[1] * speed[1] + speed[2] * speed[2]
        rest = 1.0 - 1.5 * squared
        total = post[0, x, rows, :]
        fresh[0, place, rows, :] = total
        change = jnp.zeros((tall, bz), jnp.float32)
        for first in pairs:
            proj = along(first, speed)
            equal = 2.0 * lattice_weights[first] * (rest + 4.5 * proj * proj)
            for index in (first, first + 1):
                step_x, step_y, step_z = velocity_set[index]
                slot, lane, gas_lane = (None, None, None)
                if step_y != 0:
                    slot = (y_up if step_y == 1 else y_down).index(index)
                if step_z == 1:
                    lane, gas_lane = (z_up.index(index), gas_slot)
                elif step_z == -1:
                    lane, gas_lane = (6 + z_down.index(index), 6 + gas_slot)
                arriving = moved(reader(index), index, chunk, slot, lane)
                from_gas = moved(
                    lambda low, high: gas[x + 1 - step_x, low:high, :],
                    index,
                    chunk,
                    gas_slot,
                    gas_lane,
                )
                leaving = post[opposite_of[index], x, rows, :]
                open_side = from_gas > 0.5
                value = jnp.where(open_side, equal - leaving, arriving)
                fresh[index, place, rows, :] = value
                total = total + value
                change = change + jnp.where(open_side, 0.0, arriving - leaving)
        read = mass[x, rows, :] + jnp.where(flags[x, rows, :] == 1, change, 0.0)
        mark = code[x, rows, :]
        liquid = mark >= 32.0
        converts = mark > 0.0
        level = jnp.where(liquid, total, 0.0)
        excess[kept, rows, :] = jnp.where(converts, read - level, 0.0)
        heading[kept, rows, :] = jnp.where(liquid, mark - 32.0, mark)
        settled[place, rows, :] = jnp.where(converts, level, read)


def stream_inner(
    post,
    shift,
    mass,
    flags,
    code,
    y_first,
    y_second,
    z_rows,
    corner_first,
    corner_second,
    fresh,
    settled,
    excess,
    heading,
    gas,
    low_rows,
    high_rows,
    columns,
):
    bx = flags.shape[0]
    halos = (gas, low_rows, high_rows, columns)
    own_halos(flags, y_first, y_second, z_rows, corner_first, corner_second, *halos)

    def plane(x, carry):
        stream_plane(
            x,
            post,
            shift,
            mass,
            flags,
            code,
            *halos,
            None,
            None,
            fresh,
            settled,
            excess,
            heading,
            x - 1,
            x - 1,
        )
        return carry

    lax.fori_loop(1, bx - 1, plane, 0)


def stream_outer(
    post,
    shift,
    mass,
    flags,
    code,
    y_first,
    y_second,
    z_rows,
    corner_first,
    corner_second,
    x_first,
    x_second,
    edges_first,
    edges_second,
    inner_excess,
    inner_heading,
    fresh,
    settled,
    spread,
    line_first,
    line_second,
    out_z,
    gas,
    low_rows,
    high_rows,
    columns,
    below,
    above,
    excess,
    heading,
):
    bx, by, bz = flags.shape
    halves = bz // lanes
    flip_x = odd("gx")
    halos = (gas, low_rows, high_rows, columns)
    own_halos(flags, y_first, y_second, z_rows, corner_first, corner_second, *halos)

    below[...] = select(flip_x, x_first, x_second)
    above[...] = select(flip_x, x_second, x_first)
    gas[0] = below[5]
    gas[bx + 1] = above[5]
    edges_below = select(flip_x, edges_first, edges_second)
    edges_above = select(flip_x, edges_second, edges_first)
    for found, at, x, edges in (
        (edges_below, 0, bx - 1, up_edges),
        (edges_above, bx + 1, 0, down_edges),
    ):
        for place, (side, slot) in enumerate(edges):
            line = jnp.concatenate(
                [found[half * 4 + place : half * 4 + place + 1, :] for half in range(halves)],
                axis=1,
            )
            (low_rows, high_rows)[side][at, slot : slot + 1, :] = line
        columns[at] = row_columns(found[4 * halves :, :])[x * by : x * by + by, :]
    for place, x in enumerate((0, bx - 1)):
        stream_plane(
            x,
            post,
            shift,
            mass,
            flags,
            code,
            *halos,
            below,
            above,
            fresh,
            settled,
            excess,
            heading,
            place,
            x,
        )
    for x in range(1, bx - 1):
        excess[x] = inner_excess[x - 1]
        heading[x] = inner_heading[x - 1]

    row_at, lane_at = (iota((by, bz), 0), iota((by, bz), 1))
    line_at = iota((1, bz), 1)
    tile_lane, line_lane = (iota((by, lanes), 1), iota((1, lanes), 1))

    def rows_up(rows):
        return jnp.where(row_at == 0, 0.0, pltpu.roll(rows, 1, 0))

    def rows_down(rows):
        return jnp.where(row_at == by - 1, 0.0, pltpu.roll(rows, by - 1, 0))

    def over(rows, at, step):
        if step == 1:
            return jnp.where(at == 0, 0.0, pltpu.roll(rows, 1, 1))
        return jnp.where(at == bz - 1, 0.0, pltpu.roll(rows, bz - 1, 1))

    def summed(parts):
        total = parts[0]
        for part in parts[1:]:
            total = total + part
        return total

    tile = jnp.zeros((by, lanes), jnp.float32)
    line_up = jnp.zeros((1, lanes), jnp.float32)
    line_down = jnp.zeros((1, lanes), jnp.float32)
    flip_y = odd("gy")
    line_first[...] = jnp.zeros(line_first.shape, jnp.float32)
    line_second[...] = jnp.zeros(line_second.shape, jnp.float32)
    for target in range(bx + 2):
        groups = {}
        for index in range(1, 19):
            step_x, step_y, step_z = velocity_set[index]
            x = target - 1 - step_x
            if 0 <= x < bx:
                part = jnp.where(heading[x] == float(index), excess[x], 0.0)
                groups.setdefault((step_y, step_z), []).append(part)
        groups = {key: summed(parts) for key, parts in groups.items()}
        total = jnp.zeros((by, bz), jnp.float32)
        line = {1: jnp.zeros((1, bz), jnp.float32), -1: jnp.zeros((1, bz), jnp.float32)}
        for step_z in (0, 1, -1):
            group = jnp.zeros((by, bz), jnp.float32)
            ends = {}
            if (0, step_z) in groups:
                group = group + groups[(0, step_z)]
            if (1, step_z) in groups:
                group = group + rows_up(groups[(1, step_z)])
                ends[1] = groups[(1, step_z)][by - 1 : by, :]
            if (-1, step_z) in groups:
                group = group + rows_down(groups[(-1, step_z)])
                ends[-1] = groups[(-1, step_z)][0:1, :]
            if step_z == 0:
                total = total + group
                for side in ends:
                    line[side] = line[side] + ends[side]
                continue
            total = total + over(group, lane_at, step_z)
            for side in ends:
                line[side] = line[side] + over(ends[side], line_at, step_z)
            if step_z == 1:
                spot, cut, roll = (target, slice(bz - lanes, bz), target + 1)
            else:
                spot, cut, roll = (8 + target, slice(0, lanes), 8 + target)
            tile = jnp.where(tile_lane == spot, pltpu.roll(group[:, cut], roll, 1), tile)
            if 1 in ends:
                line_up = jnp.where(
                    line_lane == spot, pltpu.roll(ends[1][:, cut], roll, 1), line_up
                )
            if -1 in ends:
                line_down = jnp.where(
                    line_lane == spot, pltpu.roll(ends[-1][:, cut], roll, 1), line_down
                )
        spread[target] = total
        line_first[target : target + 1, :] = jnp.where(flip_y, line[-1], line[1])
        line_second[target : target + 1, :] = jnp.where(flip_y, line[1], line[-1])
    rest = jnp.zeros((lanes - by - 2, lanes), jnp.float32)
    out_z[...] = column_rows([tile, line_up, line_down, rest])


def with_edges(total, target, tile, y_below, y_above):
    by, bz = total.shape
    row_at, lane_at = (iota((by, bz), 0), iota((by, bz), 1))
    total = total + jnp.where(lane_at == 0, tile[0:by, target : target + 1], 0.0)
    total = total + jnp.where(lane_at == bz - 1, tile[0:by, 8 + target : 9 + target], 0.0)
    total = total + jnp.where(row_at == 0, y_below[target : target + 1, :], 0.0)
    return total + jnp.where(row_at == by - 1, y_above[target : target + 1, :], 0.0)


def add_faces(spread, z_rows, y_first, y_second, first, second):
    last = spread.shape[0] - 1
    flip_x, flip_y = (odd("gx"), odd("gy"))
    tile = row_columns(z_rows[...])
    y_below, y_above = (select(flip_y, y_first, y_second), select(flip_y, y_second, y_first))
    up = with_edges(spread[last], last, tile, y_below, y_above)
    down = with_edges(spread[0], 0, tile, y_below, y_above)
    first[...] = jnp.where(flip_x, down, up)
    second[...] = jnp.where(flip_x, up, down)


def add_all(
    inner_settled,
    outer_settled,
    spread,
    z_rows,
    y_first,
    y_second,
    corner_first,
    corner_second,
    x_first,
    x_second,
    new_mass,
):
    bx, by, bz = new_mass.shape
    flip_x, flip_y = (odd("gx"), odd("gy"))
    tile = row_columns(z_rows[...])
    y_below, y_above = (select(flip_y, y_first, y_second), select(flip_y, y_second, y_first))
    at = iota((8, bz), 1)
    found = []
    for rows, side, corner in (
        (y_below, 0, select(flip_y, corner_first, corner_second)),
        (y_above, 1, select(flip_y, corner_second, corner_first)),
    ):
        edge = corner[:, by + side : by + side + 1]
        rows = rows + jnp.where(at == 0, edge[0:8, :], 0.0)
        found.append(rows + jnp.where(at == bz - 1, edge[8:16, :], 0.0))
    for x in range(bx):
        total = with_edges(spread[x + 1], x + 1, tile, *found)
        if x == 0:
            total = total + select(flip_x, x_first, x_second)
        if x == bx - 1:
            total = total + select(flip_x, x_second, x_first)
        if 0 < x < bx - 1:
            total = total + inner_settled[x - 1]
        else:
            total = total + outer_settled[0 if x == 0 else 1]
        new_mass[x] = total


def swapped(first, second, axis):
    devices = lax.axis_size(axis)
    ahead = [(i, (i + 1) % devices if i % 2 == 0 else i - 1) for i in range(devices)]
    behind = [(i, (i - 1) % devices if i % 2 == 0 else (i + 1) % devices) for i in range(devices)]
    return lax.ppermute(first, axis, ahead), lax.ppermute(second, axis, behind)


def both_ways(rows, lower):
    devices = lax.axis_size("gz")
    before = lax.ppermute(rows, "gz", [(i, (i + 1) % devices) for i in range(devices)])
    if devices == 2:
        return before
    after = lax.ppermute(rows, "gz", [(i, (i - 1) % devices) for i in range(devices)])
    return jnp.where(iota(rows.shape, 0) < lower, before, after)


remote = pl.BlockSpec(memory_space=pltpu.HBM)


def call(body, outs, specs=None, out_specs=None, scratch=(), cost=(0, 0)):
    extra = {} if specs is None else {"in_specs": specs}
    if out_specs is not None:
        extra["out_specs"] = out_specs
    return pl.pallas_call(
        body,
        out_shape=[
            shape
            if isinstance(shape, jax.ShapeDtypeStruct)
            else jax.ShapeDtypeStruct(shape, jnp.float32)
            for shape in outs
        ],
        scratch_shapes=[
            pltpu.VMEM(shape, jnp.float32) if isinstance(shape, tuple) else shape
            for shape in scratch
        ],
        compiler_params=pltpu.CompilerParams(vmem_limit_bytes=40 * 1024 * 1024),
        cost_estimate=pl.CostEstimate(flops=cost[0], bytes_accessed=cost[1], transcendentals=0),
        **extra,
    )


def shards(populations, stretch, mass, flags, conv_source, conv_kind, conv_direction):
    bx, by, bz = flags.shape
    cells = bx * by * bz
    box, face, tile = ((bx, by, bz), (by, bz), (bx, by, lanes))
    rows, columns = ((bx, 8, bz), (16, bx * by))

    pops, stretch, flags, flow, z_out, y_one, y_two, x_one, x_two = call(
        moments,
        [
            (19, *box),
            (6, *box),
            jax.ShapeDtypeStruct(box, jnp.int32),
            (5, *box),
            columns,
            rows,
            rows,
            (6, *face),
            (6, *face),
        ],
        specs=[remote] * 3,
        scratch=[pltpu.SemaphoreType.DMA((3, bx))],
        cost=(60 * cells, 150 * cells),
    )(
        *(
            pltpu.with_memory_space_constraint(array, pltpu.HBM)
            for array in (populations, stretch, flags)
        )
    )
    first_x = swapped(x_one, x_two, "gx")
    z_first = both_ways(z_out, 6)
    y_first = swapped(y_one, y_two, "gy")

    entries = conv_source.shape[0]
    (code,) = call(
        lambda *refs: conversions(*refs, columns=bz), [(bx * by, bz)], cost=(40 * cells, 4 * cells)
    )(*(array.reshape(1, entries) for array in (conv_source, conv_kind, conv_direction)))
    code = code.reshape(box)

    post, shift, z_out, x_one, x_two, y_one, y_two = call(
        collide,
        [(19, *box), (3, *box), columns, (6, *face), (6, *face), rows, rows],
        scratch=[(6, *face), (6, *face), rows, rows, tile, (1, *box)],
        cost=(250 * cells, 250 * cells),
    )(pops, stretch, flags, flow, *first_x, *y_first, z_first)
    z_post = both_ways(z_out, 6)
    post_y = swapped(y_one, y_two, "gy")
    post_x = swapped(x_one, x_two, "gx")
    edges = (4 * (bz // lanes) + 16, lanes)
    x_one, x_two, corner = call(forward_edges, [edges, edges, columns])(*post_y, z_post)
    corners = swapped(corner, corner, "gy")
    edges_x = swapped(x_one, x_two, "gx")

    rims = [(bx + 2, *face), (bx + 2, 8, bz), (bx + 2, 8, bz), (bx + 2, by, lanes)]
    here = (post, shift, mass, flags, code, *post_y, z_post, *corners)
    inside, beside_faces = ((bx - 2, *face), (2, *face))
    inner, inner_settled, inner_excess, inner_heading = call(
        stream_inner,
        [(19, *inside), inside, inside, inside],
        scratch=rims,
        cost=(200 * cells, 125 * cells),
    )(*here)
    outer, outer_settled, spread, y_one, y_two, z_out = call(
        stream_outer,
        [(19, *beside_faces), beside_faces, (bx + 2, *face), (8, bz), (8, bz), columns],
        scratch=rims + [(6, *face), (6, *face), box, box],
        cost=(250 * cells, 150 * cells),
    )(*here, *post_x, *edges_x, inner_excess, inner_heading)
    z_last = both_ways(z_out, 8)
    last_y = swapped(y_one, y_two, "gy")
    last_corners = swapped(z_last, z_last, "gy")
    x_one, x_two = call(add_faces, [face, face])(spread, z_last, *last_y)
    last_x = swapped(x_one, x_two, "gx")
    new_stretch, fresh = call(
        restretch,
        [(6, *box), (19, *box)],
        out_specs=[pl.BlockSpec(), remote],
        scratch=[(6, *face), (6, *face), rows, rows, tile, pltpu.SemaphoreType.DMA((3,))],
        cost=(150 * cells, 80 * cells),
    )(stretch, flow, *first_x, *y_first, z_first, inner, outer)
    (new_mass,) = call(add_all, [box])(
        inner_settled, outer_settled, spread, z_last, *last_y, *last_corners, *last_x
    )
    return (fresh, new_stretch, new_mass)


def solution(mesh):
    return jax.shard_map(
        shards,
        mesh=mesh,
        in_specs=(
            P(None, "gx", "gy", "gz"),
            P(None, "gx", "gy", "gz"),
            P("gx", "gy", "gz"),
            P("gx", "gy", "gz"),
            P(("gx", "gy", "gz")),
            P(("gx", "gy", "gz")),
            P(("gx", "gy", "gz")),
        ),
        out_specs=(P(None, "gx", "gy", "gz"), P(None, "gx", "gy", "gz"), P("gx", "gy", "gz")),
        check_vma=False,
    )
```

```python
import jax
import jax.numpy as jnp
from jax import lax
from jax.experimental import pallas as pl
from jax.experimental.pallas import tpu as pltpu
from jax.sharding import PartitionSpec as P

velocity_set = (
    (0, 0, 0),
    (1, 0, 0),
    (-1, 0, 0),
    (0, 1, 0),
    (0, -1, 0),
    (0, 0, 1),
    (0, 0, -1),
    (1, 1, 0),
    (-1, -1, 0),
    (1, -1, 0),
    (-1, 1, 0),
    (1, 0, 1),
    (-1, 0, -1),
    (1, 0, -1),
    (-1, 0, 1),
    (0, 1, 1),
    (0, -1, -1),
    (0, 1, -1),
    (0, -1, 1),
)
opposite_of = (0, 2, 1, 4, 3, 6, 5, 8, 7, 10, 9, 12, 11, 14, 13, 16, 15, 18, 17)
lattice_weights = (1.0 / 3.0,) + (1.0 / 18.0,) * 6 + (1.0 / 36.0,) * 12
symmetric_slot = ((0, 3, 4), (3, 1, 5), (4, 5, 2))
tensor_pairs = ((0, 0), (1, 1), (2, 2), (0, 1), (0, 2), (1, 2))
relax_time = 0.8
polymer_time = 8.0
polymer_coeff = 0.05


def moving(axis, sign):
    return tuple(index for index in range(19) if velocity_set[index][axis] == sign)


x_up, x_down = (moving(0, 1), moving(0, -1))
y_up, y_down = (moving(1, 1), moving(1, -1))
z_up, z_down = (moving(2, 1), moving(2, -1))
pairs = tuple(range(1, 19, 2))
gas_slot = 5
speed_slot = 6
edge_slot = 9
sides = 9
lanes = 128
tall = 8


def iota(shape, dim):
    return lax.broadcasted_iota(jnp.int32, shape, dim)


def wide(tile, width):
    return jnp.concatenate([tile] * (width // tile.shape[1]), axis=1)


def rows_of(load, chunk, chunks, step, edge):
    low = chunk * tall
    if step == 0:
        return load(low, low + tall)
    if step == 1 and chunk > 0:
        return load(low - 1, low + tall - 1)
    if step == -1 and chunk < chunks - 1:
        return load(low + 1, low + tall + 1)
    rows = load(low, low + tall)
    at = iota(rows.shape, 0)
    if step == 1:
        return jnp.where(at == 0, edge(), pltpu.roll(rows, 1, 0))
    return jnp.where(at == tall - 1, edge(), pltpu.roll(rows, tall - 1, 0))


def columns_of(rows, halo, lane, step):
    width = rows.shape[1]
    at = iota(rows.shape, 1)
    if step == 1:
        edge = wide(pltpu.roll(halo, (lanes - lane) % lanes, 1), width)
        return jnp.where(at == 0, edge, pltpu.roll(rows, 1, 1))
    edge = wide(pltpu.roll(halo, lanes - 1 - lane, 1), width)
    return jnp.where(at == width - 1, edge, pltpu.roll(rows, width - 1, 1))


def packed(high, low):
    at = iota(high[0].shape, 1)
    tile = jnp.zeros_like(high[0])
    for slot, part in enumerate(high):
        tile = jnp.where(at == slot, pltpu.roll(part, slot + 1, 1), tile)
    for place, part in enumerate(low):
        slot = len(high) + place
        tile = jnp.where(at == slot, pltpu.roll(part, slot, 1), tile)
    return tile


def along(index, vector):
    total = None
    for comp in range(3):
        sign = velocity_set[index][comp]
        if sign != 0:
            term = vector[comp] if sign > 0 else -vector[comp]
            total = term if total is None else total + term
    return total


def conversions(source, kind, heading, code, *, columns):
    count = source.shape[1]
    value = (heading[...] + 32 * kind[...]).astype(jnp.float32)
    row, column = (source[...] // columns, source[...] % columns)
    by_row = jnp.where(iota((code.shape[0], count), 0) == row, value, 0.0).astype(jnp.bfloat16)
    by_column = jnp.where(iota((columns, count), 0) == column, 1.0, 0.0).astype(jnp.bfloat16)
    code[...] = lax.dot_general(
        by_row, by_column, (((1,), (1,)), ((), ())), preferred_element_type=jnp.float32
    )


def odd(axis):
    return lax.rem(lax.axis_index(axis), 2) == 1


def select(chosen, first, second):
    return jnp.where(chosen, first[...], second[...])


def swap_rows(first, second, x, planes, high, low, flip):
    for slot, ((top, top_field), (bottom, bottom_field)) in enumerate(zip(high, low)):
        by = top.shape[2]
        up = top[top_field, x, by - 1 : by, :]
        down = bottom[bottom_field, x, 0:1, :]
        at = slot * planes + x
        first[at : at + 1, :] = jnp.where(flip, down, up)
        second[at : at + 1, :] = jnp.where(flip, up, down)


def swapped_rows(first, second, slots, low_rows, high_rows, shift):
    flip = odd("gy")
    planes = low_rows.shape[0] - 2 * shift
    for x in range(planes):
        for place, slot in enumerate(slots):
            at = slot * planes + x
            one, two = (first[at : at + 1, :], second[at : at + 1, :])
            low_rows[x + shift, place : place + 1, :] = jnp.where(flip, one, two)
            high_rows[x + shift, place : place + 1, :] = jnp.where(flip, two, one)


def column_rows(tiles, count):
    return jnp.concatenate(tiles, axis=0).T[0:count, :]


def row_columns(rows):
    rest = jnp.zeros((lanes - rows.shape[0], rows.shape[1]), jnp.float32)
    return jnp.concatenate([rows, rest], axis=0).T


def first_faces(
    stretch_in,
    flags_in,
    stretch,
    flags,
    columns,
    y_first,
    y_second,
    x_first,
    x_second,
    sems,
):
    bx, by, bz = flags.shape
    flip_x, flip_y = (odd("gx"), odd("gy"))
    copies = [
        pltpu.make_async_copy(stretch_in, stretch, sems.at[0]),
        pltpu.make_async_copy(flags_in, flags, sems.at[1]),
    ]
    for copy in copies:
        copy.start()
    for copy in copies:
        copy.wait()
    along_y = [(stretch, symmetric_slot[comp][1]) for comp in range(3)]
    tiles = []
    for x in range(bx):
        swap_rows(y_first, y_second, x, bx, along_y, along_y, flip_y)
        fields = [stretch.at[symmetric_slot[comp][2], x] for comp in range(3)]
        tiles.append(
            packed(
                [field[:, bz - lanes : bz] for field in fields],
                [field[:, 0:lanes] for field in fields],
            )
        )
    columns[...] = column_rows(tiles, columns.shape[0])
    rest = y_first.shape[0] - 3 * bx
    y_first[3 * bx :, :] = jnp.zeros((rest, bz), jnp.float32)
    y_second[3 * bx :, :] = jnp.zeros((rest, bz), jnp.float32)
    for out, last in ((x_first, flip_x), (x_second, jnp.logical_not(flip_x))):
        for comp in range(3):
            slot = symmetric_slot[comp][0]
            out[comp] = jnp.where(last, stretch[slot, 0], stretch[slot, bx - 1])
        out[3] = jnp.where(jnp.where(last, flags[0], flags[bx - 1]) == 0, 1.0, 0.0)


def moments(pops_in, pops, flow, sems):
    bx, by = pops.shape[1:3]
    copies = [
        pltpu.make_async_copy(pops_in.at[:, x], pops.at[:, x], sems.at[x]) for x in range(bx)
    ]
    for copy in copies:
        copy.start()
    for x in range(bx):
        copies[x].wait()
        for chunk in range(by // tall):
            rows = pl.ds(chunk * tall, tall)
            part = [pops[index, x, rows, :] for index in range(19)]
            density = part[0]
            for index in range(1, 19):
                density = density + part[index]
            inverse = 1.0 / density
            for comp in range(3):
                total = None
                for index in pairs:
                    sign = velocity_set[index][comp]
                    if sign != 0:
                        term = part[index] - part[index + 1]
                        term = term if sign > 0 else -term
                        total = term if total is None else total + term
                flow[comp, x, rows, :] = total * inverse
            flow[3, x, rows, :] = density
            flow[4, x, rows, :] = inverse


def beside(ref, field, x, step, halo, slot):
    last = ref.shape[1] - 1
    inside = jnp.clip(x + step, 0, last)
    beyond = x == (0 if step < 0 else last)
    return lambda low, high: jnp.where(
        beyond, halo[slot, low:high, :], ref[field, inside, low:high, :]
    )


def differences(
    ref, field, slots, x, chunk, chunks, below, above, y_below, y_above, z_halo, lane, side
):
    slot_x, slot_y, slot_z = slots
    low, high = (chunk * tall, chunk * tall + tall)

    def load(first, stop):
        return ref[field, x, first:stop, :]

    result = [None, None, None]
    if slot_x is not None:
        after = beside(ref, field, x, 1, above, slot_x)(low, high)
        before = beside(ref, field, x, -1, below, slot_x)(low, high)
        result[0] = after - before
    if slot_y is not None:
        after = rows_of(load, chunk, chunks, -1, lambda: y_above[x, slot_y : slot_y + 1, :])
        before = rows_of(load, chunk, chunks, 1, lambda: y_below[x, slot_y : slot_y + 1, :])
        result[1] = after - before
    if slot_z is not None:
        rows, halo = (load(low, high), z_halo[x, low:high, :])
        after = columns_of(rows, halo, lane + side + slot_z, -1)
        before = columns_of(rows, halo, lane + slot_z, 1)
        result[2] = after - before
    return result


def collide(
    pops,
    stretch,
    flags,
    flow,
    x_first,
    x_second,
    y_first,
    y_second,
    z_rows,
    post,
    shift,
    columns,
    ahead,
    behind,
    up_first,
    up_second,
    below,
    above,
    y_below,
    y_above,
    z_halo,
    gas,
):
    bx, by, bz = flags.shape
    chunks = by // tall
    halos = (below, above, y_below, y_above, z_halo, 0, 3)
    flip_x, flip_y = (odd("gx"), odd("gy"))
    below[...] = select(flip_x, x_first, x_second)
    above[...] = select(flip_x, x_second, x_first)
    swapped_rows(y_first, y_second, range(3), y_below, y_above, 0)
    z_halo[...] = row_columns(z_rows[...]).reshape(z_halo.shape)
    factor = 1.0 - 0.5 / relax_time
    rate = 1.0 / relax_time

    def plane(x, carry):
        for chunk in range(chunks):
            rows = pl.ds(chunk * tall, tall)
            terms = [[], [], []]
            for field in range(6):
                slots = [None, None, None]
                for comp in range(3):
                    for axis in range(3):
                        if symmetric_slot[comp][axis] == field:
                            slots[axis] = comp
                found = differences(stretch, field, slots, x, chunk, chunks, *halos)
                for axis in range(3):
                    if slots[axis] is not None:
                        terms[slots[axis]].append(found[axis])
            force = [0.5 * polymer_coeff * (part[0] + part[1] + part[2]) for part in terms]
            density, half = (flow[3, x, rows, :], 0.5 * flow[4, x, rows, :])
            moved = [flow[comp, x, rows, :] + half * force[comp] for comp in range(3)]
            for comp in range(3):
                shift[comp, x, rows, :] = moved[comp]
            squared = moved[0] * moved[0] + moved[1] * moved[1] + moved[2] * moved[2]
            work = moved[0] * force[0] + moved[1] * force[1] + moved[2] * force[2]
            weight = rate * density
            common = weight - 1.5 * weight * squared - 3.0 * factor * work
            odd = [3.0 * weight * moved[comp] + 3.0 * factor * force[comp] for comp in range(3)]
            even = [4.5 * weight * moved[comp] + 9.0 * factor * force[comp] for comp in range(3)]
            keep = 1.0 - rate
            post[0, x, rows, :] = keep * pops[0, x, rows, :] + lattice_weights[0] * common
            for index in pairs:
                both = common + along(index, moved) * along(index, even)
                differ = along(index, odd)
                scale = lattice_weights[index]
                post[index, x, rows, :] = keep * pops[index, x, rows, :] + scale * (both + differ)
                post[index + 1, x, rows, :] = keep * pops[index + 1, x, rows, :] + scale * (
                    both - differ
                )
        return carry

    lax.fori_loop(0, bx, plane, 0)

    tiles = []
    speed = [(flow, comp) for comp in range(3)]
    for x in range(bx):
        gas[0, x] = jnp.where(flags[x] == 0, 1.0, 0.0)
        high = [(post, index) for index in y_up] + [(gas, 0)] + speed
        low = [(post, index) for index in y_down] + [(gas, 0)] + speed
        swap_rows(up_first, up_second, x, bx, high, low, flip_y)
        high = [(post, index) for index in z_up] + [(gas, 0)] + speed
        low = [(post, index) for index in z_down] + [(gas, 0)] + speed
        tiles.append(
            packed(
                [ref[field, x, :, bz - lanes : bz] for ref, field in high],
                [ref[field, x, :, 0:lanes] for ref, field in low],
            )
        )
    columns[...] = column_rows(tiles, columns.shape[0])
    rest = up_first.shape[0] - sides * bx
    up_first[sides * bx :, :] = jnp.zeros((rest, bz), jnp.float32)
    up_second[sides * bx :, :] = jnp.zeros((rest, bz), jnp.float32)
    for slot in range(5):
        up, down = (post[x_up[slot], bx - 1], post[x_down[slot], 0])
        ahead[slot] = jnp.where(flip_x, down, up)
        behind[slot] = jnp.where(flip_x, up, down)
    for comp in range(3):
        up, down = (flow[comp, bx - 1], flow[comp, 0])
        ahead[5 + comp] = jnp.where(flip_x, down, up)
        behind[5 + comp] = jnp.where(flip_x, up, down)


def restretch(
    stretch,
    flow,
    x_first,
    x_second,
    y_first,
    y_second,
    z_rows,
    inner,
    outer,
    updated,
    fresh,
    below,
    above,
    y_below,
    y_above,
    z_halo,
    sems,
):
    bx, by, bz = stretch.shape[1:]
    copies = [
        pltpu.make_async_copy(inner, fresh.at[:, 1 : bx - 1], sems.at[0]),
        pltpu.make_async_copy(outer.at[:, 0], fresh.at[:, 0], sems.at[1]),
        pltpu.make_async_copy(outer.at[:, 1], fresh.at[:, bx - 1], sems.at[2]),
    ]
    for copy in copies:
        copy.start()
    chunks = by // tall
    flip_x = odd("gx")
    below[...] = select(flip_x, x_first, x_second)
    above[...] = select(flip_x, x_second, x_first)
    swapped_rows(y_first, y_second, range(speed_slot, sides), y_below, y_above, 0)
    z_halo[...] = row_columns(z_rows[...]).reshape(z_halo.shape)

    def plane(x, carry):
        for chunk in range(chunks):
            rows = pl.ds(chunk * tall, tall)
            grad = [
                differences(
                    flow,
                    comp,
                    (5 + comp, comp, comp),
                    x,
                    chunk,
                    chunks,
                    below,
                    above,
                    y_below,
                    y_above,
                    z_halo,
                    speed_slot,
                    sides,
                )
                for comp in range(3)
            ]
            part = [stretch[slot, x, rows, :] for slot in range(6)]
            full = [part[slot] + 1.0 if slot < 3 else part[slot] for slot in range(6)]

            def product(row, col):
                total = grad[row][0] * full[symmetric_slot[0][col]]
                for inner in (1, 2):
                    total = total + grad[row][inner] * full[symmetric_slot[inner][col]]
                return total

            for slot, (row, col) in enumerate(tensor_pairs):
                old = (1.0 - 1.0 / polymer_time) * part[slot]
                if row == col:
                    updated[slot, x, rows, :] = old + product(row, col)
                else:
                    updated[slot, x, rows, :] = old + 0.5 * (product(row, col) + product(col, row))
        return carry

    lax.fori_loop(0, bx, plane, 0)
    for copy in copies:
        copy.wait()


up_edges = ((0, y_up.index(7)), (0, gas_slot), (1, y_down.index(9)), (1, gas_slot))
down_edges = ((0, y_up.index(10)), (0, gas_slot), (1, y_down.index(8)), (1, gas_slot))


def forward_edges(y_first, y_second, z_rows, first_out, second_out, corner, *, bx):
    halves = y_first.shape[1] // lanes
    flip_x, flip_y = (odd("gx"), odd("gy"))
    for half in range(halves):
        cut = slice(half * lanes, half * lanes + lanes)
        for place in range(4):
            found = []
            for x, edges in ((bx - 1, up_edges), (0, down_edges)):
                side, slot = edges[place]
                row = slot * bx + x
                one = y_first[row : row + 1, cut]
                two = y_second[row : row + 1, cut]
                found.append(jnp.where(flip_y, one, two) if side == 0 else jnp.where(flip_y, two, one))
            at = half * 4 + place
            first_out[at : at + 1, :] = jnp.where(flip_x, found[1], found[0])
            second_out[at : at + 1, :] = jnp.where(flip_x, found[0], found[1])
    first_out[4 * halves :, :] = z_rows[...]
    second_out[4 * halves :, :] = z_rows[...]
    corner[...] = z_rows[...]


def own_halos(
    flags, y_first, y_second, z_rows, corner_first, corner_second, gas, low_rows, high_rows, columns
):
    bx, by = flags.shape[:2]
    flip = odd("gy")
    tile = row_columns(z_rows[...])
    corner_below = row_columns(select(flip, corner_first, corner_second))
    corner_above = row_columns(select(flip, corner_second, corner_first))
    swapped_rows(y_first, y_second, range(speed_slot), low_rows, high_rows, 1)
    for x in range(bx):
        gas[x + 1] = jnp.where(flags[x] == 0, 1.0, 0.0)
        columns[x + 1] = tile[x * by : x * by + by, :]
        end = x * by + by - 1
        low_rows[x + 1, edge_slot : edge_slot + 1, 0:lanes] = corner_below[end : end + 1, :]
        high_rows[x + 1, edge_slot : edge_slot + 1, 0:lanes] = corner_above[
            x * by : x * by + 1, :
        ]


def stream_plane(
    x,
    post,
    shift,
    mass,
    flags,
    code,
    gas,
    low_rows,
    high_rows,
    columns,
    below,
    above,
    fresh,
    settled,
    excess,
    heading,
    place,
    kept,
):
    bx, by, bz = flags.shape
    chunks = by // tall

    def reader(index):
        step = velocity_set[index][0]
        source = x - step
        if isinstance(x, int) and source < 0:
            return lambda low, high: below[x_up.index(index), low:high, :]
        if isinstance(x, int) and source >= bx:
            return lambda low, high: above[x_down.index(index), low:high, :]
        return lambda low, high: post[index, source, low:high, :]

    def moved(load, index, chunk, slot, lane):
        step_x, step_y, step_z = velocity_set[index]
        source = x + 1 - step_x
        edges = low_rows if step_y == 1 else high_rows
        rows = rows_of(load, chunk, chunks, step_y, lambda: edges[source, slot : slot + 1, :])
        if step_z == 0:
            return rows
        halo = rows_of(
            lambda low, high: columns[source, low:high, :],
            chunk,
            chunks,
            step_y,
            lambda: edges[source, edge_slot : edge_slot + 1, 0:lanes],
        )
        return columns_of(rows, halo, lane, step_z)

    for chunk in range(chunks):
        rows = pl.ds(chunk * tall, tall)
        speed = [shift[comp, x, rows, :] for comp in range(3)]
        squared = speed[0] * speed[0] + speed[1] * speed[1] + speed[2] * speed[2]
        rest = 1.0 - 1.5 * squared
        total = post[0, x, rows, :]
        fresh[0, place, rows, :] = total
        change = jnp.zeros((tall, bz), jnp.float32)
        for first in pairs:
            proj = along(first, speed)
            equal = 2.0 * lattice_weights[first] * (rest + 4.5 * proj * proj)
            for index in (first, first + 1):
                step_x, step_y, step_z = velocity_set[index]
                slot, lane, gas_lane = (None, None, None)
                if step_y != 0:
                    slot = (y_up if step_y == 1 else y_down).index(index)
                if step_z == 1:
                    lane, gas_lane = (z_up.index(index), gas_slot)
                elif step_z == -1:
                    lane, gas_lane = (sides + z_down.index(index), sides + gas_slot)
                arriving = moved(reader(index), index, chunk, slot, lane)
                from_gas = moved(
                    lambda low, high: gas[x + 1 - step_x, low:high, :],
                    index,
                    chunk,
                    gas_slot,
                    gas_lane,
                )
                leaving = post[opposite_of[index], x, rows, :]
                open_side = from_gas > 0.5
                value = jnp.where(open_side, equal - leaving, arriving)
                fresh[index, place, rows, :] = value
                total = total + value
                change = change + jnp.where(open_side, 0.0, arriving - leaving)
        read = mass[x, rows, :] + jnp.where(flags[x, rows, :] == 1, change, 0.0)
        mark = code[x, rows, :]
        liquid = mark >= 32.0
        converts = mark > 0.0
        level = jnp.where(liquid, total, 0.0)
        excess[kept, rows, :] = jnp.where(converts, read - level, 0.0)
        heading[kept, rows, :] = jnp.where(liquid, mark - 32.0, mark)
        settled[place, rows, :] = jnp.where(converts, level, read)


def stream_inner(
    post,
    shift,
    mass,
    flags,
    code,
    y_first,
    y_second,
    z_rows,
    corner_first,
    corner_second,
    fresh,
    settled,
    excess,
    heading,
    gas,
    low_rows,
    high_rows,
    columns,
):
    bx = flags.shape[0]
    halos = (gas, low_rows, high_rows, columns)
    own_halos(flags, y_first, y_second, z_rows, corner_first, corner_second, *halos)

    def plane(x, carry):
        stream_plane(
            x,
            post,
            shift,
            mass,
            flags,
            code,
            *halos,
            None,
            None,
            fresh,
            settled,
            excess,
            heading,
            x - 1,
            x - 1,
        )
        return carry

    lax.fori_loop(1, bx - 1, plane, 0)


def stream_outer(
    post,
    shift,
    mass,
    flags,
    code,
    y_first,
    y_second,
    z_rows,
    corner_first,
    corner_second,
    gas_first,
    gas_second,
    x_first,
    x_second,
    edges_first,
    edges_second,
    inner_excess,
    inner_heading,
    fresh,
    settled,
    spread,
    line_first,
    line_second,
    out_z,
    gas,
    low_rows,
    high_rows,
    columns,
    below,
    above,
    excess,
    heading,
):
    bx, by, bz = flags.shape
    halves = bz // lanes
    flip_x = odd("gx")
    halos = (gas, low_rows, high_rows, columns)
    own_halos(flags, y_first, y_second, z_rows, corner_first, corner_second, *halos)

    for slot in range(5):
        below[slot] = jnp.where(flip_x, x_first[slot], x_second[slot])
        above[slot] = jnp.where(flip_x, x_second[slot], x_first[slot])
    gas[0] = jnp.where(flip_x, gas_first[3], gas_second[3])
    gas[bx + 1] = jnp.where(flip_x, gas_second[3], gas_first[3])
    edges_below = select(flip_x, edges_first, edges_second)
    edges_above = select(flip_x, edges_second, edges_first)
    for found, at, x, edges in (
        (edges_below, 0, bx - 1, up_edges),
        (edges_above, bx + 1, 0, down_edges),
    ):
        for place, (side, slot) in enumerate(edges):
            line = jnp.concatenate(
                [found[half * 4 + place : half * 4 + place + 1, :] for half in range(halves)],
                axis=1,
            )
            (low_rows, high_rows)[side][at, slot : slot + 1, :] = line
        columns[at] = row_columns(found[4 * halves :, :])[x * by : x * by + by, :]
    for place, x in enumerate((0, bx - 1)):
        stream_plane(
            x,
            post,
            shift,
            mass,
            flags,
            code,
            *halos,
            below,
            above,
            fresh,
            settled,
            excess,
            heading,
            place,
            x,
        )
    for x in range(1, bx - 1):
        excess[x] = inner_excess[x - 1]
        heading[x] = inner_heading[x - 1]

    row_at, lane_at = (iota((by, bz), 0), iota((by, bz), 1))
    line_at = iota((1, bz), 1)
    tile_lane, line_lane = (iota((by, lanes), 1), iota((1, lanes), 1))

    def rows_up(rows):
        return jnp.where(row_at == 0, 0.0, pltpu.roll(rows, 1, 0))

    def rows_down(rows):
        return jnp.where(row_at == by - 1, 0.0, pltpu.roll(rows, by - 1, 0))

    def over(rows, at, step):
        if step == 1:
            return jnp.where(at == 0, 0.0, pltpu.roll(rows, 1, 1))
        return jnp.where(at == bz - 1, 0.0, pltpu.roll(rows, bz - 1, 1))

    def summed(parts):
        total = parts[0]
        for part in parts[1:]:
            total = total + part
        return total

    tile = jnp.zeros((by, lanes), jnp.float32)
    line_up = jnp.zeros((1, lanes), jnp.float32)
    line_down = jnp.zeros((1, lanes), jnp.float32)
    flip_y = odd("gy")
    line_first[...] = jnp.zeros(line_first.shape, jnp.float32)
    line_second[...] = jnp.zeros(line_second.shape, jnp.float32)
    for target in range(bx + 2):
        groups = {}
        for index in range(1, 19):
            step_x, step_y, step_z = velocity_set[index]
            x = target - 1 - step_x
            if 0 <= x < bx:
                part = jnp.where(heading[x] == float(index), excess[x], 0.0)
                groups.setdefault((step_y, step_z), []).append(part)
        groups = {key: summed(parts) for key, parts in groups.items()}
        total = jnp.zeros((by, bz), jnp.float32)
        line = {1: jnp.zeros((1, bz), jnp.float32), -1: jnp.zeros((1, bz), jnp.float32)}
        for step_z in (0, 1, -1):
            group = jnp.zeros((by, bz), jnp.float32)
            ends = {}
            if (0, step_z) in groups:
                group = group + groups[(0, step_z)]
            if (1, step_z) in groups:
                group = group + rows_up(groups[(1, step_z)])
                ends[1] = groups[(1, step_z)][by - 1 : by, :]
            if (-1, step_z) in groups:
                group = group + rows_down(groups[(-1, step_z)])
                ends[-1] = groups[(-1, step_z)][0:1, :]
            if step_z == 0:
                total = total + group
                for side in ends:
                    line[side] = line[side] + ends[side]
                continue
            total = total + over(group, lane_at, step_z)
            for side in ends:
                line[side] = line[side] + over(ends[side], line_at, step_z)
            if step_z == 1:
                spot, cut, roll = (target, slice(bz - lanes, bz), target + 1)
            else:
                spot, cut, roll = (8 + target, slice(0, lanes), 8 + target)
            tile = jnp.where(tile_lane == spot, pltpu.roll(group[:, cut], roll, 1), tile)
            if 1 in ends:
                line_up = jnp.where(
                    line_lane == spot, pltpu.roll(ends[1][:, cut], roll, 1), line_up
                )
            if -1 in ends:
                line_down = jnp.where(
                    line_lane == spot, pltpu.roll(ends[-1][:, cut], roll, 1), line_down
                )
        spread[target] = total
        line_first[target : target + 1, :] = jnp.where(flip_y, line[-1], line[1])
        line_second[target : target + 1, :] = jnp.where(flip_y, line[1], line[-1])
    rest = jnp.zeros((lanes - by - 2, lanes), jnp.float32)
    out_z[...] = column_rows([tile, line_up, line_down, rest], 16)


def with_edges(total, target, tile, y_below, y_above):
    by, bz = total.shape
    row_at, lane_at = (iota((by, bz), 0), iota((by, bz), 1))
    total = total + jnp.where(lane_at == 0, tile[0:by, target : target + 1], 0.0)
    total = total + jnp.where(lane_at == bz - 1, tile[0:by, 8 + target : 9 + target], 0.0)
    total = total + jnp.where(row_at == 0, y_below[target : target + 1, :], 0.0)
    return total + jnp.where(row_at == by - 1, y_above[target : target + 1, :], 0.0)


def add_faces(spread, z_rows, y_first, y_second, first, second):
    last = spread.shape[0] - 1
    flip_x, flip_y = (odd("gx"), odd("gy"))
    tile = row_columns(z_rows[...])
    y_below, y_above = (select(flip_y, y_first, y_second), select(flip_y, y_second, y_first))
    up = with_edges(spread[last], last, tile, y_below, y_above)
    down = with_edges(spread[0], 0, tile, y_below, y_above)
    first[...] = jnp.where(flip_x, down, up)
    second[...] = jnp.where(flip_x, up, down)


def add_all(
    inner_settled,
    outer_settled,
    spread,
    z_rows,
    y_first,
    y_second,
    corner_first,
    corner_second,
    x_first,
    x_second,
    new_mass,
):
    bx, by, bz = new_mass.shape
    flip_x, flip_y = (odd("gx"), odd("gy"))
    tile = row_columns(z_rows[...])
    y_below, y_above = (select(flip_y, y_first, y_second), select(flip_y, y_second, y_first))
    at = iota((8, bz), 1)
    found = []
    for rows, side, corner in (
        (y_below, 0, select(flip_y, corner_first, corner_second)),
        (y_above, 1, select(flip_y, corner_second, corner_first)),
    ):
        edge = corner[:, by + side : by + side + 1]
        rows = rows + jnp.where(at == 0, edge[0:8, :], 0.0)
        found.append(rows + jnp.where(at == bz - 1, edge[8:16, :], 0.0))
    for x in range(bx):
        total = with_edges(spread[x + 1], x + 1, tile, *found)
        if x == 0:
            total = total + select(flip_x, x_first, x_second)
        if x == bx - 1:
            total = total + select(flip_x, x_second, x_first)
        if 0 < x < bx - 1:
            total = total + inner_settled[x - 1]
        else:
            total = total + outer_settled[0 if x == 0 else 1]
        new_mass[x] = total


def swapped(first, second, axis):
    devices = lax.axis_size(axis)
    ahead = [(i, (i + 1) % devices if i % 2 == 0 else i - 1) for i in range(devices)]
    behind = [(i, (i - 1) % devices if i % 2 == 0 else (i + 1) % devices) for i in range(devices)]
    return lax.ppermute(first, axis, ahead), lax.ppermute(second, axis, behind)


def both_ways(rows, lower):
    devices = lax.axis_size("gz")
    before = lax.ppermute(rows, "gz", [(i, (i + 1) % devices) for i in range(devices)])
    if devices == 2:
        return before
    after = lax.ppermute(rows, "gz", [(i, (i - 1) % devices) for i in range(devices)])
    return jnp.where(iota(rows.shape, 0) < lower, before, after)


remote = pl.BlockSpec(memory_space=pltpu.HBM)


def call(body, outs, specs=None, out_specs=None, scratch=(), cost=(0, 0)):
    extra = {} if specs is None else {"in_specs": specs}
    if out_specs is not None:
        extra["out_specs"] = out_specs
    return pl.pallas_call(
        body,
        out_shape=[
            shape
            if isinstance(shape, jax.ShapeDtypeStruct)
            else jax.ShapeDtypeStruct(shape, jnp.float32)
            for shape in outs
        ],
        scratch_shapes=[
            pltpu.VMEM(shape, jnp.float32) if isinstance(shape, tuple) else shape
            for shape in scratch
        ],
        compiler_params=pltpu.CompilerParams(vmem_limit_bytes=40 * 1024 * 1024),
        cost_estimate=pl.CostEstimate(flops=cost[0], bytes_accessed=cost[1], transcendentals=0),
        **extra,
    )


def shards(populations, stretch, mass, flags, conv_source, conv_kind, conv_direction):
    bx, by, bz = flags.shape
    cells = bx * by * bz
    box, face, tile = ((bx, by, bz), (by, bz), (bx, by, lanes))

    stretch, flags, z_out, y_one, y_two, x_one, x_two = call(
        first_faces,
        [
            (6, *box),
            jax.ShapeDtypeStruct(box, jnp.int32),
            (8, bx * by),
            (4 * bx, bz),
            (4 * bx, bz),
            (4, *face),
            (4, *face),
        ],
        specs=[remote] * 2,
        scratch=[pltpu.SemaphoreType.DMA((2,))],
        cost=(10 * cells, 60 * cells),
    )(*(pltpu.with_memory_space_constraint(array, pltpu.HBM) for array in (stretch, flags)))
    first_x = swapped(x_one, x_two, "gx")
    z_first = both_ways(z_out, 3)
    y_first = swapped(y_one, y_two, "gy")

    entries = conv_source.shape[0]
    (code,) = call(
        lambda *refs: conversions(*refs, columns=bz), [(bx * by, bz)], cost=(40 * cells, 4 * cells)
    )(*(array.reshape(1, entries) for array in (conv_source, conv_kind, conv_direction)))
    code = code.reshape(box)

    pops, flow = call(
        moments,
        [(19, *box), (5, *box)],
        specs=[remote],
        scratch=[pltpu.SemaphoreType.DMA((bx,))],
        cost=(60 * cells, 150 * cells),
    )(pltpu.with_memory_space_constraint(populations, pltpu.HBM))

    columns, rows = ((24, bx * by), (10 * bx, bz))
    post, shift, z_out, x_one, x_two, y_one, y_two = call(
        collide,
        [(19, *box), (3, *box), columns, (8, *face), (8, *face), rows, rows],
        scratch=[(4, *face), (4, *face), (bx, 8, bz), (bx, 8, bz), tile, (1, *box)],
        cost=(300 * cells, 300 * cells),
    )(pops, stretch, flags, flow, *first_x, *y_first, z_first)
    z_post = both_ways(z_out, sides)
    post_y = swapped(y_one, y_two, "gy")
    post_x = swapped(x_one, x_two, "gx")
    edges = (4 * (bz // lanes) + columns[0], lanes)
    x_one, x_two, corner = call(
        lambda *refs: forward_edges(*refs, bx=bx), [edges, edges, columns]
    )(*post_y, z_post)
    corners = swapped(corner, corner, "gy")
    edges_x = swapped(x_one, x_two, "gx")

    rims = [(bx + 2, *face), (bx + 2, 16, bz), (bx + 2, 16, bz), (bx + 2, by, lanes)]
    here = (post, shift, mass, flags, code, *post_y, z_post, *corners)
    inside, beside_faces = ((bx - 2, *face), (2, *face))
    inner, inner_settled, inner_excess, inner_heading = call(
        stream_inner,
        [(19, *inside), inside, inside, inside],
        scratch=rims,
        cost=(200 * cells, 125 * cells),
    )(*here)
    outer, outer_settled, spread, y_one, y_two, z_out = call(
        stream_outer,
        [(19, *beside_faces), beside_faces, (bx + 2, *face), (8, bz), (8, bz), (16, bx * by)],
        scratch=rims + [(5, *face), (5, *face), box, box],
        cost=(250 * cells, 150 * cells),
    )(*here, *first_x, *post_x, *edges_x, inner_excess, inner_heading)
    z_last = both_ways(z_out, 8)
    last_y = swapped(y_one, y_two, "gy")
    last_corners = swapped(z_last, z_last, "gy")
    x_one, x_two = call(add_faces, [face, face])(spread, z_last, *last_y)
    last_x = swapped(x_one, x_two, "gx")
    new_stretch, fresh = call(
        restretch,
        [(6, *box), (19, *box)],
        out_specs=[pl.BlockSpec(), remote],
        scratch=[
            (8, *face),
            (8, *face),
            (bx, 8, bz),
            (bx, 8, bz),
            tile,
            pltpu.SemaphoreType.DMA((3,)),
        ],
        cost=(150 * cells, 80 * cells),
    )(stretch, flow, *post_x, *post_y, z_post, inner, outer)
    (new_mass,) = call(add_all, [box])(
        inner_settled, outer_settled, spread, z_last, *last_y, *last_corners, *last_x
    )
    return (fresh, new_stretch, new_mass)


def solution(mesh):
    return jax.shard_map(
        shards,
        mesh=mesh,
        in_specs=(
            P(None, "gx", "gy", "gz"),
            P(None, "gx", "gy", "gz"),
            P("gx", "gy", "gz"),
            P("gx", "gy", "gz"),
            P(("gx", "gy", "gz")),
            P(("gx", "gy", "gz")),
            P(("gx", "gy", "gz")),
        ),
        out_specs=(P(None, "gx", "gy", "gz"), P(None, "gx", "gy", "gz"), P("gx", "gy", "gz")),
        check_vma=False,
    )
```

```python
import jax
import jax.numpy as jnp
from jax import lax
from jax.experimental import pallas as pl
from jax.experimental.pallas import tpu as pltpu
from jax.sharding import PartitionSpec as P

velocity_set = (
    (0, 0, 0),
    (1, 0, 0),
    (-1, 0, 0),
    (0, 1, 0),
    (0, -1, 0),
    (0, 0, 1),
    (0, 0, -1),
    (1, 1, 0),
    (-1, -1, 0),
    (1, -1, 0),
    (-1, 1, 0),
    (1, 0, 1),
    (-1, 0, -1),
    (1, 0, -1),
    (-1, 0, 1),
    (0, 1, 1),
    (0, -1, -1),
    (0, 1, -1),
    (0, -1, 1),
)
opposite_of = (0, 2, 1, 4, 3, 6, 5, 8, 7, 10, 9, 12, 11, 14, 13, 16, 15, 18, 17)
lattice_weights = (1.0 / 3.0,) + (1.0 / 18.0,) * 6 + (1.0 / 36.0,) * 12
symmetric_slot = ((0, 3, 4), (3, 1, 5), (4, 5, 2))
tensor_pairs = ((0, 0), (1, 1), (2, 2), (0, 1), (0, 2), (1, 2))
relax_time = 0.8
polymer_time = 8.0
polymer_coeff = 0.05


def moving(axis, sign):
    return tuple(index for index in range(19) if velocity_set[index][axis] == sign)


x_up, x_down = (moving(0, 1), moving(0, -1))
y_up, y_down = (moving(1, 1), moving(1, -1))
z_up, z_down = (moving(2, 1), moving(2, -1))
pairs = tuple(range(1, 19, 2))
gas_slot = 5
speed_slot = 6
edge_slot = 9
sides = 9
lanes = 128
tall = 8


def iota(shape, dim):
    return lax.broadcasted_iota(jnp.int32, shape, dim)


def wide(tile, width):
    return jnp.concatenate([tile] * (width // tile.shape[1]), axis=1)


def rows_of(load, chunk, chunks, step, edge):
    low = chunk * tall
    if step == 0:
        return load(low, low + tall)
    if step == 1 and chunk > 0:
        return load(low - 1, low + tall - 1)
    if step == -1 and chunk < chunks - 1:
        return load(low + 1, low + tall + 1)
    rows = load(low, low + tall)
    at = iota(rows.shape, 0)
    if step == 1:
        return jnp.where(at == 0, edge(), pltpu.roll(rows, 1, 0))
    return jnp.where(at == tall - 1, edge(), pltpu.roll(rows, tall - 1, 0))


def columns_of(rows, halo, lane, step):
    width = rows.shape[1]
    at = iota(rows.shape, 1)
    if step == 1:
        edge = wide(pltpu.roll(halo, (lanes - lane) % lanes, 1), width)
        return jnp.where(at == 0, edge, pltpu.roll(rows, 1, 1))
    edge = wide(pltpu.roll(halo, lanes - 1 - lane, 1), width)
    return jnp.where(at == width - 1, edge, pltpu.roll(rows, width - 1, 1))


def packed(high, low):
    at = iota(high[0].shape, 1)
    tile = jnp.zeros_like(high[0])
    for slot, part in enumerate(high):
        tile = jnp.where(at == slot, pltpu.roll(part, slot + 1, 1), tile)
    for place, part in enumerate(low):
        slot = len(high) + place
        tile = jnp.where(at == slot, pltpu.roll(part, slot, 1), tile)
    return tile


def along(index, vector):
    total = None
    for comp in range(3):
        sign = velocity_set[index][comp]
        if sign != 0:
            term = vector[comp] if sign > 0 else -vector[comp]
            total = term if total is None else total + term
    return total


def conversions(source, kind, heading, code, *, columns):
    count = source.shape[1]
    value = (heading[...] + 32 * kind[...]).astype(jnp.float32)
    row, column = (source[...] // columns, source[...] % columns)
    by_row = jnp.where(iota((code.shape[0], count), 0) == row, value, 0.0).astype(jnp.bfloat16)
    by_column = jnp.where(iota((columns, count), 0) == column, 1.0, 0.0).astype(jnp.bfloat16)
    code[...] = lax.dot_general(
        by_row, by_column, (((1,), (1,)), ((), ())), preferred_element_type=jnp.float32
    )


def flipped(axis):
    return lax.rem(lax.axis_index(axis), 2) == 0


def select(chosen, first, second):
    return jnp.where(chosen, first[...], second[...])


def swap_rows(first, second, x, planes, high, low, flip):
    for slot, ((top, top_field), (bottom, bottom_field)) in enumerate(zip(high, low)):
        by = top.shape[2]
        up = top[top_field, x, by - 1 : by, :]
        down = bottom[bottom_field, x, 0:1, :]
        at = slot * planes + x
        first[at : at + 1, :] = jnp.where(flip, down, up)
        second[at : at + 1, :] = jnp.where(flip, up, down)


def swapped_rows(first, second, slots, low_rows, high_rows, shift):
    flip = flipped("gy")
    planes = low_rows.shape[0] - 2 * shift
    for x in range(planes):
        for place, slot in enumerate(slots):
            at = slot * planes + x
            one, two = (first[at : at + 1, :], second[at : at + 1, :])
            low_rows[x + shift, place : place + 1, :] = jnp.where(flip, one, two)
            high_rows[x + shift, place : place + 1, :] = jnp.where(flip, two, one)


def column_rows(tiles, count):
    return jnp.concatenate(tiles, axis=0).T[0:count, :]


def row_columns(rows):
    rest = jnp.zeros((lanes - rows.shape[0], rows.shape[1]), jnp.float32)
    return jnp.concatenate([rows, rest], axis=0).T


def first_faces(
    stretch_in,
    flags_in,
    stretch,
    flags,
    columns,
    y_first,
    y_second,
    x_first,
    x_second,
    sems,
):
    bx, by, bz = flags.shape
    flip_x, flip_y = (flipped("gx"), flipped("gy"))
    copies = [
        pltpu.make_async_copy(stretch_in, stretch, sems.at[0]),
        pltpu.make_async_copy(flags_in, flags, sems.at[1]),
    ]
    for copy in copies:
        copy.start()
    for copy in copies:
        copy.wait()
    along_y = [(stretch, symmetric_slot[comp][1]) for comp in range(3)]
    tiles = []
    for x in range(bx):
        swap_rows(y_first, y_second, x, bx, along_y, along_y, flip_y)
        fields = [stretch.at[symmetric_slot[comp][2], x] for comp in range(3)]
        tiles.append(
            packed(
                [field[:, bz - lanes : bz] for field in fields],
                [field[:, 0:lanes] for field in fields],
            )
        )
    columns[...] = column_rows(tiles, columns.shape[0])
    rest = y_first.shape[0] - 3 * bx
    y_first[3 * bx :, :] = jnp.zeros((rest, bz), jnp.float32)
    y_second[3 * bx :, :] = jnp.zeros((rest, bz), jnp.float32)
    for out, last in ((x_first, flip_x), (x_second, jnp.logical_not(flip_x))):
        for comp in range(3):
            slot = symmetric_slot[comp][0]
            out[comp] = jnp.where(last, stretch[slot, 0], stretch[slot, bx - 1])
        out[3] = jnp.where(jnp.where(last, flags[0], flags[bx - 1]) == 0, 1.0, 0.0)


def moments(pops_in, pops, flow, sems):
    bx, by = pops.shape[1:3]
    copies = [
        pltpu.make_async_copy(pops_in.at[:, x], pops.at[:, x], sems.at[x]) for x in range(bx)
    ]
    for copy in copies:
        copy.start()
    for x in range(bx):
        copies[x].wait()
        for chunk in range(by // tall):
            rows = pl.ds(chunk * tall, tall)
            part = [pops[index, x, rows, :] for index in range(19)]
            density = part[0]
            for index in range(1, 19):
                density = density + part[index]
            inverse = 1.0 / density
            for comp in range(3):
                total = None
                for index in pairs:
                    sign = velocity_set[index][comp]
                    if sign != 0:
                        term = part[index] - part[index + 1]
                        term = term if sign > 0 else -term
                        total = term if total is None else total + term
                flow[comp, x, rows, :] = total * inverse
            flow[3, x, rows, :] = density
            flow[4, x, rows, :] = inverse


def beside(ref, field, x, step, halo, slot):
    last = ref.shape[1] - 1
    inside = jnp.clip(x + step, 0, last)
    beyond = x == (0 if step < 0 else last)
    return lambda low, high: jnp.where(
        beyond, halo[slot, low:high, :], ref[field, inside, low:high, :]
    )


def differences(
    ref, field, slots, x, chunk, chunks, below, above, y_below, y_above, z_halo, lane, side
):
    slot_x, slot_y, slot_z = slots
    low, high = (chunk * tall, chunk * tall + tall)

    def load(first, stop):
        return ref[field, x, first:stop, :]

    result = [None, None, None]
    if slot_x is not None:
        after = beside(ref, field, x, 1, above, slot_x)(low, high)
        before = beside(ref, field, x, -1, below, slot_x)(low, high)
        result[0] = after - before
    if slot_y is not None:
        after = rows_of(load, chunk, chunks, -1, lambda: y_above[x, slot_y : slot_y + 1, :])
        before = rows_of(load, chunk, chunks, 1, lambda: y_below[x, slot_y : slot_y + 1, :])
        result[1] = after - before
    if slot_z is not None:
        rows, halo = (load(low, high), z_halo[x, low:high, :])
        after = columns_of(rows, halo, lane + side + slot_z, -1)
        before = columns_of(rows, halo, lane + slot_z, 1)
        result[2] = after - before
    return result


def collide(
    pops,
    stretch,
    flags,
    flow,
    x_first,
    x_second,
    y_first,
    y_second,
    z_rows,
    post,
    shift,
    columns,
    ahead,
    behind,
    up_first,
    up_second,
    below,
    above,
    y_below,
    y_above,
    z_halo,
    gas,
):
    bx, by, bz = flags.shape
    chunks = by // tall
    halos = (below, above, y_below, y_above, z_halo, 0, 3)
    flip_x, flip_y = (flipped("gx"), flipped("gy"))
    below[...] = select(flip_x, x_first, x_second)
    above[...] = select(flip_x, x_second, x_first)
    swapped_rows(y_first, y_second, range(3), y_below, y_above, 0)
    z_halo[...] = row_columns(z_rows[...]).reshape(z_halo.shape)
    factor = 1.0 - 0.5 / relax_time
    rate = 1.0 / relax_time

    def plane(x, carry):
        for chunk in range(chunks):
            rows = pl.ds(chunk * tall, tall)
            terms = [[], [], []]
            for field in range(6):
                slots = [None, None, None]
                for comp in range(3):
                    for axis in range(3):
                        if symmetric_slot[comp][axis] == field:
                            slots[axis] = comp
                found = differences(stretch, field, slots, x, chunk, chunks, *halos)
                for axis in range(3):
                    if slots[axis] is not None:
                        terms[slots[axis]].append(found[axis])
            force = [0.5 * polymer_coeff * (part[0] + part[1] + part[2]) for part in terms]
            density, half = (flow[3, x, rows, :], 0.5 * flow[4, x, rows, :])
            moved = [flow[comp, x, rows, :] + half * force[comp] for comp in range(3)]
            for comp in range(3):
                shift[comp, x, rows, :] = moved[comp]
            squared = moved[0] * moved[0] + moved[1] * moved[1] + moved[2] * moved[2]
            work = moved[0] * force[0] + moved[1] * force[1] + moved[2] * force[2]
            weight = rate * density
            common = weight - 1.5 * weight * squared - 3.0 * factor * work
            odd = [3.0 * weight * moved[comp] + 3.0 * factor * force[comp] for comp in range(3)]
            even = [4.5 * weight * moved[comp] + 9.0 * factor * force[comp] for comp in range(3)]
            keep = 1.0 - rate
            post[0, x, rows, :] = keep * pops[0, x, rows, :] + lattice_weights[0] * common
            for index in pairs:
                both = common + along(index, moved) * along(index, even)
                differ = along(index, odd)
                scale = lattice_weights[index]
                post[index, x, rows, :] = keep * pops[index, x, rows, :] + scale * (both + differ)
                post[index + 1, x, rows, :] = keep * pops[index + 1, x, rows, :] + scale * (
                    both - differ
                )
        return carry

    lax.fori_loop(0, bx, plane, 0)

    tiles = []
    speed = [(flow, comp) for comp in range(3)]
    for x in range(bx):
        gas[0, x] = jnp.where(flags[x] == 0, 1.0, 0.0)
        high = [(post, index) for index in y_up] + [(gas, 0)] + speed
        low = [(post, index) for index in y_down] + [(gas, 0)] + speed
        swap_rows(up_first, up_second, x, bx, high, low, flip_y)
        high = [(post, index) for index in z_up] + [(gas, 0)] + speed
        low = [(post, index) for index in z_down] + [(gas, 0)] + speed
        tiles.append(
            packed(
                [ref[field, x, :, bz - lanes : bz] for ref, field in high],
                [ref[field, x, :, 0:lanes] for ref, field in low],
            )
        )
    columns[...] = column_rows(tiles, columns.shape[0])
    rest = up_first.shape[0] - sides * bx
    up_first[sides * bx :, :] = jnp.zeros((rest, bz), jnp.float32)
    up_second[sides * bx :, :] = jnp.zeros((rest, bz), jnp.float32)
    for slot in range(5):
        up, down = (post[x_up[slot], bx - 1], post[x_down[slot], 0])
        ahead[slot] = jnp.where(flip_x, down, up)
        behind[slot] = jnp.where(flip_x, up, down)
    for comp in range(3):
        up, down = (flow[comp, bx - 1], flow[comp, 0])
        ahead[5 + comp] = jnp.where(flip_x, down, up)
        behind[5 + comp] = jnp.where(flip_x, up, down)


def restretch(
    stretch,
    flow,
    x_first,
    x_second,
    y_first,
    y_second,
    z_rows,
    inner,
    outer,
    updated,
    fresh,
    below,
    above,
    y_below,
    y_above,
    z_halo,
    sems,
):
    bx, by, bz = stretch.shape[1:]
    copies = [
        pltpu.make_async_copy(inner, fresh.at[:, 1 : bx - 1], sems.at[0]),
        pltpu.make_async_copy(outer.at[:, 0], fresh.at[:, 0], sems.at[1]),
        pltpu.make_async_copy(outer.at[:, 1], fresh.at[:, bx - 1], sems.at[2]),
    ]
    for copy in copies:
        copy.start()
    chunks = by // tall
    flip_x = flipped("gx")
    below[...] = select(flip_x, x_first, x_second)
    above[...] = select(flip_x, x_second, x_first)
    swapped_rows(y_first, y_second, range(speed_slot, sides), y_below, y_above, 0)
    z_halo[...] = row_columns(z_rows[...]).reshape(z_halo.shape)

    def plane(x, carry):
        for chunk in range(chunks):
            rows = pl.ds(chunk * tall, tall)
            grad = [
                differences(
                    flow,
                    comp,
                    (5 + comp, comp, comp),
                    x,
                    chunk,
                    chunks,
                    below,
                    above,
                    y_below,
                    y_above,
                    z_halo,
                    speed_slot,
                    sides,
                )
                for comp in range(3)
            ]
            part = [stretch[slot, x, rows, :] for slot in range(6)]
            full = [part[slot] + 1.0 if slot < 3 else part[slot] for slot in range(6)]

            def product(row, col):
                total = grad[row][0] * full[symmetric_slot[0][col]]
                for inner in (1, 2):
                    total = total + grad[row][inner] * full[symmetric_slot[inner][col]]
                return total

            for slot, (row, col) in enumerate(tensor_pairs):
                old = (1.0 - 1.0 / polymer_time) * part[slot]
                if row == col:
                    updated[slot, x, rows, :] = old + product(row, col)
                else:
                    updated[slot, x, rows, :] = old + 0.5 * (product(row, col) + product(col, row))
        return carry

    lax.fori_loop(0, bx, plane, 0)
    for copy in copies:
        copy.wait()


up_edges = ((0, y_up.index(7)), (0, gas_slot), (1, y_down.index(9)), (1, gas_slot))
down_edges = ((0, y_up.index(10)), (0, gas_slot), (1, y_down.index(8)), (1, gas_slot))


def forward_edges(y_first, y_second, z_rows, first_out, second_out, corner, *, bx):
    halves = y_first.shape[1] // lanes
    flip_x, flip_y = (flipped("gx"), flipped("gy"))
    for half in range(halves):
        cut = slice(half * lanes, half * lanes + lanes)
        for place in range(4):
            found = []
            for x, edges in ((bx - 1, up_edges), (0, down_edges)):
                side, slot = edges[place]
                row = slot * bx + x
                one = y_first[row : row + 1, cut]
                two = y_second[row : row + 1, cut]
                found.append(jnp.where(flip_y, one, two) if side == 0 else jnp.where(flip_y, two, one))
            at = half * 4 + place
            first_out[at : at + 1, :] = jnp.where(flip_x, found[1], found[0])
            second_out[at : at + 1, :] = jnp.where(flip_x, found[0], found[1])
    first_out[4 * halves :, :] = z_rows[...]
    second_out[4 * halves :, :] = z_rows[...]
    corner[...] = z_rows[...]


def own_halos(
    flags, y_first, y_second, z_rows, corner_first, corner_second, gas, low_rows, high_rows, columns
):
    bx, by = flags.shape[:2]
    flip = flipped("gy")
    tile = row_columns(z_rows[...])
    corner_below = row_columns(select(flip, corner_first, corner_second))
    corner_above = row_columns(select(flip, corner_second, corner_first))
    swapped_rows(y_first, y_second, range(speed_slot), low_rows, high_rows, 1)
    for x in range(bx):
        gas[x + 1] = jnp.where(flags[x] == 0, 1.0, 0.0)
        columns[x + 1] = tile[x * by : x * by + by, :]
        end = x * by + by - 1
        low_rows[x + 1, edge_slot : edge_slot + 1, 0:lanes] = corner_below[end : end + 1, :]
        high_rows[x + 1, edge_slot : edge_slot + 1, 0:lanes] = corner_above[
            x * by : x * by + 1, :
        ]


def stream_plane(
    x,
    post,
    shift,
    mass,
    flags,
    code,
    gas,
    low_rows,
    high_rows,
    columns,
    below,
    above,
    fresh,
    settled,
    excess,
    heading,
    place,
    kept,
):
    bx, by, bz = flags.shape
    chunks = by // tall

    def reader(index):
        step = velocity_set[index][0]
        source = x - step
        if isinstance(x, int) and source < 0:
            return lambda low, high: below[x_up.index(index), low:high, :]
        if isinstance(x, int) and source >= bx:
            return lambda low, high: above[x_down.index(index), low:high, :]
        return lambda low, high: post[index, source, low:high, :]

    def moved(load, index, chunk, slot, lane):
        step_x, step_y, step_z = velocity_set[index]
        source = x + 1 - step_x
        edges = low_rows if step_y == 1 else high_rows
        rows = rows_of(load, chunk, chunks, step_y, lambda: edges[source, slot : slot + 1, :])
        if step_z == 0:
            return rows
        halo = rows_of(
            lambda low, high: columns[source, low:high, :],
            chunk,
            chunks,
            step_y,
            lambda: edges[source, edge_slot : edge_slot + 1, 0:lanes],
        )
        return columns_of(rows, halo, lane, step_z)

    for chunk in range(chunks):
        rows = pl.ds(chunk * tall, tall)
        speed = [shift[comp, x, rows, :] for comp in range(3)]
        squared = speed[0] * speed[0] + speed[1] * speed[1] + speed[2] * speed[2]
        rest = 1.0 - 1.5 * squared
        total = post[0, x, rows, :]
        fresh[0, place, rows, :] = total
        change = jnp.zeros((tall, bz), jnp.float32)
        for first in pairs:
            proj = along(first, speed)
            equal = 2.0 * lattice_weights[first] * (rest + 4.5 * proj * proj)
            for index in (first, first + 1):
                step_x, step_y, step_z = velocity_set[index]
                slot, lane, gas_lane = (None, None, None)
                if step_y != 0:
                    slot = (y_up if step_y == 1 else y_down).index(index)
                if step_z == 1:
                    lane, gas_lane = (z_up.index(index), gas_slot)
                elif step_z == -1:
                    lane, gas_lane = (sides + z_down.index(index), sides + gas_slot)
                arriving = moved(reader(index), index, chunk, slot, lane)
                from_gas = moved(
                    lambda low, high: gas[x + 1 - step_x, low:high, :],
                    index,
                    chunk,
                    gas_slot,
                    gas_lane,
                )
                leaving = post[opposite_of[index], x, rows, :]
                open_side = from_gas > 0.5
                value = jnp.where(open_side, equal - leaving, arriving)
                fresh[index, place, rows, :] = value
                total = total + value
                change = change + jnp.where(open_side, 0.0, arriving - leaving)
        read = mass[x, rows, :] + jnp.where(flags[x, rows, :] == 1, change, 0.0)
        mark = code[x, rows, :]
        liquid = mark >= 32.0
        converts = mark > 0.0
        level = jnp.where(liquid, total, 0.0)
        excess[kept, rows, :] = jnp.where(converts, read - level, 0.0)
        heading[kept, rows, :] = jnp.where(liquid, mark - 32.0, mark)
        settled[place, rows, :] = jnp.where(converts, level, read)


def stream_inner(
    post,
    shift,
    mass,
    flags,
    code,
    y_first,
    y_second,
    z_rows,
    corner_first,
    corner_second,
    fresh,
    settled,
    excess,
    heading,
    gas,
    low_rows,
    high_rows,
    columns,
):
    bx = flags.shape[0]
    halos = (gas, low_rows, high_rows, columns)
    own_halos(flags, y_first, y_second, z_rows, corner_first, corner_second, *halos)

    def plane(x, carry):
        stream_plane(
            x,
            post,
            shift,
            mass,
            flags,
            code,
            *halos,
            None,
            None,
            fresh,
            settled,
            excess,
            heading,
            x - 1,
            x - 1,
        )
        return carry

    lax.fori_loop(1, bx - 1, plane, 0)


def stream_outer(
    post,
    shift,
    mass,
    flags,
    code,
    y_first,
    y_second,
    z_rows,
    corner_first,
    corner_second,
    gas_first,
    gas_second,
    x_first,
    x_second,
    edges_first,
    edges_second,
    inner_excess,
    inner_heading,
    fresh,
    settled,
    spread,
    line_first,
    line_second,
    out_z,
    gas,
    low_rows,
    high_rows,
    columns,
    below,
    above,
    excess,
    heading,
):
    bx, by, bz = flags.shape
    halves = bz // lanes
    flip_x = flipped("gx")
    halos = (gas, low_rows, high_rows, columns)
    own_halos(flags, y_first, y_second, z_rows, corner_first, corner_second, *halos)

    for slot in range(5):
        below[slot] = jnp.where(flip_x, x_first[slot], x_second[slot])
        above[slot] = jnp.where(flip_x, x_second[slot], x_first[slot])
    gas[0] = jnp.where(flip_x, gas_first[3], gas_second[3])
    gas[bx + 1] = jnp.where(flip_x, gas_second[3], gas_first[3])
    edges_below = select(flip_x, edges_first, edges_second)
    edges_above = select(flip_x, edges_second, edges_first)
    for found, at, x, edges in (
        (edges_below, 0, bx - 1, up_edges),
        (edges_above, bx + 1, 0, down_edges),
    ):
        for place, (side, slot) in enumerate(edges):
            line = jnp.concatenate(
                [found[half * 4 + place : half * 4 + place + 1, :] for half in range(halves)],
                axis=1,
            )
            (low_rows, high_rows)[side][at, slot : slot + 1, :] = line
        columns[at] = row_columns(found[4 * halves :, :])[x * by : x * by + by, :]
    for place, x in enumerate((0, bx - 1)):
        stream_plane(
            x,
            post,
            shift,
            mass,
            flags,
            code,
            *halos,
            below,
            above,
            fresh,
            settled,
            excess,
            heading,
            place,
            x,
        )
    for x in range(1, bx - 1):
        excess[x] = inner_excess[x - 1]
        heading[x] = inner_heading[x - 1]

    row_at, lane_at = (iota((by, bz), 0), iota((by, bz), 1))
    line_at = iota((1, bz), 1)
    tile_lane, line_lane = (iota((by, lanes), 1), iota((1, lanes), 1))

    def rows_up(rows):
        return jnp.where(row_at == 0, 0.0, pltpu.roll(rows, 1, 0))

    def rows_down(rows):
        return jnp.where(row_at == by - 1, 0.0, pltpu.roll(rows, by - 1, 0))

    def over(rows, at, step):
        if step == 1:
            return jnp.where(at == 0, 0.0, pltpu.roll(rows, 1, 1))
        return jnp.where(at == bz - 1, 0.0, pltpu.roll(rows, bz - 1, 1))

    def summed(parts):
        total = parts[0]
        for part in parts[1:]:
            total = total + part
        return total

    tile = jnp.zeros((by, lanes), jnp.float32)
    line_up = jnp.zeros((1, lanes), jnp.float32)
    line_down = jnp.zeros((1, lanes), jnp.float32)
    flip_y = flipped("gy")
    line_first[...] = jnp.zeros(line_first.shape, jnp.float32)
    line_second[...] = jnp.zeros(line_second.shape, jnp.float32)
    for target in range(bx + 2):
        groups = {}
        for index in range(1, 19):
            step_x, step_y, step_z = velocity_set[index]
            x = target - 1 - step_x
            if 0 <= x < bx:
                part = jnp.where(heading[x] == float(index), excess[x], 0.0)
                groups.setdefault((step_y, step_z), []).append(part)
        groups = {key: summed(parts) for key, parts in groups.items()}
        total = jnp.zeros((by, bz), jnp.float32)
        line = {1: jnp.zeros((1, bz), jnp.float32), -1: jnp.zeros((1, bz), jnp.float32)}
        for step_z in (0, 1, -1):
            group = jnp.zeros((by, bz), jnp.float32)
            ends = {}
            if (0, step_z) in groups:
                group = group + groups[(0, step_z)]
            if (1, step_z) in groups:
                group = group + rows_up(groups[(1, step_z)])
                ends[1] = groups[(1, step_z)][by - 1 : by, :]
            if (-1, step_z) in groups:
                group = group + rows_down(groups[(-1, step_z)])
                ends[-1] = groups[(-1, step_z)][0:1, :]
            if step_z == 0:
                total = total + group
                for side in ends:
                    line[side] = line[side] + ends[side]
                continue
            total = total + over(group, lane_at, step_z)
            for side in ends:
                line[side] = line[side] + over(ends[side], line_at, step_z)
            if step_z == 1:
                spot, cut, roll = (target, slice(bz - lanes, bz), target + 1)
            else:
                spot, cut, roll = (8 + target, slice(0, lanes), 8 + target)
            tile = jnp.where(tile_lane == spot, pltpu.roll(group[:, cut], roll, 1), tile)
            if 1 in ends:
                line_up = jnp.where(
                    line_lane == spot, pltpu.roll(ends[1][:, cut], roll, 1), line_up
                )
            if -1 in ends:
                line_down = jnp.where(
                    line_lane == spot, pltpu.roll(ends[-1][:, cut], roll, 1), line_down
                )
        spread[target] = total
        line_first[target : target + 1, :] = jnp.where(flip_y, line[-1], line[1])
        line_second[target : target + 1, :] = jnp.where(flip_y, line[1], line[-1])
    rest = jnp.zeros((lanes - by - 2, lanes), jnp.float32)
    out_z[...] = column_rows([tile, line_up, line_down, rest], 16)


def with_edges(total, target, tile, y_below, y_above):
    by, bz = total.shape
    row_at, lane_at = (iota((by, bz), 0), iota((by, bz), 1))
    total = total + jnp.where(lane_at == 0, tile[0:by, target : target + 1], 0.0)
    total = total + jnp.where(lane_at == bz - 1, tile[0:by, 8 + target : 9 + target], 0.0)
    total = total + jnp.where(row_at == 0, y_below[target : target + 1, :], 0.0)
    return total + jnp.where(row_at == by - 1, y_above[target : target + 1, :], 0.0)


def add_faces(spread, z_rows, y_first, y_second, first, second):
    last = spread.shape[0] - 1
    flip_x, flip_y = (flipped("gx"), flipped("gy"))
    tile = row_columns(z_rows[...])
    y_below, y_above = (select(flip_y, y_first, y_second), select(flip_y, y_second, y_first))
    up = with_edges(spread[last], last, tile, y_below, y_above)
    down = with_edges(spread[0], 0, tile, y_below, y_above)
    first[...] = jnp.where(flip_x, down, up)
    second[...] = jnp.where(flip_x, up, down)


def add_all(
    inner_settled,
    outer_settled,
    spread,
    z_rows,
    y_first,
    y_second,
    corner_first,
    corner_second,
    x_first,
    x_second,
    new_mass,
):
    bx, by, bz = new_mass.shape
    flip_x, flip_y = (flipped("gx"), flipped("gy"))
    tile = row_columns(z_rows[...])
    y_below, y_above = (select(flip_y, y_first, y_second), select(flip_y, y_second, y_first))
    at = iota((8, bz), 1)
    found = []
    for rows, side, corner in (
        (y_below, 0, select(flip_y, corner_first, corner_second)),
        (y_above, 1, select(flip_y, corner_second, corner_first)),
    ):
        edge = corner[:, by + side : by + side + 1]
        rows = rows + jnp.where(at == 0, edge[0:8, :], 0.0)
        found.append(rows + jnp.where(at == bz - 1, edge[8:16, :], 0.0))
    for x in range(bx):
        total = with_edges(spread[x + 1], x + 1, tile, *found)
        if x == 0:
            total = total + select(flip_x, x_first, x_second)
        if x == bx - 1:
            total = total + select(flip_x, x_second, x_first)
        if 0 < x < bx - 1:
            total = total + inner_settled[x - 1]
        else:
            total = total + outer_settled[0 if x == 0 else 1]
        new_mass[x] = total


def swapped(first, second, axis):
    devices = lax.axis_size(axis)
    ahead = [(i, (i + 1) % devices if i % 2 == 0 else i - 1) for i in range(devices)]
    behind = [(i, (i - 1) % devices if i % 2 == 0 else (i + 1) % devices) for i in range(devices)]
    return lax.ppermute(first, axis, behind), lax.ppermute(second, axis, ahead)


def both_ways(rows, lower):
    devices = lax.axis_size("gz")
    before = lax.ppermute(rows, "gz", [(i, (i + 1) % devices) for i in range(devices)])
    if devices == 2:
        return before
    after = lax.ppermute(rows, "gz", [(i, (i - 1) % devices) for i in range(devices)])
    return jnp.where(iota(rows.shape, 0) < lower, before, after)


remote = pl.BlockSpec(memory_space=pltpu.HBM)


def call(body, outs, specs=None, out_specs=None, scratch=(), cost=(0, 0)):
    extra = {} if specs is None else {"in_specs": specs}
    if out_specs is not None:
        extra["out_specs"] = out_specs
    return pl.pallas_call(
        body,
        out_shape=[
            shape
            if isinstance(shape, jax.ShapeDtypeStruct)
            else jax.ShapeDtypeStruct(shape, jnp.float32)
            for shape in outs
        ],
        scratch_shapes=[
            pltpu.VMEM(shape, jnp.float32) if isinstance(shape, tuple) else shape
            for shape in scratch
        ],
        compiler_params=pltpu.CompilerParams(vmem_limit_bytes=40 * 1024 * 1024),
        cost_estimate=pl.CostEstimate(flops=cost[0], bytes_accessed=cost[1], transcendentals=0),
        **extra,
    )


def shards(populations, stretch, mass, flags, conv_source, conv_kind, conv_direction):
    bx, by, bz = flags.shape
    cells = bx * by * bz
    box, face, tile = ((bx, by, bz), (by, bz), (bx, by, lanes))

    stretch, flags, z_out, y_one, y_two, x_one, x_two = call(
        first_faces,
        [
            (6, *box),
            jax.ShapeDtypeStruct(box, jnp.int32),
            (8, bx * by),
            (4 * bx, bz),
            (4 * bx, bz),
            (4, *face),
            (4, *face),
        ],
        specs=[remote] * 2,
        scratch=[pltpu.SemaphoreType.DMA((2,))],
        cost=(10 * cells, 60 * cells),
    )(*(pltpu.with_memory_space_constraint(array, pltpu.HBM) for array in (stretch, flags)))
    first_x = swapped(x_one, x_two, "gx")
    z_first = both_ways(z_out, 3)
    y_first = swapped(y_one, y_two, "gy")

    entries = conv_source.shape[0]
    (code,) = call(
        lambda *refs: conversions(*refs, columns=bz), [(bx * by, bz)], cost=(40 * cells, 4 * cells)
    )(*(array.reshape(1, entries) for array in (conv_source, conv_kind, conv_direction)))
    code = code.reshape(box)

    pops, flow = call(
        moments,
        [(19, *box), (5, *box)],
        specs=[remote],
        scratch=[pltpu.SemaphoreType.DMA((bx,))],
        cost=(60 * cells, 150 * cells),
    )(pltpu.with_memory_space_constraint(populations, pltpu.HBM))

    columns, rows = ((24, bx * by), (10 * bx, bz))
    post, shift, z_out, x_one, x_two, y_one, y_two = call(
        collide,
        [(19, *box), (3, *box), columns, (8, *face), (8, *face), rows, rows],
        scratch=[(4, *face), (4, *face), (bx, 8, bz), (bx, 8, bz), tile, (1, *box)],
        cost=(300 * cells, 300 * cells),
    )(pops, stretch, flags, flow, *first_x, *y_first, z_first)
    z_post = both_ways(z_out, sides)
    post_y = swapped(y_one, y_two, "gy")
    post_x = swapped(x_one, x_two, "gx")
    edges = (4 * (bz // lanes) + columns[0], lanes)
    x_one, x_two, corner = call(
        lambda *refs: forward_edges(*refs, bx=bx), [edges, edges, columns]
    )(*post_y, z_post)
    corners = swapped(corner, corner, "gy")
    edges_x = swapped(x_one, x_two, "gx")

    rims = [(bx + 2, *face), (bx + 2, 16, bz), (bx + 2, 16, bz), (bx + 2, by, lanes)]
    here = (post, shift, mass, flags, code, *post_y, z_post, *corners)
    inside, beside_faces = ((bx - 2, *face), (2, *face))
    inner, inner_settled, inner_excess, inner_heading = call(
        stream_inner,
        [(19, *inside), inside, inside, inside],
        scratch=rims,
        cost=(200 * cells, 125 * cells),
    )(*here)
    outer, outer_settled, spread, y_one, y_two, z_out = call(
        stream_outer,
        [(19, *beside_faces), beside_faces, (bx + 2, *face), (8, bz), (8, bz), (16, bx * by)],
        scratch=rims + [(5, *face), (5, *face), box, box],
        cost=(250 * cells, 150 * cells),
    )(*here, *first_x, *post_x, *edges_x, inner_excess, inner_heading)
    z_last = both_ways(z_out, 8)
    last_y = swapped(y_one, y_two, "gy")
    last_corners = swapped(z_last, z_last, "gy")
    x_one, x_two = call(add_faces, [face, face])(spread, z_last, *last_y)
    last_x = swapped(x_one, x_two, "gx")
    new_stretch, fresh = call(
        restretch,
        [(6, *box), (19, *box)],
        out_specs=[pl.BlockSpec(), remote],
        scratch=[
            (8, *face),
            (8, *face),
            (bx, 8, bz),
            (bx, 8, bz),
            tile,
            pltpu.SemaphoreType.DMA((3,)),
        ],
        cost=(150 * cells, 80 * cells),
    )(stretch, flow, *post_x, *post_y, z_post, inner, outer)
    (new_mass,) = call(add_all, [box])(
        inner_settled, outer_settled, spread, z_last, *last_y, *last_corners, *last_x
    )
    return (fresh, new_stretch, new_mass)


def solution(mesh):
    return jax.shard_map(
        shards,
        mesh=mesh,
        in_specs=(
            P(None, "gx", "gy", "gz"),
            P(None, "gx", "gy", "gz"),
            P("gx", "gy", "gz"),
            P("gx", "gy", "gz"),
            P(("gx", "gy", "gz")),
            P(("gx", "gy", "gz")),
            P(("gx", "gy", "gz")),
        ),
        out_specs=(P(None, "gx", "gy", "gz"), P(None, "gx", "gy", "gz"), P("gx", "gy", "gz")),
        check_vma=False,
    )
```

```python
import jax
import jax.numpy as jnp
from jax import lax
from jax.experimental import pallas as pl
from jax.experimental.pallas import tpu as pltpu
from jax.sharding import PartitionSpec as P

velocity_set = (
    (0, 0, 0),
    (1, 0, 0),
    (-1, 0, 0),
    (0, 1, 0),
    (0, -1, 0),
    (0, 0, 1),
    (0, 0, -1),
    (1, 1, 0),
    (-1, -1, 0),
    (1, -1, 0),
    (-1, 1, 0),
    (1, 0, 1),
    (-1, 0, -1),
    (1, 0, -1),
    (-1, 0, 1),
    (0, 1, 1),
    (0, -1, -1),
    (0, 1, -1),
    (0, -1, 1),
)
opposite_of = (0, 2, 1, 4, 3, 6, 5, 8, 7, 10, 9, 12, 11, 14, 13, 16, 15, 18, 17)
lattice_weights = (1.0 / 3.0,) + (1.0 / 18.0,) * 6 + (1.0 / 36.0,) * 12
symmetric_slot = ((0, 3, 4), (3, 1, 5), (4, 5, 2))
tensor_pairs = ((0, 0), (1, 1), (2, 2), (0, 1), (0, 2), (1, 2))
relax_time = 0.8
polymer_time = 8.0
polymer_coeff = 0.05


def moving(axis, sign):
    return tuple(index for index in range(19) if velocity_set[index][axis] == sign)


x_up, x_down = (moving(0, 1), moving(0, -1))
y_up, y_down = (moving(1, 1), moving(1, -1))
z_up, z_down = (moving(2, 1), moving(2, -1))
pairs = tuple(range(1, 19, 2))
gas_slot = 5
speed_slot = 6
edge_slot = 9
sides = 9
lanes = 128
tall = 8


def iota(shape, dim):
    return lax.broadcasted_iota(jnp.int32, shape, dim)


def wide(tile, width):
    return jnp.concatenate([tile] * (width // tile.shape[1]), axis=1)


def rows_of(load, chunk, chunks, step, edge):
    low = chunk * tall
    if step == 0:
        return load(low, low + tall)
    if step == 1 and chunk > 0:
        return load(low - 1, low + tall - 1)
    if step == -1 and chunk < chunks - 1:
        return load(low + 1, low + tall + 1)
    rows = load(low, low + tall)
    at = iota(rows.shape, 0)
    if step == 1:
        return jnp.where(at == 0, edge(), pltpu.roll(rows, 1, 0))
    return jnp.where(at == tall - 1, edge(), pltpu.roll(rows, tall - 1, 0))


def columns_of(rows, halo, lane, step):
    width = rows.shape[1]
    at = iota(rows.shape, 1)
    if step == 1:
        edge = wide(pltpu.roll(halo, (lanes - lane) % lanes, 1), width)
        return jnp.where(at == 0, edge, pltpu.roll(rows, 1, 1))
    edge = wide(pltpu.roll(halo, lanes - 1 - lane, 1), width)
    return jnp.where(at == width - 1, edge, pltpu.roll(rows, width - 1, 1))


def packed(high, low):
    at = iota(high[0].shape, 1)
    tile = jnp.zeros_like(high[0])
    for slot, part in enumerate(high):
        tile = jnp.where(at == slot, pltpu.roll(part, slot + 1, 1), tile)
    for place, part in enumerate(low):
        slot = len(high) + place
        tile = jnp.where(at == slot, pltpu.roll(part, slot, 1), tile)
    return tile


def along(index, vector):
    total = None
    for comp in range(3):
        sign = velocity_set[index][comp]
        if sign != 0:
            term = vector[comp] if sign > 0 else -vector[comp]
            total = term if total is None else total + term
    return total


def conversions(source, kind, heading, code, *, columns):
    count = source.shape[1]
    value = (heading[...] + 32 * kind[...]).astype(jnp.float32)
    row, column = (source[...] // columns, source[...] % columns)
    by_row = jnp.where(iota((code.shape[0], count), 0) == row, value, 0.0).astype(jnp.bfloat16)
    by_column = jnp.where(iota((columns, count), 0) == column, 1.0, 0.0).astype(jnp.bfloat16)
    code[...] = lax.dot_general(
        by_row, by_column, (((1,), (1,)), ((), ())), preferred_element_type=jnp.float32
    )


def odd(axis):
    return lax.rem(lax.axis_index(axis), 2) == 1


def select(chosen, first, second):
    return jnp.where(chosen, first[...], second[...])


def swap_rows(first, second, x, planes, high, low, flip):
    for slot, (top, bottom) in enumerate(zip(high, low)):
        by = top.shape[0]
        up, down = (top[by - 1 : by, :], bottom[0:1, :])
        at = slot * planes + x
        first[at : at + 1, :] = jnp.where(flip, down, up)
        second[at : at + 1, :] = jnp.where(flip, up, down)


def swapped_rows(first, second, slots, low_rows, high_rows, shift):
    flip = odd("gy")
    planes = low_rows.shape[0] - 2 * shift
    for x in range(planes):
        for place, slot in enumerate(slots):
            at = slot * planes + x
            one, two = (first[at : at + 1, :], second[at : at + 1, :])
            low_rows[x + shift, place : place + 1, :] = jnp.where(flip, one, two)
            high_rows[x + shift, place : place + 1, :] = jnp.where(flip, two, one)


def column_rows(tiles, count):
    return jnp.concatenate(tiles, axis=0).T[0:count, :]


def row_columns(rows):
    rest = jnp.zeros((lanes - rows.shape[0], rows.shape[1]), jnp.float32)
    return jnp.concatenate([rows, rest], axis=0).T


def first_faces(
    stretch_in,
    flags_in,
    stretch,
    flags,
    columns,
    y_first,
    y_second,
    x_first,
    x_second,
    sems,
):
    bx, by, bz = flags.shape
    flip_x, flip_y = (odd("gx"), odd("gy"))
    copies = [
        pltpu.make_async_copy(stretch_in, stretch, sems.at[0]),
        pltpu.make_async_copy(flags_in, flags, sems.at[1]),
    ]
    for copy in copies:
        copy.start()
    for copy in copies:
        copy.wait()
    tiles = []
    for x in range(bx):
        along_y = [stretch.at[symmetric_slot[comp][1], x] for comp in range(3)]
        swap_rows(y_first, y_second, x, bx, along_y, along_y, flip_y)
        fields = [stretch.at[symmetric_slot[comp][2], x] for comp in range(3)]
        tiles.append(
            packed(
                [field[:, bz - lanes : bz] for field in fields],
                [field[:, 0:lanes] for field in fields],
            )
        )
    columns[...] = column_rows(tiles, columns.shape[0])
    rest = y_first.shape[0] - 3 * bx
    y_first[3 * bx :, :] = jnp.zeros((rest, bz), jnp.float32)
    y_second[3 * bx :, :] = jnp.zeros((rest, bz), jnp.float32)
    for out, last in ((x_first, flip_x), (x_second, jnp.logical_not(flip_x))):
        for comp in range(3):
            slot = symmetric_slot[comp][0]
            out[comp] = jnp.where(last, stretch[slot, 0], stretch[slot, bx - 1])
        out[3] = jnp.where(jnp.where(last, flags[0], flags[bx - 1]) == 0, 1.0, 0.0)


def moments(pops_in, pops, flow, sems):
    bx, by = pops.shape[1:3]
    copies = [
        pltpu.make_async_copy(pops_in.at[:, x], pops.at[:, x], sems.at[x]) for x in range(bx)
    ]
    for copy in copies:
        copy.start()
    for x in range(bx):
        copies[x].wait()
        for chunk in range(by // tall):
            rows = pl.ds(chunk * tall, tall)
            part = [pops[index, x, rows, :] for index in range(19)]
            density = part[0]
            for index in range(1, 19):
                density = density + part[index]
            inverse = 1.0 / density
            for comp in range(3):
                total = None
                for index in pairs:
                    sign = velocity_set[index][comp]
                    if sign != 0:
                        term = part[index] - part[index + 1]
                        term = term if sign > 0 else -term
                        total = term if total is None else total + term
                flow[comp, x, rows, :] = total * inverse
            flow[3, x, rows, :] = density
            flow[4, x, rows, :] = inverse


def beside(ref, field, x, step, halo, slot):
    last = ref.shape[1] - 1
    if halo is None:
        return lambda low, high: ref[field, x + step, low:high, :]
    if isinstance(x, int):
        if 0 <= x + step <= last:
            return lambda low, high: ref[field, x + step, low:high, :]
        return lambda low, high: halo[slot, low:high, :]
    inside = jnp.clip(x + step, 0, last)
    beyond = x == (0 if step < 0 else last)
    return lambda low, high: jnp.where(
        beyond, halo[slot, low:high, :], ref[field, inside, low:high, :]
    )


def differences(
    ref, field, slots, x, chunk, chunks, below, above, y_below, y_above, z_halo, lane, side
):
    slot_x, slot_y, slot_z = slots
    low, high = (chunk * tall, chunk * tall + tall)

    def load(first, stop):
        return ref[field, x, first:stop, :]

    result = [None, None, None]
    if slot_x is not None:
        after = beside(ref, field, x, 1, above, slot_x)(low, high)
        before = beside(ref, field, x, -1, below, slot_x)(low, high)
        result[0] = after - before
    if slot_y is not None:
        after = rows_of(load, chunk, chunks, -1, lambda: y_above[x, slot_y : slot_y + 1, :])
        before = rows_of(load, chunk, chunks, 1, lambda: y_below[x, slot_y : slot_y + 1, :])
        result[1] = after - before
    if slot_z is not None:
        rows, halo = (load(low, high), z_halo[x, low:high, :])
        after = columns_of(rows, halo, lane + side + slot_z, -1)
        before = columns_of(rows, halo, lane + slot_z, 1)
        result[2] = after - before
    return result


def end_place(x, bx):
    return 0 if x == 0 else 1


def plane_of(inner, outer, field, x, bx):
    if 0 < x < bx - 1:
        return inner.at[field, x - 1]
    return outer.at[field, end_place(x, bx)]


def collide_plane(x, place, pops, stretch, flow, halos, post, shift):
    by = pops.shape[2]
    chunks = by // tall
    factor = 1.0 - 0.5 / relax_time
    rate = 1.0 / relax_time
    for chunk in range(chunks):
        rows = pl.ds(chunk * tall, tall)
        terms = [[], [], []]
        for field in range(6):
            slots = [None, None, None]
            for comp in range(3):
                for axis in range(3):
                    if symmetric_slot[comp][axis] == field:
                        slots[axis] = comp
            found = differences(stretch, field, slots, x, chunk, chunks, *halos)
            for axis in range(3):
                if slots[axis] is not None:
                    terms[slots[axis]].append(found[axis])
        force = [0.5 * polymer_coeff * (part[0] + part[1] + part[2]) for part in terms]
        density, half = (flow[3, x, rows, :], 0.5 * flow[4, x, rows, :])
        moved = [flow[comp, x, rows, :] + half * force[comp] for comp in range(3)]
        for comp in range(3):
            shift[comp, place, rows, :] = moved[comp]
        squared = moved[0] * moved[0] + moved[1] * moved[1] + moved[2] * moved[2]
        work = moved[0] * force[0] + moved[1] * force[1] + moved[2] * force[2]
        weight = rate * density
        common = weight - 1.5 * weight * squared - 3.0 * factor * work
        odd = [3.0 * weight * moved[comp] + 3.0 * factor * force[comp] for comp in range(3)]
        even = [4.5 * weight * moved[comp] + 9.0 * factor * force[comp] for comp in range(3)]
        keep = 1.0 - rate
        post[0, place, rows, :] = keep * pops[0, x, rows, :] + lattice_weights[0] * common
        for index in pairs:
            both = common + along(index, moved) * along(index, even)
            differ = along(index, odd)
            scale = lattice_weights[index]
            post[index, place, rows, :] = keep * pops[index, x, rows, :] + scale * (both + differ)
            post[index + 1, place, rows, :] = keep * pops[index + 1, x, rows, :] + scale * (
                both - differ
            )


def collide_inner(
    pops,
    stretch,
    flow,
    y_first,
    y_second,
    z_rows,
    post,
    shift,
    y_below,
    y_above,
    z_halo,
):
    swapped_rows(y_first, y_second, range(3), y_below, y_above, 0)
    z_halo[...] = row_columns(z_rows[...]).reshape(z_halo.shape)
    halos = (None, None, y_below, y_above, z_halo, 0, 3)

    def plane(x, carry):
        collide_plane(x, x - 1, pops, stretch, flow, halos, post, shift)
        return carry

    lax.fori_loop(1, pops.shape[1] - 1, plane, 0)


def collide_outer(
    pops,
    stretch,
    flags,
    flow,
    x_first,
    x_second,
    y_first,
    y_second,
    z_rows,
    inner,
    post,
    shift,
    columns,
    ahead,
    behind,
    up_first,
    up_second,
    below,
    above,
    y_below,
    y_above,
    z_halo,
    gas,
):
    bx, by, bz = flags.shape
    halos = (below, above, y_below, y_above, z_halo, 0, 3)
    flip_x, flip_y = (odd("gx"), odd("gy"))
    below[...] = select(flip_x, x_first, x_second)
    above[...] = select(flip_x, x_second, x_first)
    swapped_rows(y_first, y_second, range(3), y_below, y_above, 0)
    z_halo[...] = row_columns(z_rows[...]).reshape(z_halo.shape)
    for x in (0, bx - 1):
        collide_plane(x, end_place(x, bx), pops, stretch, flow, halos, post, shift)

    tiles = []
    for x in range(bx):
        gas[x] = jnp.where(flags[x] == 0, 1.0, 0.0)
        rest = [gas.at[x]] + [flow.at[comp, x] for comp in range(3)]

        def fields(indices):
            return [plane_of(inner, post, index, x, bx) for index in indices] + rest

        swap_rows(up_first, up_second, x, bx, fields(y_up), fields(y_down), flip_y)
        tiles.append(
            packed(
                [field[:, bz - lanes : bz] for field in fields(z_up)],
                [field[:, 0:lanes] for field in fields(z_down)],
            )
        )
    columns[...] = column_rows(tiles, columns.shape[0])
    rest = up_first.shape[0] - sides * bx
    up_first[sides * bx :, :] = jnp.zeros((rest, bz), jnp.float32)
    up_second[sides * bx :, :] = jnp.zeros((rest, bz), jnp.float32)
    for slot in range(5):
        up, down = (post[x_up[slot], 1], post[x_down[slot], 0])
        ahead[slot] = jnp.where(flip_x, down, up)
        behind[slot] = jnp.where(flip_x, up, down)
    for comp in range(3):
        up, down = (flow[comp, bx - 1], flow[comp, 0])
        ahead[5 + comp] = jnp.where(flip_x, down, up)
        behind[5 + comp] = jnp.where(flip_x, up, down)


def restretch(
    stretch,
    flow,
    x_first,
    x_second,
    y_first,
    y_second,
    z_rows,
    inner,
    outer,
    inner_slanted,
    outer_slanted,
    late,
    updated,
    fresh,
    below,
    above,
    y_below,
    y_above,
    z_halo,
    sems,
):
    bx, by, bz = stretch.shape[1:]
    moves = [
        (inner, fresh.at[0:first_slanted, 1 : bx - 1]),
        (inner_slanted, fresh.at[first_slanted:, 1 : bx - 1]),
    ]
    for place, x in enumerate((0, bx - 1)):
        moves.append((outer_slanted.at[:, place], fresh.at[first_slanted:, x]))
        order = (x_up, x_down)[place]
        start = 0
        for index in order + (first_slanted,):
            if index > start:
                run = slice(start, index)
                moves.append((outer.at[run, place], fresh.at[run, x]))
            if index in order:
                moves.append((late.at[order.index(index), place], fresh.at[index, x]))
            start = index + 1
    copies = [
        pltpu.make_async_copy(source, target, sems.at[place])
        for place, (source, target) in enumerate(moves)
    ]
    for copy in copies:
        copy.start()
    chunks = by // tall
    flip_x = odd("gx")
    below[...] = select(flip_x, x_first, x_second)
    above[...] = select(flip_x, x_second, x_first)
    swapped_rows(y_first, y_second, range(speed_slot, sides), y_below, y_above, 0)
    z_halo[...] = row_columns(z_rows[...]).reshape(z_halo.shape)

    def plane(x, carry):
        for chunk in range(chunks):
            rows = pl.ds(chunk * tall, tall)
            grad = [
                differences(
                    flow,
                    comp,
                    (5 + comp, comp, comp),
                    x,
                    chunk,
                    chunks,
                    below,
                    above,
                    y_below,
                    y_above,
                    z_halo,
                    speed_slot,
                    sides,
                )
                for comp in range(3)
            ]
            part = [stretch[slot, x, rows, :] for slot in range(6)]
            full = [part[slot] + 1.0 if slot < 3 else part[slot] for slot in range(6)]

            def product(row, col):
                total = grad[row][0] * full[symmetric_slot[0][col]]
                for inner in (1, 2):
                    total = total + grad[row][inner] * full[symmetric_slot[inner][col]]
                return total

            for slot, (row, col) in enumerate(tensor_pairs):
                old = (1.0 - 1.0 / polymer_time) * part[slot]
                if row == col:
                    updated[slot, x, rows, :] = old + product(row, col)
                else:
                    updated[slot, x, rows, :] = old + 0.5 * (product(row, col) + product(col, row))
        return carry

    lax.fori_loop(0, bx, plane, 0)
    for copy in copies:
        copy.wait()


up_edges = ((0, y_up.index(7)), (0, gas_slot), (1, y_down.index(9)), (1, gas_slot))
down_edges = ((0, y_up.index(10)), (0, gas_slot), (1, y_down.index(8)), (1, gas_slot))


def forward_edges(y_first, y_second, z_rows, first_out, second_out, corner, *, bx):
    halves = y_first.shape[1] // lanes
    flip_x, flip_y = (odd("gx"), odd("gy"))
    for half in range(halves):
        cut = slice(half * lanes, half * lanes + lanes)
        for place in range(4):
            found = []
            for x, edges in ((bx - 1, up_edges), (0, down_edges)):
                side, slot = edges[place]
                row = slot * bx + x
                one = y_first[row : row + 1, cut]
                two = y_second[row : row + 1, cut]
                found.append(jnp.where(flip_y, one, two) if side == 0 else jnp.where(flip_y, two, one))
            at = half * 4 + place
            first_out[at : at + 1, :] = jnp.where(flip_x, found[1], found[0])
            second_out[at : at + 1, :] = jnp.where(flip_x, found[0], found[1])
    first_out[4 * halves :, :] = z_rows[...]
    second_out[4 * halves :, :] = z_rows[...]
    corner[...] = z_rows[...]


def own_halos(flags, y_first, y_second, z_rows, gas, low_rows, high_rows, columns):
    bx, by = flags.shape[:2]
    tile = row_columns(z_rows[...])
    swapped_rows(y_first, y_second, range(speed_slot), low_rows, high_rows, 1)
    for x in range(bx):
        gas[x + 1] = jnp.where(flags[x] == 0, 1.0, 0.0)
        columns[x + 1] = tile[x * by : x * by + by, :]


def own_corners(corner_first, corner_second, low_rows, high_rows):
    bx = low_rows.shape[0] - 2
    flip = odd("gy")
    corner_below = row_columns(select(flip, corner_first, corner_second))
    corner_above = row_columns(select(flip, corner_second, corner_first))
    by = corner_below.shape[0] // bx
    for x in range(bx):
        end = x * by + by - 1
        low_rows[x + 1, edge_slot : edge_slot + 1, 0:lanes] = corner_below[end : end + 1, :]
        high_rows[x + 1, edge_slot : edge_slot + 1, 0:lanes] = corner_above[
            x * by : x * by + 1, :
        ]


def pass_on(x, chunk, indices, source, leaving_of, speed, halos, fresh, place, total, change):
    gas, low_rows, high_rows, columns = halos
    by = gas.shape[1]
    chunks = by // tall
    rows = pl.ds(chunk * tall, tall)
    rest = 1.0 - 1.5 * (speed[0] * speed[0] + speed[1] * speed[1] + speed[2] * speed[2])
    equals = {}

    def moved(load, index, slot, lane):
        step_x, step_y, step_z = velocity_set[index]
        plane = x + 1 - step_x
        edges = low_rows if step_y == 1 else high_rows
        found = rows_of(load, chunk, chunks, step_y, lambda: edges[plane, slot : slot + 1, :])
        if step_z == 0:
            return found
        halo = rows_of(
            lambda low, high: columns[plane, low:high, :],
            chunk,
            chunks,
            step_y,
            lambda: edges[plane, edge_slot : edge_slot + 1, 0:lanes],
        )
        return columns_of(found, halo, lane, step_z)

    for index in indices:
        step_x, step_y, step_z = velocity_set[index]
        first = min(index, opposite_of[index])
        if first not in equals:
            proj = along(first, speed)
            equals[first] = 2.0 * lattice_weights[first] * (rest + 4.5 * proj * proj)
        slot, lane, gas_lane = (None, None, None)
        if step_y != 0:
            slot = (y_up if step_y == 1 else y_down).index(index)
        if step_z == 1:
            lane, gas_lane = (z_up.index(index), gas_slot)
        elif step_z == -1:
            lane, gas_lane = (sides + z_down.index(index), sides + gas_slot)
        field = source(index)
        marks = gas.at[x + 1 - step_x]
        arriving = moved(lambda low, high: field[low:high, :], index, slot, lane)
        from_gas = moved(lambda low, high: marks[low:high, :], index, gas_slot, gas_lane)
        leaving = leaving_of(opposite_of[index])[rows, :]
        open_side = from_gas > 0.5
        value = jnp.where(open_side, equals[first] - leaving, arriving)
        fresh(index)[place, rows, :] = value
        total = total + value
        change = change + jnp.where(open_side, 0.0, arriving - leaving)
    return total, change


def settle(x, rows, mass, flags, code, total, change):
    read = mass[x, rows, :] + jnp.where(flags[x, rows, :] == 1, change, 0.0)
    mark = code[x, rows, :]
    liquid = mark >= 32.0
    converts = mark > 0.0
    level = jnp.where(liquid, total, 0.0)
    excess = jnp.where(converts, read - level, 0.0)
    heading = jnp.where(liquid, mark - 32.0, mark)
    return jnp.where(converts, level, read), excess, heading


slanted = tuple(index for index in range(19) if velocity_set[index][1] * velocity_set[index][2])
first_slanted = slanted[0]


def from_inside(x, bx):
    found = [index for index in range(1, 19) if 0 <= x - velocity_set[index][0] < bx]
    return [index for index in found if index not in slanted]


def from_beyond(x, bx):
    return [index for index in range(1, 19) if not 0 <= x - velocity_set[index][0] < bx]


def stream_early(
    inner_post,
    outer_post,
    inner_shift,
    outer_shift,
    flags,
    y_first,
    y_second,
    z_rows,
    inner,
    outer,
    totals,
    changes,
    gas,
    low_rows,
    high_rows,
    columns,
):
    bx, by, bz = flags.shape
    halos = (gas, low_rows, high_rows, columns)
    own_halos(flags, y_first, y_second, z_rows, *halos)

    for x in range(bx):
        inside = 0 < x < bx - 1
        place = x - 1 if inside else end_place(x, bx)
        fresh = inner if inside else outer
        for chunk in range(by // tall):
            rows = pl.ds(chunk * tall, tall)
            total = plane_of(inner_post, outer_post, 0, x, bx)[rows, :]
            fresh[0, place, rows, :] = total
            total, change = pass_on(
                x,
                chunk,
                from_inside(x, bx),
                lambda index: plane_of(
                    inner_post, outer_post, index, x - velocity_set[index][0], bx
                ),
                lambda index: plane_of(inner_post, outer_post, index, x, bx),
                [plane_of(inner_shift, outer_shift, comp, x, bx)[rows, :] for comp in range(3)],
                halos,
                lambda index: fresh.at[index],
                place,
                total,
                jnp.zeros((tall, bz), jnp.float32),
            )
            totals[x, rows, :] = total
            changes[x, rows, :] = change


def stream_slanted(
    inner_post,
    outer_post,
    inner_shift,
    outer_shift,
    mass,
    flags,
    code,
    y_first,
    y_second,
    z_rows,
    corner_first,
    corner_second,
    totals,
    changes,
    inner,
    outer,
    settled,
    excess,
    heading,
    end_totals,
    end_changes,
    gas,
    low_rows,
    high_rows,
    columns,
):
    bx, by, bz = flags.shape
    halos = (gas, low_rows, high_rows, columns)
    own_halos(flags, y_first, y_second, z_rows, *halos)
    own_corners(corner_first, corner_second, low_rows, high_rows)

    for x in range(bx):
        inside = 0 < x < bx - 1
        place = x - 1 if inside else end_place(x, bx)
        fresh = inner if inside else outer
        for chunk in range(by // tall):
            rows = pl.ds(chunk * tall, tall)
            total, change = pass_on(
                x,
                chunk,
                slanted,
                lambda index: plane_of(inner_post, outer_post, index, x, bx),
                lambda index: plane_of(inner_post, outer_post, index, x, bx),
                [plane_of(inner_shift, outer_shift, comp, x, bx)[rows, :] for comp in range(3)],
                halos,
                lambda index: fresh.at[index - first_slanted],
                place,
                totals[x, rows, :],
                changes[x, rows, :],
            )
            if inside:
                now = settle(x, rows, mass, flags, code, total, change)
                settled[place, rows, :], excess[place, rows, :], heading[place, rows, :] = now
            else:
                end_totals[place, rows, :] = total
                end_changes[place, rows, :] = change


def stream_late(
    post,
    shift,
    mass,
    flags,
    code,
    totals,
    changes,
    gas_first,
    gas_second,
    x_first,
    x_second,
    edges_first,
    edges_second,
    inner_excess,
    inner_heading,
    late,
    settled,
    spread,
    line_first,
    line_second,
    out_z,
    gas,
    low_rows,
    high_rows,
    columns,
    below,
    above,
    excess,
    heading,
):
    bx, by, bz = flags.shape
    halves = bz // lanes
    flip_x = odd("gx")
    halos = (gas, low_rows, high_rows, columns)

    for slot in range(5):
        below[slot] = jnp.where(flip_x, x_first[slot], x_second[slot])
        above[slot] = jnp.where(flip_x, x_second[slot], x_first[slot])
    gas[0] = jnp.where(flip_x, gas_first[3], gas_second[3])
    gas[bx + 1] = jnp.where(flip_x, gas_second[3], gas_first[3])
    edges_below = select(flip_x, edges_first, edges_second)
    edges_above = select(flip_x, edges_second, edges_first)
    for found, at, x, edges in (
        (edges_below, 0, bx - 1, up_edges),
        (edges_above, bx + 1, 0, down_edges),
    ):
        for place, (side, slot) in enumerate(edges):
            line = jnp.concatenate(
                [found[half * 4 + place : half * 4 + place + 1, :] for half in range(halves)],
                axis=1,
            )
            (low_rows, high_rows)[side][at, slot : slot + 1, :] = line
        columns[at] = row_columns(found[4 * halves :, :])[x * by : x * by + by, :]
    for place, x in enumerate((0, bx - 1)):
        halo, order = ((below, x_up), (above, x_down))[place]
        for chunk in range(by // tall):
            rows = pl.ds(chunk * tall, tall)
            total, change = pass_on(
                x,
                chunk,
                from_beyond(x, bx),
                lambda index: halo.at[order.index(index)],
                lambda index: post.at[index, place],
                [shift[comp, place, rows, :] for comp in range(3)],
                halos,
                lambda index: late.at[order.index(index)],
                place,
                totals[place, rows, :],
                changes[place, rows, :],
            )
            now = settle(x, rows, mass, flags, code, total, change)
            settled[place, rows, :], excess[x, rows, :], heading[x, rows, :] = now
    for x in range(1, bx - 1):
        excess[x] = inner_excess[x - 1]
        heading[x] = inner_heading[x - 1]

    row_at, lane_at = (iota((by, bz), 0), iota((by, bz), 1))
    line_at = iota((1, bz), 1)
    tile_lane, line_lane = (iota((by, lanes), 1), iota((1, lanes), 1))

    def rows_up(rows):
        return jnp.where(row_at == 0, 0.0, pltpu.roll(rows, 1, 0))

    def rows_down(rows):
        return jnp.where(row_at == by - 1, 0.0, pltpu.roll(rows, by - 1, 0))

    def over(rows, at, step):
        if step == 1:
            return jnp.where(at == 0, 0.0, pltpu.roll(rows, 1, 1))
        return jnp.where(at == bz - 1, 0.0, pltpu.roll(rows, bz - 1, 1))

    def summed(parts):
        total = parts[0]
        for part in parts[1:]:
            total = total + part
        return total

    tile = jnp.zeros((by, lanes), jnp.float32)
    line_up = jnp.zeros((1, lanes), jnp.float32)
    line_down = jnp.zeros((1, lanes), jnp.float32)
    flip_y = odd("gy")
    line_first[...] = jnp.zeros(line_first.shape, jnp.float32)
    line_second[...] = jnp.zeros(line_second.shape, jnp.float32)
    for target in range(bx + 2):
        groups = {}
        for index in range(1, 19):
            step_x, step_y, step_z = velocity_set[index]
            x = target - 1 - step_x
            if 0 <= x < bx:
                part = jnp.where(heading[x] == float(index), excess[x], 0.0)
                groups.setdefault((step_y, step_z), []).append(part)
        groups = {key: summed(parts) for key, parts in groups.items()}
        total = jnp.zeros((by, bz), jnp.float32)
        line = {1: jnp.zeros((1, bz), jnp.float32), -1: jnp.zeros((1, bz), jnp.float32)}
        for step_z in (0, 1, -1):
            group = jnp.zeros((by, bz), jnp.float32)
            ends = {}
            if (0, step_z) in groups:
                group = group + groups[(0, step_z)]
            if (1, step_z) in groups:
                group = group + rows_up(groups[(1, step_z)])
                ends[1] = groups[(1, step_z)][by - 1 : by, :]
            if (-1, step_z) in groups:
                group = group + rows_down(groups[(-1, step_z)])
                ends[-1] = groups[(-1, step_z)][0:1, :]
            if step_z == 0:
                total = total + group
                for side in ends:
                    line[side] = line[side] + ends[side]
                continue
            total = total + over(group, lane_at, step_z)
            for side in ends:
                line[side] = line[side] + over(ends[side], line_at, step_z)
            if step_z == 1:
                spot, cut, roll = (target, slice(bz - lanes, bz), target + 1)
            else:
                spot, cut, roll = (8 + target, slice(0, lanes), 8 + target)
            tile = jnp.where(tile_lane == spot, pltpu.roll(group[:, cut], roll, 1), tile)
            if 1 in ends:
                line_up = jnp.where(
                    line_lane == spot, pltpu.roll(ends[1][:, cut], roll, 1), line_up
                )
            if -1 in ends:
                line_down = jnp.where(
                    line_lane == spot, pltpu.roll(ends[-1][:, cut], roll, 1), line_down
                )
        spread[target] = total
        line_first[target : target + 1, :] = jnp.where(flip_y, line[-1], line[1])
        line_second[target : target + 1, :] = jnp.where(flip_y, line[1], line[-1])
    rest = jnp.zeros((lanes - by - 2, lanes), jnp.float32)
    out_z[...] = column_rows([tile, line_up, line_down, rest], 16)


def with_edges(total, target, tile, y_below, y_above):
    by, bz = total.shape
    row_at, lane_at = (iota((by, bz), 0), iota((by, bz), 1))
    total = total + jnp.where(lane_at == 0, tile[0:by, target : target + 1], 0.0)
    total = total + jnp.where(lane_at == bz - 1, tile[0:by, 8 + target : 9 + target], 0.0)
    total = total + jnp.where(row_at == 0, y_below[target : target + 1, :], 0.0)
    return total + jnp.where(row_at == by - 1, y_above[target : target + 1, :], 0.0)


def add_faces(spread, z_rows, y_first, y_second, first, second):
    last = spread.shape[0] - 1
    flip_x, flip_y = (odd("gx"), odd("gy"))
    tile = row_columns(z_rows[...])
    y_below, y_above = (select(flip_y, y_first, y_second), select(flip_y, y_second, y_first))
    up = with_edges(spread[last], last, tile, y_below, y_above)
    down = with_edges(spread[0], 0, tile, y_below, y_above)
    first[...] = jnp.where(flip_x, down, up)
    second[...] = jnp.where(flip_x, up, down)


def add_all(
    inner_settled,
    outer_settled,
    spread,
    z_rows,
    y_first,
    y_second,
    corner_first,
    corner_second,
    x_first,
    x_second,
    new_mass,
):
    bx, by, bz = new_mass.shape
    flip_x, flip_y = (odd("gx"), odd("gy"))
    tile = row_columns(z_rows[...])
    y_below, y_above = (select(flip_y, y_first, y_second), select(flip_y, y_second, y_first))
    at = iota((8, bz), 1)
    found = []
    for rows, side, corner in (
        (y_below, 0, select(flip_y, corner_first, corner_second)),
        (y_above, 1, select(flip_y, corner_second, corner_first)),
    ):
        edge = corner[:, by + side : by + side + 1]
        rows = rows + jnp.where(at == 0, edge[0:8, :], 0.0)
        found.append(rows + jnp.where(at == bz - 1, edge[8:16, :], 0.0))
    for x in range(bx):
        total = with_edges(spread[x + 1], x + 1, tile, *found)
        if x == 0:
            total = total + select(flip_x, x_first, x_second)
        if x == bx - 1:
            total = total + select(flip_x, x_second, x_first)
        if 0 < x < bx - 1:
            total = total + inner_settled[x - 1]
        else:
            total = total + outer_settled[0 if x == 0 else 1]
        new_mass[x] = total


def swapped(first, second, axis):
    devices = lax.axis_size(axis)
    ahead = [(i, (i + 1) % devices if i % 2 == 0 else i - 1) for i in range(devices)]
    behind = [(i, (i - 1) % devices if i % 2 == 0 else (i + 1) % devices) for i in range(devices)]
    return lax.ppermute(first, axis, ahead), lax.ppermute(second, axis, behind)


def both_ways(rows, lower):
    devices = lax.axis_size("gz")
    before = lax.ppermute(rows, "gz", [(i, (i + 1) % devices) for i in range(devices)])
    if devices == 2:
        return before
    after = lax.ppermute(rows, "gz", [(i, (i - 1) % devices) for i in range(devices)])
    return jnp.where(iota(rows.shape, 0) < lower, before, after)


remote = pl.BlockSpec(memory_space=pltpu.HBM)


def call(body, outs, specs=None, out_specs=None, scratch=(), cost=(0, 0)):
    extra = {} if specs is None else {"in_specs": specs}
    if out_specs is not None:
        extra["out_specs"] = out_specs
    return pl.pallas_call(
        body,
        out_shape=[
            shape
            if isinstance(shape, jax.ShapeDtypeStruct)
            else jax.ShapeDtypeStruct(shape, jnp.float32)
            for shape in outs
        ],
        scratch_shapes=[
            pltpu.VMEM(shape, jnp.float32) if isinstance(shape, tuple) else shape
            for shape in scratch
        ],
        compiler_params=pltpu.CompilerParams(vmem_limit_bytes=40 * 1024 * 1024),
        cost_estimate=pl.CostEstimate(flops=cost[0], bytes_accessed=cost[1], transcendentals=0),
        **extra,
    )


def shards(populations, stretch, mass, flags, conv_source, conv_kind, conv_direction):
    bx, by, bz = flags.shape
    cells = bx * by * bz
    box, face, tile = ((bx, by, bz), (by, bz), (bx, by, lanes))

    stretch, flags, z_out, y_one, y_two, x_one, x_two = call(
        first_faces,
        [
            (6, *box),
            jax.ShapeDtypeStruct(box, jnp.int32),
            (8, bx * by),
            (4 * bx, bz),
            (4 * bx, bz),
            (4, *face),
            (4, *face),
        ],
        specs=[remote] * 2,
        scratch=[pltpu.SemaphoreType.DMA((2,))],
        cost=(10 * cells, 60 * cells),
    )(*(pltpu.with_memory_space_constraint(array, pltpu.HBM) for array in (stretch, flags)))
    first_x = swapped(x_one, x_two, "gx")
    z_first = both_ways(z_out, 3)
    y_first = swapped(y_one, y_two, "gy")

    entries = conv_source.shape[0]
    (code,) = call(
        lambda *refs: conversions(*refs, columns=bz), [(bx * by, bz)], cost=(40 * cells, 4 * cells)
    )(*(array.reshape(1, entries) for array in (conv_source, conv_kind, conv_direction)))
    code = code.reshape(box)

    pops, flow = call(
        moments,
        [(19, *box), (5, *box)],
        specs=[remote],
        scratch=[pltpu.SemaphoreType.DMA((bx,))],
        cost=(60 * cells, 150 * cells),
    )(pltpu.with_memory_space_constraint(populations, pltpu.HBM))

    columns, rows = ((24, bx * by), (10 * bx, bz))
    sides_y = [(bx, 8, bz), (bx, 8, bz), tile]
    inside, ends = ((bx - 2, *face), (2, *face))
    inner_post, inner_shift = call(
        collide_inner,
        [(19, *inside), (3, *inside)],
        scratch=sides_y,
        cost=(150 * cells, 150 * cells),
    )(pops, stretch, flow, *y_first, z_first)
    outer_post, outer_shift, z_out, x_one, x_two, y_one, y_two = call(
        collide_outer,
        [(19, *ends), (3, *ends), columns, (8, *face), (8, *face), rows, rows],
        scratch=[(4, *face), (4, *face)] + sides_y + [box],
        cost=(150 * cells, 150 * cells),
    )(pops, stretch, flags, flow, *first_x, *y_first, z_first, inner_post)
    z_post = both_ways(z_out, sides)
    post_y = swapped(y_one, y_two, "gy")
    post_x = swapped(x_one, x_two, "gx")
    edges = (4 * (bz // lanes) + columns[0], lanes)
    x_one, x_two, corner = call(
        lambda *refs: forward_edges(*refs, bx=bx), [edges, edges, columns]
    )(*post_y, z_post)
    corners = swapped(corner, corner, "gy")
    edges_x = swapped(x_one, x_two, "gx")

    rims = [(bx + 2, *face), (bx + 2, 16, bz), (bx + 2, 16, bz), (bx + 2, by, lanes)]
    posts = (inner_post, outer_post, inner_shift, outer_shift)
    inner, outer, totals, changes = call(
        stream_early,
        [(first_slanted, *inside), (first_slanted, *ends), box, box],
        scratch=rims,
        cost=(350 * cells, 200 * cells),
    )(*posts, flags, *post_y, z_post)
    (
        inner_slanted,
        outer_slanted,
        inner_settled,
        inner_excess,
        inner_heading,
        totals,
        changes,
    ) = call(
        stream_slanted,
        [(4, *inside), (4, *ends), inside, inside, inside, ends, ends],
        scratch=rims,
        cost=(100 * cells, 60 * cells),
    )(*posts, mass, flags, code, *post_y, z_post, *corners, totals, changes)
    late, outer_settled, spread, y_one, y_two, z_out = call(
        stream_late,
        [(5, *ends), ends, (bx + 2, *face), (8, bz), (8, bz), (16, bx * by)],
        scratch=rims + [(5, *face), (5, *face), box, box],
        cost=(150 * cells, 100 * cells),
    )(
        outer_post,
        outer_shift,
        mass,
        flags,
        code,
        totals,
        changes,
        *first_x,
        *post_x,
        *edges_x,
        inner_excess,
        inner_heading,
    )
    z_last = both_ways(z_out, 8)
    last_y = swapped(y_one, y_two, "gy")
    last_corners = swapped(z_last, z_last, "gy")
    x_one, x_two = call(add_faces, [face, face])(spread, z_last, *last_y)
    last_x = swapped(x_one, x_two, "gx")
    new_stretch, fresh = call(
        restretch,
        [(6, *box), (19, *box)],
        out_specs=[pl.BlockSpec(), remote],
        scratch=[
            (8, *face),
            (8, *face),
            (bx, 8, bz),
            (bx, 8, bz),
            tile,
            pltpu.SemaphoreType.DMA((32,)),
        ],
        cost=(150 * cells, 80 * cells),
    )(
        stretch,
        flow,
        *post_x,
        *post_y,
        z_post,
        inner,
        outer,
        inner_slanted,
        outer_slanted,
        late,
    )
    (new_mass,) = call(add_all, [box])(
        inner_settled, outer_settled, spread, z_last, *last_y, *last_corners, *last_x
    )
    return (fresh, new_stretch, new_mass)


def solution(mesh):
    return jax.shard_map(
        shards,
        mesh=mesh,
        in_specs=(
            P(None, "gx", "gy", "gz"),
            P(None, "gx", "gy", "gz"),
            P("gx", "gy", "gz"),
            P("gx", "gy", "gz"),
            P(("gx", "gy", "gz")),
            P(("gx", "gy", "gz")),
            P(("gx", "gy", "gz")),
        ),
        out_specs=(P(None, "gx", "gy", "gz"), P(None, "gx", "gy", "gz"), P("gx", "gy", "gz")),
        check_vma=False,
    )
```

```python
import jax
import jax.numpy as jnp
from jax import lax
from jax.experimental import pallas as pl
from jax.experimental.pallas import tpu as pltpu
from jax.sharding import PartitionSpec as P

velocity_set = (
    (0, 0, 0),
    (1, 0, 0),
    (-1, 0, 0),
    (0, 1, 0),
    (0, -1, 0),
    (0, 0, 1),
    (0, 0, -1),
    (1, 1, 0),
    (-1, -1, 0),
    (1, -1, 0),
    (-1, 1, 0),
    (1, 0, 1),
    (-1, 0, -1),
    (1, 0, -1),
    (-1, 0, 1),
    (0, 1, 1),
    (0, -1, -1),
    (0, 1, -1),
    (0, -1, 1),
)
opposite_of = (0, 2, 1, 4, 3, 6, 5, 8, 7, 10, 9, 12, 11, 14, 13, 16, 15, 18, 17)
lattice_weights = (1.0 / 3.0,) + (1.0 / 18.0,) * 6 + (1.0 / 36.0,) * 12
symmetric_slot = ((0, 3, 4), (3, 1, 5), (4, 5, 2))
tensor_pairs = ((0, 0), (1, 1), (2, 2), (0, 1), (0, 2), (1, 2))
relax_time = 0.8
polymer_time = 8.0
polymer_coeff = 0.05


def moving(axis, sign):
    return tuple(index for index in range(19) if velocity_set[index][axis] == sign)


x_up, x_down = (moving(0, 1), moving(0, -1))
y_up, y_down = (moving(1, 1), moving(1, -1))
z_up, z_down = (moving(2, 1), moving(2, -1))
pairs = tuple(range(1, 19, 2))
gas_slot = 5
speed_slot = 6
edge_slot = 9
sides = 9
lanes = 128
tall = 8


def iota(shape, dim):
    return lax.broadcasted_iota(jnp.int32, shape, dim)


def wide(tile, width):
    return jnp.concatenate([tile] * (width // tile.shape[1]), axis=1)


def rows_of(load, chunk, chunks, step, edge):
    low = chunk * tall
    if step == 0:
        return load(low, low + tall)
    if step == 1 and chunk > 0:
        return load(low - 1, low + tall - 1)
    if step == -1 and chunk < chunks - 1:
        return load(low + 1, low + tall + 1)
    rows = load(low, low + tall)
    at = iota(rows.shape, 0)
    if step == 1:
        return jnp.where(at == 0, edge(), pltpu.roll(rows, 1, 0))
    return jnp.where(at == tall - 1, edge(), pltpu.roll(rows, tall - 1, 0))


def columns_of(rows, halo, lane, step):
    width = rows.shape[1]
    at = iota(rows.shape, 1)
    if step == 1:
        edge = wide(pltpu.roll(halo, (lanes - lane) % lanes, 1), width)
        return jnp.where(at == 0, edge, pltpu.roll(rows, 1, 1))
    edge = wide(pltpu.roll(halo, lanes - 1 - lane, 1), width)
    return jnp.where(at == width - 1, edge, pltpu.roll(rows, width - 1, 1))


def packed(high, low):
    at = iota(high[0].shape, 1)
    tile = jnp.zeros_like(high[0])
    for slot, part in enumerate(high):
        tile = jnp.where(at == slot, pltpu.roll(part, slot + 1, 1), tile)
    for place, part in enumerate(low):
        slot = len(high) + place
        tile = jnp.where(at == slot, pltpu.roll(part, slot, 1), tile)
    return tile


def along(index, vector):
    total = None
    for comp in range(3):
        sign = velocity_set[index][comp]
        if sign != 0:
            term = vector[comp] if sign > 0 else -vector[comp]
            total = term if total is None else total + term
    return total


def conversions(source, kind, heading, code, *, columns):
    count = source.shape[1]
    value = (heading[...] + 32 * kind[...]).astype(jnp.float32)
    row, column = (source[...] // columns, source[...] % columns)
    by_row = jnp.where(iota((code.shape[0], count), 0) == row, value, 0.0).astype(jnp.bfloat16)
    by_column = jnp.where(iota((columns, count), 0) == column, 1.0, 0.0).astype(jnp.bfloat16)
    code[...] = lax.dot_general(
        by_row, by_column, (((1,), (1,)), ((), ())), preferred_element_type=jnp.float32
    )


def odd(axis):
    return lax.rem(lax.axis_index(axis), 2) == 1


def select(chosen, first, second):
    return jnp.where(chosen, first[...], second[...])


def swap_rows(first, second, x, planes, high, low, flip):
    for slot, (top, bottom) in enumerate(zip(high, low)):
        by = top.shape[0]
        up, down = (top[by - 1 : by, :], bottom[0:1, :])
        at = slot * planes + x
        first[at : at + 1, :] = jnp.where(flip, down, up)
        second[at : at + 1, :] = jnp.where(flip, up, down)


def swapped_rows(first, second, slots, low_rows, high_rows, shift):
    flip = odd("gy")
    planes = low_rows.shape[0] - 2 * shift
    for x in range(planes):
        for place, slot in enumerate(slots):
            at = slot * planes + x
            one, two = (first[at : at + 1, :], second[at : at + 1, :])
            low_rows[x + shift, place : place + 1, :] = jnp.where(flip, one, two)
            high_rows[x + shift, place : place + 1, :] = jnp.where(flip, two, one)


def column_rows(tiles, count):
    return jnp.concatenate(tiles, axis=0).T[0:count, :]


def row_columns(rows):
    rest = jnp.zeros((lanes - rows.shape[0], rows.shape[1]), jnp.float32)
    return jnp.concatenate([rows, rest], axis=0).T


def first_faces(
    stretch_in,
    flags_in,
    stretch,
    flags,
    columns,
    y_first,
    y_second,
    x_first,
    x_second,
    sems,
):
    bx, by, bz = flags.shape
    flip_x, flip_y = (odd("gx"), odd("gy"))
    copies = [
        pltpu.make_async_copy(stretch_in, stretch, sems.at[0]),
        pltpu.make_async_copy(flags_in, flags, sems.at[1]),
    ]
    for copy in copies:
        copy.start()
    for copy in copies:
        copy.wait()
    tiles = []
    for x in range(bx):
        along_y = [stretch.at[symmetric_slot[comp][1], x] for comp in range(3)]
        swap_rows(y_first, y_second, x, bx, along_y, along_y, flip_y)
        fields = [stretch.at[symmetric_slot[comp][2], x] for comp in range(3)]
        tiles.append(
            packed(
                [field[:, bz - lanes : bz] for field in fields],
                [field[:, 0:lanes] for field in fields],
            )
        )
    columns[...] = column_rows(tiles, columns.shape[0])
    rest = y_first.shape[0] - 3 * bx
    y_first[3 * bx :, :] = jnp.zeros((rest, bz), jnp.float32)
    y_second[3 * bx :, :] = jnp.zeros((rest, bz), jnp.float32)
    for out, last in ((x_first, flip_x), (x_second, jnp.logical_not(flip_x))):
        for comp in range(3):
            slot = symmetric_slot[comp][0]
            out[comp] = jnp.where(last, stretch[slot, 0], stretch[slot, bx - 1])
        out[3] = jnp.where(jnp.where(last, flags[0], flags[bx - 1]) == 0, 1.0, 0.0)


def moments(pops_in, pops, flow, sems):
    bx, by = pops.shape[1:3]
    copies = [
        pltpu.make_async_copy(pops_in.at[:, x], pops.at[:, x], sems.at[x]) for x in range(bx)
    ]
    for copy in copies:
        copy.start()
    for x in range(bx):
        copies[x].wait()
        for chunk in range(by // tall):
            rows = pl.ds(chunk * tall, tall)
            part = [pops[index, x, rows, :] for index in range(19)]
            density = part[0]
            for index in range(1, 19):
                density = density + part[index]
            inverse = 1.0 / density
            for comp in range(3):
                total = None
                for index in pairs:
                    sign = velocity_set[index][comp]
                    if sign != 0:
                        term = part[index] - part[index + 1]
                        term = term if sign > 0 else -term
                        total = term if total is None else total + term
                flow[comp, x, rows, :] = total * inverse
            flow[3, x, rows, :] = density
            flow[4, x, rows, :] = inverse


def beside(ref, field, x, step, halo, slot):
    last = ref.shape[1] - 1
    if halo is None:
        return lambda low, high: ref[field, x + step, low:high, :]
    if isinstance(x, int):
        if 0 <= x + step <= last:
            return lambda low, high: ref[field, x + step, low:high, :]
        return lambda low, high: halo[slot, low:high, :]
    inside = jnp.clip(x + step, 0, last)
    beyond = x == (0 if step < 0 else last)
    return lambda low, high: jnp.where(
        beyond, halo[slot, low:high, :], ref[field, inside, low:high, :]
    )


def differences(
    ref, field, slots, x, chunk, chunks, below, above, y_below, y_above, z_halo, lane, side
):
    slot_x, slot_y, slot_z = slots
    low, high = (chunk * tall, chunk * tall + tall)

    def load(first, stop):
        return ref[field, x, first:stop, :]

    result = [None, None, None]
    if slot_x is not None:
        after = beside(ref, field, x, 1, above, slot_x)(low, high)
        before = beside(ref, field, x, -1, below, slot_x)(low, high)
        result[0] = after - before
    if slot_y is not None:
        after = rows_of(load, chunk, chunks, -1, lambda: y_above[x, slot_y : slot_y + 1, :])
        before = rows_of(load, chunk, chunks, 1, lambda: y_below[x, slot_y : slot_y + 1, :])
        result[1] = after - before
    if slot_z is not None:
        rows, halo = (load(low, high), z_halo[x, low:high, :])
        after = columns_of(rows, halo, lane + side + slot_z, -1)
        before = columns_of(rows, halo, lane + slot_z, 1)
        result[2] = after - before
    return result


def end_place(x, bx):
    return 0 if x == 0 else 1


def plane_of(inner, outer, field, x, bx):
    if 0 < x < bx - 1:
        return inner.at[field, x - 1]
    return outer.at[field, end_place(x, bx)]


def collide_plane(x, place, pops, stretch, flow, halos, post, shift):
    by = pops.shape[2]
    chunks = by // tall
    factor = 1.0 - 0.5 / relax_time
    rate = 1.0 / relax_time
    for chunk in range(chunks):
        rows = pl.ds(chunk * tall, tall)
        terms = [[], [], []]
        for field in range(6):
            slots = [None, None, None]
            for comp in range(3):
                for axis in range(3):
                    if symmetric_slot[comp][axis] == field:
                        slots[axis] = comp
            found = differences(stretch, field, slots, x, chunk, chunks, *halos)
            for axis in range(3):
                if slots[axis] is not None:
                    terms[slots[axis]].append(found[axis])
        force = [0.5 * polymer_coeff * (part[0] + part[1] + part[2]) for part in terms]
        density, half = (flow[3, x, rows, :], 0.5 * flow[4, x, rows, :])
        moved = [flow[comp, x, rows, :] + half * force[comp] for comp in range(3)]
        for comp in range(3):
            shift[comp, place, rows, :] = moved[comp]
        squared = moved[0] * moved[0] + moved[1] * moved[1] + moved[2] * moved[2]
        work = moved[0] * force[0] + moved[1] * force[1] + moved[2] * force[2]
        weight = rate * density
        common = weight - 1.5 * weight * squared - 3.0 * factor * work
        odd = [3.0 * weight * moved[comp] + 3.0 * factor * force[comp] for comp in range(3)]
        even = [4.5 * weight * moved[comp] + 9.0 * factor * force[comp] for comp in range(3)]
        keep = 1.0 - rate
        post[0, place, rows, :] = keep * pops[0, x, rows, :] + lattice_weights[0] * common
        for index in pairs:
            both = common + along(index, moved) * along(index, even)
            differ = along(index, odd)
            scale = lattice_weights[index]
            post[index, place, rows, :] = keep * pops[index, x, rows, :] + scale * (both + differ)
            post[index + 1, place, rows, :] = keep * pops[index + 1, x, rows, :] + scale * (
                both - differ
            )


def collide_inner(
    pops,
    stretch,
    flow,
    z_rows,
    y_first,
    y_second,
    post,
    shift,
    y_below,
    y_above,
    z_halo,
):
    swapped_rows(y_first, y_second, range(3), y_below, y_above, 0)
    z_halo[...] = row_columns(z_rows[...]).reshape(z_halo.shape)
    halos = (None, None, y_below, y_above, z_halo, 0, 3)

    def plane(x, carry):
        collide_plane(x, x - 1, pops, stretch, flow, halos, post, shift)
        return carry

    lax.fori_loop(1, pops.shape[1] - 1, plane, 0)


def collide_outer(
    pops,
    stretch,
    flags,
    flow,
    x_first,
    x_second,
    y_first,
    y_second,
    z_rows,
    inner,
    post,
    shift,
    columns,
    ahead,
    behind,
    up_first,
    up_second,
    below,
    above,
    y_below,
    y_above,
    z_halo,
    gas,
):
    bx, by, bz = flags.shape
    halos = (below, above, y_below, y_above, z_halo, 0, 3)
    flip_x, flip_y = (odd("gx"), odd("gy"))
    below[...] = select(flip_x, x_first, x_second)
    above[...] = select(flip_x, x_second, x_first)
    swapped_rows(y_first, y_second, range(3), y_below, y_above, 0)
    z_halo[...] = row_columns(z_rows[...]).reshape(z_halo.shape)
    for x in (0, bx - 1):
        collide_plane(x, end_place(x, bx), pops, stretch, flow, halos, post, shift)

    tiles = []
    for x in range(bx):
        gas[x] = jnp.where(flags[x] == 0, 1.0, 0.0)
        rest = [gas.at[x]] + [flow.at[comp, x] for comp in range(3)]

        def fields(indices):
            return [plane_of(inner, post, index, x, bx) for index in indices] + rest

        swap_rows(up_first, up_second, x, bx, fields(y_up), fields(y_down), flip_y)
        tiles.append(
            packed(
                [field[:, bz - lanes : bz] for field in fields(z_up)],
                [field[:, 0:lanes] for field in fields(z_down)],
            )
        )
    columns[...] = column_rows(tiles, columns.shape[0])
    rest = up_first.shape[0] - sides * bx
    up_first[sides * bx :, :] = jnp.zeros((rest, bz), jnp.float32)
    up_second[sides * bx :, :] = jnp.zeros((rest, bz), jnp.float32)
    for slot in range(5):
        up, down = (post[x_up[slot], 1], post[x_down[slot], 0])
        ahead[slot] = jnp.where(flip_x, down, up)
        behind[slot] = jnp.where(flip_x, up, down)
    for comp in range(3):
        up, down = (flow[comp, bx - 1], flow[comp, 0])
        ahead[5 + comp] = jnp.where(flip_x, down, up)
        behind[5 + comp] = jnp.where(flip_x, up, down)


def restretch(
    stretch,
    flow,
    x_second,
    x_first,
    y_first,
    y_second,
    z_rows,
    inner,
    outer,
    inner_slanted,
    outer_slanted,
    late,
    updated,
    fresh,
    below,
    above,
    y_below,
    y_above,
    z_halo,
    sems,
):
    bx, by, bz = stretch.shape[1:]
    moves = [
        (inner, fresh.at[0:first_slanted, 1 : bx - 1]),
        (inner_slanted, fresh.at[first_slanted:, 1 : bx - 1]),
    ]
    for place, x in enumerate((0, bx - 1)):
        moves.append((outer_slanted.at[:, place], fresh.at[first_slanted:, x]))
        order = (x_up, x_down)[place]
        start = 0
        for index in order + (first_slanted,):
            if index > start:
                run = slice(start, index)
                moves.append((outer.at[run, place], fresh.at[run, x]))
            if index in order:
                moves.append((late.at[order.index(index), place], fresh.at[index, x]))
            start = index + 1
    copies = [
        pltpu.make_async_copy(source, target, sems.at[place])
        for place, (source, target) in enumerate(moves)
    ]
    for copy in copies:
        copy.start()
    chunks = by // tall
    flip_x = odd("gx")
    below[...] = select(flip_x, x_first, x_second)
    above[...] = select(flip_x, x_second, x_first)
    swapped_rows(y_first, y_second, range(speed_slot, sides), y_below, y_above, 0)
    z_halo[...] = row_columns(z_rows[...]).reshape(z_halo.shape)

    def plane(x, carry):
        for chunk in range(chunks):
            rows = pl.ds(chunk * tall, tall)
            grad = [
                differences(
                    flow,
                    comp,
                    (5 + comp, comp, comp),
                    x,
                    chunk,
                    chunks,
                    below,
                    above,
                    y_below,
                    y_above,
                    z_halo,
                    speed_slot,
                    sides,
                )
                for comp in range(3)
            ]
            part = [stretch[slot, x, rows, :] for slot in range(6)]
            full = [part[slot] + 1.0 if slot < 3 else part[slot] for slot in range(6)]

            def product(row, col):
                total = grad[row][0] * full[symmetric_slot[0][col]]
                for inner in (1, 2):
                    total = total + grad[row][inner] * full[symmetric_slot[inner][col]]
                return total

            for slot, (row, col) in enumerate(tensor_pairs):
                old = (1.0 - 1.0 / polymer_time) * part[slot]
                if row == col:
                    updated[slot, x, rows, :] = old + product(row, col)
                else:
                    updated[slot, x, rows, :] = old + 0.5 * (product(row, col) + product(col, row))
        return carry

    lax.fori_loop(0, bx, plane, 0)
    for copy in copies:
        copy.wait()


up_edges = ((0, y_up.index(7)), (0, gas_slot), (1, y_down.index(9)), (1, gas_slot))
down_edges = ((0, y_up.index(10)), (0, gas_slot), (1, y_down.index(8)), (1, gas_slot))


def forward_edges(z_rows, y_first, y_second, first_out, second_out, corner, *, bx):
    halves = y_first.shape[1] // lanes
    flip_x, flip_y = (odd("gx"), odd("gy"))
    for half in range(halves):
        cut = slice(half * lanes, half * lanes + lanes)
        for place in range(4):
            found = []
            for x, edges in ((bx - 1, up_edges), (0, down_edges)):
                side, slot = edges[place]
                row = slot * bx + x
                one = y_first[row : row + 1, cut]
                two = y_second[row : row + 1, cut]
                found.append(jnp.where(flip_y, one, two) if side == 0 else jnp.where(flip_y, two, one))
            at = half * 4 + place
            first_out[at : at + 1, :] = jnp.where(flip_x, found[1], found[0])
            second_out[at : at + 1, :] = jnp.where(flip_x, found[0], found[1])
    first_out[4 * halves :, :] = z_rows[...]
    second_out[4 * halves :, :] = z_rows[...]
    corner[...] = z_rows[...]


def own_halos(flags, y_first, y_second, z_rows, gas, low_rows, high_rows, columns):
    bx, by = flags.shape[:2]
    tile = row_columns(z_rows[...])
    swapped_rows(y_first, y_second, range(speed_slot), low_rows, high_rows, 1)
    for x in range(bx):
        gas[x + 1] = jnp.where(flags[x] == 0, 1.0, 0.0)
        columns[x + 1] = tile[x * by : x * by + by, :]


def own_corners(corner_first, corner_second, low_rows, high_rows):
    bx = low_rows.shape[0] - 2
    flip = odd("gy")
    corner_below = row_columns(select(flip, corner_first, corner_second))
    corner_above = row_columns(select(flip, corner_second, corner_first))
    by = corner_below.shape[0] // bx
    for x in range(bx):
        end = x * by + by - 1
        low_rows[x + 1, edge_slot : edge_slot + 1, 0:lanes] = corner_below[end : end + 1, :]
        high_rows[x + 1, edge_slot : edge_slot + 1, 0:lanes] = corner_above[
            x * by : x * by + 1, :
        ]


def pass_on(x, chunk, indices, source, leaving_of, speed, halos, fresh, place, total, change):
    gas, low_rows, high_rows, columns = halos
    by = gas.shape[1]
    chunks = by // tall
    rows = pl.ds(chunk * tall, tall)
    rest = 1.0 - 1.5 * (speed[0] * speed[0] + speed[1] * speed[1] + speed[2] * speed[2])
    equals = {}

    def moved(load, index, slot, lane):
        step_x, step_y, step_z = velocity_set[index]
        plane = x + 1 - step_x
        edges = low_rows if step_y == 1 else high_rows
        found = rows_of(load, chunk, chunks, step_y, lambda: edges[plane, slot : slot + 1, :])
        if step_z == 0:
            return found
        halo = rows_of(
            lambda low, high: columns[plane, low:high, :],
            chunk,
            chunks,
            step_y,
            lambda: edges[plane, edge_slot : edge_slot + 1, 0:lanes],
        )
        return columns_of(found, halo, lane, step_z)

    for index in indices:
        step_x, step_y, step_z = velocity_set[index]
        first = min(index, opposite_of[index])
        if first not in equals:
            proj = along(first, speed)
            equals[first] = 2.0 * lattice_weights[first] * (rest + 4.5 * proj * proj)
        slot, lane, gas_lane = (None, None, None)
        if step_y != 0:
            slot = (y_up if step_y == 1 else y_down).index(index)
        if step_z == 1:
            lane, gas_lane = (z_up.index(index), gas_slot)
        elif step_z == -1:
            lane, gas_lane = (sides + z_down.index(index), sides + gas_slot)
        field = source(index)
        marks = gas.at[x + 1 - step_x]
        arriving = moved(lambda low, high: field[low:high, :], index, slot, lane)
        from_gas = moved(lambda low, high: marks[low:high, :], index, gas_slot, gas_lane)
        leaving = leaving_of(opposite_of[index])[rows, :]
        open_side = from_gas > 0.5
        value = jnp.where(open_side, equals[first] - leaving, arriving)
        fresh(index)[place, rows, :] = value
        total = total + value
        change = change + jnp.where(open_side, 0.0, arriving - leaving)
    return total, change


def settle(x, rows, mass, flags, code, total, change):
    read = mass[x, rows, :] + jnp.where(flags[x, rows, :] == 1, change, 0.0)
    mark = code[x, rows, :]
    liquid = mark >= 32.0
    converts = mark > 0.0
    level = jnp.where(liquid, total, 0.0)
    excess = jnp.where(converts, read - level, 0.0)
    heading = jnp.where(liquid, mark - 32.0, mark)
    return jnp.where(converts, level, read), excess, heading


slanted = tuple(index for index in range(19) if velocity_set[index][1] * velocity_set[index][2])
first_slanted = slanted[0]


def from_inside(x, bx):
    found = [index for index in range(1, 19) if 0 <= x - velocity_set[index][0] < bx]
    return [index for index in found if index not in slanted]


def from_beyond(x, bx):
    return [index for index in range(1, 19) if not 0 <= x - velocity_set[index][0] < bx]


def stream_early(
    inner_post,
    outer_post,
    inner_shift,
    outer_shift,
    flags,
    y_first,
    y_second,
    z_rows,
    inner,
    outer,
    totals,
    changes,
    gas,
    low_rows,
    high_rows,
    columns,
):
    bx, by, bz = flags.shape
    halos = (gas, low_rows, high_rows, columns)
    own_halos(flags, y_first, y_second, z_rows, *halos)

    for x in range(bx):
        inside = 0 < x < bx - 1
        place = x - 1 if inside else end_place(x, bx)
        fresh = inner if inside else outer
        for chunk in range(by // tall):
            rows = pl.ds(chunk * tall, tall)
            total = plane_of(inner_post, outer_post, 0, x, bx)[rows, :]
            fresh[0, place, rows, :] = total
            total, change = pass_on(
                x,
                chunk,
                from_inside(x, bx),
                lambda index: plane_of(
                    inner_post, outer_post, index, x - velocity_set[index][0], bx
                ),
                lambda index: plane_of(inner_post, outer_post, index, x, bx),
                [plane_of(inner_shift, outer_shift, comp, x, bx)[rows, :] for comp in range(3)],
                halos,
                lambda index: fresh.at[index],
                place,
                total,
                jnp.zeros((tall, bz), jnp.float32),
            )
            totals[x, rows, :] = total
            changes[x, rows, :] = change


def stream_slanted(
    inner_post,
    outer_post,
    inner_shift,
    outer_shift,
    mass,
    flags,
    code,
    y_first,
    y_second,
    z_rows,
    corner_first,
    corner_second,
    totals,
    changes,
    inner,
    outer,
    settled,
    excess,
    heading,
    end_totals,
    end_changes,
    gas,
    low_rows,
    high_rows,
    columns,
):
    bx, by, bz = flags.shape
    halos = (gas, low_rows, high_rows, columns)
    own_halos(flags, y_first, y_second, z_rows, *halos)
    own_corners(corner_first, corner_second, low_rows, high_rows)

    for x in range(bx):
        inside = 0 < x < bx - 1
        place = x - 1 if inside else end_place(x, bx)
        fresh = inner if inside else outer
        for chunk in range(by // tall):
            rows = pl.ds(chunk * tall, tall)
            total, change = pass_on(
                x,
                chunk,
                slanted,
                lambda index: plane_of(inner_post, outer_post, index, x, bx),
                lambda index: plane_of(inner_post, outer_post, index, x, bx),
                [plane_of(inner_shift, outer_shift, comp, x, bx)[rows, :] for comp in range(3)],
                halos,
                lambda index: fresh.at[index - first_slanted],
                place,
                totals[x, rows, :],
                changes[x, rows, :],
            )
            if inside:
                now = settle(x, rows, mass, flags, code, total, change)
                settled[place, rows, :], excess[place, rows, :], heading[place, rows, :] = now
            else:
                end_totals[place, rows, :] = total
                end_changes[place, rows, :] = change


def stream_late(
    post,
    shift,
    mass,
    flags,
    code,
    totals,
    changes,
    gas_first,
    gas_second,
    x_second,
    x_first,
    edges_first,
    edges_second,
    inner_excess,
    inner_heading,
    late,
    settled,
    spread,
    line_first,
    line_second,
    out_z,
    gas,
    low_rows,
    high_rows,
    columns,
    below,
    above,
    excess,
    heading,
):
    bx, by, bz = flags.shape
    halves = bz // lanes
    flip_x = odd("gx")
    halos = (gas, low_rows, high_rows, columns)

    for slot in range(5):
        below[slot] = jnp.where(flip_x, x_first[slot], x_second[slot])
        above[slot] = jnp.where(flip_x, x_second[slot], x_first[slot])
    gas[0] = jnp.where(flip_x, gas_first[3], gas_second[3])
    gas[bx + 1] = jnp.where(flip_x, gas_second[3], gas_first[3])
    edges_below = select(flip_x, edges_first, edges_second)
    edges_above = select(flip_x, edges_second, edges_first)
    for found, at, x, edges in (
        (edges_below, 0, bx - 1, up_edges),
        (edges_above, bx + 1, 0, down_edges),
    ):
        for place, (side, slot) in enumerate(edges):
            line = jnp.concatenate(
                [found[half * 4 + place : half * 4 + place + 1, :] for half in range(halves)],
                axis=1,
            )
            (low_rows, high_rows)[side][at, slot : slot + 1, :] = line
        columns[at] = row_columns(found[4 * halves :, :])[x * by : x * by + by, :]
    for place, x in enumerate((0, bx - 1)):
        halo, order = ((below, x_up), (above, x_down))[place]
        for chunk in range(by // tall):
            rows = pl.ds(chunk * tall, tall)
            total, change = pass_on(
                x,
                chunk,
                from_beyond(x, bx),
                lambda index: halo.at[order.index(index)],
                lambda index: post.at[index, place],
                [shift[comp, place, rows, :] for comp in range(3)],
                halos,
                lambda index: late.at[order.index(index)],
                place,
                totals[place, rows, :],
                changes[place, rows, :],
            )
            now = settle(x, rows, mass, flags, code, total, change)
            settled[place, rows, :], excess[x, rows, :], heading[x, rows, :] = now
    for x in range(1, bx - 1):
        excess[x] = inner_excess[x - 1]
        heading[x] = inner_heading[x - 1]

    row_at, lane_at = (iota((by, bz), 0), iota((by, bz), 1))
    line_at = iota((1, bz), 1)
    tile_lane, line_lane = (iota((by, lanes), 1), iota((1, lanes), 1))

    def rows_up(rows):
        return jnp.where(row_at == 0, 0.0, pltpu.roll(rows, 1, 0))

    def rows_down(rows):
        return jnp.where(row_at == by - 1, 0.0, pltpu.roll(rows, by - 1, 0))

    def over(rows, at, step):
        if step == 1:
            return jnp.where(at == 0, 0.0, pltpu.roll(rows, 1, 1))
        return jnp.where(at == bz - 1, 0.0, pltpu.roll(rows, bz - 1, 1))

    def summed(parts):
        total = parts[0]
        for part in parts[1:]:
            total = total + part
        return total

    tile = jnp.zeros((by, lanes), jnp.float32)
    line_up = jnp.zeros((1, lanes), jnp.float32)
    line_down = jnp.zeros((1, lanes), jnp.float32)
    flip_y = odd("gy")
    line_first[...] = jnp.zeros(line_first.shape, jnp.float32)
    line_second[...] = jnp.zeros(line_second.shape, jnp.float32)
    for target in range(bx + 2):
        groups = {}
        for index in range(1, 19):
            step_x, step_y, step_z = velocity_set[index]
            x = target - 1 - step_x
            if 0 <= x < bx:
                part = jnp.where(heading[x] == float(index), excess[x], 0.0)
                groups.setdefault((step_y, step_z), []).append(part)
        groups = {key: summed(parts) for key, parts in groups.items()}
        total = jnp.zeros((by, bz), jnp.float32)
        line = {1: jnp.zeros((1, bz), jnp.float32), -1: jnp.zeros((1, bz), jnp.float32)}
        for step_z in (0, 1, -1):
            group = jnp.zeros((by, bz), jnp.float32)
            ends = {}
            if (0, step_z) in groups:
                group = group + groups[(0, step_z)]
            if (1, step_z) in groups:
                group = group + rows_up(groups[(1, step_z)])
                ends[1] = groups[(1, step_z)][by - 1 : by, :]
            if (-1, step_z) in groups:
                group = group + rows_down(groups[(-1, step_z)])
                ends[-1] = groups[(-1, step_z)][0:1, :]
            if step_z == 0:
                total = total + group
                for side in ends:
                    line[side] = line[side] + ends[side]
                continue
            total = total + over(group, lane_at, step_z)
            for side in ends:
                line[side] = line[side] + over(ends[side], line_at, step_z)
            if step_z == 1:
                spot, cut, roll = (target, slice(bz - lanes, bz), target + 1)
            else:
                spot, cut, roll = (8 + target, slice(0, lanes), 8 + target)
            tile = jnp.where(tile_lane == spot, pltpu.roll(group[:, cut], roll, 1), tile)
            if 1 in ends:
                line_up = jnp.where(
                    line_lane == spot, pltpu.roll(ends[1][:, cut], roll, 1), line_up
                )
            if -1 in ends:
                line_down = jnp.where(
                    line_lane == spot, pltpu.roll(ends[-1][:, cut], roll, 1), line_down
                )
        spread[target] = total
        line_first[target : target + 1, :] = jnp.where(flip_y, line[-1], line[1])
        line_second[target : target + 1, :] = jnp.where(flip_y, line[1], line[-1])
    rest = jnp.zeros((lanes - by - 2, lanes), jnp.float32)
    out_z[...] = column_rows([tile, line_up, line_down, rest], 16)


def with_edges(total, target, tile, y_below, y_above):
    by, bz = total.shape
    row_at, lane_at = (iota((by, bz), 0), iota((by, bz), 1))
    total = total + jnp.where(lane_at == 0, tile[0:by, target : target + 1], 0.0)
    total = total + jnp.where(lane_at == bz - 1, tile[0:by, 8 + target : 9 + target], 0.0)
    total = total + jnp.where(row_at == 0, y_below[target : target + 1, :], 0.0)
    return total + jnp.where(row_at == by - 1, y_above[target : target + 1, :], 0.0)


def add_faces(spread, z_rows, y_first, y_second, first, second):
    last = spread.shape[0] - 1
    flip_x, flip_y = (odd("gx"), odd("gy"))
    tile = row_columns(z_rows[...])
    y_below, y_above = (select(flip_y, y_first, y_second), select(flip_y, y_second, y_first))
    up = with_edges(spread[last], last, tile, y_below, y_above)
    down = with_edges(spread[0], 0, tile, y_below, y_above)
    first[...] = jnp.where(flip_x, down, up)
    second[...] = jnp.where(flip_x, up, down)


def add_all(
    inner_settled,
    outer_settled,
    spread,
    z_rows,
    y_first,
    y_second,
    corner_first,
    corner_second,
    x_second,
    x_first,
    new_mass,
):
    bx, by, bz = new_mass.shape
    flip_x, flip_y = (odd("gx"), odd("gy"))
    tile = row_columns(z_rows[...])
    y_below, y_above = (select(flip_y, y_first, y_second), select(flip_y, y_second, y_first))
    at = iota((8, bz), 1)
    found = []
    for rows, side, corner in (
        (y_below, 0, select(flip_y, corner_first, corner_second)),
        (y_above, 1, select(flip_y, corner_second, corner_first)),
    ):
        edge = corner[:, by + side : by + side + 1]
        rows = rows + jnp.where(at == 0, edge[0:8, :], 0.0)
        found.append(rows + jnp.where(at == bz - 1, edge[8:16, :], 0.0))
    for x in range(bx):
        total = with_edges(spread[x + 1], x + 1, tile, *found)
        if x == 0:
            total = total + select(flip_x, x_first, x_second)
        if x == bx - 1:
            total = total + select(flip_x, x_second, x_first)
        if 0 < x < bx - 1:
            total = total + inner_settled[x - 1]
        else:
            total = total + outer_settled[0 if x == 0 else 1]
        new_mass[x] = total


def swapped(first, second, axis):
    devices = lax.axis_size(axis)
    ahead = [(i, (i + 1) % devices if i % 2 == 0 else i - 1) for i in range(devices)]
    behind = [(i, (i - 1) % devices if i % 2 == 0 else (i + 1) % devices) for i in range(devices)]
    return lax.ppermute(first, axis, ahead), lax.ppermute(second, axis, behind)


def both_ways(rows, lower):
    devices = lax.axis_size("gz")
    before = lax.ppermute(rows, "gz", [(i, (i + 1) % devices) for i in range(devices)])
    if devices == 2:
        return before
    after = lax.ppermute(rows, "gz", [(i, (i - 1) % devices) for i in range(devices)])
    return jnp.where(iota(rows.shape, 0) < lower, before, after)


remote = pl.BlockSpec(memory_space=pltpu.HBM)


def call(body, outs, specs=None, out_specs=None, scratch=(), cost=(0, 0)):
    extra = {} if specs is None else {"in_specs": specs}
    if out_specs is not None:
        extra["out_specs"] = out_specs
    return pl.pallas_call(
        body,
        out_shape=[
            shape
            if isinstance(shape, jax.ShapeDtypeStruct)
            else jax.ShapeDtypeStruct(shape, jnp.float32)
            for shape in outs
        ],
        scratch_shapes=[
            pltpu.VMEM(shape, jnp.float32) if isinstance(shape, tuple) else shape
            for shape in scratch
        ],
        compiler_params=pltpu.CompilerParams(vmem_limit_bytes=40 * 1024 * 1024),
        cost_estimate=pl.CostEstimate(flops=cost[0], bytes_accessed=cost[1], transcendentals=0),
        **extra,
    )


def shards(populations, stretch, mass, flags, conv_source, conv_kind, conv_direction):
    bx, by, bz = flags.shape
    cells = bx * by * bz
    box, face, tile = ((bx, by, bz), (by, bz), (bx, by, lanes))

    stretch, flags, z_out, y_one, y_two, x_one, x_two = call(
        first_faces,
        [
            (6, *box),
            jax.ShapeDtypeStruct(box, jnp.int32),
            (8, bx * by),
            (4 * bx, bz),
            (4 * bx, bz),
            (4, *face),
            (4, *face),
        ],
        specs=[remote] * 2,
        scratch=[pltpu.SemaphoreType.DMA((2,))],
        cost=(10 * cells, 60 * cells),
    )(*(pltpu.with_memory_space_constraint(array, pltpu.HBM) for array in (stretch, flags)))
    first_x = swapped(x_one, x_two, "gx")
    z_first = both_ways(z_out, 3)
    y_first = swapped(y_one, y_two, "gy")

    entries = conv_source.shape[0]
    (code,) = call(
        lambda *refs: conversions(*refs, columns=bz), [(bx * by, bz)], cost=(40 * cells, 4 * cells)
    )(*(array.reshape(1, entries) for array in (conv_source, conv_kind, conv_direction)))
    code = code.reshape(box)

    pops, flow = call(
        moments,
        [(19, *box), (5, *box)],
        specs=[remote],
        scratch=[pltpu.SemaphoreType.DMA((bx,))],
        cost=(60 * cells, 150 * cells),
    )(pltpu.with_memory_space_constraint(populations, pltpu.HBM))

    columns, rows = ((24, bx * by), (10 * bx, bz))
    sides_y = [(bx, 8, bz), (bx, 8, bz), tile]
    inside, ends = ((bx - 2, *face), (2, *face))
    inner_post, inner_shift = call(
        collide_inner,
        [(19, *inside), (3, *inside)],
        scratch=sides_y,
        cost=(150 * cells, 150 * cells),
    )(pops, stretch, flow, z_first, *y_first)
    outer_post, outer_shift, z_out, x_one, x_two, y_one, y_two = call(
        collide_outer,
        [(19, *ends), (3, *ends), columns, (8, *face), (8, *face), rows, rows],
        scratch=[(4, *face), (4, *face)] + sides_y + [box],
        cost=(150 * cells, 150 * cells),
    )(pops, stretch, flags, flow, *first_x, *y_first, z_first, inner_post)
    z_post = both_ways(z_out, sides)
    post_y = swapped(y_one, y_two, "gy")
    post_x = swapped(x_one, x_two, "gx")
    edges = (4 * (bz // lanes) + columns[0], lanes)
    x_one, x_two, corner = call(
        lambda *refs: forward_edges(*refs, bx=bx), [edges, edges, columns]
    )(z_post, *post_y)
    corners = swapped(corner, corner, "gy")
    edges_x = swapped(x_one, x_two, "gx")

    rims = [(bx + 2, *face), (bx + 2, 16, bz), (bx + 2, 16, bz), (bx + 2, by, lanes)]
    posts = (inner_post, outer_post, inner_shift, outer_shift)
    inner, outer, totals, changes = call(
        stream_early,
        [(first_slanted, *inside), (first_slanted, *ends), box, box],
        scratch=rims,
        cost=(350 * cells, 200 * cells),
    )(*posts, flags, *post_y, z_post)
    (
        inner_slanted,
        outer_slanted,
        inner_settled,
        inner_excess,
        inner_heading,
        totals,
        changes,
    ) = call(
        stream_slanted,
        [(4, *inside), (4, *ends), inside, inside, inside, ends, ends],
        scratch=rims,
        cost=(100 * cells, 60 * cells),
    )(*posts, mass, flags, code, *post_y, z_post, *corners, totals, changes)
    late, outer_settled, spread, y_one, y_two, z_out = call(
        stream_late,
        [(5, *ends), ends, (bx + 2, *face), (8, bz), (8, bz), (16, bx * by)],
        scratch=rims + [(5, *face), (5, *face), box, box],
        cost=(150 * cells, 100 * cells),
    )(
        outer_post,
        outer_shift,
        mass,
        flags,
        code,
        totals,
        changes,
        *first_x,
        *post_x[::-1],
        *edges_x,
        inner_excess,
        inner_heading,
    )
    z_last = both_ways(z_out, 8)
    last_y = swapped(y_one, y_two, "gy")
    last_corners = swapped(z_last, z_last, "gy")
    x_one, x_two = call(add_faces, [face, face])(spread, z_last, *last_y)
    last_x = swapped(x_one, x_two, "gx")
    new_stretch, fresh = call(
        restretch,
        [(6, *box), (19, *box)],
        out_specs=[pl.BlockSpec(), remote],
        scratch=[
            (8, *face),
            (8, *face),
            (bx, 8, bz),
            (bx, 8, bz),
            tile,
            pltpu.SemaphoreType.DMA((32,)),
        ],
        cost=(150 * cells, 80 * cells),
    )(
        stretch,
        flow,
        *post_x[::-1],
        *post_y,
        z_post,
        inner,
        outer,
        inner_slanted,
        outer_slanted,
        late,
    )
    (new_mass,) = call(add_all, [box])(
        inner_settled, outer_settled, spread, z_last, *last_y, *last_corners, *last_x[::-1]
    )
    return (fresh, new_stretch, new_mass)


def solution(mesh):
    return jax.shard_map(
        shards,
        mesh=mesh,
        in_specs=(
            P(None, "gx", "gy", "gz"),
            P(None, "gx", "gy", "gz"),
            P("gx", "gy", "gz"),
            P("gx", "gy", "gz"),
            P(("gx", "gy", "gz")),
            P(("gx", "gy", "gz")),
            P(("gx", "gy", "gz")),
        ),
        out_specs=(P(None, "gx", "gy", "gz"), P(None, "gx", "gy", "gz"), P("gx", "gy", "gz")),
        check_vma=False,
    )
```

```python
import jax
import jax.numpy as jnp
from jax import lax
from jax.experimental import pallas as pl
from jax.experimental.pallas import tpu as pltpu
from jax.sharding import PartitionSpec as P

velocity_set = (
    (0, 0, 0),
    (1, 0, 0),
    (-1, 0, 0),
    (0, 1, 0),
    (0, -1, 0),
    (0, 0, 1),
    (0, 0, -1),
    (1, 1, 0),
    (-1, -1, 0),
    (1, -1, 0),
    (-1, 1, 0),
    (1, 0, 1),
    (-1, 0, -1),
    (1, 0, -1),
    (-1, 0, 1),
    (0, 1, 1),
    (0, -1, -1),
    (0, 1, -1),
    (0, -1, 1),
)
opposite_of = (0, 2, 1, 4, 3, 6, 5, 8, 7, 10, 9, 12, 11, 14, 13, 16, 15, 18, 17)
lattice_weights = (1.0 / 3.0,) + (1.0 / 18.0,) * 6 + (1.0 / 36.0,) * 12
symmetric_slot = ((0, 3, 4), (3, 1, 5), (4, 5, 2))
tensor_pairs = ((0, 0), (1, 1), (2, 2), (0, 1), (0, 2), (1, 2))
relax_time = 0.8
polymer_time = 8.0
polymer_coeff = 0.05


def moving(axis, sign):
    return tuple(index for index in range(19) if velocity_set[index][axis] == sign)


x_up, x_down = (moving(0, 1), moving(0, -1))
y_up, y_down = (moving(1, 1), moving(1, -1))
z_up, z_down = (moving(2, 1), moving(2, -1))
pairs = tuple(range(1, 19, 2))
gas_slot = 5
speed_slot = 6
edge_slot = 9
sides = 9
lanes = 128
tall = 8


def iota(shape, dim):
    return lax.broadcasted_iota(jnp.int32, shape, dim)


def wide(tile, width):
    return jnp.concatenate([tile] * (width // tile.shape[1]), axis=1)


def rows_of(load, chunk, chunks, step, edge):
    low = chunk * tall
    if step == 0:
        return load(low, low + tall)
    if step == 1 and chunk > 0:
        return load(low - 1, low + tall - 1)
    if step == -1 and chunk < chunks - 1:
        return load(low + 1, low + tall + 1)
    rows = load(low, low + tall)
    at = iota(rows.shape, 0)
    if step == 1:
        return jnp.where(at == 0, edge(), pltpu.roll(rows, 1, 0))
    return jnp.where(at == tall - 1, edge(), pltpu.roll(rows, tall - 1, 0))


def columns_of(rows, halo, lane, step):
    width = rows.shape[1]
    at = iota(rows.shape, 1)
    if step == 1:
        edge = wide(pltpu.roll(halo, (lanes - lane) % lanes, 1), width)
        return jnp.where(at == 0, edge, pltpu.roll(rows, 1, 1))
    edge = wide(pltpu.roll(halo, lanes - 1 - lane, 1), width)
    return jnp.where(at == width - 1, edge, pltpu.roll(rows, width - 1, 1))


def packed(high, low):
    at = iota(high[0].shape, 1)
    tile = jnp.zeros_like(high[0])
    for slot, part in enumerate(high):
        tile = jnp.where(at == slot, pltpu.roll(part, slot + 1, 1), tile)
    for place, part in enumerate(low):
        slot = len(high) + place
        tile = jnp.where(at == slot, pltpu.roll(part, slot, 1), tile)
    return tile


def along(index, vector):
    total = None
    for comp in range(3):
        sign = velocity_set[index][comp]
        if sign != 0:
            term = vector[comp] if sign > 0 else -vector[comp]
            total = term if total is None else total + term
    return total


def conversions(source, kind, heading, code, *, columns):
    count = source.shape[1]
    value = (heading[...] + 32 * kind[...]).astype(jnp.float32)
    row, column = (source[...] // columns, source[...] % columns)
    by_row = jnp.where(iota((code.shape[0], count), 0) == row, value, 0.0).astype(jnp.bfloat16)
    by_column = jnp.where(iota((columns, count), 0) == column, 1.0, 0.0).astype(jnp.bfloat16)
    code[...] = lax.dot_general(
        by_row, by_column, (((1,), (1,)), ((), ())), preferred_element_type=jnp.float32
    )


def odd(axis):
    return lax.rem(lax.axis_index(axis), 2) == 1


def select(chosen, first, second):
    return jnp.where(chosen, first[...], second[...])


def swap_rows(first, second, x, planes, high, low, flip):
    for slot, (top, bottom) in enumerate(zip(high, low)):
        by = top.shape[0]
        up, down = (top[by - 1 : by, :], bottom[0:1, :])
        at = slot * planes + x
        first[at : at + 1, :] = jnp.where(flip, down, up)
        second[at : at + 1, :] = jnp.where(flip, up, down)


def swapped_rows(first, second, slots, low_rows, high_rows, shift):
    flip = odd("gy")
    planes = low_rows.shape[0] - 2 * shift
    for x in range(planes):
        for place, slot in enumerate(slots):
            at = slot * planes + x
            one, two = (first[at : at + 1, :], second[at : at + 1, :])
            low_rows[x + shift, place : place + 1, :] = jnp.where(flip, one, two)
            high_rows[x + shift, place : place + 1, :] = jnp.where(flip, two, one)


def column_rows(tiles, count):
    return jnp.concatenate(tiles, axis=0).T[0:count, :]


def row_columns(rows):
    rest = jnp.zeros((lanes - rows.shape[0], rows.shape[1]), jnp.float32)
    return jnp.concatenate([rows, rest], axis=0).T


def first_faces(
    stretch_in,
    flags_in,
    stretch,
    flags,
    columns,
    y_first,
    y_second,
    x_first,
    x_second,
    sems,
):
    bx, by, bz = flags.shape
    flip_x, flip_y = (odd("gx"), odd("gy"))
    copies = [
        pltpu.make_async_copy(stretch_in, stretch, sems.at[0]),
        pltpu.make_async_copy(flags_in, flags, sems.at[1]),
    ]
    for copy in copies:
        copy.start()
    for copy in copies:
        copy.wait()
    tiles = []
    for x in range(bx):
        along_y = [stretch.at[symmetric_slot[comp][1], x] for comp in range(3)]
        swap_rows(y_first, y_second, x, bx, along_y, along_y, flip_y)
        fields = [stretch.at[symmetric_slot[comp][2], x] for comp in range(3)]
        tiles.append(
            packed(
                [field[:, bz - lanes : bz] for field in fields],
                [field[:, 0:lanes] for field in fields],
            )
        )
    columns[...] = column_rows(tiles, columns.shape[0])
    rest = y_first.shape[0] - 3 * bx
    y_first[3 * bx :, :] = jnp.zeros((rest, bz), jnp.float32)
    y_second[3 * bx :, :] = jnp.zeros((rest, bz), jnp.float32)
    for out, last in ((x_first, flip_x), (x_second, jnp.logical_not(flip_x))):
        for comp in range(3):
            slot = symmetric_slot[comp][0]
            out[comp] = jnp.where(last, stretch[slot, 0], stretch[slot, bx - 1])
        out[3] = jnp.where(jnp.where(last, flags[0], flags[bx - 1]) == 0, 1.0, 0.0)


def moments(pops_in, pops, flow, sems):
    bx, by = pops.shape[1:3]
    copies = [
        pltpu.make_async_copy(pops_in.at[:, x], pops.at[:, x], sems.at[x]) for x in range(bx)
    ]
    for copy in copies:
        copy.start()
    for x in range(bx):
        copies[x].wait()
        for chunk in range(by // tall):
            rows = pl.ds(chunk * tall, tall)
            part = [pops[index, x, rows, :] for index in range(19)]
            density = part[0]
            for index in range(1, 19):
                density = density + part[index]
            inverse = 1.0 / density
            for comp in range(3):
                total = None
                for index in pairs:
                    sign = velocity_set[index][comp]
                    if sign != 0:
                        term = part[index] - part[index + 1]
                        term = term if sign > 0 else -term
                        total = term if total is None else total + term
                flow[comp, x, rows, :] = total * inverse
            flow[3, x, rows, :] = density
            flow[4, x, rows, :] = inverse


def beside(ref, field, x, step, halo, slot):
    last = ref.shape[1] - 1
    if halo is None:
        return lambda low, high: ref[field, x + step, low:high, :]
    if isinstance(x, int):
        if 0 <= x + step <= last:
            return lambda low, high: ref[field, x + step, low:high, :]
        return lambda low, high: halo[slot, low:high, :]
    inside = jnp.clip(x + step, 0, last)
    beyond = x == (0 if step < 0 else last)
    return lambda low, high: jnp.where(
        beyond, halo[slot, low:high, :], ref[field, inside, low:high, :]
    )


def differences(
    ref, field, slots, x, chunk, chunks, below, above, y_below, y_above, z_halo, lane, side
):
    slot_x, slot_y, slot_z = slots
    low, high = (chunk * tall, chunk * tall + tall)

    def load(first, stop):
        return ref[field, x, first:stop, :]

    result = [None, None, None]
    if slot_x is not None:
        after = beside(ref, field, x, 1, above, slot_x)(low, high)
        before = beside(ref, field, x, -1, below, slot_x)(low, high)
        result[0] = after - before
    if slot_y is not None:
        after = rows_of(load, chunk, chunks, -1, lambda: y_above[x, slot_y : slot_y + 1, :])
        before = rows_of(load, chunk, chunks, 1, lambda: y_below[x, slot_y : slot_y + 1, :])
        result[1] = after - before
    if slot_z is not None:
        rows, halo = (load(low, high), z_halo[x, low:high, :])
        after = columns_of(rows, halo, lane + side + slot_z, -1)
        before = columns_of(rows, halo, lane + slot_z, 1)
        result[2] = after - before
    return result


def end_place(x, bx):
    return 0 if x == 0 else 1


def plane_of(inner, outer, field, x, bx):
    if 0 < x < bx - 1:
        return inner.at[field, x - 1]
    return outer.at[field, end_place(x, bx)]


def collide_plane(x, place, pops, stretch, flow, halos, post, shift):
    by = pops.shape[2]
    chunks = by // tall
    factor = 1.0 - 0.5 / relax_time
    rate = 1.0 / relax_time
    for chunk in range(chunks):
        rows = pl.ds(chunk * tall, tall)
        terms = [[], [], []]
        for field in range(6):
            slots = [None, None, None]
            for comp in range(3):
                for axis in range(3):
                    if symmetric_slot[comp][axis] == field:
                        slots[axis] = comp
            found = differences(stretch, field, slots, x, chunk, chunks, *halos)
            for axis in range(3):
                if slots[axis] is not None:
                    terms[slots[axis]].append(found[axis])
        force = [0.5 * polymer_coeff * (part[0] + part[1] + part[2]) for part in terms]
        density, half = (flow[3, x, rows, :], 0.5 * flow[4, x, rows, :])
        moved = [flow[comp, x, rows, :] + half * force[comp] for comp in range(3)]
        for comp in range(3):
            shift[comp, place, rows, :] = moved[comp]
        squared = moved[0] * moved[0] + moved[1] * moved[1] + moved[2] * moved[2]
        work = moved[0] * force[0] + moved[1] * force[1] + moved[2] * force[2]
        weight = rate * density
        common = weight - 1.5 * weight * squared - 3.0 * factor * work
        odd = [3.0 * weight * moved[comp] + 3.0 * factor * force[comp] for comp in range(3)]
        even = [4.5 * weight * moved[comp] + 9.0 * factor * force[comp] for comp in range(3)]
        keep = 1.0 - rate
        post[0, place, rows, :] = keep * pops[0, x, rows, :] + lattice_weights[0] * common
        for index in pairs:
            both = common + along(index, moved) * along(index, even)
            differ = along(index, odd)
            scale = lattice_weights[index]
            post[index, place, rows, :] = keep * pops[index, x, rows, :] + scale * (both + differ)
            post[index + 1, place, rows, :] = keep * pops[index + 1, x, rows, :] + scale * (
                both - differ
            )


def collide_inner(
    pops,
    stretch,
    flow,
    z_rows,
    y_first,
    y_second,
    post,
    shift,
    y_below,
    y_above,
    z_halo,
):
    swapped_rows(y_first, y_second, range(3), y_below, y_above, 0)
    z_halo[...] = row_columns(z_rows[...]).reshape(z_halo.shape)
    halos = (None, None, y_below, y_above, z_halo, 0, 3)

    def plane(x, carry):
        collide_plane(x, x - 1, pops, stretch, flow, halos, post, shift)
        return carry

    lax.fori_loop(1, pops.shape[1] - 1, plane, 0)


def collide_outer(
    pops,
    stretch,
    flags,
    flow,
    x_first,
    x_second,
    y_first,
    y_second,
    z_rows,
    inner,
    post,
    shift,
    columns,
    ahead,
    behind,
    up_first,
    up_second,
    below,
    above,
    y_below,
    y_above,
    z_halo,
    gas,
):
    bx, by, bz = flags.shape
    halos = (below, above, y_below, y_above, z_halo, 0, 3)
    flip_x, flip_y = (odd("gx"), odd("gy"))
    below[...] = select(flip_x, x_first, x_second)
    above[...] = select(flip_x, x_second, x_first)
    swapped_rows(y_first, y_second, range(3), y_below, y_above, 0)
    z_halo[...] = row_columns(z_rows[...]).reshape(z_halo.shape)
    for x in (0, bx - 1):
        collide_plane(x, end_place(x, bx), pops, stretch, flow, halos, post, shift)

    tiles = []
    for x in range(bx):
        gas[x] = jnp.where(flags[x] == 0, 1.0, 0.0)
        rest = [gas.at[x]] + [flow.at[comp, x] for comp in range(3)]

        def fields(indices):
            return [plane_of(inner, post, index, x, bx) for index in indices] + rest

        swap_rows(up_first, up_second, x, bx, fields(y_up), fields(y_down), flip_y)
        tiles.append(
            packed(
                [field[:, bz - lanes : bz] for field in fields(z_up)],
                [field[:, 0:lanes] for field in fields(z_down)],
            )
        )
    columns[...] = column_rows(tiles, columns.shape[0])
    rest = up_first.shape[0] - sides * bx
    up_first[sides * bx :, :] = jnp.zeros((rest, bz), jnp.float32)
    up_second[sides * bx :, :] = jnp.zeros((rest, bz), jnp.float32)
    for slot in range(5):
        up, down = (post[x_up[slot], 1], post[x_down[slot], 0])
        ahead[slot] = jnp.where(flip_x, down, up)
        behind[slot] = jnp.where(flip_x, up, down)
    for comp in range(3):
        up, down = (flow[comp, bx - 1], flow[comp, 0])
        ahead[5 + comp] = jnp.where(flip_x, down, up)
        behind[5 + comp] = jnp.where(flip_x, up, down)


def restretch_plane(x, place, stretch, flow, halos, updated):
    chunks = stretch.shape[2] // tall
    for chunk in range(chunks):
        rows = pl.ds(chunk * tall, tall)
        grad = [
            differences(
                flow, comp, (comp, comp, comp), x, chunk, chunks, *halos, speed_slot, sides
            )
            for comp in range(3)
        ]
        part = [stretch[slot, x, rows, :] for slot in range(6)]
        full = [part[slot] + 1.0 if slot < 3 else part[slot] for slot in range(6)]

        def product(row, col):
            total = grad[row][0] * full[symmetric_slot[0][col]]
            for inner in (1, 2):
                total = total + grad[row][inner] * full[symmetric_slot[inner][col]]
            return total

        for slot, (row, col) in enumerate(tensor_pairs):
            old = (1.0 - 1.0 / polymer_time) * part[slot]
            if row == col:
                updated[slot, place, rows, :] = old + product(row, col)
            else:
                updated[slot, place, rows, :] = old + 0.5 * (product(row, col) + product(col, row))


def restretch_inner(
    stretch,
    flow,
    y_first,
    y_second,
    z_rows,
    new_stretch,
    mark,
    updated,
    y_below,
    y_above,
    z_halo,
    sem,
):
    bx = stretch.shape[1]
    swapped_rows(y_first, y_second, range(speed_slot, sides), y_below, y_above, 0)
    z_halo[...] = row_columns(z_rows[...]).reshape(z_halo.shape)
    halos = (None, None, y_below, y_above, z_halo)

    def plane(x, carry):
        restretch_plane(x, x - 1, stretch, flow, halos, updated)
        return carry

    lax.fori_loop(1, bx - 1, plane, 0)
    copy = pltpu.make_async_copy(updated, new_stretch.at[:, 1 : bx - 1], sem)
    copy.start()
    mark[...] = jnp.zeros(mark.shape, jnp.float32)
    copy.wait()


def restretch_outer(
    stretch,
    flow,
    x_first,
    x_second,
    y_first,
    y_second,
    z_rows,
    inner_stretch,
    new_stretch,
    updated,
    below,
    above,
    y_below,
    y_above,
    z_halo,
    sems,
):
    bx = stretch.shape[1]
    flip_x = odd("gx")
    for comp in range(3):
        below[comp] = jnp.where(flip_x, x_first[5 + comp], x_second[5 + comp])
        above[comp] = jnp.where(flip_x, x_second[5 + comp], x_first[5 + comp])
    swapped_rows(y_first, y_second, range(speed_slot, sides), y_below, y_above, 0)
    z_halo[...] = row_columns(z_rows[...]).reshape(z_halo.shape)
    halos = (below, above, y_below, y_above, z_halo)
    copies = []
    for place, x in enumerate((0, bx - 1)):
        restretch_plane(x, place, stretch, flow, halos, updated)
        copies.append(
            pltpu.make_async_copy(updated.at[:, place], new_stretch.at[:, x], sems.at[place])
        )
        copies[-1].start()
    for copy in copies:
        copy.wait()


def store(inner, outer, inner_slanted, outer_slanted, late, fresh, mark, sems):
    bx = fresh.shape[1]
    moves = [
        (inner, fresh.at[0:first_slanted, 1 : bx - 1]),
        (inner_slanted, fresh.at[first_slanted:, 1 : bx - 1]),
    ]
    for place, x in enumerate((0, bx - 1)):
        moves.append((outer_slanted.at[:, place], fresh.at[first_slanted:, x]))
        order = (x_up, x_down)[place]
        start = 0
        for index in order + (first_slanted,):
            if index > start:
                run = slice(start, index)
                moves.append((outer.at[run, place], fresh.at[run, x]))
            if index in order:
                moves.append((late.at[order.index(index), place], fresh.at[index, x]))
            start = index + 1
    copies = [
        pltpu.make_async_copy(source, target, sems.at[place])
        for place, (source, target) in enumerate(moves)
    ]
    for copy in copies:
        copy.start()
    mark[...] = jnp.zeros(mark.shape, jnp.float32)
    for copy in copies:
        copy.wait()


up_edges = ((0, y_up.index(7)), (0, gas_slot), (1, y_down.index(9)), (1, gas_slot))
down_edges = ((0, y_up.index(10)), (0, gas_slot), (1, y_down.index(8)), (1, gas_slot))


def forward_edges(z_rows, y_first, y_second, first_out, second_out, corner, *, bx):
    halves = y_first.shape[1] // lanes
    flip_x, flip_y = (odd("gx"), odd("gy"))
    for half in range(halves):
        cut = slice(half * lanes, half * lanes + lanes)
        for place in range(4):
            found = []
            for x, edges in ((bx - 1, up_edges), (0, down_edges)):
                side, slot = edges[place]
                row = slot * bx + x
                one = y_first[row : row + 1, cut]
                two = y_second[row : row + 1, cut]
                found.append(jnp.where(flip_y, one, two) if side == 0 else jnp.where(flip_y, two, one))
            at = half * 4 + place
            first_out[at : at + 1, :] = jnp.where(flip_x, found[1], found[0])
            second_out[at : at + 1, :] = jnp.where(flip_x, found[0], found[1])
    first_out[4 * halves :, :] = z_rows[...]
    second_out[4 * halves :, :] = z_rows[...]
    corner[...] = z_rows[...]


def own_halos(flags, y_first, y_second, z_rows, gas, low_rows, high_rows, columns):
    bx, by = flags.shape[:2]
    tile = row_columns(z_rows[...])
    swapped_rows(y_first, y_second, range(speed_slot), low_rows, high_rows, 1)
    for x in range(bx):
        gas[x + 1] = jnp.where(flags[x] == 0, 1.0, 0.0)
        columns[x + 1] = tile[x * by : x * by + by, :]


def own_corners(corner_first, corner_second, low_rows, high_rows):
    bx = low_rows.shape[0] - 2
    flip = odd("gy")
    corner_below = row_columns(select(flip, corner_first, corner_second))
    corner_above = row_columns(select(flip, corner_second, corner_first))
    by = corner_below.shape[0] // bx
    for x in range(bx):
        end = x * by + by - 1
        low_rows[x + 1, edge_slot : edge_slot + 1, 0:lanes] = corner_below[end : end + 1, :]
        high_rows[x + 1, edge_slot : edge_slot + 1, 0:lanes] = corner_above[
            x * by : x * by + 1, :
        ]


def pass_on(x, chunk, indices, source, leaving_of, speed, halos, fresh, place, total, change):
    gas, low_rows, high_rows, columns = halos
    by = gas.shape[1]
    chunks = by // tall
    rows = pl.ds(chunk * tall, tall)
    rest = 1.0 - 1.5 * (speed[0] * speed[0] + speed[1] * speed[1] + speed[2] * speed[2])
    equals = {}

    def moved(load, index, slot, lane):
        step_x, step_y, step_z = velocity_set[index]
        plane = x + 1 - step_x
        edges = low_rows if step_y == 1 else high_rows
        found = rows_of(load, chunk, chunks, step_y, lambda: edges[plane, slot : slot + 1, :])
        if step_z == 0:
            return found
        halo = rows_of(
            lambda low, high: columns[plane, low:high, :],
            chunk,
            chunks,
            step_y,
            lambda: edges[plane, edge_slot : edge_slot + 1, 0:lanes],
        )
        return columns_of(found, halo, lane, step_z)

    for index in indices:
        step_x, step_y, step_z = velocity_set[index]
        first = min(index, opposite_of[index])
        if first not in equals:
            proj = along(first, speed)
            equals[first] = 2.0 * lattice_weights[first] * (rest + 4.5 * proj * proj)
        slot, lane, gas_lane = (None, None, None)
        if step_y != 0:
            slot = (y_up if step_y == 1 else y_down).index(index)
        if step_z == 1:
            lane, gas_lane = (z_up.index(index), gas_slot)
        elif step_z == -1:
            lane, gas_lane = (sides + z_down.index(index), sides + gas_slot)
        field = source(index)
        marks = gas.at[x + 1 - step_x]
        arriving = moved(lambda low, high: field[low:high, :], index, slot, lane)
        from_gas = moved(lambda low, high: marks[low:high, :], index, gas_slot, gas_lane)
        leaving = leaving_of(opposite_of[index])[rows, :]
        open_side = from_gas > 0.5
        value = jnp.where(open_side, equals[first] - leaving, arriving)
        fresh(index)[place, rows, :] = value
        total = total + value
        change = change + jnp.where(open_side, 0.0, arriving - leaving)
    return total, change


def settle(x, rows, mass, flags, code, total, change):
    read = mass[x, rows, :] + jnp.where(flags[x, rows, :] == 1, change, 0.0)
    mark = code[x, rows, :]
    liquid = mark >= 32.0
    converts = mark > 0.0
    level = jnp.where(liquid, total, 0.0)
    excess = jnp.where(converts, read - level, 0.0)
    heading = jnp.where(liquid, mark - 32.0, mark)
    return jnp.where(converts, level, read), excess, heading


slanted = tuple(index for index in range(19) if velocity_set[index][1] * velocity_set[index][2])
first_slanted = slanted[0]


def from_inside(x, bx):
    found = [index for index in range(1, 19) if 0 <= x - velocity_set[index][0] < bx]
    return [index for index in found if index not in slanted]


def from_beyond(x, bx):
    return [index for index in range(1, 19) if not 0 <= x - velocity_set[index][0] < bx]


def stream_early(
    inner_post,
    outer_post,
    inner_shift,
    outer_shift,
    flags,
    y_first,
    y_second,
    z_rows,
    inner,
    outer,
    totals,
    changes,
    gas,
    low_rows,
    high_rows,
    columns,
):
    bx, by, bz = flags.shape
    halos = (gas, low_rows, high_rows, columns)
    own_halos(flags, y_first, y_second, z_rows, *halos)

    for x in range(bx):
        inside = 0 < x < bx - 1
        place = x - 1 if inside else end_place(x, bx)
        fresh = inner if inside else outer
        for chunk in range(by // tall):
            rows = pl.ds(chunk * tall, tall)
            total = plane_of(inner_post, outer_post, 0, x, bx)[rows, :]
            fresh[0, place, rows, :] = total
            total, change = pass_on(
                x,
                chunk,
                from_inside(x, bx),
                lambda index: plane_of(
                    inner_post, outer_post, index, x - velocity_set[index][0], bx
                ),
                lambda index: plane_of(inner_post, outer_post, index, x, bx),
                [plane_of(inner_shift, outer_shift, comp, x, bx)[rows, :] for comp in range(3)],
                halos,
                lambda index: fresh.at[index],
                place,
                total,
                jnp.zeros((tall, bz), jnp.float32),
            )
            totals[x, rows, :] = total
            changes[x, rows, :] = change


def stream_slanted(
    inner_post,
    outer_post,
    inner_shift,
    outer_shift,
    mass,
    flags,
    code,
    y_first,
    y_second,
    z_rows,
    corner_first,
    corner_second,
    totals,
    changes,
    inner,
    outer,
    settled,
    excess,
    heading,
    end_totals,
    end_changes,
    gas,
    low_rows,
    high_rows,
    columns,
):
    bx, by, bz = flags.shape
    halos = (gas, low_rows, high_rows, columns)
    own_halos(flags, y_first, y_second, z_rows, *halos)
    own_corners(corner_first, corner_second, low_rows, high_rows)

    for x in range(bx):
        inside = 0 < x < bx - 1
        place = x - 1 if inside else end_place(x, bx)
        fresh = inner if inside else outer
        for chunk in range(by // tall):
            rows = pl.ds(chunk * tall, tall)
            total, change = pass_on(
                x,
                chunk,
                slanted,
                lambda index: plane_of(inner_post, outer_post, index, x, bx),
                lambda index: plane_of(inner_post, outer_post, index, x, bx),
                [plane_of(inner_shift, outer_shift, comp, x, bx)[rows, :] for comp in range(3)],
                halos,
                lambda index: fresh.at[index - first_slanted],
                place,
                totals[x, rows, :],
                changes[x, rows, :],
            )
            if inside:
                now = settle(x, rows, mass, flags, code, total, change)
                settled[place, rows, :], excess[place, rows, :], heading[place, rows, :] = now
            else:
                end_totals[place, rows, :] = total
                end_changes[place, rows, :] = change


def stream_late(
    post,
    shift,
    mass,
    flags,
    code,
    totals,
    changes,
    gas_first,
    gas_second,
    x_first,
    x_second,
    edges_first,
    edges_second,
    inner_excess,
    inner_heading,
    after,
    late,
    settled,
    spread,
    line_first,
    line_second,
    out_z,
    gas,
    low_rows,
    high_rows,
    columns,
    below,
    above,
    excess,
    heading,
):
    bx, by, bz = flags.shape
    halves = bz // lanes
    flip_x = odd("gx")
    halos = (gas, low_rows, high_rows, columns)

    for slot in range(5):
        below[slot] = jnp.where(flip_x, x_first[slot], x_second[slot])
        above[slot] = jnp.where(flip_x, x_second[slot], x_first[slot])
    gas[0] = jnp.where(flip_x, gas_first[3], gas_second[3])
    gas[bx + 1] = jnp.where(flip_x, gas_second[3], gas_first[3])
    edges_below = select(flip_x, edges_first, edges_second)
    edges_above = select(flip_x, edges_second, edges_first)
    for found, at, x, edges in (
        (edges_below, 0, bx - 1, up_edges),
        (edges_above, bx + 1, 0, down_edges),
    ):
        for place, (side, slot) in enumerate(edges):
            line = jnp.concatenate(
                [found[half * 4 + place : half * 4 + place + 1, :] for half in range(halves)],
                axis=1,
            )
            (low_rows, high_rows)[side][at, slot : slot + 1, :] = line
        columns[at] = row_columns(found[4 * halves :, :])[x * by : x * by + by, :]
    for place, x in enumerate((0, bx - 1)):
        halo, order = ((below, x_up), (above, x_down))[place]
        for chunk in range(by // tall):
            rows = pl.ds(chunk * tall, tall)
            total, change = pass_on(
                x,
                chunk,
                from_beyond(x, bx),
                lambda index: halo.at[order.index(index)],
                lambda index: post.at[index, place],
                [shift[comp, place, rows, :] for comp in range(3)],
                halos,
                lambda index: late.at[order.index(index)],
                place,
                totals[place, rows, :],
                changes[place, rows, :],
            )
            now = settle(x, rows, mass, flags, code, total, change)
            settled[place, rows, :], excess[x, rows, :], heading[x, rows, :] = now
    for x in range(1, bx - 1):
        excess[x] = inner_excess[x - 1]
        heading[x] = inner_heading[x - 1]

    row_at, lane_at = (iota((by, bz), 0), iota((by, bz), 1))
    line_at = iota((1, bz), 1)
    tile_lane, line_lane = (iota((by, lanes), 1), iota((1, lanes), 1))

    def rows_up(rows):
        return jnp.where(row_at == 0, 0.0, pltpu.roll(rows, 1, 0))

    def rows_down(rows):
        return jnp.where(row_at == by - 1, 0.0, pltpu.roll(rows, by - 1, 0))

    def over(rows, at, step):
        if step == 1:
            return jnp.where(at == 0, 0.0, pltpu.roll(rows, 1, 1))
        return jnp.where(at == bz - 1, 0.0, pltpu.roll(rows, bz - 1, 1))

    def summed(parts):
        total = parts[0]
        for part in parts[1:]:
            total = total + part
        return total

    tile = jnp.zeros((by, lanes), jnp.float32)
    line_up = jnp.zeros((1, lanes), jnp.float32)
    line_down = jnp.zeros((1, lanes), jnp.float32)
    flip_y = odd("gy")
    line_first[...] = jnp.zeros(line_first.shape, jnp.float32)
    line_second[...] = jnp.zeros(line_second.shape, jnp.float32)
    for target in range(bx + 2):
        groups = {}
        for index in range(1, 19):
            step_x, step_y, step_z = velocity_set[index]
            x = target - 1 - step_x
            if 0 <= x < bx:
                part = jnp.where(heading[x] == float(index), excess[x], 0.0)
                groups.setdefault((step_y, step_z), []).append(part)
        groups = {key: summed(parts) for key, parts in groups.items()}
        total = jnp.zeros((by, bz), jnp.float32)
        line = {1: jnp.zeros((1, bz), jnp.float32), -1: jnp.zeros((1, bz), jnp.float32)}
        for step_z in (0, 1, -1):
            group = jnp.zeros((by, bz), jnp.float32)
            ends = {}
            if (0, step_z) in groups:
                group = group + groups[(0, step_z)]
            if (1, step_z) in groups:
                group = group + rows_up(groups[(1, step_z)])
                ends[1] = groups[(1, step_z)][by - 1 : by, :]
            if (-1, step_z) in groups:
                group = group + rows_down(groups[(-1, step_z)])
                ends[-1] = groups[(-1, step_z)][0:1, :]
            if step_z == 0:
                total = total + group
                for side in ends:
                    line[side] = line[side] + ends[side]
                continue
            total = total + over(group, lane_at, step_z)
            for side in ends:
                line[side] = line[side] + over(ends[side], line_at, step_z)
            if step_z == 1:
                spot, cut, roll = (target, slice(bz - lanes, bz), target + 1)
            else:
                spot, cut, roll = (8 + target, slice(0, lanes), 8 + target)
            tile = jnp.where(tile_lane == spot, pltpu.roll(group[:, cut], roll, 1), tile)
            if 1 in ends:
                line_up = jnp.where(
                    line_lane == spot, pltpu.roll(ends[1][:, cut], roll, 1), line_up
                )
            if -1 in ends:
                line_down = jnp.where(
                    line_lane == spot, pltpu.roll(ends[-1][:, cut], roll, 1), line_down
                )
        spread[target] = total
        line_first[target : target + 1, :] = jnp.where(flip_y, line[-1], line[1])
        line_second[target : target + 1, :] = jnp.where(flip_y, line[1], line[-1])
    rest = jnp.zeros((lanes - by - 2, lanes), jnp.float32)
    out_z[...] = column_rows([tile, line_up, line_down, rest], 16)


def with_edges(total, target, tile, y_below, y_above):
    by, bz = total.shape
    row_at, lane_at = (iota((by, bz), 0), iota((by, bz), 1))
    total = total + jnp.where(lane_at == 0, tile[0:by, target : target + 1], 0.0)
    total = total + jnp.where(lane_at == bz - 1, tile[0:by, 8 + target : 9 + target], 0.0)
    total = total + jnp.where(row_at == 0, y_below[target : target + 1, :], 0.0)
    return total + jnp.where(row_at == by - 1, y_above[target : target + 1, :], 0.0)


def add_faces(spread, z_rows, y_first, y_second, after, first, second):
    last = spread.shape[0] - 1
    flip_x, flip_y = (odd("gx"), odd("gy"))
    tile = row_columns(z_rows[...])
    y_below, y_above = (select(flip_y, y_first, y_second), select(flip_y, y_second, y_first))
    up = with_edges(spread[last], last, tile, y_below, y_above)
    down = with_edges(spread[0], 0, tile, y_below, y_above)
    first[...] = jnp.where(flip_x, down, up)
    second[...] = jnp.where(flip_x, up, down)


def add_all(
    inner_settled,
    outer_settled,
    spread,
    z_rows,
    y_first,
    y_second,
    corner_first,
    corner_second,
    x_second,
    x_first,
    new_mass,
):
    bx, by, bz = new_mass.shape
    flip_x, flip_y = (odd("gx"), odd("gy"))
    tile = row_columns(z_rows[...])
    y_below, y_above = (select(flip_y, y_first, y_second), select(flip_y, y_second, y_first))
    at = iota((8, bz), 1)
    found = []
    for rows, side, corner in (
        (y_below, 0, select(flip_y, corner_first, corner_second)),
        (y_above, 1, select(flip_y, corner_second, corner_first)),
    ):
        edge = corner[:, by + side : by + side + 1]
        rows = rows + jnp.where(at == 0, edge[0:8, :], 0.0)
        found.append(rows + jnp.where(at == bz - 1, edge[8:16, :], 0.0))
    for x in range(bx):
        total = with_edges(spread[x + 1], x + 1, tile, *found)
        if x == 0:
            total = total + select(flip_x, x_first, x_second)
        if x == bx - 1:
            total = total + select(flip_x, x_second, x_first)
        if 0 < x < bx - 1:
            total = total + inner_settled[x - 1]
        else:
            total = total + outer_settled[0 if x == 0 else 1]
        new_mass[x] = total


def swapped(first, second, axis):
    devices = lax.axis_size(axis)
    ahead = [(i, (i + 1) % devices if i % 2 == 0 else i - 1) for i in range(devices)]
    behind = [(i, (i - 1) % devices if i % 2 == 0 else (i + 1) % devices) for i in range(devices)]
    return lax.ppermute(first, axis, ahead), lax.ppermute(second, axis, behind)


def both_ways(rows, lower):
    devices = lax.axis_size("gz")
    before = lax.ppermute(rows, "gz", [(i, (i + 1) % devices) for i in range(devices)])
    if devices == 2:
        return before
    after = lax.ppermute(rows, "gz", [(i, (i - 1) % devices) for i in range(devices)])
    return jnp.where(iota(rows.shape, 0) < lower, before, after)


remote = pl.BlockSpec(memory_space=pltpu.HBM)


def call(body, outs, specs=None, out_specs=None, scratch=(), cost=(0, 0), aliases=None):
    extra = {} if specs is None else {"in_specs": specs}
    if out_specs is not None:
        extra["out_specs"] = out_specs
    return pl.pallas_call(
        body,
        out_shape=[
            shape
            if isinstance(shape, jax.ShapeDtypeStruct)
            else jax.ShapeDtypeStruct(shape, jnp.float32)
            for shape in outs
        ],
        scratch_shapes=[
            pltpu.VMEM(shape, jnp.float32) if isinstance(shape, tuple) else shape
            for shape in scratch
        ],
        compiler_params=pltpu.CompilerParams(vmem_limit_bytes=40 * 1024 * 1024),
        input_output_aliases=aliases or {},
        cost_estimate=pl.CostEstimate(flops=cost[0], bytes_accessed=cost[1], transcendentals=0),
        **extra,
    )


def shards(populations, stretch, mass, flags, conv_source, conv_kind, conv_direction):
    bx, by, bz = flags.shape
    cells = bx * by * bz
    box, face, tile = ((bx, by, bz), (by, bz), (bx, by, lanes))

    stretch, flags, z_out, y_one, y_two, x_one, x_two = call(
        first_faces,
        [
            (6, *box),
            jax.ShapeDtypeStruct(box, jnp.int32),
            (8, bx * by),
            (4 * bx, bz),
            (4 * bx, bz),
            (4, *face),
            (4, *face),
        ],
        specs=[remote] * 2,
        scratch=[pltpu.SemaphoreType.DMA((2,))],
        cost=(10 * cells, 60 * cells),
    )(*(pltpu.with_memory_space_constraint(array, pltpu.HBM) for array in (stretch, flags)))
    first_x = swapped(x_one, x_two, "gx")
    z_first = both_ways(z_out, 3)
    y_first = swapped(y_one, y_two, "gy")

    entries = conv_source.shape[0]
    (code,) = call(
        lambda *refs: conversions(*refs, columns=bz), [(bx * by, bz)], cost=(40 * cells, 4 * cells)
    )(*(array.reshape(1, entries) for array in (conv_source, conv_kind, conv_direction)))
    code = code.reshape(box)

    pops, flow = call(
        moments,
        [(19, *box), (5, *box)],
        specs=[remote],
        scratch=[pltpu.SemaphoreType.DMA((bx,))],
        cost=(60 * cells, 150 * cells),
    )(pltpu.with_memory_space_constraint(populations, pltpu.HBM))

    columns, rows = ((24, bx * by), (10 * bx, bz))
    sides_y = [(bx, 8, bz), (bx, 8, bz), tile]
    inside, ends = ((bx - 2, *face), (2, *face))
    inner_post, inner_shift = call(
        collide_inner,
        [(19, *inside), (3, *inside)],
        scratch=sides_y,
        cost=(150 * cells, 150 * cells),
    )(pops, stretch, flow, z_first, *y_first)
    outer_post, outer_shift, z_out, x_one, x_two, y_one, y_two = call(
        collide_outer,
        [(19, *ends), (3, *ends), columns, (8, *face), (8, *face), rows, rows],
        scratch=[(4, *face), (4, *face)] + sides_y + [box],
        cost=(150 * cells, 150 * cells),
    )(pops, stretch, flags, flow, *first_x, *y_first, z_first, inner_post)
    z_post = both_ways(z_out, sides)
    post_y = swapped(y_one, y_two, "gy")
    post_x = swapped(x_one, x_two, "gx")
    edges = (4 * (bz // lanes) + columns[0], lanes)
    x_one, x_two, corner = call(
        lambda *refs: forward_edges(*refs, bx=bx), [edges, edges, columns]
    )(z_post, *post_y)
    corners = swapped(corner, corner, "gy")
    edges_x = swapped(x_one, x_two, "gx")

    rims = [(bx + 2, *face), (bx + 2, 16, bz), (bx + 2, 16, bz), (bx + 2, by, lanes)]
    posts = (inner_post, outer_post, inner_shift, outer_shift)
    inner, outer, totals, changes = call(
        stream_early,
        [(first_slanted, *inside), (first_slanted, *ends), box, box],
        scratch=rims,
        cost=(350 * cells, 200 * cells),
    )(*posts, flags, *post_y, z_post)
    (
        inner_slanted,
        outer_slanted,
        inner_settled,
        inner_excess,
        inner_heading,
        totals,
        changes,
    ) = call(
        stream_slanted,
        [(4, *inside), (4, *ends), inside, inside, inside, ends, ends],
        scratch=rims,
        cost=(100 * cells, 60 * cells),
    )(*posts, mass, flags, code, *post_y, z_post, *corners, totals, changes)
    mark = (tall, lanes)
    new_stretch, inner_done = call(
        restretch_inner,
        [(6, *box), mark],
        out_specs=[remote, pl.BlockSpec()],
        scratch=[(6, *inside)] + sides_y + [pltpu.SemaphoreType.DMA],
        cost=(80 * cells, 40 * cells),
    )(stretch, flow, *post_y, z_post)
    late, outer_settled, spread, y_one, y_two, z_out = call(
        stream_late,
        [(5, *ends), ends, (bx + 2, *face), (8, bz), (8, bz), (16, bx * by)],
        scratch=rims + [(5, *face), (5, *face), box, box],
        cost=(150 * cells, 100 * cells),
    )(
        outer_post,
        outer_shift,
        mass,
        flags,
        code,
        totals,
        changes,
        *first_x,
        *post_x,
        *edges_x,
        inner_excess,
        inner_heading,
        inner_done,
    )
    z_last = both_ways(z_out, 8)
    last_y = swapped(y_one, y_two, "gy")
    last_corners = swapped(z_last, z_last, "gy")
    fresh, stored = call(
        store,
        [(19, *box), mark],
        out_specs=[remote, pl.BlockSpec()],
        scratch=[pltpu.SemaphoreType.DMA((32,))],
        cost=(0, 160 * cells),
    )(inner, outer, inner_slanted, outer_slanted, late)
    x_one, x_two = call(add_faces, [face, face])(spread, z_last, *last_y, stored)
    last_x = swapped(x_one, x_two, "gx")
    (new_stretch,) = call(
        restretch_outer,
        [(6, *box)],
        specs=[pl.BlockSpec()] * 7 + [remote],
        out_specs=[remote],
        scratch=[(6, *ends), (3, *face), (3, *face)]
        + sides_y
        + [pltpu.SemaphoreType.DMA((2,))],
        cost=(80 * cells, 40 * cells),
        aliases={7: 0},
    )(stretch, flow, *post_x, *post_y, z_post, new_stretch)
    (new_mass,) = call(add_all, [box])(
        inner_settled, outer_settled, spread, z_last, *last_y, *last_corners, *last_x[::-1]
    )
    return (fresh, new_stretch, new_mass)


def solution(mesh):
    return jax.shard_map(
        shards,
        mesh=mesh,
        in_specs=(
            P(None, "gx", "gy", "gz"),
            P(None, "gx", "gy", "gz"),
            P("gx", "gy", "gz"),
            P("gx", "gy", "gz"),
            P(("gx", "gy", "gz")),
            P(("gx", "gy", "gz")),
            P(("gx", "gy", "gz")),
        ),
        out_specs=(P(None, "gx", "gy", "gz"), P(None, "gx", "gy", "gz"), P("gx", "gy", "gz")),
        check_vma=False,
    )
```

```python
import jax
import jax.numpy as jnp
from jax import lax
from jax.experimental import pallas as pl
from jax.experimental.pallas import tpu as pltpu
from jax.sharding import PartitionSpec as P

velocity_set = (
    (0, 0, 0),
    (1, 0, 0),
    (-1, 0, 0),
    (0, 1, 0),
    (0, -1, 0),
    (0, 0, 1),
    (0, 0, -1),
    (1, 1, 0),
    (-1, -1, 0),
    (1, -1, 0),
    (-1, 1, 0),
    (1, 0, 1),
    (-1, 0, -1),
    (1, 0, -1),
    (-1, 0, 1),
    (0, 1, 1),
    (0, -1, -1),
    (0, 1, -1),
    (0, -1, 1),
)
opposite_of = (0, 2, 1, 4, 3, 6, 5, 8, 7, 10, 9, 12, 11, 14, 13, 16, 15, 18, 17)
lattice_weights = (1.0 / 3.0,) + (1.0 / 18.0,) * 6 + (1.0 / 36.0,) * 12
symmetric_slot = ((0, 3, 4), (3, 1, 5), (4, 5, 2))
tensor_pairs = ((0, 0), (1, 1), (2, 2), (0, 1), (0, 2), (1, 2))
relax_time = 0.8
polymer_time = 8.0
polymer_coeff = 0.05


def moving(axis, sign):
    return tuple(index for index in range(19) if velocity_set[index][axis] == sign)


x_up, x_down = (moving(0, 1), moving(0, -1))
y_up, y_down = (moving(1, 1), moving(1, -1))
z_up, z_down = (moving(2, 1), moving(2, -1))
pairs = tuple(range(1, 19, 2))
gas_slot = 5
speed_slot = 6
edge_slot = 9
sides = 9
lanes = 128
tall = 8


def iota(shape, dim):
    return lax.broadcasted_iota(jnp.int32, shape, dim)


def wide(tile, width):
    return jnp.concatenate([tile] * (width // tile.shape[1]), axis=1)


def rows_of(load, chunk, chunks, step, edge):
    low = chunk * tall
    if step == 0:
        return load(low, low + tall)
    if step == 1 and chunk > 0:
        return load(low - 1, low + tall - 1)
    if step == -1 and chunk < chunks - 1:
        return load(low + 1, low + tall + 1)
    rows = load(low, low + tall)
    at = iota(rows.shape, 0)
    if step == 1:
        return jnp.where(at == 0, edge(), pltpu.roll(rows, 1, 0))
    return jnp.where(at == tall - 1, edge(), pltpu.roll(rows, tall - 1, 0))


def columns_of(rows, halo, lane, step):
    width = rows.shape[1]
    at = iota(rows.shape, 1)
    if step == 1:
        edge = wide(pltpu.roll(halo, (lanes - lane) % lanes, 1), width)
        return jnp.where(at == 0, edge, pltpu.roll(rows, 1, 1))
    edge = wide(pltpu.roll(halo, lanes - 1 - lane, 1), width)
    return jnp.where(at == width - 1, edge, pltpu.roll(rows, width - 1, 1))


def packed(high, low):
    at = iota(high[0].shape, 1)
    tile = jnp.zeros_like(high[0])
    for slot, part in enumerate(high):
        tile = jnp.where(at == slot, pltpu.roll(part, slot + 1, 1), tile)
    for place, part in enumerate(low):
        slot = len(high) + place
        tile = jnp.where(at == slot, pltpu.roll(part, slot, 1), tile)
    return tile


def along(index, vector):
    total = None
    for comp in range(3):
        sign = velocity_set[index][comp]
        if sign != 0:
            term = vector[comp] if sign > 0 else -vector[comp]
            total = term if total is None else total + term
    return total


def conversions(source, kind, heading, code, mark, *, columns):
    count = source.shape[1]
    value = (heading[...] + 32 * kind[...]).astype(jnp.float32)
    row, column = (source[...] // columns, source[...] % columns)
    by_row = jnp.where(iota((code.shape[0], count), 0) == row, value, 0.0).astype(jnp.bfloat16)
    by_column = jnp.where(iota((columns, count), 0) == column, 1.0, 0.0).astype(jnp.bfloat16)
    code[...] = lax.dot_general(
        by_row, by_column, (((1,), (1,)), ((), ())), preferred_element_type=jnp.float32
    )
    mark[...] = jnp.zeros(mark.shape, jnp.float32)


def odd(axis):
    return lax.rem(lax.axis_index(axis), 2) == 1


def select(chosen, first, second):
    return jnp.where(chosen, first[...], second[...])


def swap_rows(first, second, x, planes, high, low, flip):
    for slot, (top, bottom) in enumerate(zip(high, low)):
        by = top.shape[0]
        up, down = (top[by - 1 : by, :], bottom[0:1, :])
        at = slot * planes + x
        first[at : at + 1, :] = jnp.where(flip, down, up)
        second[at : at + 1, :] = jnp.where(flip, up, down)


def swapped_rows(first, second, slots, low_rows, high_rows, shift):
    flip = odd("gy")
    planes = low_rows.shape[0] - 2 * shift
    for x in range(planes):
        for place, slot in enumerate(slots):
            at = slot * planes + x
            one, two = (first[at : at + 1, :], second[at : at + 1, :])
            low_rows[x + shift, place : place + 1, :] = jnp.where(flip, one, two)
            high_rows[x + shift, place : place + 1, :] = jnp.where(flip, two, one)


def column_rows(tiles, count):
    return jnp.concatenate(tiles, axis=0).T[0:count, :]


def row_columns(rows):
    rest = jnp.zeros((lanes - rows.shape[0], rows.shape[1]), jnp.float32)
    return jnp.concatenate([rows, rest], axis=0).T


def first_faces(
    stretch_in,
    flags_in,
    stretch,
    flags,
    columns,
    y_first,
    y_second,
    x_first,
    x_second,
    sems,
):
    bx, by, bz = flags.shape
    flip_x, flip_y = (odd("gx"), odd("gy"))
    copies = [
        pltpu.make_async_copy(stretch_in, stretch, sems.at[0]),
        pltpu.make_async_copy(flags_in, flags, sems.at[1]),
    ]
    for copy in copies:
        copy.start()
    for copy in copies:
        copy.wait()
    tiles = []
    for x in range(bx):
        along_y = [stretch.at[symmetric_slot[comp][1], x] for comp in range(3)]
        swap_rows(y_first, y_second, x, bx, along_y, along_y, flip_y)
        fields = [stretch.at[symmetric_slot[comp][2], x] for comp in range(3)]
        tiles.append(
            packed(
                [field[:, bz - lanes : bz] for field in fields],
                [field[:, 0:lanes] for field in fields],
            )
        )
    columns[...] = column_rows(tiles, columns.shape[0])
    rest = y_first.shape[0] - 3 * bx
    y_first[3 * bx :, :] = jnp.zeros((rest, bz), jnp.float32)
    y_second[3 * bx :, :] = jnp.zeros((rest, bz), jnp.float32)
    for out, last in ((x_first, flip_x), (x_second, jnp.logical_not(flip_x))):
        for comp in range(3):
            slot = symmetric_slot[comp][0]
            out[comp] = jnp.where(last, stretch[slot, 0], stretch[slot, bx - 1])
        out[3] = jnp.where(jnp.where(last, flags[0], flags[bx - 1]) == 0, 1.0, 0.0)


def moments(pops_in, pops, flow, sems):
    bx, by = pops.shape[1:3]
    copies = [
        pltpu.make_async_copy(pops_in.at[:, x], pops.at[:, x], sems.at[x]) for x in range(bx)
    ]
    for copy in copies:
        copy.start()
    for x in range(bx):
        copies[x].wait()
        for chunk in range(by // tall):
            rows = pl.ds(chunk * tall, tall)
            part = [pops[index, x, rows, :] for index in range(19)]
            density = part[0]
            for index in range(1, 19):
                density = density + part[index]
            inverse = 1.0 / density
            for comp in range(3):
                total = None
                for index in pairs:
                    sign = velocity_set[index][comp]
                    if sign != 0:
                        term = part[index] - part[index + 1]
                        term = term if sign > 0 else -term
                        total = term if total is None else total + term
                flow[comp, x, rows, :] = total * inverse
            flow[3, x, rows, :] = density
            flow[4, x, rows, :] = inverse


def beside(ref, field, x, step, halo, slot):
    last = ref.shape[1] - 1
    if halo is None:
        return lambda low, high: ref[field, x + step, low:high, :]
    if isinstance(x, int):
        if 0 <= x + step <= last:
            return lambda low, high: ref[field, x + step, low:high, :]
        return lambda low, high: halo[slot, low:high, :]
    inside = jnp.clip(x + step, 0, last)
    beyond = x == (0 if step < 0 else last)
    return lambda low, high: jnp.where(
        beyond, halo[slot, low:high, :], ref[field, inside, low:high, :]
    )


def differences(
    ref, field, slots, x, chunk, chunks, below, above, y_below, y_above, z_halo, lane, side
):
    slot_x, slot_y, slot_z = slots
    low, high = (chunk * tall, chunk * tall + tall)

    def load(first, stop):
        return ref[field, x, first:stop, :]

    result = [None, None, None]
    if slot_x is not None:
        after = beside(ref, field, x, 1, above, slot_x)(low, high)
        before = beside(ref, field, x, -1, below, slot_x)(low, high)
        result[0] = after - before
    if slot_y is not None:
        after = rows_of(load, chunk, chunks, -1, lambda: y_above[x, slot_y : slot_y + 1, :])
        before = rows_of(load, chunk, chunks, 1, lambda: y_below[x, slot_y : slot_y + 1, :])
        result[1] = after - before
    if slot_z is not None:
        rows, halo = (load(low, high), z_halo[x, low:high, :])
        after = columns_of(rows, halo, lane + side + slot_z, -1)
        before = columns_of(rows, halo, lane + slot_z, 1)
        result[2] = after - before
    return result


def end_place(x, bx):
    return 0 if x == 0 else 1


def plane_of(inner, outer, field, x, bx):
    if 0 < x < bx - 1:
        return inner.at[field, x - 1]
    return outer.at[field, end_place(x, bx)]


def collide_plane(x, place, pops, stretch, flow, halos, post, shift):
    by = pops.shape[2]
    chunks = by // tall
    factor = 1.0 - 0.5 / relax_time
    rate = 1.0 / relax_time
    for chunk in range(chunks):
        rows = pl.ds(chunk * tall, tall)
        terms = [[], [], []]
        for field in range(6):
            slots = [None, None, None]
            for comp in range(3):
                for axis in range(3):
                    if symmetric_slot[comp][axis] == field:
                        slots[axis] = comp
            found = differences(stretch, field, slots, x, chunk, chunks, *halos)
            for axis in range(3):
                if slots[axis] is not None:
                    terms[slots[axis]].append(found[axis])
        force = [0.5 * polymer_coeff * (part[0] + part[1] + part[2]) for part in terms]
        density, half = (flow[3, x, rows, :], 0.5 * flow[4, x, rows, :])
        moved = [flow[comp, x, rows, :] + half * force[comp] for comp in range(3)]
        for comp in range(3):
            shift[comp, place, rows, :] = moved[comp]
        squared = moved[0] * moved[0] + moved[1] * moved[1] + moved[2] * moved[2]
        work = moved[0] * force[0] + moved[1] * force[1] + moved[2] * force[2]
        weight = rate * density
        common = weight - 1.5 * weight * squared - 3.0 * factor * work
        odd = [3.0 * weight * moved[comp] + 3.0 * factor * force[comp] for comp in range(3)]
        even = [4.5 * weight * moved[comp] + 9.0 * factor * force[comp] for comp in range(3)]
        keep = 1.0 - rate
        post[0, place, rows, :] = keep * pops[0, x, rows, :] + lattice_weights[0] * common
        for index in pairs:
            both = common + along(index, moved) * along(index, even)
            differ = along(index, odd)
            scale = lattice_weights[index]
            post[index, place, rows, :] = keep * pops[index, x, rows, :] + scale * (both + differ)
            post[index + 1, place, rows, :] = keep * pops[index + 1, x, rows, :] + scale * (
                both - differ
            )


def collide_inner(
    pops,
    stretch,
    flow,
    z_rows,
    y_first,
    y_second,
    post,
    shift,
    y_below,
    y_above,
    z_halo,
):
    swapped_rows(y_first, y_second, range(3), y_below, y_above, 0)
    z_halo[...] = row_columns(z_rows[...]).reshape(z_halo.shape)
    halos = (None, None, y_below, y_above, z_halo, 0, 3)

    def plane(x, carry):
        collide_plane(x, x - 1, pops, stretch, flow, halos, post, shift)
        return carry

    lax.fori_loop(1, pops.shape[1] - 1, plane, 0)


def collide_outer(
    pops,
    stretch,
    flags,
    flow,
    x_first,
    x_second,
    y_first,
    y_second,
    z_rows,
    inner,
    post,
    shift,
    columns,
    ahead,
    behind,
    up_first,
    up_second,
    below,
    above,
    y_below,
    y_above,
    z_halo,
    gas,
):
    bx, by, bz = flags.shape
    halos = (below, above, y_below, y_above, z_halo, 0, 3)
    flip_x, flip_y = (odd("gx"), odd("gy"))
    below[...] = select(flip_x, x_first, x_second)
    above[...] = select(flip_x, x_second, x_first)
    swapped_rows(y_first, y_second, range(3), y_below, y_above, 0)
    z_halo[...] = row_columns(z_rows[...]).reshape(z_halo.shape)
    for x in (0, bx - 1):
        collide_plane(x, end_place(x, bx), pops, stretch, flow, halos, post, shift)

    tiles = []
    for x in range(bx):
        gas[x] = jnp.where(flags[x] == 0, 1.0, 0.0)
        rest = [gas.at[x]] + [flow.at[comp, x] for comp in range(3)]

        def fields(indices):
            return [plane_of(inner, post, index, x, bx) for index in indices] + rest

        swap_rows(up_first, up_second, x, bx, fields(y_up), fields(y_down), flip_y)
        tiles.append(
            packed(
                [field[:, bz - lanes : bz] for field in fields(z_up)],
                [field[:, 0:lanes] for field in fields(z_down)],
            )
        )
    columns[...] = column_rows(tiles, columns.shape[0])
    rest = up_first.shape[0] - sides * bx
    up_first[sides * bx :, :] = jnp.zeros((rest, bz), jnp.float32)
    up_second[sides * bx :, :] = jnp.zeros((rest, bz), jnp.float32)
    for slot in range(5):
        up, down = (post[x_up[slot], 1], post[x_down[slot], 0])
        ahead[slot] = jnp.where(flip_x, down, up)
        behind[slot] = jnp.where(flip_x, up, down)
    for comp in range(3):
        up, down = (flow[comp, bx - 1], flow[comp, 0])
        ahead[5 + comp] = jnp.where(flip_x, down, up)
        behind[5 + comp] = jnp.where(flip_x, up, down)


def restretch_plane(x, place, stretch, flow, halos, updated):
    chunks = stretch.shape[2] // tall
    for chunk in range(chunks):
        rows = pl.ds(chunk * tall, tall)
        grad = [
            differences(
                flow, comp, (comp, comp, comp), x, chunk, chunks, *halos, speed_slot, sides
            )
            for comp in range(3)
        ]
        part = [stretch[slot, x, rows, :] for slot in range(6)]
        full = [part[slot] + 1.0 if slot < 3 else part[slot] for slot in range(6)]

        def product(row, col):
            total = grad[row][0] * full[symmetric_slot[0][col]]
            for inner in (1, 2):
                total = total + grad[row][inner] * full[symmetric_slot[inner][col]]
            return total

        for slot, (row, col) in enumerate(tensor_pairs):
            old = (1.0 - 1.0 / polymer_time) * part[slot]
            if row == col:
                updated[slot, place, rows, :] = old + product(row, col)
            else:
                updated[slot, place, rows, :] = old + 0.5 * (product(row, col) + product(col, row))


def restretch_inner(
    stretch,
    flow,
    y_first,
    y_second,
    z_rows,
    new_stretch,
    mark,
    updated,
    y_below,
    y_above,
    z_halo,
    sem,
):
    bx = stretch.shape[1]
    swapped_rows(y_first, y_second, range(speed_slot, sides), y_below, y_above, 0)
    z_halo[...] = row_columns(z_rows[...]).reshape(z_halo.shape)
    halos = (None, None, y_below, y_above, z_halo)

    def plane(x, carry):
        restretch_plane(x, x - 1, stretch, flow, halos, updated)
        return carry

    lax.fori_loop(1, bx - 1, plane, 0)
    copy = pltpu.make_async_copy(updated, new_stretch.at[:, 1 : bx - 1], sem)
    copy.start()
    mark[...] = jnp.zeros(mark.shape, jnp.float32)
    copy.wait()


def restretch_outer(
    stretch,
    flow,
    x_first,
    x_second,
    y_first,
    y_second,
    z_rows,
    inner_stretch,
    after,
    new_stretch,
    mark,
    updated,
    below,
    above,
    y_below,
    y_above,
    z_halo,
    sems,
):
    bx = stretch.shape[1]
    flip_x = odd("gx")
    for comp in range(3):
        below[comp] = jnp.where(flip_x, x_first[5 + comp], x_second[5 + comp])
        above[comp] = jnp.where(flip_x, x_second[5 + comp], x_first[5 + comp])
    swapped_rows(y_first, y_second, range(speed_slot, sides), y_below, y_above, 0)
    z_halo[...] = row_columns(z_rows[...]).reshape(z_halo.shape)
    halos = (below, above, y_below, y_above, z_halo)
    copies = []
    for place, x in enumerate((0, bx - 1)):
        restretch_plane(x, place, stretch, flow, halos, updated)
        copies.append(
            pltpu.make_async_copy(updated.at[:, place], new_stretch.at[:, x], sems.at[place])
        )
        copies[-1].start()
    mark[...] = jnp.zeros(mark.shape, jnp.float32)
    for copy in copies:
        copy.wait()


def store(inner, outer, inner_slanted, outer_slanted, late, fresh, sems):
    bx = fresh.shape[1]
    moves = [
        (inner, fresh.at[0:first_slanted, 1 : bx - 1]),
        (inner_slanted, fresh.at[first_slanted:, 1 : bx - 1]),
    ]
    for place, x in enumerate((0, bx - 1)):
        moves.append((outer_slanted.at[:, place], fresh.at[first_slanted:, x]))
        order = (x_up, x_down)[place]
        start = 0
        for index in order + (first_slanted,):
            if index > start:
                run = slice(start, index)
                moves.append((outer.at[run, place], fresh.at[run, x]))
            if index in order:
                moves.append((late.at[order.index(index), place], fresh.at[index, x]))
            start = index + 1
    copies = [
        pltpu.make_async_copy(source, target, sems.at[place])
        for place, (source, target) in enumerate(moves)
    ]
    for copy in copies:
        copy.start()
    for copy in copies:
        copy.wait()


up_edges = ((0, y_up.index(7)), (0, gas_slot), (1, y_down.index(9)), (1, gas_slot))
down_edges = ((0, y_up.index(10)), (0, gas_slot), (1, y_down.index(8)), (1, gas_slot))


def forward_edges(z_rows, y_first, y_second, after, first_out, second_out, corner, *, bx):
    halves = y_first.shape[1] // lanes
    flip_x, flip_y = (odd("gx"), odd("gy"))
    for half in range(halves):
        cut = slice(half * lanes, half * lanes + lanes)
        for place in range(4):
            found = []
            for x, edges in ((bx - 1, up_edges), (0, down_edges)):
                side, slot = edges[place]
                row = slot * bx + x
                one = y_first[row : row + 1, cut]
                two = y_second[row : row + 1, cut]
                found.append(jnp.where(flip_y, one, two) if side == 0 else jnp.where(flip_y, two, one))
            at = half * 4 + place
            first_out[at : at + 1, :] = jnp.where(flip_x, found[1], found[0])
            second_out[at : at + 1, :] = jnp.where(flip_x, found[0], found[1])
    first_out[4 * halves :, :] = z_rows[...]
    second_out[4 * halves :, :] = z_rows[...]
    corner[...] = z_rows[...]


def own_halos(flags, y_first, y_second, z_rows, gas, low_rows, high_rows, columns):
    bx, by = flags.shape[:2]
    tile = row_columns(z_rows[...])
    swapped_rows(y_first, y_second, range(speed_slot), low_rows, high_rows, 1)
    for x in range(bx):
        gas[x + 1] = jnp.where(flags[x] == 0, 1.0, 0.0)
        columns[x + 1] = tile[x * by : x * by + by, :]


def own_corners(corner_first, corner_second, low_rows, high_rows):
    bx = low_rows.shape[0] - 2
    flip = odd("gy")
    corner_below = row_columns(select(flip, corner_first, corner_second))
    corner_above = row_columns(select(flip, corner_second, corner_first))
    by = corner_below.shape[0] // bx
    for x in range(bx):
        end = x * by + by - 1
        low_rows[x + 1, edge_slot : edge_slot + 1, 0:lanes] = corner_below[end : end + 1, :]
        high_rows[x + 1, edge_slot : edge_slot + 1, 0:lanes] = corner_above[
            x * by : x * by + 1, :
        ]


def pass_on(x, chunk, indices, source, leaving_of, speed, halos, fresh, place, total, change):
    gas, low_rows, high_rows, columns = halos
    by = gas.shape[1]
    chunks = by // tall
    rows = pl.ds(chunk * tall, tall)
    rest = 1.0 - 1.5 * (speed[0] * speed[0] + speed[1] * speed[1] + speed[2] * speed[2])
    equals = {}

    def moved(load, index, slot, lane):
        step_x, step_y, step_z = velocity_set[index]
        plane = x + 1 - step_x
        edges = low_rows if step_y == 1 else high_rows
        found = rows_of(load, chunk, chunks, step_y, lambda: edges[plane, slot : slot + 1, :])
        if step_z == 0:
            return found
        halo = rows_of(
            lambda low, high: columns[plane, low:high, :],
            chunk,
            chunks,
            step_y,
            lambda: edges[plane, edge_slot : edge_slot + 1, 0:lanes],
        )
        return columns_of(found, halo, lane, step_z)

    for index in indices:
        step_x, step_y, step_z = velocity_set[index]
        first = min(index, opposite_of[index])
        if first not in equals:
            proj = along(first, speed)
            equals[first] = 2.0 * lattice_weights[first] * (rest + 4.5 * proj * proj)
        slot, lane, gas_lane = (None, None, None)
        if step_y != 0:
            slot = (y_up if step_y == 1 else y_down).index(index)
        if step_z == 1:
            lane, gas_lane = (z_up.index(index), gas_slot)
        elif step_z == -1:
            lane, gas_lane = (sides + z_down.index(index), sides + gas_slot)
        field = source(index)
        marks = gas.at[x + 1 - step_x]
        arriving = moved(lambda low, high: field[low:high, :], index, slot, lane)
        from_gas = moved(lambda low, high: marks[low:high, :], index, gas_slot, gas_lane)
        leaving = leaving_of(opposite_of[index])[rows, :]
        open_side = from_gas > 0.5
        value = jnp.where(open_side, equals[first] - leaving, arriving)
        fresh(index)[place, rows, :] = value
        total = total + value
        change = change + jnp.where(open_side, 0.0, arriving - leaving)
    return total, change


def settle(x, rows, mass, flags, code, total, change):
    read = mass[x, rows, :] + jnp.where(flags[x, rows, :] == 1, change, 0.0)
    mark = code[x, rows, :]
    liquid = mark >= 32.0
    converts = mark > 0.0
    level = jnp.where(liquid, total, 0.0)
    excess = jnp.where(converts, read - level, 0.0)
    heading = jnp.where(liquid, mark - 32.0, mark)
    return jnp.where(converts, level, read), excess, heading


slanted = tuple(index for index in range(19) if velocity_set[index][1] * velocity_set[index][2])
first_slanted = slanted[0]


def from_inside(x, bx):
    found = [index for index in range(1, 19) if 0 <= x - velocity_set[index][0] < bx]
    return [index for index in found if index not in slanted]


def from_beyond(x, bx):
    return [index for index in range(1, 19) if not 0 <= x - velocity_set[index][0] < bx]


def stream_early(
    inner_post,
    outer_post,
    inner_shift,
    outer_shift,
    flags,
    y_first,
    y_second,
    z_rows,
    inner,
    outer,
    totals,
    changes,
    gas,
    low_rows,
    high_rows,
    columns,
):
    bx, by, bz = flags.shape
    halos = (gas, low_rows, high_rows, columns)
    own_halos(flags, y_first, y_second, z_rows, *halos)

    for x in range(bx):
        inside = 0 < x < bx - 1
        place = x - 1 if inside else end_place(x, bx)
        fresh = inner if inside else outer
        for chunk in range(by // tall):
            rows = pl.ds(chunk * tall, tall)
            total = plane_of(inner_post, outer_post, 0, x, bx)[rows, :]
            fresh[0, place, rows, :] = total
            total, change = pass_on(
                x,
                chunk,
                from_inside(x, bx),
                lambda index: plane_of(
                    inner_post, outer_post, index, x - velocity_set[index][0], bx
                ),
                lambda index: plane_of(inner_post, outer_post, index, x, bx),
                [plane_of(inner_shift, outer_shift, comp, x, bx)[rows, :] for comp in range(3)],
                halos,
                lambda index: fresh.at[index],
                place,
                total,
                jnp.zeros((tall, bz), jnp.float32),
            )
            totals[x, rows, :] = total
            changes[x, rows, :] = change


def stream_slanted(
    inner_post,
    outer_post,
    inner_shift,
    outer_shift,
    mass,
    flags,
    code,
    y_first,
    y_second,
    z_rows,
    corner_first,
    corner_second,
    totals,
    changes,
    inner,
    outer,
    settled,
    excess,
    heading,
    end_totals,
    end_changes,
    gas,
    low_rows,
    high_rows,
    columns,
):
    bx, by, bz = flags.shape
    halos = (gas, low_rows, high_rows, columns)
    own_halos(flags, y_first, y_second, z_rows, *halos)
    own_corners(corner_first, corner_second, low_rows, high_rows)

    for x in range(bx):
        inside = 0 < x < bx - 1
        place = x - 1 if inside else end_place(x, bx)
        fresh = inner if inside else outer
        for chunk in range(by // tall):
            rows = pl.ds(chunk * tall, tall)
            total, change = pass_on(
                x,
                chunk,
                slanted,
                lambda index: plane_of(inner_post, outer_post, index, x, bx),
                lambda index: plane_of(inner_post, outer_post, index, x, bx),
                [plane_of(inner_shift, outer_shift, comp, x, bx)[rows, :] for comp in range(3)],
                halos,
                lambda index: fresh.at[index - first_slanted],
                place,
                totals[x, rows, :],
                changes[x, rows, :],
            )
            if inside:
                now = settle(x, rows, mass, flags, code, total, change)
                settled[place, rows, :], excess[place, rows, :], heading[place, rows, :] = now
            else:
                end_totals[place, rows, :] = total
                end_changes[place, rows, :] = change


def stream_late(
    post,
    shift,
    mass,
    flags,
    code,
    totals,
    changes,
    gas_first,
    gas_second,
    x_first,
    x_second,
    edges_first,
    edges_second,
    inner_excess,
    inner_heading,
    after,
    late,
    settled,
    spread,
    line_first,
    line_second,
    out_z,
    gas,
    low_rows,
    high_rows,
    columns,
    below,
    above,
    excess,
    heading,
):
    bx, by, bz = flags.shape
    halves = bz // lanes
    flip_x = odd("gx")
    halos = (gas, low_rows, high_rows, columns)

    for slot in range(5):
        below[slot] = jnp.where(flip_x, x_first[slot], x_second[slot])
        above[slot] = jnp.where(flip_x, x_second[slot], x_first[slot])
    gas[0] = jnp.where(flip_x, gas_first[3], gas_second[3])
    gas[bx + 1] = jnp.where(flip_x, gas_second[3], gas_first[3])
    edges_below = select(flip_x, edges_first, edges_second)
    edges_above = select(flip_x, edges_second, edges_first)
    for found, at, x, edges in (
        (edges_below, 0, bx - 1, up_edges),
        (edges_above, bx + 1, 0, down_edges),
    ):
        for place, (side, slot) in enumerate(edges):
            line = jnp.concatenate(
                [found[half * 4 + place : half * 4 + place + 1, :] for half in range(halves)],
                axis=1,
            )
            (low_rows, high_rows)[side][at, slot : slot + 1, :] = line
        columns[at] = row_columns(found[4 * halves :, :])[x * by : x * by + by, :]
    for place, x in enumerate((0, bx - 1)):
        halo, order = ((below, x_up), (above, x_down))[place]
        for chunk in range(by // tall):
            rows = pl.ds(chunk * tall, tall)
            total, change = pass_on(
                x,
                chunk,
                from_beyond(x, bx),
                lambda index: halo.at[order.index(index)],
                lambda index: post.at[index, place],
                [shift[comp, place, rows, :] for comp in range(3)],
                halos,
                lambda index: late.at[order.index(index)],
                place,
                totals[place, rows, :],
                changes[place, rows, :],
            )
            now = settle(x, rows, mass, flags, code, total, change)
            settled[place, rows, :], excess[x, rows, :], heading[x, rows, :] = now
    for x in range(1, bx - 1):
        excess[x] = inner_excess[x - 1]
        heading[x] = inner_heading[x - 1]

    row_at, lane_at = (iota((by, bz), 0), iota((by, bz), 1))
    line_at = iota((1, bz), 1)
    tile_lane, line_lane = (iota((by, lanes), 1), iota((1, lanes), 1))

    def rows_up(rows):
        return jnp.where(row_at == 0, 0.0, pltpu.roll(rows, 1, 0))

    def rows_down(rows):
        return jnp.where(row_at == by - 1, 0.0, pltpu.roll(rows, by - 1, 0))

    def over(rows, at, step):
        if step == 1:
            return jnp.where(at == 0, 0.0, pltpu.roll(rows, 1, 1))
        return jnp.where(at == bz - 1, 0.0, pltpu.roll(rows, bz - 1, 1))

    def summed(parts):
        total = parts[0]
        for part in parts[1:]:
            total = total + part
        return total

    tile = jnp.zeros((by, lanes), jnp.float32)
    line_up = jnp.zeros((1, lanes), jnp.float32)
    line_down = jnp.zeros((1, lanes), jnp.float32)
    flip_y = odd("gy")
    line_first[...] = jnp.zeros(line_first.shape, jnp.float32)
    line_second[...] = jnp.zeros(line_second.shape, jnp.float32)
    for target in range(bx + 2):
        groups = {}
        for index in range(1, 19):
            step_x, step_y, step_z = velocity_set[index]
            x = target - 1 - step_x
            if 0 <= x < bx:
                part = jnp.where(heading[x] == float(index), excess[x], 0.0)
                groups.setdefault((step_y, step_z), []).append(part)
        groups = {key: summed(parts) for key, parts in groups.items()}
        total = jnp.zeros((by, bz), jnp.float32)
        line = {1: jnp.zeros((1, bz), jnp.float32), -1: jnp.zeros((1, bz), jnp.float32)}
        for step_z in (0, 1, -1):
            group = jnp.zeros((by, bz), jnp.float32)
            ends = {}
            if (0, step_z) in groups:
                group = group + groups[(0, step_z)]
            if (1, step_z) in groups:
                group = group + rows_up(groups[(1, step_z)])
                ends[1] = groups[(1, step_z)][by - 1 : by, :]
            if (-1, step_z) in groups:
                group = group + rows_down(groups[(-1, step_z)])
                ends[-1] = groups[(-1, step_z)][0:1, :]
            if step_z == 0:
                total = total + group
                for side in ends:
                    line[side] = line[side] + ends[side]
                continue
            total = total + over(group, lane_at, step_z)
            for side in ends:
                line[side] = line[side] + over(ends[side], line_at, step_z)
            if step_z == 1:
                spot, cut, roll = (target, slice(bz - lanes, bz), target + 1)
            else:
                spot, cut, roll = (8 + target, slice(0, lanes), 8 + target)
            tile = jnp.where(tile_lane == spot, pltpu.roll(group[:, cut], roll, 1), tile)
            if 1 in ends:
                line_up = jnp.where(
                    line_lane == spot, pltpu.roll(ends[1][:, cut], roll, 1), line_up
                )
            if -1 in ends:
                line_down = jnp.where(
                    line_lane == spot, pltpu.roll(ends[-1][:, cut], roll, 1), line_down
                )
        spread[target] = total
        line_first[target : target + 1, :] = jnp.where(flip_y, line[-1], line[1])
        line_second[target : target + 1, :] = jnp.where(flip_y, line[1], line[-1])
    rest = jnp.zeros((lanes - by - 2, lanes), jnp.float32)
    out_z[...] = column_rows([tile, line_up, line_down, rest], 16)


def with_edges(total, target, tile, y_below, y_above):
    by, bz = total.shape
    row_at, lane_at = (iota((by, bz), 0), iota((by, bz), 1))
    total = total + jnp.where(lane_at == 0, tile[0:by, target : target + 1], 0.0)
    total = total + jnp.where(lane_at == bz - 1, tile[0:by, 8 + target : 9 + target], 0.0)
    total = total + jnp.where(row_at == 0, y_below[target : target + 1, :], 0.0)
    return total + jnp.where(row_at == by - 1, y_above[target : target + 1, :], 0.0)


def add_faces(spread, z_rows, y_first, y_second, after, first, second):
    last = spread.shape[0] - 1
    flip_x, flip_y = (odd("gx"), odd("gy"))
    tile = row_columns(z_rows[...])
    y_below, y_above = (select(flip_y, y_first, y_second), select(flip_y, y_second, y_first))
    up = with_edges(spread[last], last, tile, y_below, y_above)
    down = with_edges(spread[0], 0, tile, y_below, y_above)
    first[...] = jnp.where(flip_x, down, up)
    second[...] = jnp.where(flip_x, up, down)


def add_all(
    inner_settled,
    outer_settled,
    spread,
    z_rows,
    y_first,
    y_second,
    corner_first,
    corner_second,
    x_second,
    x_first,
    new_mass,
):
    bx, by, bz = new_mass.shape
    flip_x, flip_y = (odd("gx"), odd("gy"))
    tile = row_columns(z_rows[...])
    y_below, y_above = (select(flip_y, y_first, y_second), select(flip_y, y_second, y_first))
    at = iota((8, bz), 1)
    found = []
    for rows, side, corner in (
        (y_below, 0, select(flip_y, corner_first, corner_second)),
        (y_above, 1, select(flip_y, corner_second, corner_first)),
    ):
        edge = corner[:, by + side : by + side + 1]
        rows = rows + jnp.where(at == 0, edge[0:8, :], 0.0)
        found.append(rows + jnp.where(at == bz - 1, edge[8:16, :], 0.0))
    for x in range(bx):
        total = with_edges(spread[x + 1], x + 1, tile, *found)
        if x == 0:
            total = total + select(flip_x, x_first, x_second)
        if x == bx - 1:
            total = total + select(flip_x, x_second, x_first)
        if 0 < x < bx - 1:
            total = total + inner_settled[x - 1]
        else:
            total = total + outer_settled[0 if x == 0 else 1]
        new_mass[x] = total


def swapped(first, second, axis):
    devices = lax.axis_size(axis)
    ahead = [(i, (i + 1) % devices if i % 2 == 0 else i - 1) for i in range(devices)]
    behind = [(i, (i - 1) % devices if i % 2 == 0 else (i + 1) % devices) for i in range(devices)]
    return lax.ppermute(first, axis, ahead), lax.ppermute(second, axis, behind)


def both_ways(rows, lower):
    devices = lax.axis_size("gz")
    before = lax.ppermute(rows, "gz", [(i, (i + 1) % devices) for i in range(devices)])
    if devices == 2:
        return before
    after = lax.ppermute(rows, "gz", [(i, (i - 1) % devices) for i in range(devices)])
    return jnp.where(iota(rows.shape, 0) < lower, before, after)


remote = pl.BlockSpec(memory_space=pltpu.HBM)
anywhere = pl.BlockSpec(memory_space=pl.ANY)


def call(body, outs, specs=None, out_specs=None, scratch=(), cost=(0, 0), aliases=None):
    extra = {} if specs is None else {"in_specs": specs}
    if out_specs is not None:
        extra["out_specs"] = out_specs
    return pl.pallas_call(
        body,
        out_shape=[
            shape
            if isinstance(shape, jax.ShapeDtypeStruct)
            else jax.ShapeDtypeStruct(shape, jnp.float32)
            for shape in outs
        ],
        scratch_shapes=[
            pltpu.VMEM(shape, jnp.float32) if isinstance(shape, tuple) else shape
            for shape in scratch
        ],
        compiler_params=pltpu.CompilerParams(vmem_limit_bytes=40 * 1024 * 1024),
        input_output_aliases=aliases or {},
        cost_estimate=pl.CostEstimate(flops=cost[0], bytes_accessed=cost[1], transcendentals=0),
        **extra,
    )


def shards(populations, stretch, mass, flags, conv_source, conv_kind, conv_direction):
    bx, by, bz = flags.shape
    cells = bx * by * bz
    box, face, tile = ((bx, by, bz), (by, bz), (bx, by, lanes))

    stretch, flags, z_out, y_one, y_two, x_one, x_two = call(
        first_faces,
        [
            (6, *box),
            jax.ShapeDtypeStruct(box, jnp.int32),
            (8, bx * by),
            (4 * bx, bz),
            (4 * bx, bz),
            (4, *face),
            (4, *face),
        ],
        specs=[remote] * 2,
        scratch=[pltpu.SemaphoreType.DMA((2,))],
        cost=(10 * cells, 60 * cells),
    )(*(pltpu.with_memory_space_constraint(array, pltpu.HBM) for array in (stretch, flags)))
    first_x = swapped(x_one, x_two, "gx")
    z_first = both_ways(z_out, 3)
    y_first = swapped(y_one, y_two, "gy")

    entries = conv_source.shape[0]
    mark = (tall, lanes)
    code, code_done = call(
        lambda *refs: conversions(*refs, columns=bz),
        [(bx * by, bz), mark],
        cost=(40 * cells, 4 * cells),
    )(*(array.reshape(1, entries) for array in (conv_source, conv_kind, conv_direction)))
    code = code.reshape(box)

    pops, flow = call(
        moments,
        [(19, *box), (5, *box)],
        specs=[remote],
        scratch=[pltpu.SemaphoreType.DMA((bx,))],
        cost=(60 * cells, 150 * cells),
    )(pltpu.with_memory_space_constraint(populations, pltpu.HBM))

    columns, rows = ((24, bx * by), (10 * bx, bz))
    sides_y = [(bx, 8, bz), (bx, 8, bz), tile]
    inside, ends = ((bx - 2, *face), (2, *face))
    inner_post, inner_shift = call(
        collide_inner,
        [(19, *inside), (3, *inside)],
        scratch=sides_y,
        cost=(150 * cells, 150 * cells),
    )(pops, stretch, flow, z_first, *y_first)
    outer_post, outer_shift, z_out, x_one, x_two, y_one, y_two = call(
        collide_outer,
        [(19, *ends), (3, *ends), columns, (8, *face), (8, *face), rows, rows],
        scratch=[(4, *face), (4, *face)] + sides_y + [box],
        cost=(150 * cells, 150 * cells),
    )(pops, stretch, flags, flow, *first_x, *y_first, z_first, inner_post)
    z_post = both_ways(z_out, sides)
    post_y = swapped(y_one, y_two, "gy")
    post_x = swapped(x_one, x_two, "gx")
    edges = (4 * (bz // lanes) + columns[0], lanes)
    x_one, x_two, corner = call(
        lambda *refs: forward_edges(*refs, bx=bx), [edges, edges, columns]
    )(z_post, *post_y, code_done)
    corners = swapped(corner, corner, "gy")
    edges_x = swapped(x_one, x_two, "gx")

    rims = [(bx + 2, *face), (bx + 2, 16, bz), (bx + 2, 16, bz), (bx + 2, by, lanes)]
    posts = (inner_post, outer_post, inner_shift, outer_shift)
    inner, outer, totals, changes = call(
        stream_early,
        [(first_slanted, *inside), (first_slanted, *ends), box, box],
        scratch=rims,
        cost=(350 * cells, 200 * cells),
    )(*posts, flags, *post_y, z_post)
    (
        inner_slanted,
        outer_slanted,
        inner_settled,
        inner_excess,
        inner_heading,
        totals,
        changes,
    ) = call(
        stream_slanted,
        [(4, *inside), (4, *ends), inside, inside, inside, ends, ends],
        scratch=rims,
        cost=(100 * cells, 60 * cells),
    )(*posts, mass, flags, code, *post_y, z_post, *corners, totals, changes)
    new_stretch, inner_done = call(
        restretch_inner,
        [(6, *box), mark],
        out_specs=[remote, pl.BlockSpec()],
        scratch=[(6, *inside)] + sides_y + [pltpu.SemaphoreType.DMA],
        cost=(80 * cells, 40 * cells),
    )(stretch, flow, *post_y, z_post)
    late, outer_settled, spread, y_one, y_two, z_out = call(
        stream_late,
        [(5, *ends), ends, (bx + 2, *face), (8, bz), (8, bz), (16, bx * by)],
        scratch=rims + [(5, *face), (5, *face), box, box],
        cost=(150 * cells, 100 * cells),
    )(
        outer_post,
        outer_shift,
        mass,
        flags,
        code,
        totals,
        changes,
        *first_x,
        *post_x,
        *edges_x,
        inner_excess,
        inner_heading,
        inner_done,
    )
    z_last = both_ways(z_out, 8)
    last_y = swapped(y_one, y_two, "gy")
    last_corners = swapped(z_last, z_last, "gy")
    new_stretch, outer_done = call(
        restretch_outer,
        [(6, *box), mark],
        specs=[pl.BlockSpec()] * 7 + [remote, anywhere],
        out_specs=[remote, pl.BlockSpec()],
        scratch=[(6, *ends), (3, *face), (3, *face)]
        + sides_y
        + [pltpu.SemaphoreType.DMA((2,))],
        cost=(80 * cells, 40 * cells),
        aliases={7: 0},
    )(stretch, flow, *post_x, *post_y, z_post, new_stretch, outer_settled)
    x_one, x_two = call(add_faces, [face, face])(spread, z_last, *last_y, outer_done)
    last_x = swapped(x_one, x_two, "gx")
    (fresh,) = call(
        store,
        [(19, *box)],
        out_specs=[remote],
        scratch=[pltpu.SemaphoreType.DMA((32,))],
        cost=(0, 160 * cells),
    )(inner, outer, inner_slanted, outer_slanted, late)
    (new_mass,) = call(add_all, [box])(
        inner_settled, outer_settled, spread, z_last, *last_y, *last_corners, *last_x[::-1]
    )
    return (fresh, new_stretch, new_mass)


def solution(mesh):
    return jax.shard_map(
        shards,
        mesh=mesh,
        in_specs=(
            P(None, "gx", "gy", "gz"),
            P(None, "gx", "gy", "gz"),
            P("gx", "gy", "gz"),
            P("gx", "gy", "gz"),
            P(("gx", "gy", "gz")),
            P(("gx", "gy", "gz")),
            P(("gx", "gy", "gz")),
        ),
        out_specs=(P(None, "gx", "gy", "gz"), P(None, "gx", "gy", "gz"), P("gx", "gy", "gz")),
        check_vma=False,
    )
```

```python
import jax
import jax.numpy as jnp
from jax import lax
from jax.experimental import pallas as pl
from jax.experimental.pallas import tpu as pltpu
from jax.sharding import PartitionSpec as P

velocity_set = (
    (0, 0, 0),
    (1, 0, 0),
    (-1, 0, 0),
    (0, 1, 0),
    (0, -1, 0),
    (0, 0, 1),
    (0, 0, -1),
    (1, 1, 0),
    (-1, -1, 0),
    (1, -1, 0),
    (-1, 1, 0),
    (1, 0, 1),
    (-1, 0, -1),
    (1, 0, -1),
    (-1, 0, 1),
    (0, 1, 1),
    (0, -1, -1),
    (0, 1, -1),
    (0, -1, 1),
)
opposite_of = (0, 2, 1, 4, 3, 6, 5, 8, 7, 10, 9, 12, 11, 14, 13, 16, 15, 18, 17)
lattice_weights = (1.0 / 3.0,) + (1.0 / 18.0,) * 6 + (1.0 / 36.0,) * 12
symmetric_slot = ((0, 3, 4), (3, 1, 5), (4, 5, 2))
tensor_pairs = ((0, 0), (1, 1), (2, 2), (0, 1), (0, 2), (1, 2))
relax_time = 0.8
polymer_time = 8.0
polymer_coeff = 0.05


def moving(axis, sign):
    return tuple(index for index in range(19) if velocity_set[index][axis] == sign)


x_up, x_down = (moving(0, 1), moving(0, -1))
y_up, y_down = (moving(1, 1), moving(1, -1))
z_up, z_down = (moving(2, 1), moving(2, -1))
pairs = tuple(range(1, 19, 2))
gas_slot = 5
speed_slot = 6
edge_slot = 9
sides = 9
lanes = 128
tall = 8


def iota(shape, dim):
    return lax.broadcasted_iota(jnp.int32, shape, dim)


def wide(tile, width):
    return jnp.concatenate([tile] * (width // tile.shape[1]), axis=1)


def rows_of(load, chunk, chunks, step, edge):
    low = chunk * tall
    if step == 0:
        return load(low, low + tall)
    if step == 1 and chunk > 0:
        return load(low - 1, low + tall - 1)
    if step == -1 and chunk < chunks - 1:
        return load(low + 1, low + tall + 1)
    rows = load(low, low + tall)
    at = iota(rows.shape, 0)
    if step == 1:
        return jnp.where(at == 0, edge(), pltpu.roll(rows, 1, 0))
    return jnp.where(at == tall - 1, edge(), pltpu.roll(rows, tall - 1, 0))


def columns_of(rows, halo, lane, step):
    width = rows.shape[1]
    at = iota(rows.shape, 1)
    if step == 1:
        edge = wide(pltpu.roll(halo, (lanes - lane) % lanes, 1), width)
        return jnp.where(at == 0, edge, pltpu.roll(rows, 1, 1))
    edge = wide(pltpu.roll(halo, lanes - 1 - lane, 1), width)
    return jnp.where(at == width - 1, edge, pltpu.roll(rows, width - 1, 1))


def packed(high, low):
    at = iota(high[0].shape, 1)
    tile = jnp.zeros_like(high[0])
    for slot, part in enumerate(high):
        tile = jnp.where(at == slot, pltpu.roll(part, slot + 1, 1), tile)
    for place, part in enumerate(low):
        slot = len(high) + place
        tile = jnp.where(at == slot, pltpu.roll(part, slot, 1), tile)
    return tile


def along(index, vector):
    total = None
    for comp in range(3):
        sign = velocity_set[index][comp]
        if sign != 0:
            term = vector[comp] if sign > 0 else -vector[comp]
            total = term if total is None else total + term
    return total


def conversions(source, kind, heading, code, mark, *, columns):
    count = source.shape[1]
    value = (heading[...] + 32 * kind[...]).astype(jnp.float32)
    row, column = (source[...] // columns, source[...] % columns)
    by_row = jnp.where(iota((code.shape[0], count), 0) == row, value, 0.0).astype(jnp.bfloat16)
    by_column = jnp.where(iota((columns, count), 0) == column, 1.0, 0.0).astype(jnp.bfloat16)
    code[...] = lax.dot_general(
        by_row, by_column, (((1,), (1,)), ((), ())), preferred_element_type=jnp.float32
    )
    mark[...] = jnp.zeros(mark.shape, jnp.float32)


def odd(axis):
    return lax.rem(lax.axis_index(axis), 2) == 1


def select(chosen, first, second):
    return jnp.where(chosen, first[...], second[...])


def swap_rows(first, second, x, planes, high, low, flip):
    for slot, (top, bottom) in enumerate(zip(high, low)):
        by = top.shape[0]
        up, down = (top[by - 1 : by, :], bottom[0:1, :])
        at = slot * planes + x
        first[at : at + 1, :] = jnp.where(flip, down, up)
        second[at : at + 1, :] = jnp.where(flip, up, down)


def swapped_rows(first, second, slots, low_rows, high_rows, shift):
    flip = odd("gy")
    planes = low_rows.shape[0] - 2 * shift
    for x in range(planes):
        for place, slot in enumerate(slots):
            at = slot * planes + x
            one, two = (first[at : at + 1, :], second[at : at + 1, :])
            low_rows[x + shift, place : place + 1, :] = jnp.where(flip, one, two)
            high_rows[x + shift, place : place + 1, :] = jnp.where(flip, two, one)


def column_rows(tiles, count):
    return jnp.concatenate(tiles, axis=0).T[0:count, :]


def row_columns(rows):
    rest = jnp.zeros((lanes - rows.shape[0], rows.shape[1]), jnp.float32)
    return jnp.concatenate([rows, rest], axis=0).T


def first_faces(
    stretch_in,
    flags_in,
    stretch,
    flags,
    columns,
    y_first,
    y_second,
    x_first,
    x_second,
    sems,
):
    bx, by, bz = flags.shape
    flip_x, flip_y = (odd("gx"), odd("gy"))
    order = (0, bx - 1) + tuple(range(1, bx - 1))
    copies = {}
    for x in order:
        copies[x] = (
            pltpu.make_async_copy(stretch_in.at[:, x], stretch.at[:, x], sems.at[0, x]),
            pltpu.make_async_copy(flags_in.at[x], flags.at[x], sems.at[1, x]),
        )
        for copy in copies[x]:
            copy.start()
    for x in order[0:2]:
        for copy in copies[x]:
            copy.wait()
    for out, last in ((x_first, flip_x), (x_second, jnp.logical_not(flip_x))):
        for comp in range(3):
            slot = symmetric_slot[comp][0]
            out[comp] = jnp.where(last, stretch[slot, 0], stretch[slot, bx - 1])
        out[3] = jnp.where(jnp.where(last, flags[0], flags[bx - 1]) == 0, 1.0, 0.0)
    for x in order[2:]:
        for copy in copies[x]:
            copy.wait()
    tiles = []
    for x in range(bx):
        along_y = [stretch.at[symmetric_slot[comp][1], x] for comp in range(3)]
        swap_rows(y_first, y_second, x, bx, along_y, along_y, flip_y)
        fields = [stretch.at[symmetric_slot[comp][2], x] for comp in range(3)]
        tiles.append(
            packed(
                [field[:, bz - lanes : bz] for field in fields],
                [field[:, 0:lanes] for field in fields],
            )
        )
    columns[...] = column_rows(tiles, columns.shape[0])
    rest = y_first.shape[0] - 3 * bx
    y_first[3 * bx :, :] = jnp.zeros((rest, bz), jnp.float32)
    y_second[3 * bx :, :] = jnp.zeros((rest, bz), jnp.float32)


def moments(pops_in, pops, flow, sems):
    bx, by = pops.shape[1:3]
    copies = [
        pltpu.make_async_copy(pops_in.at[:, x], pops.at[:, x], sems.at[x]) for x in range(bx)
    ]
    for copy in copies:
        copy.start()
    for x in range(bx):
        copies[x].wait()
        for chunk in range(by // tall):
            rows = pl.ds(chunk * tall, tall)
            part = [pops[index, x, rows, :] for index in range(19)]
            density = part[0]
            for index in range(1, 19):
                density = density + part[index]
            inverse = 1.0 / density
            for comp in range(3):
                total = None
                for index in pairs:
                    sign = velocity_set[index][comp]
                    if sign != 0:
                        term = part[index] - part[index + 1]
                        term = term if sign > 0 else -term
                        total = term if total is None else total + term
                flow[comp, x, rows, :] = total * inverse
            flow[3, x, rows, :] = density
            flow[4, x, rows, :] = inverse


def beside(ref, field, x, step, halo, slot):
    last = ref.shape[1] - 1
    if halo is None:
        return lambda low, high: ref[field, x + step, low:high, :]
    if isinstance(x, int):
        if 0 <= x + step <= last:
            return lambda low, high: ref[field, x + step, low:high, :]
        return lambda low, high: halo[slot, low:high, :]
    inside = jnp.clip(x + step, 0, last)
    beyond = x == (0 if step < 0 else last)
    return lambda low, high: jnp.where(
        beyond, halo[slot, low:high, :], ref[field, inside, low:high, :]
    )


def differences(
    ref, field, slots, x, chunk, chunks, below, above, y_below, y_above, z_halo, lane, side
):
    slot_x, slot_y, slot_z = slots
    low, high = (chunk * tall, chunk * tall + tall)

    def load(first, stop):
        return ref[field, x, first:stop, :]

    result = [None, None, None]
    if slot_x is not None:
        after = beside(ref, field, x, 1, above, slot_x)(low, high)
        before = beside(ref, field, x, -1, below, slot_x)(low, high)
        result[0] = after - before
    if slot_y is not None:
        after = rows_of(load, chunk, chunks, -1, lambda: y_above[x, slot_y : slot_y + 1, :])
        before = rows_of(load, chunk, chunks, 1, lambda: y_below[x, slot_y : slot_y + 1, :])
        result[1] = after - before
    if slot_z is not None:
        rows, halo = (load(low, high), z_halo[x, low:high, :])
        after = columns_of(rows, halo, lane + side + slot_z, -1)
        before = columns_of(rows, halo, lane + slot_z, 1)
        result[2] = after - before
    return result


def end_place(x, bx):
    return 0 if x == 0 else 1


def plane_of(inner, outer, field, x, bx):
    if 0 < x < bx - 1:
        return inner.at[field, x - 1]
    return outer.at[field, end_place(x, bx)]


def collide_plane(x, place, pops, stretch, flow, halos, post, shift):
    by = pops.shape[2]
    chunks = by // tall
    factor = 1.0 - 0.5 / relax_time
    rate = 1.0 / relax_time
    for chunk in range(chunks):
        rows = pl.ds(chunk * tall, tall)
        terms = [[], [], []]
        for field in range(6):
            slots = [None, None, None]
            for comp in range(3):
                for axis in range(3):
                    if symmetric_slot[comp][axis] == field:
                        slots[axis] = comp
            found = differences(stretch, field, slots, x, chunk, chunks, *halos)
            for axis in range(3):
                if slots[axis] is not None:
                    terms[slots[axis]].append(found[axis])
        force = [0.5 * polymer_coeff * (part[0] + part[1] + part[2]) for part in terms]
        density, half = (flow[3, x, rows, :], 0.5 * flow[4, x, rows, :])
        moved = [flow[comp, x, rows, :] + half * force[comp] for comp in range(3)]
        for comp in range(3):
            shift[comp, place, rows, :] = moved[comp]
        squared = moved[0] * moved[0] + moved[1] * moved[1] + moved[2] * moved[2]
        work = moved[0] * force[0] + moved[1] * force[1] + moved[2] * force[2]
        weight = rate * density
        common = weight - 1.5 * weight * squared - 3.0 * factor * work
        odd = [3.0 * weight * moved[comp] + 3.0 * factor * force[comp] for comp in range(3)]
        even = [4.5 * weight * moved[comp] + 9.0 * factor * force[comp] for comp in range(3)]
        keep = 1.0 - rate
        post[0, place, rows, :] = keep * pops[0, x, rows, :] + lattice_weights[0] * common
        for index in pairs:
            both = common + along(index, moved) * along(index, even)
            differ = along(index, odd)
            scale = lattice_weights[index]
            post[index, place, rows, :] = keep * pops[index, x, rows, :] + scale * (both + differ)
            post[index + 1, place, rows, :] = keep * pops[index + 1, x, rows, :] + scale * (
                both - differ
            )


def collide_inner(
    pops,
    stretch,
    flow,
    z_rows,
    y_first,
    y_second,
    post,
    shift,
    y_below,
    y_above,
    z_halo,
):
    swapped_rows(y_first, y_second, range(3), y_below, y_above, 0)
    z_halo[...] = row_columns(z_rows[...]).reshape(z_halo.shape)
    halos = (None, None, y_below, y_above, z_halo, 0, 3)

    def plane(x, carry):
        collide_plane(x, x - 1, pops, stretch, flow, halos, post, shift)
        return carry

    lax.fori_loop(1, pops.shape[1] - 1, plane, 0)


def collide_outer(
    pops,
    stretch,
    flags,
    flow,
    x_first,
    x_second,
    y_first,
    y_second,
    z_rows,
    inner,
    post,
    shift,
    columns,
    ahead,
    behind,
    up_first,
    up_second,
    below,
    above,
    y_below,
    y_above,
    z_halo,
    gas,
):
    bx, by, bz = flags.shape
    halos = (below, above, y_below, y_above, z_halo, 0, 3)
    flip_x, flip_y = (odd("gx"), odd("gy"))
    below[...] = select(flip_x, x_first, x_second)
    above[...] = select(flip_x, x_second, x_first)
    swapped_rows(y_first, y_second, range(3), y_below, y_above, 0)
    z_halo[...] = row_columns(z_rows[...]).reshape(z_halo.shape)
    for x in (0, bx - 1):
        collide_plane(x, end_place(x, bx), pops, stretch, flow, halos, post, shift)

    tiles = []
    for x in range(bx):
        gas[x] = jnp.where(flags[x] == 0, 1.0, 0.0)
        rest = [gas.at[x]] + [flow.at[comp, x] for comp in range(3)]

        def fields(indices):
            return [plane_of(inner, post, index, x, bx) for index in indices] + rest

        swap_rows(up_first, up_second, x, bx, fields(y_up), fields(y_down), flip_y)
        tiles.append(
            packed(
                [field[:, bz - lanes : bz] for field in fields(z_up)],
                [field[:, 0:lanes] for field in fields(z_down)],
            )
        )
    columns[...] = column_rows(tiles, columns.shape[0])
    rest = up_first.shape[0] - sides * bx
    up_first[sides * bx :, :] = jnp.zeros((rest, bz), jnp.float32)
    up_second[sides * bx :, :] = jnp.zeros((rest, bz), jnp.float32)
    for slot in range(5):
        up, down = (post[x_up[slot], 1], post[x_down[slot], 0])
        ahead[slot] = jnp.where(flip_x, down, up)
        behind[slot] = jnp.where(flip_x, up, down)
    for comp in range(3):
        up, down = (flow[comp, bx - 1], flow[comp, 0])
        ahead[5 + comp] = jnp.where(flip_x, down, up)
        behind[5 + comp] = jnp.where(flip_x, up, down)


def restretch_plane(x, place, stretch, flow, halos, updated):
    chunks = stretch.shape[2] // tall
    for chunk in range(chunks):
        rows = pl.ds(chunk * tall, tall)
        grad = [
            differences(
                flow, comp, (comp, comp, comp), x, chunk, chunks, *halos, speed_slot, sides
            )
            for comp in range(3)
        ]
        part = [stretch[slot, x, rows, :] for slot in range(6)]
        full = [part[slot] + 1.0 if slot < 3 else part[slot] for slot in range(6)]

        def product(row, col):
            total = grad[row][0] * full[symmetric_slot[0][col]]
            for inner in (1, 2):
                total = total + grad[row][inner] * full[symmetric_slot[inner][col]]
            return total

        for slot, (row, col) in enumerate(tensor_pairs):
            old = (1.0 - 1.0 / polymer_time) * part[slot]
            if row == col:
                updated[slot, place, rows, :] = old + product(row, col)
            else:
                updated[slot, place, rows, :] = old + 0.5 * (product(row, col) + product(col, row))


def restretch_inner(
    stretch,
    flow,
    y_first,
    y_second,
    z_rows,
    new_stretch,
    mark,
    updated,
    y_below,
    y_above,
    z_halo,
    sem,
):
    bx = stretch.shape[1]
    swapped_rows(y_first, y_second, range(speed_slot, sides), y_below, y_above, 0)
    z_halo[...] = row_columns(z_rows[...]).reshape(z_halo.shape)
    halos = (None, None, y_below, y_above, z_halo)

    def plane(x, carry):
        restretch_plane(x, x - 1, stretch, flow, halos, updated)
        return carry

    lax.fori_loop(1, bx - 1, plane, 0)
    copy = pltpu.make_async_copy(updated, new_stretch.at[:, 1 : bx - 1], sem)
    copy.start()
    mark[...] = jnp.zeros(mark.shape, jnp.float32)
    copy.wait()


def restretch_outer(
    stretch,
    flow,
    x_first,
    x_second,
    y_first,
    y_second,
    z_rows,
    inner_stretch,
    after,
    new_stretch,
    mark,
    updated,
    below,
    above,
    y_below,
    y_above,
    z_halo,
    sems,
):
    bx = stretch.shape[1]
    flip_x = odd("gx")
    for comp in range(3):
        below[comp] = jnp.where(flip_x, x_first[5 + comp], x_second[5 + comp])
        above[comp] = jnp.where(flip_x, x_second[5 + comp], x_first[5 + comp])
    swapped_rows(y_first, y_second, range(speed_slot, sides), y_below, y_above, 0)
    z_halo[...] = row_columns(z_rows[...]).reshape(z_halo.shape)
    halos = (below, above, y_below, y_above, z_halo)
    copies = []
    for place, x in enumerate((0, bx - 1)):
        restretch_plane(x, place, stretch, flow, halos, updated)
        copies.append(
            pltpu.make_async_copy(updated.at[:, place], new_stretch.at[:, x], sems.at[place])
        )
        copies[-1].start()
    mark[...] = jnp.zeros(mark.shape, jnp.float32)
    for copy in copies:
        copy.wait()


def store(inner, outer, inner_slanted, outer_slanted, late, fresh, sems):
    bx = fresh.shape[1]
    moves = [
        (inner, fresh.at[0:first_slanted, 1 : bx - 1]),
        (inner_slanted, fresh.at[first_slanted:, 1 : bx - 1]),
    ]
    for place, x in enumerate((0, bx - 1)):
        moves.append((outer_slanted.at[:, place], fresh.at[first_slanted:, x]))
        order = (x_up, x_down)[place]
        start = 0
        for index in order + (first_slanted,):
            if index > start:
                run = slice(start, index)
                moves.append((outer.at[run, place], fresh.at[run, x]))
            if index in order:
                moves.append((late.at[order.index(index), place], fresh.at[index, x]))
            start = index + 1
    copies = [
        pltpu.make_async_copy(source, target, sems.at[place])
        for place, (source, target) in enumerate(moves)
    ]
    for copy in copies:
        copy.start()
    for copy in copies:
        copy.wait()


up_edges = ((0, y_up.index(7)), (0, gas_slot), (1, y_down.index(9)), (1, gas_slot))
down_edges = ((0, y_up.index(10)), (0, gas_slot), (1, y_down.index(8)), (1, gas_slot))


def forward_edges(z_rows, y_first, y_second, after, first_out, second_out, corner, *, bx):
    halves = y_first.shape[1] // lanes
    flip_x, flip_y = (odd("gx"), odd("gy"))
    for half in range(halves):
        cut = slice(half * lanes, half * lanes + lanes)
        for place in range(4):
            found = []
            for x, edges in ((bx - 1, up_edges), (0, down_edges)):
                side, slot = edges[place]
                row = slot * bx + x
                one = y_first[row : row + 1, cut]
                two = y_second[row : row + 1, cut]
                found.append(jnp.where(flip_y, one, two) if side == 0 else jnp.where(flip_y, two, one))
            at = half * 4 + place
            first_out[at : at + 1, :] = jnp.where(flip_x, found[1], found[0])
            second_out[at : at + 1, :] = jnp.where(flip_x, found[0], found[1])
    first_out[4 * halves :, :] = z_rows[...]
    second_out[4 * halves :, :] = z_rows[...]
    corner[...] = z_rows[...]


def own_halos(flags, y_first, y_second, z_rows, gas, low_rows, high_rows, columns):
    bx, by = flags.shape[:2]
    tile = row_columns(z_rows[...])
    swapped_rows(y_first, y_second, range(speed_slot), low_rows, high_rows, 1)
    for x in range(bx):
        gas[x + 1] = jnp.where(flags[x] == 0, 1.0, 0.0)
        columns[x + 1] = tile[x * by : x * by + by, :]


def own_corners(corner_first, corner_second, low_rows, high_rows):
    bx = low_rows.shape[0] - 2
    flip = odd("gy")
    corner_below = row_columns(select(flip, corner_first, corner_second))
    corner_above = row_columns(select(flip, corner_second, corner_first))
    by = corner_below.shape[0] // bx
    for x in range(bx):
        end = x * by + by - 1
        low_rows[x + 1, edge_slot : edge_slot + 1, 0:lanes] = corner_below[end : end + 1, :]
        high_rows[x + 1, edge_slot : edge_slot + 1, 0:lanes] = corner_above[
            x * by : x * by + 1, :
        ]


def pass_on(x, chunk, indices, source, leaving_of, speed, halos, fresh, place, total, change):
    gas, low_rows, high_rows, columns = halos
    by = gas.shape[1]
    chunks = by // tall
    rows = pl.ds(chunk * tall, tall)
    rest = 1.0 - 1.5 * (speed[0] * speed[0] + speed[1] * speed[1] + speed[2] * speed[2])
    equals = {}

    def moved(load, index, slot, lane):
        step_x, step_y, step_z = velocity_set[index]
        plane = x + 1 - step_x
        edges = low_rows if step_y == 1 else high_rows
        found = rows_of(load, chunk, chunks, step_y, lambda: edges[plane, slot : slot + 1, :])
        if step_z == 0:
            return found
        halo = rows_of(
            lambda low, high: columns[plane, low:high, :],
            chunk,
            chunks,
            step_y,
            lambda: edges[plane, edge_slot : edge_slot + 1, 0:lanes],
        )
        return columns_of(found, halo, lane, step_z)

    for index in indices:
        step_x, step_y, step_z = velocity_set[index]
        first = min(index, opposite_of[index])
        if first not in equals:
            proj = along(first, speed)
            equals[first] = 2.0 * lattice_weights[first] * (rest + 4.5 * proj * proj)
        slot, lane, gas_lane = (None, None, None)
        if step_y != 0:
            slot = (y_up if step_y == 1 else y_down).index(index)
        if step_z == 1:
            lane, gas_lane = (z_up.index(index), gas_slot)
        elif step_z == -1:
            lane, gas_lane = (sides + z_down.index(index), sides + gas_slot)
        field = source(index)
        marks = gas.at[x + 1 - step_x]
        arriving = moved(lambda low, high: field[low:high, :], index, slot, lane)
        from_gas = moved(lambda low, high: marks[low:high, :], index, gas_slot, gas_lane)
        leaving = leaving_of(opposite_of[index])[rows, :]
        open_side = from_gas > 0.5
        value = jnp.where(open_side, equals[first] - leaving, arriving)
        fresh(index)[place, rows, :] = value
        total = total + value
        change = change + jnp.where(open_side, 0.0, arriving - leaving)
    return total, change


def settle(x, rows, mass, flags, code, total, change):
    read = mass[x, rows, :] + jnp.where(flags[x, rows, :] == 1, change, 0.0)
    mark = code[x, rows, :]
    liquid = mark >= 32.0
    converts = mark > 0.0
    level = jnp.where(liquid, total, 0.0)
    excess = jnp.where(converts, read - level, 0.0)
    heading = jnp.where(liquid, mark - 32.0, mark)
    return jnp.where(converts, level, read), excess, heading


slanted = tuple(index for index in range(19) if velocity_set[index][1] * velocity_set[index][2])
first_slanted = slanted[0]


def from_inside(x, bx):
    found = [index for index in range(1, 19) if 0 <= x - velocity_set[index][0] < bx]
    return [index for index in found if index not in slanted]


def from_beyond(x, bx):
    return [index for index in range(1, 19) if not 0 <= x - velocity_set[index][0] < bx]


def stream_early(
    inner_post,
    outer_post,
    inner_shift,
    outer_shift,
    flags,
    y_first,
    y_second,
    z_rows,
    inner,
    outer,
    totals,
    changes,
    gas,
    low_rows,
    high_rows,
    columns,
):
    bx, by, bz = flags.shape
    halos = (gas, low_rows, high_rows, columns)
    own_halos(flags, y_first, y_second, z_rows, *halos)

    for x in range(bx):
        inside = 0 < x < bx - 1
        place = x - 1 if inside else end_place(x, bx)
        fresh = inner if inside else outer
        for chunk in range(by // tall):
            rows = pl.ds(chunk * tall, tall)
            total = plane_of(inner_post, outer_post, 0, x, bx)[rows, :]
            fresh[0, place, rows, :] = total
            total, change = pass_on(
                x,
                chunk,
                from_inside(x, bx),
                lambda index: plane_of(
                    inner_post, outer_post, index, x - velocity_set[index][0], bx
                ),
                lambda index: plane_of(inner_post, outer_post, index, x, bx),
                [plane_of(inner_shift, outer_shift, comp, x, bx)[rows, :] for comp in range(3)],
                halos,
                lambda index: fresh.at[index],
                place,
                total,
                jnp.zeros((tall, bz), jnp.float32),
            )
            totals[x, rows, :] = total
            changes[x, rows, :] = change


def stream_slanted(
    inner_post,
    outer_post,
    inner_shift,
    outer_shift,
    mass,
    flags,
    code,
    y_first,
    y_second,
    z_rows,
    corner_first,
    corner_second,
    totals,
    changes,
    inner,
    outer,
    settled,
    excess,
    heading,
    end_totals,
    end_changes,
    gas,
    low_rows,
    high_rows,
    columns,
):
    bx, by, bz = flags.shape
    halos = (gas, low_rows, high_rows, columns)
    own_halos(flags, y_first, y_second, z_rows, *halos)
    own_corners(corner_first, corner_second, low_rows, high_rows)

    for x in range(bx):
        inside = 0 < x < bx - 1
        place = x - 1 if inside else end_place(x, bx)
        fresh = inner if inside else outer
        for chunk in range(by // tall):
            rows = pl.ds(chunk * tall, tall)
            total, change = pass_on(
                x,
                chunk,
                slanted,
                lambda index: plane_of(inner_post, outer_post, index, x, bx),
                lambda index: plane_of(inner_post, outer_post, index, x, bx),
                [plane_of(inner_shift, outer_shift, comp, x, bx)[rows, :] for comp in range(3)],
                halos,
                lambda index: fresh.at[index - first_slanted],
                place,
                totals[x, rows, :],
                changes[x, rows, :],
            )
            if inside:
                now = settle(x, rows, mass, flags, code, total, change)
                settled[place, rows, :], excess[place, rows, :], heading[place, rows, :] = now
            else:
                end_totals[place, rows, :] = total
                end_changes[place, rows, :] = change


def stream_late(
    post,
    shift,
    mass,
    flags,
    code,
    totals,
    changes,
    gas_first,
    gas_second,
    x_first,
    x_second,
    edges_first,
    edges_second,
    inner_excess,
    inner_heading,
    after,
    late,
    settled,
    spread,
    line_first,
    line_second,
    out_z,
    gas,
    low_rows,
    high_rows,
    columns,
    below,
    above,
    excess,
    heading,
):
    bx, by, bz = flags.shape
    halves = bz // lanes
    flip_x = odd("gx")
    halos = (gas, low_rows, high_rows, columns)

    for slot in range(5):
        below[slot] = jnp.where(flip_x, x_first[slot], x_second[slot])
        above[slot] = jnp.where(flip_x, x_second[slot], x_first[slot])
    gas[0] = jnp.where(flip_x, gas_first[3], gas_second[3])
    gas[bx + 1] = jnp.where(flip_x, gas_second[3], gas_first[3])
    edges_below = select(flip_x, edges_first, edges_second)
    edges_above = select(flip_x, edges_second, edges_first)
    for found, at, x, edges in (
        (edges_below, 0, bx - 1, up_edges),
        (edges_above, bx + 1, 0, down_edges),
    ):
        for place, (side, slot) in enumerate(edges):
            line = jnp.concatenate(
                [found[half * 4 + place : half * 4 + place + 1, :] for half in range(halves)],
                axis=1,
            )
            (low_rows, high_rows)[side][at, slot : slot + 1, :] = line
        columns[at] = row_columns(found[4 * halves :, :])[x * by : x * by + by, :]
    for place, x in enumerate((0, bx - 1)):
        halo, order = ((below, x_up), (above, x_down))[place]
        for chunk in range(by // tall):
            rows = pl.ds(chunk * tall, tall)
            total, change = pass_on(
                x,
                chunk,
                from_beyond(x, bx),
                lambda index: halo.at[order.index(index)],
                lambda index: post.at[index, place],
                [shift[comp, place, rows, :] for comp in range(3)],
                halos,
                lambda index: late.at[order.index(index)],
                place,
                totals[place, rows, :],
                changes[place, rows, :],
            )
            now = settle(x, rows, mass, flags, code, total, change)
            settled[place, rows, :], excess[x, rows, :], heading[x, rows, :] = now
    for x in range(1, bx - 1):
        excess[x] = inner_excess[x - 1]
        heading[x] = inner_heading[x - 1]

    row_at, lane_at = (iota((by, bz), 0), iota((by, bz), 1))
    line_at = iota((1, bz), 1)
    tile_lane, line_lane = (iota((by, lanes), 1), iota((1, lanes), 1))

    def rows_up(rows):
        return jnp.where(row_at == 0, 0.0, pltpu.roll(rows, 1, 0))

    def rows_down(rows):
        return jnp.where(row_at == by - 1, 0.0, pltpu.roll(rows, by - 1, 0))

    def over(rows, at, step):
        if step == 1:
            return jnp.where(at == 0, 0.0, pltpu.roll(rows, 1, 1))
        return jnp.where(at == bz - 1, 0.0, pltpu.roll(rows, bz - 1, 1))

    def summed(parts):
        total = parts[0]
        for part in parts[1:]:
            total = total + part
        return total

    tile = jnp.zeros((by, lanes), jnp.float32)
    line_up = jnp.zeros((1, lanes), jnp.float32)
    line_down = jnp.zeros((1, lanes), jnp.float32)
    flip_y = odd("gy")
    line_first[...] = jnp.zeros(line_first.shape, jnp.float32)
    line_second[...] = jnp.zeros(line_second.shape, jnp.float32)
    for target in range(bx + 2):
        groups = {}
        for index in range(1, 19):
            step_x, step_y, step_z = velocity_set[index]
            x = target - 1 - step_x
            if 0 <= x < bx:
                part = jnp.where(heading[x] == float(index), excess[x], 0.0)
                groups.setdefault((step_y, step_z), []).append(part)
        groups = {key: summed(parts) for key, parts in groups.items()}
        total = jnp.zeros((by, bz), jnp.float32)
        line = {1: jnp.zeros((1, bz), jnp.float32), -1: jnp.zeros((1, bz), jnp.float32)}
        for step_z in (0, 1, -1):
            group = jnp.zeros((by, bz), jnp.float32)
            ends = {}
            if (0, step_z) in groups:
                group = group + groups[(0, step_z)]
            if (1, step_z) in groups:
                group = group + rows_up(groups[(1, step_z)])
                ends[1] = groups[(1, step_z)][by - 1 : by, :]
            if (-1, step_z) in groups:
                group = group + rows_down(groups[(-1, step_z)])
                ends[-1] = groups[(-1, step_z)][0:1, :]
            if step_z == 0:
                total = total + group
                for side in ends:
                    line[side] = line[side] + ends[side]
                continue
            total = total + over(group, lane_at, step_z)
            for side in ends:
                line[side] = line[side] + over(ends[side], line_at, step_z)
            if step_z == 1:
                spot, cut, roll = (target, slice(bz - lanes, bz), target + 1)
            else:
                spot, cut, roll = (8 + target, slice(0, lanes), 8 + target)
            tile = jnp.where(tile_lane == spot, pltpu.roll(group[:, cut], roll, 1), tile)
            if 1 in ends:
                line_up = jnp.where(
                    line_lane == spot, pltpu.roll(ends[1][:, cut], roll, 1), line_up
                )
            if -1 in ends:
                line_down = jnp.where(
                    line_lane == spot, pltpu.roll(ends[-1][:, cut], roll, 1), line_down
                )
        spread[target] = total
        line_first[target : target + 1, :] = jnp.where(flip_y, line[-1], line[1])
        line_second[target : target + 1, :] = jnp.where(flip_y, line[1], line[-1])
    rest = jnp.zeros((lanes - by - 2, lanes), jnp.float32)
    out_z[...] = column_rows([tile, line_up, line_down, rest], 16)


def with_edges(total, target, tile, y_below, y_above):
    by, bz = total.shape
    row_at, lane_at = (iota((by, bz), 0), iota((by, bz), 1))
    total = total + jnp.where(lane_at == 0, tile[0:by, target : target + 1], 0.0)
    total = total + jnp.where(lane_at == bz - 1, tile[0:by, 8 + target : 9 + target], 0.0)
    total = total + jnp.where(row_at == 0, y_below[target : target + 1, :], 0.0)
    return total + jnp.where(row_at == by - 1, y_above[target : target + 1, :], 0.0)


def add_faces(spread, z_rows, y_first, y_second, after, first, second):
    last = spread.shape[0] - 1
    flip_x, flip_y = (odd("gx"), odd("gy"))
    tile = row_columns(z_rows[...])
    y_below, y_above = (select(flip_y, y_first, y_second), select(flip_y, y_second, y_first))
    up = with_edges(spread[last], last, tile, y_below, y_above)
    down = with_edges(spread[0], 0, tile, y_below, y_above)
    first[...] = jnp.where(flip_x, down, up)
    second[...] = jnp.where(flip_x, up, down)


def add_sides(inner_settled, outer_settled, spread, z_rows, y_first, y_second, summed):
    bx = summed.shape[0]
    flip = odd("gy")
    tile = row_columns(z_rows[...])
    sides_y = (select(flip, y_first, y_second), select(flip, y_second, y_first))
    for x in range(bx):
        inside = 0 < x < bx - 1
        own = inner_settled[x - 1] if inside else outer_settled[end_place(x, bx)]
        summed[x] = own + with_edges(spread[x + 1], x + 1, tile, *sides_y)


def add_last(summed, corner_first, corner_second, x_second, x_first, new_mass, total, sems):
    bx, by, bz = new_mass.shape
    flip_x, flip_y = (odd("gx"), odd("gy"))
    at = iota((8, bz), 1)
    edges = []
    for side, corner in (
        (0, select(flip_y, corner_first, corner_second)),
        (1, select(flip_y, corner_second, corner_first)),
    ):
        edge = corner[:, by + side : by + side + 1]
        edges.append(
            jnp.where(at == 0, edge[0:8, :], 0.0) + jnp.where(at == bz - 1, edge[8:16, :], 0.0)
        )
    copies = []
    for x in range(bx):
        now = summed[x]
        if x == 0:
            now = now + select(flip_x, x_first, x_second)
        if x == bx - 1:
            now = now + select(flip_x, x_second, x_first)
        total[x] = now
        for row, edge in ((0, edges[0]), (by - 1, edges[1])):
            total[x, row : row + 1, :] = now[row : row + 1, :] + edge[x + 1 : x + 2, :]
        copies.append(pltpu.make_async_copy(total.at[x], new_mass.at[x], sems.at[x]))
        copies[-1].start()
    for copy in copies:
        copy.wait()


def swapped(first, second, axis):
    devices = lax.axis_size(axis)
    ahead = [(i, (i + 1) % devices if i % 2 == 0 else i - 1) for i in range(devices)]
    behind = [(i, (i - 1) % devices if i % 2 == 0 else (i + 1) % devices) for i in range(devices)]
    return lax.ppermute(first, axis, ahead), lax.ppermute(second, axis, behind)


def both_ways(rows, lower):
    devices = lax.axis_size("gz")
    before = lax.ppermute(rows, "gz", [(i, (i + 1) % devices) for i in range(devices)])
    if devices == 2:
        return before
    after = lax.ppermute(rows, "gz", [(i, (i - 1) % devices) for i in range(devices)])
    return jnp.where(iota(rows.shape, 0) < lower, before, after)


remote = pl.BlockSpec(memory_space=pltpu.HBM)
anywhere = pl.BlockSpec(memory_space=pl.ANY)


def call(body, outs, specs=None, out_specs=None, scratch=(), cost=(0, 0), aliases=None):
    extra = {} if specs is None else {"in_specs": specs}
    if out_specs is not None:
        extra["out_specs"] = out_specs
    return pl.pallas_call(
        body,
        out_shape=[
            shape
            if isinstance(shape, jax.ShapeDtypeStruct)
            else jax.ShapeDtypeStruct(shape, jnp.float32)
            for shape in outs
        ],
        scratch_shapes=[
            pltpu.VMEM(shape, jnp.float32) if isinstance(shape, tuple) else shape
            for shape in scratch
        ],
        compiler_params=pltpu.CompilerParams(vmem_limit_bytes=40 * 1024 * 1024),
        input_output_aliases=aliases or {},
        cost_estimate=pl.CostEstimate(flops=cost[0], bytes_accessed=cost[1], transcendentals=0),
        **extra,
    )


def shards(populations, stretch, mass, flags, conv_source, conv_kind, conv_direction):
    bx, by, bz = flags.shape
    cells = bx * by * bz
    box, face, tile = ((bx, by, bz), (by, bz), (bx, by, lanes))

    stretch, flags, z_out, y_one, y_two, x_one, x_two = call(
        first_faces,
        [
            (6, *box),
            jax.ShapeDtypeStruct(box, jnp.int32),
            (8, bx * by),
            (4 * bx, bz),
            (4 * bx, bz),
            (4, *face),
            (4, *face),
        ],
        specs=[remote] * 2,
        scratch=[pltpu.SemaphoreType.DMA((2, bx))],
        cost=(10 * cells, 60 * cells),
    )(*(pltpu.with_memory_space_constraint(array, pltpu.HBM) for array in (stretch, flags)))
    first_x = swapped(x_one, x_two, "gx")
    z_first = both_ways(z_out, 3)
    y_first = swapped(y_one, y_two, "gy")

    entries = conv_source.shape[0]
    mark = (tall, lanes)
    code, code_done = call(
        lambda *refs: conversions(*refs, columns=bz),
        [(bx * by, bz), mark],
        cost=(40 * cells, 4 * cells),
    )(*(array.reshape(1, entries) for array in (conv_source, conv_kind, conv_direction)))
    code = code.reshape(box)

    pops, flow = call(
        moments,
        [(19, *box), (5, *box)],
        specs=[remote],
        scratch=[pltpu.SemaphoreType.DMA((bx,))],
        cost=(60 * cells, 150 * cells),
    )(pltpu.with_memory_space_constraint(populations, pltpu.HBM))

    columns, rows = ((24, bx * by), (10 * bx, bz))
    sides_y = [(bx, 8, bz), (bx, 8, bz), tile]
    inside, ends = ((bx - 2, *face), (2, *face))
    inner_post, inner_shift = call(
        collide_inner,
        [(19, *inside), (3, *inside)],
        scratch=sides_y,
        cost=(150 * cells, 150 * cells),
    )(pops, stretch, flow, z_first, *y_first)
    outer_post, outer_shift, z_out, x_one, x_two, y_one, y_two = call(
        collide_outer,
        [(19, *ends), (3, *ends), columns, (8, *face), (8, *face), rows, rows],
        scratch=[(4, *face), (4, *face)] + sides_y + [box],
        cost=(150 * cells, 150 * cells),
    )(pops, stretch, flags, flow, *first_x, *y_first, z_first, inner_post)
    z_post = both_ways(z_out, sides)
    post_y = swapped(y_one, y_two, "gy")
    post_x = swapped(x_one, x_two, "gx")
    edges = (4 * (bz // lanes) + columns[0], lanes)
    x_one, x_two, corner = call(
        lambda *refs: forward_edges(*refs, bx=bx), [edges, edges, columns]
    )(z_post, *post_y, code_done)
    corners = swapped(corner, corner, "gy")
    edges_x = swapped(x_one, x_two, "gx")

    rims = [(bx + 2, *face), (bx + 2, 16, bz), (bx + 2, 16, bz), (bx + 2, by, lanes)]
    posts = (inner_post, outer_post, inner_shift, outer_shift)
    inner, outer, totals, changes = call(
        stream_early,
        [(first_slanted, *inside), (first_slanted, *ends), box, box],
        scratch=rims,
        cost=(350 * cells, 200 * cells),
    )(*posts, flags, *post_y, z_post)
    (
        inner_slanted,
        outer_slanted,
        inner_settled,
        inner_excess,
        inner_heading,
        totals,
        changes,
    ) = call(
        stream_slanted,
        [(4, *inside), (4, *ends), inside, inside, inside, ends, ends],
        scratch=rims,
        cost=(100 * cells, 60 * cells),
    )(*posts, mass, flags, code, *post_y, z_post, *corners, totals, changes)
    new_stretch, inner_done = call(
        restretch_inner,
        [(6, *box), mark],
        out_specs=[remote, pl.BlockSpec()],
        scratch=[(6, *inside)] + sides_y + [pltpu.SemaphoreType.DMA],
        cost=(80 * cells, 40 * cells),
    )(stretch, flow, *post_y, z_post)
    late, outer_settled, spread, y_one, y_two, z_out = call(
        stream_late,
        [(5, *ends), ends, (bx + 2, *face), (8, bz), (8, bz), (16, bx * by)],
        scratch=rims + [(5, *face), (5, *face), box, box],
        cost=(150 * cells, 100 * cells),
    )(
        outer_post,
        outer_shift,
        mass,
        flags,
        code,
        totals,
        changes,
        *first_x,
        *post_x,
        *edges_x,
        inner_excess,
        inner_heading,
        inner_done,
    )
    z_last = both_ways(z_out, 8)
    last_y = swapped(y_one, y_two, "gy")
    last_corners = swapped(z_last, z_last, "gy")
    new_stretch, outer_done = call(
        restretch_outer,
        [(6, *box), mark],
        specs=[pl.BlockSpec()] * 7 + [remote, anywhere],
        out_specs=[remote, pl.BlockSpec()],
        scratch=[(6, *ends), (3, *face), (3, *face)]
        + sides_y
        + [pltpu.SemaphoreType.DMA((2,))],
        cost=(80 * cells, 40 * cells),
        aliases={7: 0},
    )(stretch, flow, *post_x, *post_y, z_post, new_stretch, outer_settled)
    x_one, x_two = call(add_faces, [face, face])(spread, z_last, *last_y, outer_done)
    last_x = swapped(x_one, x_two, "gx")
    (fresh,) = call(
        store,
        [(19, *box)],
        out_specs=[remote],
        scratch=[pltpu.SemaphoreType.DMA((32,))],
        cost=(0, 160 * cells),
    )(inner, outer, inner_slanted, outer_slanted, late)
    (summed,) = call(add_sides, [box], cost=(10 * cells, 12 * cells))(
        inner_settled, outer_settled, spread, z_last, *last_y
    )
    (new_mass,) = call(
        add_last,
        [box],
        out_specs=[remote],
        scratch=[box, pltpu.SemaphoreType.DMA((bx,))],
    )(summed, *last_corners, *last_x[::-1])
    return (fresh, new_stretch, new_mass)


def solution(mesh):
    return jax.shard_map(
        shards,
        mesh=mesh,
        in_specs=(
            P(None, "gx", "gy", "gz"),
            P(None, "gx", "gy", "gz"),
            P("gx", "gy", "gz"),
            P("gx", "gy", "gz"),
            P(("gx", "gy", "gz")),
            P(("gx", "gy", "gz")),
            P(("gx", "gy", "gz")),
        ),
        out_specs=(P(None, "gx", "gy", "gz"), P(None, "gx", "gy", "gz"), P("gx", "gy", "gz")),
        check_vma=False,
    )
```

```python
import jax
import jax.numpy as jnp
from jax import lax
from jax.experimental import pallas as pl
from jax.experimental.pallas import tpu as pltpu
from jax.sharding import PartitionSpec as P

velocity_set = (
    (0, 0, 0),
    (1, 0, 0),
    (-1, 0, 0),
    (0, 1, 0),
    (0, -1, 0),
    (0, 0, 1),
    (0, 0, -1),
    (1, 1, 0),
    (-1, -1, 0),
    (1, -1, 0),
    (-1, 1, 0),
    (1, 0, 1),
    (-1, 0, -1),
    (1, 0, -1),
    (-1, 0, 1),
    (0, 1, 1),
    (0, -1, -1),
    (0, 1, -1),
    (0, -1, 1),
)
opposite_of = (0, 2, 1, 4, 3, 6, 5, 8, 7, 10, 9, 12, 11, 14, 13, 16, 15, 18, 17)
lattice_weights = (1.0 / 3.0,) + (1.0 / 18.0,) * 6 + (1.0 / 36.0,) * 12
symmetric_slot = ((0, 3, 4), (3, 1, 5), (4, 5, 2))
tensor_pairs = ((0, 0), (1, 1), (2, 2), (0, 1), (0, 2), (1, 2))
relax_time = 0.8
polymer_time = 8.0
polymer_coeff = 0.05


def moving(axis, sign):
    return tuple(index for index in range(19) if velocity_set[index][axis] == sign)


x_up, x_down = (moving(0, 1), moving(0, -1))
y_up, y_down = (moving(1, 1), moving(1, -1))
z_up, z_down = (moving(2, 1), moving(2, -1))
pairs = tuple(range(1, 19, 2))
gas_slot = 5
speed_slot = 6
edge_slot = 9
sides = 9
lanes = 128
tall = 8


def iota(shape, dim):
    return lax.broadcasted_iota(jnp.int32, shape, dim)


def wide(tile, width):
    return jnp.concatenate([tile] * (width // tile.shape[1]), axis=1)


def rows_of(load, chunk, chunks, step, edge):
    low = chunk * tall
    if step == 0:
        return load(low, low + tall)
    if step == 1 and chunk > 0:
        return load(low - 1, low + tall - 1)
    if step == -1 and chunk < chunks - 1:
        return load(low + 1, low + tall + 1)
    rows = load(low, low + tall)
    at = iota(rows.shape, 0)
    if step == 1:
        return jnp.where(at == 0, edge(), pltpu.roll(rows, 1, 0))
    return jnp.where(at == tall - 1, edge(), pltpu.roll(rows, tall - 1, 0))


def columns_of(rows, halo, lane, step):
    width = rows.shape[1]
    at = iota(rows.shape, 1)
    if step == 1:
        edge = wide(pltpu.roll(halo, (lanes - lane) % lanes, 1), width)
        return jnp.where(at == 0, edge, pltpu.roll(rows, 1, 1))
    edge = wide(pltpu.roll(halo, lanes - 1 - lane, 1), width)
    return jnp.where(at == width - 1, edge, pltpu.roll(rows, width - 1, 1))


def packed(high, low):
    at = iota(high[0].shape, 1)
    tile = jnp.zeros_like(high[0])
    for slot, part in enumerate(high):
        tile = jnp.where(at == slot, pltpu.roll(part, slot + 1, 1), tile)
    for place, part in enumerate(low):
        slot = len(high) + place
        tile = jnp.where(at == slot, pltpu.roll(part, slot, 1), tile)
    return tile


def along(index, vector):
    total = None
    for comp in range(3):
        sign = velocity_set[index][comp]
        if sign != 0:
            term = vector[comp] if sign > 0 else -vector[comp]
            total = term if total is None else total + term
    return total


def conversions(source, kind, heading, code, *, columns):
    count = source.shape[1]
    value = (heading[...] + 32 * kind[...]).astype(jnp.float32)
    row, column = (source[...] // columns, source[...] % columns)
    by_row = jnp.where(iota((code.shape[0], count), 0) == row, value, 0.0).astype(jnp.bfloat16)
    by_column = jnp.where(iota((columns, count), 0) == column, 1.0, 0.0).astype(jnp.bfloat16)
    code[...] = lax.dot_general(
        by_row, by_column, (((1,), (1,)), ((), ())), preferred_element_type=jnp.float32
    )


def odd(axis):
    return lax.rem(lax.axis_index(axis), 2) == 1


def select(chosen, first, second):
    return jnp.where(chosen, first[...], second[...])


def swap_rows(first, second, x, planes, high, low, flip):
    for slot, (top, bottom) in enumerate(zip(high, low)):
        by = top.shape[0]
        up, down = (top[by - 1 : by, :], bottom[0:1, :])
        at = slot * planes + x
        first[at : at + 1, :] = jnp.where(flip, down, up)
        second[at : at + 1, :] = jnp.where(flip, up, down)


def swapped_rows(first, second, slots, low_rows, high_rows, shift):
    flip = odd("gy")
    planes = low_rows.shape[0] - 2 * shift
    for x in range(planes):
        for place, slot in enumerate(slots):
            at = slot * planes + x
            one, two = (first[at : at + 1, :], second[at : at + 1, :])
            low_rows[x + shift, place : place + 1, :] = jnp.where(flip, one, two)
            high_rows[x + shift, place : place + 1, :] = jnp.where(flip, two, one)


def column_rows(tiles, count):
    return jnp.concatenate(tiles, axis=0).T[0:count, :]


def row_columns(rows):
    rest = jnp.zeros((lanes - rows.shape[0], rows.shape[1]), jnp.float32)
    return jnp.concatenate([rows, rest], axis=0).T


def first_faces(
    stretch_in,
    flags_in,
    stretch,
    flags,
    columns,
    y_first,
    y_second,
    x_first,
    x_second,
    sems,
):
    bx, by, bz = flags.shape
    flip_x, flip_y = (odd("gx"), odd("gy"))
    copies = [
        pltpu.make_async_copy(stretch_in, stretch, sems.at[0]),
        pltpu.make_async_copy(flags_in, flags, sems.at[1]),
    ]
    for copy in copies:
        copy.start()
    for copy in copies:
        copy.wait()
    tiles = []
    for x in range(bx):
        along_y = [stretch.at[symmetric_slot[comp][1], x] for comp in range(3)]
        swap_rows(y_first, y_second, x, bx, along_y, along_y, flip_y)
        fields = [stretch.at[symmetric_slot[comp][2], x] for comp in range(3)]
        tiles.append(
            packed(
                [field[:, bz - lanes : bz] for field in fields],
                [field[:, 0:lanes] for field in fields],
            )
        )
    columns[...] = column_rows(tiles, columns.shape[0])
    rest = y_first.shape[0] - 3 * bx
    y_first[3 * bx :, :] = jnp.zeros((rest, bz), jnp.float32)
    y_second[3 * bx :, :] = jnp.zeros((rest, bz), jnp.float32)
    for out, last in ((x_first, flip_x), (x_second, jnp.logical_not(flip_x))):
        for comp in range(3):
            slot = symmetric_slot[comp][0]
            out[comp] = jnp.where(last, stretch[slot, 0], stretch[slot, bx - 1])
        out[3] = jnp.where(jnp.where(last, flags[0], flags[bx - 1]) == 0, 1.0, 0.0)


def moments(pops_in, pops, flow, sems):
    bx, by = pops.shape[1:3]
    copies = [
        pltpu.make_async_copy(pops_in.at[:, x], pops.at[:, x], sems.at[x]) for x in range(bx)
    ]
    for copy in copies:
        copy.start()
    for x in range(bx):
        copies[x].wait()
        for chunk in range(by // tall):
            rows = pl.ds(chunk * tall, tall)
            part = [pops[index, x, rows, :] for index in range(19)]
            density = part[0]
            for index in range(1, 19):
                density = density + part[index]
            inverse = 1.0 / density
            for comp in range(3):
                total = None
                for index in pairs:
                    sign = velocity_set[index][comp]
                    if sign != 0:
                        term = part[index] - part[index + 1]
                        term = term if sign > 0 else -term
                        total = term if total is None else total + term
                flow[comp, x, rows, :] = total * inverse
            flow[3, x, rows, :] = density
            flow[4, x, rows, :] = inverse


def beside(ref, field, x, step, halo, slot):
    last = ref.shape[1] - 1
    if halo is None:
        return lambda low, high: ref[field, x + step, low:high, :]
    if isinstance(x, int):
        if 0 <= x + step <= last:
            return lambda low, high: ref[field, x + step, low:high, :]
        return lambda low, high: halo[slot, low:high, :]
    inside = jnp.clip(x + step, 0, last)
    beyond = x == (0 if step < 0 else last)
    return lambda low, high: jnp.where(
        beyond, halo[slot, low:high, :], ref[field, inside, low:high, :]
    )


def differences(
    ref, field, slots, x, chunk, chunks, below, above, y_below, y_above, z_halo, lane, side
):
    slot_x, slot_y, slot_z = slots
    low, high = (chunk * tall, chunk * tall + tall)

    def load(first, stop):
        return ref[field, x, first:stop, :]

    result = [None, None, None]
    if slot_x is not None:
        after = beside(ref, field, x, 1, above, slot_x)(low, high)
        before = beside(ref, field, x, -1, below, slot_x)(low, high)
        result[0] = after - before
    if slot_y is not None:
        after = rows_of(load, chunk, chunks, -1, lambda: y_above[x, slot_y : slot_y + 1, :])
        before = rows_of(load, chunk, chunks, 1, lambda: y_below[x, slot_y : slot_y + 1, :])
        result[1] = after - before
    if slot_z is not None:
        rows, halo = (load(low, high), z_halo[x, low:high, :])
        after = columns_of(rows, halo, lane + side + slot_z, -1)
        before = columns_of(rows, halo, lane + slot_z, 1)
        result[2] = after - before
    return result


def end_place(x, bx):
    return 0 if x == 0 else 1


def plane_of(inner, outer, field, x, bx):
    if 0 < x < bx - 1:
        return inner.at[field, x - 1]
    return outer.at[field, end_place(x, bx)]


def collide_plane(x, place, pops, stretch, flow, halos, post, shift):
    by = pops.shape[2]
    chunks = by // tall
    factor = 1.0 - 0.5 / relax_time
    rate = 1.0 / relax_time
    for chunk in range(chunks):
        rows = pl.ds(chunk * tall, tall)
        terms = [[], [], []]
        for field in range(6):
            slots = [None, None, None]
            for comp in range(3):
                for axis in range(3):
                    if symmetric_slot[comp][axis] == field:
                        slots[axis] = comp
            found = differences(stretch, field, slots, x, chunk, chunks, *halos)
            for axis in range(3):
                if slots[axis] is not None:
                    terms[slots[axis]].append(found[axis])
        force = [0.5 * polymer_coeff * (part[0] + part[1] + part[2]) for part in terms]
        density, half = (flow[3, x, rows, :], 0.5 * flow[4, x, rows, :])
        moved = [flow[comp, x, rows, :] + half * force[comp] for comp in range(3)]
        for comp in range(3):
            shift[comp, place, rows, :] = moved[comp]
        squared = moved[0] * moved[0] + moved[1] * moved[1] + moved[2] * moved[2]
        work = moved[0] * force[0] + moved[1] * force[1] + moved[2] * force[2]
        weight = rate * density
        common = weight - 1.5 * weight * squared - 3.0 * factor * work
        odd = [3.0 * weight * moved[comp] + 3.0 * factor * force[comp] for comp in range(3)]
        even = [4.5 * weight * moved[comp] + 9.0 * factor * force[comp] for comp in range(3)]
        keep = 1.0 - rate
        post[0, place, rows, :] = keep * pops[0, x, rows, :] + lattice_weights[0] * common
        for index in pairs:
            both = common + along(index, moved) * along(index, even)
            differ = along(index, odd)
            scale = lattice_weights[index]
            post[index, place, rows, :] = keep * pops[index, x, rows, :] + scale * (both + differ)
            post[index + 1, place, rows, :] = keep * pops[index + 1, x, rows, :] + scale * (
                both - differ
            )


def collide_inner(
    pops,
    stretch,
    flow,
    z_rows,
    y_first,
    y_second,
    post,
    shift,
    y_below,
    y_above,
    z_halo,
):
    swapped_rows(y_first, y_second, range(3), y_below, y_above, 0)
    z_halo[...] = row_columns(z_rows[...]).reshape(z_halo.shape)
    halos = (None, None, y_below, y_above, z_halo, 0, 3)

    def plane(x, carry):
        collide_plane(x, x - 1, pops, stretch, flow, halos, post, shift)
        return carry

    lax.fori_loop(1, pops.shape[1] - 1, plane, 0)


def collide_outer(
    pops,
    stretch,
    flags,
    flow,
    x_first,
    x_second,
    y_first,
    y_second,
    z_rows,
    inner,
    post,
    shift,
    columns,
    ahead,
    behind,
    up_first,
    up_second,
    below,
    above,
    y_below,
    y_above,
    z_halo,
    gas,
):
    bx, by, bz = flags.shape
    halos = (below, above, y_below, y_above, z_halo, 0, 3)
    flip_x, flip_y = (odd("gx"), odd("gy"))
    below[...] = select(flip_x, x_first, x_second)
    above[...] = select(flip_x, x_second, x_first)
    swapped_rows(y_first, y_second, range(3), y_below, y_above, 0)
    z_halo[...] = row_columns(z_rows[...]).reshape(z_halo.shape)
    for x in (0, bx - 1):
        collide_plane(x, end_place(x, bx), pops, stretch, flow, halos, post, shift)

    tiles = []
    for x in range(bx):
        gas[x] = jnp.where(flags[x] == 0, 1.0, 0.0)
        rest = [gas.at[x]] + [flow.at[comp, x] for comp in range(3)]

        def fields(indices):
            return [plane_of(inner, post, index, x, bx) for index in indices] + rest

        swap_rows(up_first, up_second, x, bx, fields(y_up), fields(y_down), flip_y)
        tiles.append(
            packed(
                [field[:, bz - lanes : bz] for field in fields(z_up)],
                [field[:, 0:lanes] for field in fields(z_down)],
            )
        )
    columns[...] = column_rows(tiles, columns.shape[0])
    rest = up_first.shape[0] - sides * bx
    up_first[sides * bx :, :] = jnp.zeros((rest, bz), jnp.float32)
    up_second[sides * bx :, :] = jnp.zeros((rest, bz), jnp.float32)
    for slot in range(5):
        up, down = (post[x_up[slot], 1], post[x_down[slot], 0])
        ahead[slot] = jnp.where(flip_x, down, up)
        behind[slot] = jnp.where(flip_x, up, down)


def restretch_plane(x, place, stretch, flow, halos, updated):
    chunks = stretch.shape[2] // tall
    for chunk in range(chunks):
        rows = pl.ds(chunk * tall, tall)
        grad = [
            differences(
                flow, comp, (comp, comp, comp), x, chunk, chunks, *halos, speed_slot, sides
            )
            for comp in range(3)
        ]
        part = [stretch[slot, x, rows, :] for slot in range(6)]
        full = [part[slot] + 1.0 if slot < 3 else part[slot] for slot in range(6)]

        def product(row, col):
            total = grad[row][0] * full[symmetric_slot[0][col]]
            for inner in (1, 2):
                total = total + grad[row][inner] * full[symmetric_slot[inner][col]]
            return total

        for slot, (row, col) in enumerate(tensor_pairs):
            old = (1.0 - 1.0 / polymer_time) * part[slot]
            if row == col:
                updated[slot, place, rows, :] = old + product(row, col)
            else:
                updated[slot, place, rows, :] = old + 0.5 * (product(row, col) + product(col, row))


def restretch_inner(
    stretch,
    flow,
    y_first,
    y_second,
    z_rows,
    new_stretch,
    mark,
    updated,
    y_below,
    y_above,
    z_halo,
    sem,
):
    bx = stretch.shape[1]
    swapped_rows(y_first, y_second, range(speed_slot, sides), y_below, y_above, 0)
    z_halo[...] = row_columns(z_rows[...]).reshape(z_halo.shape)
    halos = (None, None, y_below, y_above, z_halo)

    def plane(x, carry):
        restretch_plane(x, x - 1, stretch, flow, halos, updated)
        return carry

    lax.fori_loop(1, bx - 1, plane, 0)
    copy = pltpu.make_async_copy(updated, new_stretch.at[:, 1 : bx - 1], sem)
    copy.start()
    mark[...] = jnp.zeros(mark.shape, jnp.float32)
    copy.wait()


def restretch_outer(
    stretch,
    flow,
    x_first,
    x_second,
    y_first,
    y_second,
    z_rows,
    inner_stretch,
    new_stretch,
    mark,
    updated,
    below,
    above,
    y_below,
    y_above,
    z_halo,
    sems,
):
    bx = stretch.shape[1]
    flip_x = odd("gx")
    for comp in range(3):
        below[comp] = jnp.where(flip_x, x_first[comp], x_second[comp])
        above[comp] = jnp.where(flip_x, x_second[comp], x_first[comp])
    swapped_rows(y_first, y_second, range(speed_slot, sides), y_below, y_above, 0)
    z_halo[...] = row_columns(z_rows[...]).reshape(z_halo.shape)
    halos = (below, above, y_below, y_above, z_halo)
    copies = []
    for place, x in enumerate((0, bx - 1)):
        restretch_plane(x, place, stretch, flow, halos, updated)
        copies.append(
            pltpu.make_async_copy(updated.at[:, place], new_stretch.at[:, x], sems.at[place])
        )
        copies[-1].start()
    mark[...] = jnp.zeros(mark.shape, jnp.float32)
    for copy in copies:
        copy.wait()


def store(inner, outer, inner_slanted, outer_slanted, late, fresh, sems):
    bx = fresh.shape[1]
    moves = [
        (inner, fresh.at[0:first_slanted, 1 : bx - 1]),
        (inner_slanted, fresh.at[first_slanted:, 1 : bx - 1]),
    ]
    for place, x in enumerate((0, bx - 1)):
        moves.append((outer_slanted.at[:, place], fresh.at[first_slanted:, x]))
        order = (x_up, x_down)[place]
        start = 0
        for index in order + (first_slanted,):
            if index > start:
                run = slice(start, index)
                moves.append((outer.at[run, place], fresh.at[run, x]))
            if index in order:
                moves.append((late.at[order.index(index), place], fresh.at[index, x]))
            start = index + 1
    copies = [
        pltpu.make_async_copy(source, target, sems.at[place])
        for place, (source, target) in enumerate(moves)
    ]
    for copy in copies:
        copy.start()
    for copy in copies:
        copy.wait()


up_edges = ((0, y_up.index(7)), (0, gas_slot), (1, y_down.index(9)), (1, gas_slot))
down_edges = ((0, y_up.index(10)), (0, gas_slot), (1, y_down.index(8)), (1, gas_slot))


def forward_edges(z_rows, y_first, y_second, first_out, second_out, corner, *, bx):
    halves = y_first.shape[1] // lanes
    flip_x, flip_y = (odd("gx"), odd("gy"))
    for half in range(halves):
        cut = slice(half * lanes, half * lanes + lanes)
        for place in range(4):
            found = []
            for x, edges in ((bx - 1, up_edges), (0, down_edges)):
                side, slot = edges[place]
                row = slot * bx + x
                one = y_first[row : row + 1, cut]
                two = y_second[row : row + 1, cut]
                found.append(jnp.where(flip_y, one, two) if side == 0 else jnp.where(flip_y, two, one))
            at = half * 4 + place
            first_out[at : at + 1, :] = jnp.where(flip_x, found[1], found[0])
            second_out[at : at + 1, :] = jnp.where(flip_x, found[0], found[1])
    first_out[4 * halves :, :] = z_rows[...]
    second_out[4 * halves :, :] = z_rows[...]
    corner[...] = z_rows[...]


def own_halos(flags, y_first, y_second, z_rows, gas, low_rows, high_rows, columns):
    bx, by = flags.shape[:2]
    tile = row_columns(z_rows[...])
    swapped_rows(y_first, y_second, range(speed_slot), low_rows, high_rows, 1)
    for x in range(bx):
        gas[x + 1] = jnp.where(flags[x] == 0, 1.0, 0.0)
        columns[x + 1] = tile[x * by : x * by + by, :]


def own_corners(corner_first, corner_second, low_rows, high_rows):
    bx = low_rows.shape[0] - 2
    flip = odd("gy")
    corner_below = row_columns(select(flip, corner_first, corner_second))
    corner_above = row_columns(select(flip, corner_second, corner_first))
    by = corner_below.shape[0] // bx
    for x in range(bx):
        end = x * by + by - 1
        low_rows[x + 1, edge_slot : edge_slot + 1, 0:lanes] = corner_below[end : end + 1, :]
        high_rows[x + 1, edge_slot : edge_slot + 1, 0:lanes] = corner_above[
            x * by : x * by + 1, :
        ]


def pass_on(x, chunk, indices, source, leaving_of, speed, halos, fresh, place, total, change):
    gas, low_rows, high_rows, columns = halos
    by = gas.shape[1]
    chunks = by // tall
    rows = pl.ds(chunk * tall, tall)
    rest = 1.0 - 1.5 * (speed[0] * speed[0] + speed[1] * speed[1] + speed[2] * speed[2])
    equals = {}

    def moved(load, index, slot, lane):
        step_x, step_y, step_z = velocity_set[index]
        plane = x + 1 - step_x
        edges = low_rows if step_y == 1 else high_rows
        found = rows_of(load, chunk, chunks, step_y, lambda: edges[plane, slot : slot + 1, :])
        if step_z == 0:
            return found
        halo = rows_of(
            lambda low, high: columns[plane, low:high, :],
            chunk,
            chunks,
            step_y,
            lambda: edges[plane, edge_slot : edge_slot + 1, 0:lanes],
        )
        return columns_of(found, halo, lane, step_z)

    for index in indices:
        step_x, step_y, step_z = velocity_set[index]
        first = min(index, opposite_of[index])
        if first not in equals:
            proj = along(first, speed)
            equals[first] = 2.0 * lattice_weights[first] * (rest + 4.5 * proj * proj)
        slot, lane, gas_lane = (None, None, None)
        if step_y != 0:
            slot = (y_up if step_y == 1 else y_down).index(index)
        if step_z == 1:
            lane, gas_lane = (z_up.index(index), gas_slot)
        elif step_z == -1:
            lane, gas_lane = (sides + z_down.index(index), sides + gas_slot)
        field = source(index)
        marks = gas.at[x + 1 - step_x]
        arriving = moved(lambda low, high: field[low:high, :], index, slot, lane)
        from_gas = moved(lambda low, high: marks[low:high, :], index, gas_slot, gas_lane)
        leaving = leaving_of(opposite_of[index])[rows, :]
        open_side = from_gas > 0.5
        value = jnp.where(open_side, equals[first] - leaving, arriving)
        fresh(index)[place, rows, :] = value
        total = total + value
        change = change + jnp.where(open_side, 0.0, arriving - leaving)
    return total, change


def settle(x, rows, mass, flags, code, total, change):
    read = mass[x, rows, :] + jnp.where(flags[x, rows, :] == 1, change, 0.0)
    mark = code[x, rows, :]
    liquid = mark >= 32.0
    converts = mark > 0.0
    level = jnp.where(liquid, total, 0.0)
    excess = jnp.where(converts, read - level, 0.0)
    heading = jnp.where(liquid, mark - 32.0, mark)
    return jnp.where(converts, level, read), excess, heading


slanted = tuple(index for index in range(19) if velocity_set[index][1] * velocity_set[index][2])
first_slanted = slanted[0]


def from_inside(x, bx):
    found = [index for index in range(1, 19) if 0 <= x - velocity_set[index][0] < bx]
    return [index for index in found if index not in slanted]


def from_beyond(x, bx):
    return [index for index in range(1, 19) if not 0 <= x - velocity_set[index][0] < bx]


def stream_early(
    inner_post,
    outer_post,
    inner_shift,
    outer_shift,
    flags,
    y_first,
    y_second,
    z_rows,
    inner,
    outer,
    totals,
    changes,
    gas,
    low_rows,
    high_rows,
    columns,
):
    bx, by, bz = flags.shape
    halos = (gas, low_rows, high_rows, columns)
    own_halos(flags, y_first, y_second, z_rows, *halos)

    for x in range(bx):
        inside = 0 < x < bx - 1
        place = x - 1 if inside else end_place(x, bx)
        fresh = inner if inside else outer
        for chunk in range(by // tall):
            rows = pl.ds(chunk * tall, tall)
            total = plane_of(inner_post, outer_post, 0, x, bx)[rows, :]
            fresh[0, place, rows, :] = total
            total, change = pass_on(
                x,
                chunk,
                from_inside(x, bx),
                lambda index: plane_of(
                    inner_post, outer_post, index, x - velocity_set[index][0], bx
                ),
                lambda index: plane_of(inner_post, outer_post, index, x, bx),
                [plane_of(inner_shift, outer_shift, comp, x, bx)[rows, :] for comp in range(3)],
                halos,
                lambda index: fresh.at[index],
                place,
                total,
                jnp.zeros((tall, bz), jnp.float32),
            )
            totals[x, rows, :] = total
            changes[x, rows, :] = change


def stream_slanted(
    inner_post,
    outer_post,
    inner_shift,
    outer_shift,
    mass,
    flags,
    code,
    y_first,
    y_second,
    z_rows,
    corner_first,
    corner_second,
    totals,
    changes,
    inner,
    outer,
    settled,
    excess,
    heading,
    end_totals,
    end_changes,
    gas,
    low_rows,
    high_rows,
    columns,
):
    bx, by, bz = flags.shape
    halos = (gas, low_rows, high_rows, columns)
    own_halos(flags, y_first, y_second, z_rows, *halos)
    own_corners(corner_first, corner_second, low_rows, high_rows)

    for x in range(bx):
        inside = 0 < x < bx - 1
        place = x - 1 if inside else end_place(x, bx)
        fresh = inner if inside else outer
        for chunk in range(by // tall):
            rows = pl.ds(chunk * tall, tall)
            total, change = pass_on(
                x,
                chunk,
                slanted,
                lambda index: plane_of(inner_post, outer_post, index, x, bx),
                lambda index: plane_of(inner_post, outer_post, index, x, bx),
                [plane_of(inner_shift, outer_shift, comp, x, bx)[rows, :] for comp in range(3)],
                halos,
                lambda index: fresh.at[index - first_slanted],
                place,
                totals[x, rows, :],
                changes[x, rows, :],
            )
            if inside:
                now = settle(x, rows, mass, flags, code, total, change)
                settled[place, rows, :], excess[place, rows, :], heading[place, rows, :] = now
            else:
                end_totals[place, rows, :] = total
                end_changes[place, rows, :] = change


def stream_late(
    post,
    shift,
    mass,
    flags,
    code,
    totals,
    changes,
    gas_first,
    gas_second,
    x_first,
    x_second,
    edges_first,
    edges_second,
    inner_excess,
    inner_heading,
    flow,
    after,
    late,
    v_first,
    v_second,
    settled,
    spread,
    line_first,
    line_second,
    out_z,
    gas,
    low_rows,
    high_rows,
    columns,
    below,
    above,
    excess,
    heading,
):
    bx, by, bz = flags.shape
    halves = bz // lanes
    flip_x = odd("gx")
    halos = (gas, low_rows, high_rows, columns)

    for comp in range(3):
        up, down = (flow[comp, bx - 1], flow[comp, 0])
        v_first[comp] = jnp.where(flip_x, down, up)
        v_second[comp] = jnp.where(flip_x, up, down)
    for slot in range(5):
        below[slot] = jnp.where(flip_x, x_first[slot], x_second[slot])
        above[slot] = jnp.where(flip_x, x_second[slot], x_first[slot])
    gas[0] = jnp.where(flip_x, gas_first[3], gas_second[3])
    gas[bx + 1] = jnp.where(flip_x, gas_second[3], gas_first[3])
    edges_below = select(flip_x, edges_first, edges_second)
    edges_above = select(flip_x, edges_second, edges_first)
    for found, at, x, edges in (
        (edges_below, 0, bx - 1, up_edges),
        (edges_above, bx + 1, 0, down_edges),
    ):
        for place, (side, slot) in enumerate(edges):
            line = jnp.concatenate(
                [found[half * 4 + place : half * 4 + place + 1, :] for half in range(halves)],
                axis=1,
            )
            (low_rows, high_rows)[side][at, slot : slot + 1, :] = line
        columns[at] = row_columns(found[4 * halves :, :])[x * by : x * by + by, :]
    for place, x in enumerate((0, bx - 1)):
        halo, order = ((below, x_up), (above, x_down))[place]
        for chunk in range(by // tall):
            rows = pl.ds(chunk * tall, tall)
            total, change = pass_on(
                x,
                chunk,
                from_beyond(x, bx),
                lambda index: halo.at[order.index(index)],
                lambda index: post.at[index, place],
                [shift[comp, place, rows, :] for comp in range(3)],
                halos,
                lambda index: late.at[order.index(index)],
                place,
                totals[place, rows, :],
                changes[place, rows, :],
            )
            now = settle(x, rows, mass, flags, code, total, change)
            settled[place, rows, :], excess[x, rows, :], heading[x, rows, :] = now
    for x in range(1, bx - 1):
        excess[x] = inner_excess[x - 1]
        heading[x] = inner_heading[x - 1]

    row_at, lane_at = (iota((by, bz), 0), iota((by, bz), 1))
    line_at = iota((1, bz), 1)
    tile_lane, line_lane = (iota((by, lanes), 1), iota((1, lanes), 1))

    def rows_up(rows):
        return jnp.where(row_at == 0, 0.0, pltpu.roll(rows, 1, 0))

    def rows_down(rows):
        return jnp.where(row_at == by - 1, 0.0, pltpu.roll(rows, by - 1, 0))

    def over(rows, at, step):
        if step == 1:
            return jnp.where(at == 0, 0.0, pltpu.roll(rows, 1, 1))
        return jnp.where(at == bz - 1, 0.0, pltpu.roll(rows, bz - 1, 1))

    def summed(parts):
        total = parts[0]
        for part in parts[1:]:
            total = total + part
        return total

    tile = jnp.zeros((by, lanes), jnp.float32)
    line_up = jnp.zeros((1, lanes), jnp.float32)
    line_down = jnp.zeros((1, lanes), jnp.float32)
    flip_y = odd("gy")
    line_first[...] = jnp.zeros(line_first.shape, jnp.float32)
    line_second[...] = jnp.zeros(line_second.shape, jnp.float32)
    for target in range(bx + 2):
        groups = {}
        for index in range(1, 19):
            step_x, step_y, step_z = velocity_set[index]
            x = target - 1 - step_x
            if 0 <= x < bx:
                part = jnp.where(heading[x] == float(index), excess[x], 0.0)
                groups.setdefault((step_y, step_z), []).append(part)
        groups = {key: summed(parts) for key, parts in groups.items()}
        total = jnp.zeros((by, bz), jnp.float32)
        line = {1: jnp.zeros((1, bz), jnp.float32), -1: jnp.zeros((1, bz), jnp.float32)}
        for step_z in (0, 1, -1):
            group = jnp.zeros((by, bz), jnp.float32)
            ends = {}
            if (0, step_z) in groups:
                group = group + groups[(0, step_z)]
            if (1, step_z) in groups:
                group = group + rows_up(groups[(1, step_z)])
                ends[1] = groups[(1, step_z)][by - 1 : by, :]
            if (-1, step_z) in groups:
                group = group + rows_down(groups[(-1, step_z)])
                ends[-1] = groups[(-1, step_z)][0:1, :]
            if step_z == 0:
                total = total + group
                for side in ends:
                    line[side] = line[side] + ends[side]
                continue
            total = total + over(group, lane_at, step_z)
            for side in ends:
                line[side] = line[side] + over(ends[side], line_at, step_z)
            if step_z == 1:
                spot, cut, roll = (target, slice(bz - lanes, bz), target + 1)
            else:
                spot, cut, roll = (8 + target, slice(0, lanes), 8 + target)
            tile = jnp.where(tile_lane == spot, pltpu.roll(group[:, cut], roll, 1), tile)
            if 1 in ends:
                line_up = jnp.where(
                    line_lane == spot, pltpu.roll(ends[1][:, cut], roll, 1), line_up
                )
            if -1 in ends:
                line_down = jnp.where(
                    line_lane == spot, pltpu.roll(ends[-1][:, cut], roll, 1), line_down
                )
        spread[target] = total
        line_first[target : target + 1, :] = jnp.where(flip_y, line[-1], line[1])
        line_second[target : target + 1, :] = jnp.where(flip_y, line[1], line[-1])
    rest = jnp.zeros((lanes - by - 2, lanes), jnp.float32)
    out_z[...] = column_rows([tile, line_up, line_down, rest], 16)


def with_edges(total, target, tile, y_below, y_above):
    by, bz = total.shape
    row_at, lane_at = (iota((by, bz), 0), iota((by, bz), 1))
    total = total + jnp.where(lane_at == 0, tile[0:by, target : target + 1], 0.0)
    total = total + jnp.where(lane_at == bz - 1, tile[0:by, 8 + target : 9 + target], 0.0)
    total = total + jnp.where(row_at == 0, y_below[target : target + 1, :], 0.0)
    return total + jnp.where(row_at == by - 1, y_above[target : target + 1, :], 0.0)


def add_faces(spread, z_rows, y_first, y_second, first, second):
    last = spread.shape[0] - 1
    flip_x, flip_y = (odd("gx"), odd("gy"))
    tile = row_columns(z_rows[...])
    y_below, y_above = (select(flip_y, y_first, y_second), select(flip_y, y_second, y_first))
    up = with_edges(spread[last], last, tile, y_below, y_above)
    down = with_edges(spread[0], 0, tile, y_below, y_above)
    first[...] = jnp.where(flip_x, down, up)
    second[...] = jnp.where(flip_x, up, down)


def add_all(
    inner_settled,
    outer_settled,
    spread,
    z_rows,
    y_first,
    y_second,
    corner_first,
    corner_second,
    x_second,
    x_first,
    after,
    new_mass,
):
    bx, by, bz = new_mass.shape
    flip_x, flip_y = (odd("gx"), odd("gy"))
    tile = row_columns(z_rows[...])
    y_below, y_above = (select(flip_y, y_first, y_second), select(flip_y, y_second, y_first))
    at = iota((8, bz), 1)
    found = []
    for rows, side, corner in (
        (y_below, 0, select(flip_y, corner_first, corner_second)),
        (y_above, 1, select(flip_y, corner_second, corner_first)),
    ):
        edge = corner[:, by + side : by + side + 1]
        rows = rows + jnp.where(at == 0, edge[0:8, :], 0.0)
        found.append(rows + jnp.where(at == bz - 1, edge[8:16, :], 0.0))
    for x in range(bx):
        total = with_edges(spread[x + 1], x + 1, tile, *found)
        if x == 0:
            total = total + select(flip_x, x_first, x_second)
        if x == bx - 1:
            total = total + select(flip_x, x_second, x_first)
        if 0 < x < bx - 1:
            total = total + inner_settled[x - 1]
        else:
            total = total + outer_settled[0 if x == 0 else 1]
        new_mass[x] = total


def swapped(first, second, axis):
    devices = lax.axis_size(axis)
    ahead = [(i, (i + 1) % devices if i % 2 == 0 else i - 1) for i in range(devices)]
    behind = [(i, (i - 1) % devices if i % 2 == 0 else (i + 1) % devices) for i in range(devices)]
    return lax.ppermute(first, axis, ahead), lax.ppermute(second, axis, behind)


def both_ways(rows, lower):
    devices = lax.axis_size("gz")
    before = lax.ppermute(rows, "gz", [(i, (i + 1) % devices) for i in range(devices)])
    if devices == 2:
        return before
    after = lax.ppermute(rows, "gz", [(i, (i - 1) % devices) for i in range(devices)])
    return jnp.where(iota(rows.shape, 0) < lower, before, after)


remote = pl.BlockSpec(memory_space=pltpu.HBM)
anywhere = pl.BlockSpec(memory_space=pl.ANY)


def call(body, outs, specs=None, out_specs=None, scratch=(), cost=(0, 0), aliases=None):
    extra = {} if specs is None else {"in_specs": specs}
    if out_specs is not None:
        extra["out_specs"] = out_specs
    return pl.pallas_call(
        body,
        out_shape=[
            shape
            if isinstance(shape, jax.ShapeDtypeStruct)
            else jax.ShapeDtypeStruct(shape, jnp.float32)
            for shape in outs
        ],
        scratch_shapes=[
            pltpu.VMEM(shape, jnp.float32) if isinstance(shape, tuple) else shape
            for shape in scratch
        ],
        compiler_params=pltpu.CompilerParams(vmem_limit_bytes=40 * 1024 * 1024),
        input_output_aliases=aliases or {},
        cost_estimate=pl.CostEstimate(flops=cost[0], bytes_accessed=cost[1], transcendentals=0),
        **extra,
    )


def shards(populations, stretch, mass, flags, conv_source, conv_kind, conv_direction):
    bx, by, bz = flags.shape
    cells = bx * by * bz
    box, face, tile = ((bx, by, bz), (by, bz), (bx, by, lanes))

    stretch, flags, z_out, y_one, y_two, x_one, x_two = call(
        first_faces,
        [
            (6, *box),
            jax.ShapeDtypeStruct(box, jnp.int32),
            (8, bx * by),
            (4 * bx, bz),
            (4 * bx, bz),
            (4, *face),
            (4, *face),
        ],
        specs=[remote] * 2,
        scratch=[pltpu.SemaphoreType.DMA((2,))],
        cost=(10 * cells, 60 * cells),
    )(*(pltpu.with_memory_space_constraint(array, pltpu.HBM) for array in (stretch, flags)))
    first_x = swapped(x_one, x_two, "gx")
    z_first = both_ways(z_out, 3)
    y_first = swapped(y_one, y_two, "gy")

    entries = conv_source.shape[0]
    mark = (tall, lanes)
    (code,) = call(
        lambda *refs: conversions(*refs, columns=bz),
        [(bx * by, bz)],
        cost=(40 * cells, 4 * cells),
    )(*(array.reshape(1, entries) for array in (conv_source, conv_kind, conv_direction)))
    code = code.reshape(box)

    pops, flow = call(
        moments,
        [(19, *box), (5, *box)],
        specs=[remote],
        scratch=[pltpu.SemaphoreType.DMA((bx,))],
        cost=(60 * cells, 150 * cells),
    )(pltpu.with_memory_space_constraint(populations, pltpu.HBM))

    columns, rows = ((24, bx * by), (10 * bx, bz))
    sides_y = [(bx, 8, bz), (bx, 8, bz), tile]
    inside, ends = ((bx - 2, *face), (2, *face))
    inner_post, inner_shift = call(
        collide_inner,
        [(19, *inside), (3, *inside)],
        scratch=sides_y,
        cost=(150 * cells, 150 * cells),
    )(pops, stretch, flow, z_first, *y_first)
    outer_post, outer_shift, z_out, x_one, x_two, y_one, y_two = call(
        collide_outer,
        [(19, *ends), (3, *ends), columns, (5, *face), (5, *face), rows, rows],
        scratch=[(4, *face), (4, *face)] + sides_y + [box],
        cost=(150 * cells, 150 * cells),
    )(pops, stretch, flags, flow, *first_x, *y_first, z_first, inner_post)
    z_post = both_ways(z_out, sides)
    post_y = swapped(y_one, y_two, "gy")
    post_x = swapped(x_one, x_two, "gx")
    edges = (4 * (bz // lanes) + columns[0], lanes)
    x_one, x_two, corner = call(
        lambda *refs: forward_edges(*refs, bx=bx), [edges, edges, columns], cost=(4 * 10**9, 0)
    )(z_post, *post_y)
    corners = swapped(corner, corner, "gy")
    edges_x = swapped(x_one, x_two, "gx")

    rims = [(bx + 2, *face), (bx + 2, 16, bz), (bx + 2, 16, bz), (bx + 2, by, lanes)]
    posts = (inner_post, outer_post, inner_shift, outer_shift)
    inner, outer, totals, changes = call(
        stream_early,
        [(first_slanted, *inside), (first_slanted, *ends), box, box],
        scratch=rims,
        cost=(350 * cells, 200 * cells),
    )(*posts, flags, *post_y, z_post)
    (
        inner_slanted,
        outer_slanted,
        inner_settled,
        inner_excess,
        inner_heading,
        totals,
        changes,
    ) = call(
        stream_slanted,
        [(4, *inside), (4, *ends), inside, inside, inside, ends, ends],
        scratch=rims,
        cost=(100 * cells, 60 * cells),
    )(*posts, mass, flags, code, *post_y, z_post, *corners, totals, changes)
    new_stretch, inner_done = call(
        restretch_inner,
        [(6, *box), mark],
        out_specs=[remote, pl.BlockSpec()],
        scratch=[(6, *inside)] + sides_y + [pltpu.SemaphoreType.DMA],
        cost=(80 * cells, 40 * cells),
    )(stretch, flow, *post_y, z_post)
    late, v_one, v_two, outer_settled, spread, y_one, y_two, z_out = call(
        stream_late,
        [
            (5, *ends),
            (3, *face),
            (3, *face),
            ends,
            (bx + 2, *face),
            (8, bz),
            (8, bz),
            (16, bx * by),
        ],
        scratch=rims + [(5, *face), (5, *face), box, box],
        cost=(150 * cells, 100 * cells),
    )(
        outer_post,
        outer_shift,
        mass,
        flags,
        code,
        totals,
        changes,
        *first_x,
        *post_x,
        *edges_x,
        inner_excess,
        inner_heading,
        flow,
        inner_done,
    )
    z_last = both_ways(z_out, 8)
    last_y = swapped(y_one, y_two, "gy")
    last_corners = swapped(z_last, z_last, "gy")
    flow_x = swapped(v_one, v_two, "gx")
    x_one, x_two = call(add_faces, [face, face], cost=(4 * 10**9, 0))(spread, z_last, *last_y)
    last_x = swapped(x_one, x_two, "gx")
    (fresh,) = call(
        store,
        [(19, *box)],
        out_specs=[remote],
        scratch=[pltpu.SemaphoreType.DMA((32,))],
        cost=(0, 160 * cells),
    )(inner, outer, inner_slanted, outer_slanted, late)
    new_stretch, outer_done = call(
        restretch_outer,
        [(6, *box), mark],
        specs=[pl.BlockSpec()] * 7 + [remote],
        out_specs=[remote, pl.BlockSpec()],
        scratch=[(6, *ends), (3, *face), (3, *face)]
        + sides_y
        + [pltpu.SemaphoreType.DMA((2,))],
        cost=(80 * cells, 40 * cells),
        aliases={7: 0},
    )(stretch, flow, *flow_x, *post_y, z_post, new_stretch)
    (new_mass,) = call(add_all, [box])(
        inner_settled, outer_settled, spread, z_last, *last_y, *last_corners, *last_x[::-1], outer_done
    )
    return (fresh, new_stretch, new_mass)


def solution(mesh):
    return jax.shard_map(
        shards,
        mesh=mesh,
        in_specs=(
            P(None, "gx", "gy", "gz"),
            P(None, "gx", "gy", "gz"),
            P("gx", "gy", "gz"),
            P("gx", "gy", "gz"),
            P(("gx", "gy", "gz")),
            P(("gx", "gy", "gz")),
            P(("gx", "gy", "gz")),
        ),
        out_specs=(P(None, "gx", "gy", "gz"), P(None, "gx", "gy", "gz"), P("gx", "gy", "gz")),
        check_vma=False,
    )
```

```python
import jax
import jax.numpy as jnp
from jax import lax
from jax.experimental import pallas as pl
from jax.experimental.pallas import tpu as pltpu
from jax.sharding import PartitionSpec as P

velocity_set = (
    (0, 0, 0),
    (1, 0, 0),
    (-1, 0, 0),
    (0, 1, 0),
    (0, -1, 0),
    (0, 0, 1),
    (0, 0, -1),
    (1, 1, 0),
    (-1, -1, 0),
    (1, -1, 0),
    (-1, 1, 0),
    (1, 0, 1),
    (-1, 0, -1),
    (1, 0, -1),
    (-1, 0, 1),
    (0, 1, 1),
    (0, -1, -1),
    (0, 1, -1),
    (0, -1, 1),
)
opposite_of = (0, 2, 1, 4, 3, 6, 5, 8, 7, 10, 9, 12, 11, 14, 13, 16, 15, 18, 17)
lattice_weights = (1.0 / 3.0,) + (1.0 / 18.0,) * 6 + (1.0 / 36.0,) * 12
symmetric_slot = ((0, 3, 4), (3, 1, 5), (4, 5, 2))
tensor_pairs = ((0, 0), (1, 1), (2, 2), (0, 1), (0, 2), (1, 2))
relax_time = 0.8
polymer_time = 8.0
polymer_coeff = 0.05


def moving(axis, sign):
    return tuple(index for index in range(19) if velocity_set[index][axis] == sign)


x_up, x_down = (moving(0, 1), moving(0, -1))
y_up, y_down = (moving(1, 1), moving(1, -1))
z_up, z_down = (moving(2, 1), moving(2, -1))
pairs = tuple(range(1, 19, 2))
gas_slot = 5
speed_slot = 6
edge_slot = 9
sides = 9
lanes = 128
tall = 8


def iota(shape, dim):
    return lax.broadcasted_iota(jnp.int32, shape, dim)


def wide(tile, width):
    return jnp.concatenate([tile] * (width // tile.shape[1]), axis=1)


def rows_of(load, chunk, chunks, step, edge):
    low = chunk * tall
    if step == 0:
        return load(low, low + tall)
    if step == 1 and chunk > 0:
        return load(low - 1, low + tall - 1)
    if step == -1 and chunk < chunks - 1:
        return load(low + 1, low + tall + 1)
    rows = load(low, low + tall)
    at = iota(rows.shape, 0)
    if step == 1:
        return jnp.where(at == 0, edge(), pltpu.roll(rows, 1, 0))
    return jnp.where(at == tall - 1, edge(), pltpu.roll(rows, tall - 1, 0))


def columns_of(rows, halo, lane, step):
    width = rows.shape[1]
    at = iota(rows.shape, 1)
    if step == 1:
        edge = wide(pltpu.roll(halo, (lanes - lane) % lanes, 1), width)
        return jnp.where(at == 0, edge, pltpu.roll(rows, 1, 1))
    edge = wide(pltpu.roll(halo, lanes - 1 - lane, 1), width)
    return jnp.where(at == width - 1, edge, pltpu.roll(rows, width - 1, 1))


def packed(high, low):
    at = iota(high[0].shape, 1)
    tile = jnp.zeros_like(high[0])
    for slot, part in enumerate(high):
        tile = jnp.where(at == slot, pltpu.roll(part, slot + 1, 1), tile)
    for place, part in enumerate(low):
        slot = len(high) + place
        tile = jnp.where(at == slot, pltpu.roll(part, slot, 1), tile)
    return tile


def along(index, vector):
    total = None
    for comp in range(3):
        sign = velocity_set[index][comp]
        if sign != 0:
            term = vector[comp] if sign > 0 else -vector[comp]
            total = term if total is None else total + term
    return total


def conversions(source, kind, heading, code, *, columns):
    count = source.shape[1]
    value = (heading[...] + 32 * kind[...]).astype(jnp.float32)
    row, column = (source[...] // columns, source[...] % columns)
    by_row = jnp.where(iota((code.shape[0], count), 0) == row, value, 0.0).astype(jnp.bfloat16)
    by_column = jnp.where(iota((columns, count), 0) == column, 1.0, 0.0).astype(jnp.bfloat16)
    code[...] = lax.dot_general(
        by_row, by_column, (((1,), (1,)), ((), ())), preferred_element_type=jnp.float32
    )


def odd(axis):
    return lax.rem(lax.axis_index(axis), 2) == 1


def select(chosen, first, second):
    return jnp.where(chosen, first[...], second[...])


def swap_rows(first, second, x, planes, high, low, flip):
    for slot, (top, bottom) in enumerate(zip(high, low)):
        by = top.shape[0]
        up, down = (top[by - 1 : by, :], bottom[0:1, :])
        at = slot * planes + x
        first[at : at + 1, :] = jnp.where(flip, down, up)
        second[at : at + 1, :] = jnp.where(flip, up, down)


def swapped_rows(first, second, slots, low_rows, high_rows, shift):
    flip = odd("gy")
    planes = low_rows.shape[0] - 2 * shift
    for x in range(planes):
        for place, slot in enumerate(slots):
            at = slot * planes + x
            one, two = (first[at : at + 1, :], second[at : at + 1, :])
            low_rows[x + shift, place : place + 1, :] = jnp.where(flip, one, two)
            high_rows[x + shift, place : place + 1, :] = jnp.where(flip, two, one)


def column_rows(tiles, count):
    return jnp.concatenate(tiles, axis=0).T[0:count, :]


def row_columns(rows):
    rest = jnp.zeros((lanes - rows.shape[0], rows.shape[1]), jnp.float32)
    return jnp.concatenate([rows, rest], axis=0).T


def first_faces(
    stretch_in,
    flags_in,
    stretch,
    flags,
    columns,
    y_first,
    y_second,
    x_first,
    x_second,
    sems,
):
    bx, by, bz = flags.shape
    flip_x, flip_y = (odd("gx"), odd("gy"))
    copies = [
        pltpu.make_async_copy(stretch_in, stretch, sems.at[0]),
        pltpu.make_async_copy(flags_in, flags, sems.at[1]),
    ]
    for copy in copies:
        copy.start()
    for copy in copies:
        copy.wait()
    tiles = []
    for x in range(bx):
        along_y = [stretch.at[symmetric_slot[comp][1], x] for comp in range(3)]
        swap_rows(y_first, y_second, x, bx, along_y, along_y, flip_y)
        fields = [stretch.at[symmetric_slot[comp][2], x] for comp in range(3)]
        tiles.append(
            packed(
                [field[:, bz - lanes : bz] for field in fields],
                [field[:, 0:lanes] for field in fields],
            )
        )
    columns[...] = column_rows(tiles, columns.shape[0])
    rest = y_first.shape[0] - 3 * bx
    y_first[3 * bx :, :] = jnp.zeros((rest, bz), jnp.float32)
    y_second[3 * bx :, :] = jnp.zeros((rest, bz), jnp.float32)
    for out, last in ((x_first, flip_x), (x_second, jnp.logical_not(flip_x))):
        for comp in range(3):
            slot = symmetric_slot[comp][0]
            out[comp] = jnp.where(last, stretch[slot, 0], stretch[slot, bx - 1])
        out[3] = jnp.where(jnp.where(last, flags[0], flags[bx - 1]) == 0, 1.0, 0.0)


def moments(pops_in, pops, flow, sems):
    bx, by = pops.shape[1:3]
    copies = [
        pltpu.make_async_copy(pops_in.at[:, x], pops.at[:, x], sems.at[x]) for x in range(bx)
    ]
    for copy in copies:
        copy.start()
    for x in range(bx):
        copies[x].wait()
        for chunk in range(by // tall):
            rows = pl.ds(chunk * tall, tall)
            part = [pops[index, x, rows, :] for index in range(19)]
            density = part[0]
            for index in range(1, 19):
                density = density + part[index]
            inverse = 1.0 / density
            for comp in range(3):
                total = None
                for index in pairs:
                    sign = velocity_set[index][comp]
                    if sign != 0:
                        term = part[index] - part[index + 1]
                        term = term if sign > 0 else -term
                        total = term if total is None else total + term
                flow[comp, x, rows, :] = total * inverse
            flow[3, x, rows, :] = density
            flow[4, x, rows, :] = inverse


def beside(ref, field, x, step, halo, slot):
    last = ref.shape[1] - 1
    if halo is None:
        return lambda low, high: ref[field, x + step, low:high, :]
    if isinstance(x, int):
        if 0 <= x + step <= last:
            return lambda low, high: ref[field, x + step, low:high, :]
        return lambda low, high: halo[slot, low:high, :]
    inside = jnp.clip(x + step, 0, last)
    beyond = x == (0 if step < 0 else last)
    return lambda low, high: jnp.where(
        beyond, halo[slot, low:high, :], ref[field, inside, low:high, :]
    )


def differences(
    ref, field, slots, x, chunk, chunks, below, above, y_below, y_above, z_halo, lane, side
):
    slot_x, slot_y, slot_z = slots
    low, high = (chunk * tall, chunk * tall + tall)

    def load(first, stop):
        return ref[field, x, first:stop, :]

    result = [None, None, None]
    if slot_x is not None:
        after = beside(ref, field, x, 1, above, slot_x)(low, high)
        before = beside(ref, field, x, -1, below, slot_x)(low, high)
        result[0] = after - before
    if slot_y is not None:
        after = rows_of(load, chunk, chunks, -1, lambda: y_above[x, slot_y : slot_y + 1, :])
        before = rows_of(load, chunk, chunks, 1, lambda: y_below[x, slot_y : slot_y + 1, :])
        result[1] = after - before
    if slot_z is not None:
        rows, halo = (load(low, high), z_halo[x, low:high, :])
        after = columns_of(rows, halo, lane + side + slot_z, -1)
        before = columns_of(rows, halo, lane + slot_z, 1)
        result[2] = after - before
    return result


def end_place(x, bx):
    return 0 if x == 0 else 1


def plane_of(inner, outer, field, x, bx):
    if 0 < x < bx - 1:
        return inner.at[field, x - 1]
    return outer.at[field, end_place(x, bx)]


def collide_plane(x, place, pops, stretch, flow, halos, post, shift):
    by = pops.shape[2]
    chunks = by // tall
    factor = 1.0 - 0.5 / relax_time
    rate = 1.0 / relax_time
    for chunk in range(chunks):
        rows = pl.ds(chunk * tall, tall)
        terms = [[], [], []]
        for field in range(6):
            slots = [None, None, None]
            for comp in range(3):
                for axis in range(3):
                    if symmetric_slot[comp][axis] == field:
                        slots[axis] = comp
            found = differences(stretch, field, slots, x, chunk, chunks, *halos)
            for axis in range(3):
                if slots[axis] is not None:
                    terms[slots[axis]].append(found[axis])
        force = [0.5 * polymer_coeff * (part[0] + part[1] + part[2]) for part in terms]
        density, half = (flow[3, x, rows, :], 0.5 * flow[4, x, rows, :])
        moved = [flow[comp, x, rows, :] + half * force[comp] for comp in range(3)]
        for comp in range(3):
            shift[comp, place, rows, :] = moved[comp]
        squared = moved[0] * moved[0] + moved[1] * moved[1] + moved[2] * moved[2]
        work = moved[0] * force[0] + moved[1] * force[1] + moved[2] * force[2]
        weight = rate * density
        common = weight - 1.5 * weight * squared - 3.0 * factor * work
        odd = [3.0 * weight * moved[comp] + 3.0 * factor * force[comp] for comp in range(3)]
        even = [4.5 * weight * moved[comp] + 9.0 * factor * force[comp] for comp in range(3)]
        keep = 1.0 - rate
        post[0, place, rows, :] = keep * pops[0, x, rows, :] + lattice_weights[0] * common
        for index in pairs:
            both = common + along(index, moved) * along(index, even)
            differ = along(index, odd)
            scale = lattice_weights[index]
            post[index, place, rows, :] = keep * pops[index, x, rows, :] + scale * (both + differ)
            post[index + 1, place, rows, :] = keep * pops[index + 1, x, rows, :] + scale * (
                both - differ
            )


def collide_inner(
    pops,
    stretch,
    flow,
    z_rows,
    y_first,
    y_second,
    post,
    shift,
    y_below,
    y_above,
    z_halo,
):
    swapped_rows(y_first, y_second, range(3), y_below, y_above, 0)
    z_halo[...] = row_columns(z_rows[...]).reshape(z_halo.shape)
    halos = (None, None, y_below, y_above, z_halo, 0, 3)

    def plane(x, carry):
        collide_plane(x, x - 1, pops, stretch, flow, halos, post, shift)
        return carry

    lax.fori_loop(1, pops.shape[1] - 1, plane, 0)


def collide_outer(
    pops,
    stretch,
    flags,
    flow,
    x_first,
    x_second,
    y_first,
    y_second,
    z_rows,
    inner,
    post,
    shift,
    columns,
    ahead,
    behind,
    up_first,
    up_second,
    below,
    above,
    y_below,
    y_above,
    z_halo,
    gas,
):
    bx, by, bz = flags.shape
    halos = (below, above, y_below, y_above, z_halo, 0, 3)
    flip_x, flip_y = (odd("gx"), odd("gy"))
    below[...] = select(flip_x, x_first, x_second)
    above[...] = select(flip_x, x_second, x_first)
    swapped_rows(y_first, y_second, range(3), y_below, y_above, 0)
    z_halo[...] = row_columns(z_rows[...]).reshape(z_halo.shape)
    for x in (0, bx - 1):
        collide_plane(x, end_place(x, bx), pops, stretch, flow, halos, post, shift)

    tiles = []
    for x in range(bx):
        gas[x] = jnp.where(flags[x] == 0, 1.0, 0.0)
        rest = [gas.at[x]] + [flow.at[comp, x] for comp in range(3)]

        def fields(indices):
            return [plane_of(inner, post, index, x, bx) for index in indices] + rest

        swap_rows(up_first, up_second, x, bx, fields(y_up), fields(y_down), flip_y)
        tiles.append(
            packed(
                [field[:, bz - lanes : bz] for field in fields(z_up)],
                [field[:, 0:lanes] for field in fields(z_down)],
            )
        )
    columns[...] = column_rows(tiles, columns.shape[0])
    rest = up_first.shape[0] - sides * bx
    up_first[sides * bx :, :] = jnp.zeros((rest, bz), jnp.float32)
    up_second[sides * bx :, :] = jnp.zeros((rest, bz), jnp.float32)
    for slot in range(5):
        up, down = (post[x_up[slot], 1], post[x_down[slot], 0])
        ahead[slot] = jnp.where(flip_x, down, up)
        behind[slot] = jnp.where(flip_x, up, down)


def restretch_plane(x, place, stretch, flow, halos, updated):
    chunks = stretch.shape[2] // tall
    for chunk in range(chunks):
        rows = pl.ds(chunk * tall, tall)
        grad = [
            differences(
                flow, comp, (comp, comp, comp), x, chunk, chunks, *halos, speed_slot, sides
            )
            for comp in range(3)
        ]
        part = [stretch[slot, x, rows, :] for slot in range(6)]
        full = [part[slot] + 1.0 if slot < 3 else part[slot] for slot in range(6)]

        def product(row, col):
            total = grad[row][0] * full[symmetric_slot[0][col]]
            for inner in (1, 2):
                total = total + grad[row][inner] * full[symmetric_slot[inner][col]]
            return total

        for slot, (row, col) in enumerate(tensor_pairs):
            old = (1.0 - 1.0 / polymer_time) * part[slot]
            if row == col:
                updated[slot, place, rows, :] = old + product(row, col)
            else:
                updated[slot, place, rows, :] = old + 0.5 * (product(row, col) + product(col, row))


def restretch_inner(
    stretch,
    flow,
    y_first,
    y_second,
    z_rows,
    new_stretch,
    mark,
    updated,
    y_below,
    y_above,
    z_halo,
    sem,
):
    bx = stretch.shape[1]
    swapped_rows(y_first, y_second, range(speed_slot, sides), y_below, y_above, 0)
    z_halo[...] = row_columns(z_rows[...]).reshape(z_halo.shape)
    halos = (None, None, y_below, y_above, z_halo)

    def plane(x, carry):
        restretch_plane(x, x - 1, stretch, flow, halos, updated)
        return carry

    lax.fori_loop(1, bx - 1, plane, 0)
    copy = pltpu.make_async_copy(updated, new_stretch.at[:, 1 : bx - 1], sem)
    copy.start()
    mark[...] = jnp.zeros(mark.shape, jnp.float32)
    copy.wait()


def restretch_outer(
    stretch,
    flow,
    x_first,
    x_second,
    y_first,
    y_second,
    z_rows,
    inner_stretch,
    inner,
    outer,
    inner_slanted,
    outer_slanted,
    late,
    new_stretch,
    fresh,
    mark,
    updated,
    below,
    above,
    y_below,
    y_above,
    z_halo,
    sems,
    store_sems,
):
    bx = stretch.shape[1]
    moves = stored(inner, outer, inner_slanted, outer_slanted, late, fresh, store_sems)
    for copy in moves:
        copy.start()
    flip_x = odd("gx")
    for comp in range(3):
        below[comp] = jnp.where(flip_x, x_first[comp], x_second[comp])
        above[comp] = jnp.where(flip_x, x_second[comp], x_first[comp])
    swapped_rows(y_first, y_second, range(speed_slot, sides), y_below, y_above, 0)
    z_halo[...] = row_columns(z_rows[...]).reshape(z_halo.shape)
    halos = (below, above, y_below, y_above, z_halo)
    copies = []
    for place, x in enumerate((0, bx - 1)):
        restretch_plane(x, place, stretch, flow, halos, updated)
        copies.append(
            pltpu.make_async_copy(updated.at[:, place], new_stretch.at[:, x], sems.at[place])
        )
        copies[-1].start()
    mark[...] = jnp.zeros(mark.shape, jnp.float32)
    for copy in copies + moves:
        copy.wait()


def stored(inner, outer, inner_slanted, outer_slanted, late, fresh, sems):
    bx = fresh.shape[1]
    moves = [
        (inner, fresh.at[0:first_slanted, 1 : bx - 1]),
        (inner_slanted, fresh.at[first_slanted:, 1 : bx - 1]),
    ]
    for place, x in enumerate((0, bx - 1)):
        moves.append((outer_slanted.at[:, place], fresh.at[first_slanted:, x]))
        order = (x_up, x_down)[place]
        start = 0
        for index in order + (first_slanted,):
            if index > start:
                run = slice(start, index)
                moves.append((outer.at[run, place], fresh.at[run, x]))
            if index in order:
                moves.append((late.at[order.index(index), place], fresh.at[index, x]))
            start = index + 1
    return [
        pltpu.make_async_copy(source, target, sems.at[place])
        for place, (source, target) in enumerate(moves)
    ]


up_edges = ((0, y_up.index(7)), (0, gas_slot), (1, y_down.index(9)), (1, gas_slot))
down_edges = ((0, y_up.index(10)), (0, gas_slot), (1, y_down.index(8)), (1, gas_slot))


def forward_edges(z_rows, y_first, y_second, first_out, second_out, corner, *, bx):
    halves = y_first.shape[1] // lanes
    flip_x, flip_y = (odd("gx"), odd("gy"))
    for half in range(halves):
        cut = slice(half * lanes, half * lanes + lanes)
        for place in range(4):
            found = []
            for x, edges in ((bx - 1, up_edges), (0, down_edges)):
                side, slot = edges[place]
                row = slot * bx + x
                one = y_first[row : row + 1, cut]
                two = y_second[row : row + 1, cut]
                found.append(jnp.where(flip_y, one, two) if side == 0 else jnp.where(flip_y, two, one))
            at = half * 4 + place
            first_out[at : at + 1, :] = jnp.where(flip_x, found[1], found[0])
            second_out[at : at + 1, :] = jnp.where(flip_x, found[0], found[1])
    first_out[4 * halves :, :] = z_rows[...]
    second_out[4 * halves :, :] = z_rows[...]
    corner[...] = z_rows[...]


def own_halos(flags, y_first, y_second, z_rows, gas, low_rows, high_rows, columns):
    bx, by = flags.shape[:2]
    tile = row_columns(z_rows[...])
    swapped_rows(y_first, y_second, range(speed_slot), low_rows, high_rows, 1)
    for x in range(bx):
        gas[x + 1] = jnp.where(flags[x] == 0, 1.0, 0.0)
        columns[x + 1] = tile[x * by : x * by + by, :]


def own_corners(corner_first, corner_second, low_rows, high_rows):
    bx = low_rows.shape[0] - 2
    flip = odd("gy")
    corner_below = row_columns(select(flip, corner_first, corner_second))
    corner_above = row_columns(select(flip, corner_second, corner_first))
    by = corner_below.shape[0] // bx
    for x in range(bx):
        end = x * by + by - 1
        low_rows[x + 1, edge_slot : edge_slot + 1, 0:lanes] = corner_below[end : end + 1, :]
        high_rows[x + 1, edge_slot : edge_slot + 1, 0:lanes] = corner_above[
            x * by : x * by + 1, :
        ]


def pass_on(x, chunk, indices, source, leaving_of, speed, halos, fresh, place, total, change):
    gas, low_rows, high_rows, columns = halos
    by = gas.shape[1]
    chunks = by // tall
    rows = pl.ds(chunk * tall, tall)
    rest = 1.0 - 1.5 * (speed[0] * speed[0] + speed[1] * speed[1] + speed[2] * speed[2])
    equals = {}

    def moved(load, index, slot, lane):
        step_x, step_y, step_z = velocity_set[index]
        plane = x + 1 - step_x
        edges = low_rows if step_y == 1 else high_rows
        found = rows_of(load, chunk, chunks, step_y, lambda: edges[plane, slot : slot + 1, :])
        if step_z == 0:
            return found
        halo = rows_of(
            lambda low, high: columns[plane, low:high, :],
            chunk,
            chunks,
            step_y,
            lambda: edges[plane, edge_slot : edge_slot + 1, 0:lanes],
        )
        return columns_of(found, halo, lane, step_z)

    for index in indices:
        step_x, step_y, step_z = velocity_set[index]
        first = min(index, opposite_of[index])
        if first not in equals:
            proj = along(first, speed)
            equals[first] = 2.0 * lattice_weights[first] * (rest + 4.5 * proj * proj)
        slot, lane, gas_lane = (None, None, None)
        if step_y != 0:
            slot = (y_up if step_y == 1 else y_down).index(index)
        if step_z == 1:
            lane, gas_lane = (z_up.index(index), gas_slot)
        elif step_z == -1:
            lane, gas_lane = (sides + z_down.index(index), sides + gas_slot)
        field = source(index)
        marks = gas.at[x + 1 - step_x]
        arriving = moved(lambda low, high: field[low:high, :], index, slot, lane)
        from_gas = moved(lambda low, high: marks[low:high, :], index, gas_slot, gas_lane)
        leaving = leaving_of(opposite_of[index])[rows, :]
        open_side = from_gas > 0.5
        value = jnp.where(open_side, equals[first] - leaving, arriving)
        fresh(index)[place, rows, :] = value
        total = total + value
        change = change + jnp.where(open_side, 0.0, arriving - leaving)
    return total, change


def settle(x, rows, mass, flags, code, total, change):
    read = mass[x, rows, :] + jnp.where(flags[x, rows, :] == 1, change, 0.0)
    mark = code[x, rows, :]
    liquid = mark >= 32.0
    converts = mark > 0.0
    level = jnp.where(liquid, total, 0.0)
    excess = jnp.where(converts, read - level, 0.0)
    heading = jnp.where(liquid, mark - 32.0, mark)
    return jnp.where(converts, level, read), excess, heading


slanted = tuple(index for index in range(19) if velocity_set[index][1] * velocity_set[index][2])
first_slanted = slanted[0]


def from_inside(x, bx):
    found = [index for index in range(1, 19) if 0 <= x - velocity_set[index][0] < bx]
    return [index for index in found if index not in slanted]


def from_beyond(x, bx):
    return [index for index in range(1, 19) if not 0 <= x - velocity_set[index][0] < bx]


def stream_early(
    inner_post,
    outer_post,
    inner_shift,
    outer_shift,
    flags,
    y_first,
    y_second,
    z_rows,
    inner,
    outer,
    totals,
    changes,
    gas,
    low_rows,
    high_rows,
    columns,
):
    bx, by, bz = flags.shape
    halos = (gas, low_rows, high_rows, columns)
    own_halos(flags, y_first, y_second, z_rows, *halos)

    for x in range(bx):
        inside = 0 < x < bx - 1
        place = x - 1 if inside else end_place(x, bx)
        fresh = inner if inside else outer
        for chunk in range(by // tall):
            rows = pl.ds(chunk * tall, tall)
            total = plane_of(inner_post, outer_post, 0, x, bx)[rows, :]
            fresh[0, place, rows, :] = total
            total, change = pass_on(
                x,
                chunk,
                from_inside(x, bx),
                lambda index: plane_of(
                    inner_post, outer_post, index, x - velocity_set[index][0], bx
                ),
                lambda index: plane_of(inner_post, outer_post, index, x, bx),
                [plane_of(inner_shift, outer_shift, comp, x, bx)[rows, :] for comp in range(3)],
                halos,
                lambda index: fresh.at[index],
                place,
                total,
                jnp.zeros((tall, bz), jnp.float32),
            )
            totals[x, rows, :] = total
            changes[x, rows, :] = change


def stream_slanted(
    inner_post,
    outer_post,
    inner_shift,
    outer_shift,
    mass,
    flags,
    code,
    y_first,
    y_second,
    z_rows,
    corner_first,
    corner_second,
    totals,
    changes,
    inner,
    outer,
    settled,
    excess,
    heading,
    end_totals,
    end_changes,
    gas,
    low_rows,
    high_rows,
    columns,
):
    bx, by, bz = flags.shape
    halos = (gas, low_rows, high_rows, columns)
    own_halos(flags, y_first, y_second, z_rows, *halos)
    own_corners(corner_first, corner_second, low_rows, high_rows)

    for x in range(bx):
        inside = 0 < x < bx - 1
        place = x - 1 if inside else end_place(x, bx)
        fresh = inner if inside else outer
        for chunk in range(by // tall):
            rows = pl.ds(chunk * tall, tall)
            total, change = pass_on(
                x,
                chunk,
                slanted,
                lambda index: plane_of(inner_post, outer_post, index, x, bx),
                lambda index: plane_of(inner_post, outer_post, index, x, bx),
                [plane_of(inner_shift, outer_shift, comp, x, bx)[rows, :] for comp in range(3)],
                halos,
                lambda index: fresh.at[index - first_slanted],
                place,
                totals[x, rows, :],
                changes[x, rows, :],
            )
            if inside:
                now = settle(x, rows, mass, flags, code, total, change)
                settled[place, rows, :], excess[place, rows, :], heading[place, rows, :] = now
            else:
                end_totals[place, rows, :] = total
                end_changes[place, rows, :] = change


def stream_late(
    post,
    shift,
    mass,
    flags,
    code,
    totals,
    changes,
    gas_first,
    gas_second,
    x_second,
    x_first,
    edges_first,
    edges_second,
    inner_excess,
    inner_heading,
    flow,
    after,
    late,
    v_first,
    v_second,
    settled,
    spread,
    line_first,
    line_second,
    out_z,
    gas,
    low_rows,
    high_rows,
    columns,
    below,
    above,
    excess,
    heading,
):
    bx, by, bz = flags.shape
    halves = bz // lanes
    flip_x = odd("gx")
    halos = (gas, low_rows, high_rows, columns)

    for comp in range(3):
        up, down = (flow[comp, bx - 1], flow[comp, 0])
        v_first[comp] = jnp.where(flip_x, down, up)
        v_second[comp] = jnp.where(flip_x, up, down)
    for slot in range(5):
        below[slot] = jnp.where(flip_x, x_first[slot], x_second[slot])
        above[slot] = jnp.where(flip_x, x_second[slot], x_first[slot])
    gas[0] = jnp.where(flip_x, gas_first[3], gas_second[3])
    gas[bx + 1] = jnp.where(flip_x, gas_second[3], gas_first[3])
    edges_below = select(flip_x, edges_first, edges_second)
    edges_above = select(flip_x, edges_second, edges_first)
    for found, at, x, edges in (
        (edges_below, 0, bx - 1, up_edges),
        (edges_above, bx + 1, 0, down_edges),
    ):
        for place, (side, slot) in enumerate(edges):
            line = jnp.concatenate(
                [found[half * 4 + place : half * 4 + place + 1, :] for half in range(halves)],
                axis=1,
            )
            (low_rows, high_rows)[side][at, slot : slot + 1, :] = line
        columns[at] = row_columns(found[4 * halves :, :])[x * by : x * by + by, :]
    for place, x in enumerate((0, bx - 1)):
        halo, order = ((below, x_up), (above, x_down))[place]
        for chunk in range(by // tall):
            rows = pl.ds(chunk * tall, tall)
            total, change = pass_on(
                x,
                chunk,
                from_beyond(x, bx),
                lambda index: halo.at[order.index(index)],
                lambda index: post.at[index, place],
                [shift[comp, place, rows, :] for comp in range(3)],
                halos,
                lambda index: late.at[order.index(index)],
                place,
                totals[place, rows, :],
                changes[place, rows, :],
            )
            now = settle(x, rows, mass, flags, code, total, change)
            settled[place, rows, :], excess[x, rows, :], heading[x, rows, :] = now
    for x in range(1, bx - 1):
        excess[x] = inner_excess[x - 1]
        heading[x] = inner_heading[x - 1]

    row_at, lane_at = (iota((by, bz), 0), iota((by, bz), 1))
    line_at = iota((1, bz), 1)
    tile_lane, line_lane = (iota((by, lanes), 1), iota((1, lanes), 1))

    def rows_up(rows):
        return jnp.where(row_at == 0, 0.0, pltpu.roll(rows, 1, 0))

    def rows_down(rows):
        return jnp.where(row_at == by - 1, 0.0, pltpu.roll(rows, by - 1, 0))

    def over(rows, at, step):
        if step == 1:
            return jnp.where(at == 0, 0.0, pltpu.roll(rows, 1, 1))
        return jnp.where(at == bz - 1, 0.0, pltpu.roll(rows, bz - 1, 1))

    def summed(parts):
        total = parts[0]
        for part in parts[1:]:
            total = total + part
        return total

    tile = jnp.zeros((by, lanes), jnp.float32)
    line_up = jnp.zeros((1, lanes), jnp.float32)
    line_down = jnp.zeros((1, lanes), jnp.float32)
    flip_y = odd("gy")
    line_first[...] = jnp.zeros(line_first.shape, jnp.float32)
    line_second[...] = jnp.zeros(line_second.shape, jnp.float32)
    for target in range(bx + 2):
        groups = {}
        for index in range(1, 19):
            step_x, step_y, step_z = velocity_set[index]
            x = target - 1 - step_x
            if 0 <= x < bx:
                part = jnp.where(heading[x] == float(index), excess[x], 0.0)
                groups.setdefault((step_y, step_z), []).append(part)
        groups = {key: summed(parts) for key, parts in groups.items()}
        total = jnp.zeros((by, bz), jnp.float32)
        line = {1: jnp.zeros((1, bz), jnp.float32), -1: jnp.zeros((1, bz), jnp.float32)}
        for step_z in (0, 1, -1):
            group = jnp.zeros((by, bz), jnp.float32)
            ends = {}
            if (0, step_z) in groups:
                group = group + groups[(0, step_z)]
            if (1, step_z) in groups:
                group = group + rows_up(groups[(1, step_z)])
                ends[1] = groups[(1, step_z)][by - 1 : by, :]
            if (-1, step_z) in groups:
                group = group + rows_down(groups[(-1, step_z)])
                ends[-1] = groups[(-1, step_z)][0:1, :]
            if step_z == 0:
                total = total + group
                for side in ends:
                    line[side] = line[side] + ends[side]
                continue
            total = total + over(group, lane_at, step_z)
            for side in ends:
                line[side] = line[side] + over(ends[side], line_at, step_z)
            if step_z == 1:
                spot, cut, roll = (target, slice(bz - lanes, bz), target + 1)
            else:
                spot, cut, roll = (8 + target, slice(0, lanes), 8 + target)
            tile = jnp.where(tile_lane == spot, pltpu.roll(group[:, cut], roll, 1), tile)
            if 1 in ends:
                line_up = jnp.where(
                    line_lane == spot, pltpu.roll(ends[1][:, cut], roll, 1), line_up
                )
            if -1 in ends:
                line_down = jnp.where(
                    line_lane == spot, pltpu.roll(ends[-1][:, cut], roll, 1), line_down
                )
        spread[target] = total
        line_first[target : target + 1, :] = jnp.where(flip_y, line[-1], line[1])
        line_second[target : target + 1, :] = jnp.where(flip_y, line[1], line[-1])
    rest = jnp.zeros((lanes - by - 2, lanes), jnp.float32)
    out_z[...] = column_rows([tile, line_up, line_down, rest], 16)


def with_edges(total, target, tile, y_below, y_above):
    by, bz = total.shape
    row_at, lane_at = (iota((by, bz), 0), iota((by, bz), 1))
    total = total + jnp.where(lane_at == 0, tile[0:by, target : target + 1], 0.0)
    total = total + jnp.where(lane_at == bz - 1, tile[0:by, 8 + target : 9 + target], 0.0)
    total = total + jnp.where(row_at == 0, y_below[target : target + 1, :], 0.0)
    return total + jnp.where(row_at == by - 1, y_above[target : target + 1, :], 0.0)


def add_faces(spread, z_rows, y_first, y_second, first, second):
    last = spread.shape[0] - 1
    flip_x, flip_y = (odd("gx"), odd("gy"))
    tile = row_columns(z_rows[...])
    y_below, y_above = (select(flip_y, y_first, y_second), select(flip_y, y_second, y_first))
    up = with_edges(spread[last], last, tile, y_below, y_above)
    down = with_edges(spread[0], 0, tile, y_below, y_above)
    first[...] = jnp.where(flip_x, down, up)
    second[...] = jnp.where(flip_x, up, down)


def add_all(
    inner_settled,
    outer_settled,
    spread,
    z_rows,
    y_first,
    y_second,
    corner_first,
    corner_second,
    x_second,
    x_first,
    after,
    new_mass,
):
    bx, by, bz = new_mass.shape
    flip_x, flip_y = (odd("gx"), odd("gy"))
    tile = row_columns(z_rows[...])
    y_below, y_above = (select(flip_y, y_first, y_second), select(flip_y, y_second, y_first))
    at = iota((8, bz), 1)
    found = []
    for rows, side, corner in (
        (y_below, 0, select(flip_y, corner_first, corner_second)),
        (y_above, 1, select(flip_y, corner_second, corner_first)),
    ):
        edge = corner[:, by + side : by + side + 1]
        rows = rows + jnp.where(at == 0, edge[0:8, :], 0.0)
        found.append(rows + jnp.where(at == bz - 1, edge[8:16, :], 0.0))
    for x in range(bx):
        total = with_edges(spread[x + 1], x + 1, tile, *found)
        if x == 0:
            total = total + select(flip_x, x_first, x_second)
        if x == bx - 1:
            total = total + select(flip_x, x_second, x_first)
        if 0 < x < bx - 1:
            total = total + inner_settled[x - 1]
        else:
            total = total + outer_settled[0 if x == 0 else 1]
        new_mass[x] = total


def swapped(first, second, axis):
    devices = lax.axis_size(axis)
    ahead = [(i, (i + 1) % devices if i % 2 == 0 else i - 1) for i in range(devices)]
    behind = [(i, (i - 1) % devices if i % 2 == 0 else (i + 1) % devices) for i in range(devices)]
    return lax.ppermute(first, axis, ahead), lax.ppermute(second, axis, behind)


def both_ways(rows, lower):
    devices = lax.axis_size("gz")
    before = lax.ppermute(rows, "gz", [(i, (i + 1) % devices) for i in range(devices)])
    if devices == 2:
        return before
    after = lax.ppermute(rows, "gz", [(i, (i - 1) % devices) for i in range(devices)])
    return jnp.where(iota(rows.shape, 0) < lower, before, after)


remote = pl.BlockSpec(memory_space=pltpu.HBM)
anywhere = pl.BlockSpec(memory_space=pl.ANY)


def call(body, outs, specs=None, out_specs=None, scratch=(), cost=(0, 0), aliases=None):
    extra = {} if specs is None else {"in_specs": specs}
    if out_specs is not None:
        extra["out_specs"] = out_specs
    return pl.pallas_call(
        body,
        out_shape=[
            shape
            if isinstance(shape, jax.ShapeDtypeStruct)
            else jax.ShapeDtypeStruct(shape, jnp.float32)
            for shape in outs
        ],
        scratch_shapes=[
            pltpu.VMEM(shape, jnp.float32) if isinstance(shape, tuple) else shape
            for shape in scratch
        ],
        compiler_params=pltpu.CompilerParams(vmem_limit_bytes=40 * 1024 * 1024),
        input_output_aliases=aliases or {},
        cost_estimate=pl.CostEstimate(flops=cost[0], bytes_accessed=cost[1], transcendentals=0),
        **extra,
    )


def shards(populations, stretch, mass, flags, conv_source, conv_kind, conv_direction):
    bx, by, bz = flags.shape
    cells = bx * by * bz
    box, face, tile = ((bx, by, bz), (by, bz), (bx, by, lanes))

    stretch, flags, z_out, y_one, y_two, x_one, x_two = call(
        first_faces,
        [
            (6, *box),
            jax.ShapeDtypeStruct(box, jnp.int32),
            (8, bx * by),
            (4 * bx, bz),
            (4 * bx, bz),
            (4, *face),
            (4, *face),
        ],
        specs=[remote] * 2,
        scratch=[pltpu.SemaphoreType.DMA((2,))],
        cost=(10 * cells, 60 * cells),
    )(*(pltpu.with_memory_space_constraint(array, pltpu.HBM) for array in (stretch, flags)))
    first_x = swapped(x_one, x_two, "gx")
    z_first = both_ways(z_out, 3)
    y_first = swapped(y_one, y_two, "gy")

    entries = conv_source.shape[0]
    mark = (tall, lanes)
    (code,) = call(
        lambda *refs: conversions(*refs, columns=bz),
        [(bx * by, bz)],
        cost=(40 * cells, 4 * cells),
    )(*(array.reshape(1, entries) for array in (conv_source, conv_kind, conv_direction)))
    code = code.reshape(box)

    pops, flow = call(
        moments,
        [(19, *box), (5, *box)],
        specs=[remote],
        scratch=[pltpu.SemaphoreType.DMA((bx,))],
        cost=(60 * cells, 150 * cells),
    )(pltpu.with_memory_space_constraint(populations, pltpu.HBM))

    columns, rows = ((24, bx * by), (10 * bx, bz))
    sides_y = [(bx, 8, bz), (bx, 8, bz), tile]
    inside, ends = ((bx - 2, *face), (2, *face))
    inner_post, inner_shift = call(
        collide_inner,
        [(19, *inside), (3, *inside)],
        scratch=sides_y,
        cost=(150 * cells, 150 * cells),
    )(pops, stretch, flow, z_first, *y_first)
    outer_post, outer_shift, z_out, x_one, x_two, y_one, y_two = call(
        collide_outer,
        [(19, *ends), (3, *ends), columns, (5, *face), (5, *face), rows, rows],
        scratch=[(4, *face), (4, *face)] + sides_y + [box],
        cost=(150 * cells, 150 * cells),
    )(pops, stretch, flags, flow, *first_x, *y_first, z_first, inner_post)
    z_post = both_ways(z_out, sides)
    post_y = swapped(y_one, y_two, "gy")
    post_x = swapped(x_one, x_two, "gx")
    edges = (4 * (bz // lanes) + columns[0], lanes)
    x_one, x_two, corner = call(
        lambda *refs: forward_edges(*refs, bx=bx), [edges, edges, columns], cost=(4 * 10**9, 0)
    )(z_post, *post_y)
    corners = swapped(corner, corner, "gy")
    edges_x = swapped(x_one, x_two, "gx")

    rims = [(bx + 2, *face), (bx + 2, 16, bz), (bx + 2, 16, bz), (bx + 2, by, lanes)]
    posts = (inner_post, outer_post, inner_shift, outer_shift)
    inner, outer, totals, changes = call(
        stream_early,
        [(first_slanted, *inside), (first_slanted, *ends), box, box],
        scratch=rims,
        cost=(350 * cells, 200 * cells),
    )(*posts, flags, *post_y, z_post)
    (
        inner_slanted,
        outer_slanted,
        inner_settled,
        inner_excess,
        inner_heading,
        totals,
        changes,
    ) = call(
        stream_slanted,
        [(4, *inside), (4, *ends), inside, inside, inside, ends, ends],
        scratch=rims,
        cost=(100 * cells, 60 * cells),
    )(*posts, mass, flags, code, *post_y, z_post, *corners, totals, changes)
    new_stretch, inner_done = call(
        restretch_inner,
        [(6, *box), mark],
        out_specs=[remote, pl.BlockSpec()],
        scratch=[(6, *inside)] + sides_y + [pltpu.SemaphoreType.DMA],
        cost=(80 * cells, 40 * cells),
    )(stretch, flow, *post_y, z_post)
    late, v_one, v_two, outer_settled, spread, y_one, y_two, z_out = call(
        stream_late,
        [
            (5, *ends),
            (3, *face),
            (3, *face),
            ends,
            (bx + 2, *face),
            (8, bz),
            (8, bz),
            (16, bx * by),
        ],
        scratch=rims + [(5, *face), (5, *face), box, box],
        cost=(150 * cells, 100 * cells),
    )(
        outer_post,
        outer_shift,
        mass,
        flags,
        code,
        totals,
        changes,
        *first_x,
        *post_x[::-1],
        *edges_x,
        inner_excess,
        inner_heading,
        flow,
        inner_done,
    )
    z_last = both_ways(z_out, 8)
    last_y = swapped(y_one, y_two, "gy")
    last_corners = swapped(z_last, z_last, "gy")
    flow_x = swapped(v_one, v_two, "gx")
    x_one, x_two = call(add_faces, [face, face], cost=(4 * 10**9, 0))(spread, z_last, *last_y)
    last_x = swapped(x_one, x_two, "gx")
    new_stretch, fresh, outer_done = call(
        restretch_outer,
        [(6, *box), (19, *box), mark],
        specs=[pl.BlockSpec()] * 7 + [remote] + [pl.BlockSpec()] * 5,
        out_specs=[remote, remote, pl.BlockSpec()],
        scratch=[(6, *ends), (3, *face), (3, *face)]
        + sides_y
        + [pltpu.SemaphoreType.DMA((2,)), pltpu.SemaphoreType.DMA((32,))],
        cost=(80 * cells, 200 * cells),
        aliases={7: 0},
    )(
        stretch,
        flow,
        *flow_x,
        *post_y,
        z_post,
        new_stretch,
        inner,
        outer,
        inner_slanted,
        outer_slanted,
        late,
    )
    (new_mass,) = call(add_all, [box])(
        inner_settled, outer_settled, spread, z_last, *last_y, *last_corners, *last_x[::-1], outer_done
    )
    return (fresh, new_stretch, new_mass)


def solution(mesh):
    return jax.shard_map(
        shards,
        mesh=mesh,
        in_specs=(
            P(None, "gx", "gy", "gz"),
            P(None, "gx", "gy", "gz"),
            P("gx", "gy", "gz"),
            P("gx", "gy", "gz"),
            P(("gx", "gy", "gz")),
            P(("gx", "gy", "gz")),
            P(("gx", "gy", "gz")),
        ),
        out_specs=(P(None, "gx", "gy", "gz"), P(None, "gx", "gy", "gz"), P("gx", "gy", "gz")),
        check_vma=False,
    )
```

```python
import jax
import jax.numpy as jnp
from jax import lax
from jax.experimental import pallas as pl
from jax.experimental.pallas import tpu as pltpu
from jax.sharding import PartitionSpec as P

velocity_set = (
    (0, 0, 0),
    (1, 0, 0),
    (-1, 0, 0),
    (0, 1, 0),
    (0, -1, 0),
    (0, 0, 1),
    (0, 0, -1),
    (1, 1, 0),
    (-1, -1, 0),
    (1, -1, 0),
    (-1, 1, 0),
    (1, 0, 1),
    (-1, 0, -1),
    (1, 0, -1),
    (-1, 0, 1),
    (0, 1, 1),
    (0, -1, -1),
    (0, 1, -1),
    (0, -1, 1),
)
opposite_of = (0, 2, 1, 4, 3, 6, 5, 8, 7, 10, 9, 12, 11, 14, 13, 16, 15, 18, 17)
lattice_weights = (1.0 / 3.0,) + (1.0 / 18.0,) * 6 + (1.0 / 36.0,) * 12
symmetric_slot = ((0, 3, 4), (3, 1, 5), (4, 5, 2))
tensor_pairs = ((0, 0), (1, 1), (2, 2), (0, 1), (0, 2), (1, 2))
relax_time = 0.8
polymer_time = 8.0
polymer_coeff = 0.05


def moving(axis, sign):
    return tuple(index for index in range(19) if velocity_set[index][axis] == sign)


x_up, x_down = (moving(0, 1), moving(0, -1))
y_up, y_down = (moving(1, 1), moving(1, -1))
z_up, z_down = (moving(2, 1), moving(2, -1))
pairs = tuple(range(1, 19, 2))
gas_slot = 5
speed_slot = 6
edge_slot = 9
sides = 9
lanes = 128
tall = 8


def iota(shape, dim):
    return lax.broadcasted_iota(jnp.int32, shape, dim)


def wide(tile, width):
    return jnp.concatenate([tile] * (width // tile.shape[1]), axis=1)


def rows_of(load, chunk, chunks, step, edge):
    low = chunk * tall
    if step == 0:
        return load(low, low + tall)
    if step == 1 and chunk > 0:
        return load(low - 1, low + tall - 1)
    if step == -1 and chunk < chunks - 1:
        return load(low + 1, low + tall + 1)
    rows = load(low, low + tall)
    at = iota(rows.shape, 0)
    if step == 1:
        return jnp.where(at == 0, edge(), pltpu.roll(rows, 1, 0))
    return jnp.where(at == tall - 1, edge(), pltpu.roll(rows, tall - 1, 0))


def columns_of(rows, halo, lane, step):
    width = rows.shape[1]
    at = iota(rows.shape, 1)
    if step == 1:
        edge = wide(pltpu.roll(halo, (lanes - lane) % lanes, 1), width)
        return jnp.where(at == 0, edge, pltpu.roll(rows, 1, 1))
    edge = wide(pltpu.roll(halo, lanes - 1 - lane, 1), width)
    return jnp.where(at == width - 1, edge, pltpu.roll(rows, width - 1, 1))


def packed(high, low):
    at = iota(high[0].shape, 1)
    tile = jnp.zeros_like(high[0])
    for slot, part in enumerate(high):
        tile = jnp.where(at == slot, pltpu.roll(part, slot + 1, 1), tile)
    for place, part in enumerate(low):
        slot = len(high) + place
        tile = jnp.where(at == slot, pltpu.roll(part, slot, 1), tile)
    return tile


def along(index, vector):
    total = None
    for comp in range(3):
        sign = velocity_set[index][comp]
        if sign != 0:
            term = vector[comp] if sign > 0 else -vector[comp]
            total = term if total is None else total + term
    return total


def conversions(source, kind, heading, code, *, columns):
    count = source.shape[1]
    value = (heading[...] + 32 * kind[...]).astype(jnp.float32)
    row, column = (source[...] // columns, source[...] % columns)
    by_row = jnp.where(iota((code.shape[0], count), 0) == row, value, 0.0).astype(jnp.bfloat16)
    by_column = jnp.where(iota((columns, count), 0) == column, 1.0, 0.0).astype(jnp.bfloat16)
    code[...] = lax.dot_general(
        by_row, by_column, (((1,), (1,)), ((), ())), preferred_element_type=jnp.float32
    )


def odd(axis):
    return lax.rem(lax.axis_index(axis), 2) == 1


def select(chosen, first, second):
    return jnp.where(chosen, first[...], second[...])


def swap_rows(first, second, x, planes, high, low, flip):
    for slot, (top, bottom) in enumerate(zip(high, low)):
        by = top.shape[0]
        up, down = (top[by - 1 : by, :], bottom[0:1, :])
        at = slot * planes + x
        first[at : at + 1, :] = jnp.where(flip, down, up)
        second[at : at + 1, :] = jnp.where(flip, up, down)


def swapped_rows(first, second, slots, low_rows, high_rows, shift):
    flip = odd("gy")
    planes = low_rows.shape[0] - 2 * shift
    for x in range(planes):
        for place, slot in enumerate(slots):
            at = slot * planes + x
            one, two = (first[at : at + 1, :], second[at : at + 1, :])
            low_rows[x + shift, place : place + 1, :] = jnp.where(flip, one, two)
            high_rows[x + shift, place : place + 1, :] = jnp.where(flip, two, one)


def column_rows(tiles, count):
    return jnp.concatenate(tiles, axis=0).T[0:count, :]


def row_columns(rows):
    rest = jnp.zeros((lanes - rows.shape[0], rows.shape[1]), jnp.float32)
    return jnp.concatenate([rows, rest], axis=0).T


def first_faces(
    stretch_in,
    flags_in,
    stretch,
    flags,
    columns,
    y_first,
    y_second,
    x_first,
    x_second,
    sems,
):
    bx, by, bz = flags.shape
    flip_x, flip_y = (odd("gx"), odd("gy"))
    copies = [
        pltpu.make_async_copy(stretch_in, stretch, sems.at[0]),
        pltpu.make_async_copy(flags_in, flags, sems.at[1]),
    ]
    for copy in copies:
        copy.start()
    for copy in copies:
        copy.wait()
    tiles = []
    for x in range(bx):
        along_y = [stretch.at[symmetric_slot[comp][1], x] for comp in range(3)]
        swap_rows(y_first, y_second, x, bx, along_y, along_y, flip_y)
        fields = [stretch.at[symmetric_slot[comp][2], x] for comp in range(3)]
        tiles.append(
            packed(
                [field[:, bz - lanes : bz] for field in fields],
                [field[:, 0:lanes] for field in fields],
            )
        )
    columns[...] = column_rows(tiles, columns.shape[0])
    rest = y_first.shape[0] - 3 * bx
    y_first[3 * bx :, :] = jnp.zeros((rest, bz), jnp.float32)
    y_second[3 * bx :, :] = jnp.zeros((rest, bz), jnp.float32)
    for out, last in ((x_first, flip_x), (x_second, jnp.logical_not(flip_x))):
        for comp in range(3):
            slot = symmetric_slot[comp][0]
            out[comp] = jnp.where(last, stretch[slot, 0], stretch[slot, bx - 1])
        out[3] = jnp.where(jnp.where(last, flags[0], flags[bx - 1]) == 0, 1.0, 0.0)


def moments(pops_in, pops, flow, sems):
    bx, by = pops.shape[1:3]
    copies = [
        pltpu.make_async_copy(pops_in.at[:, x], pops.at[:, x], sems.at[x]) for x in range(bx)
    ]
    for copy in copies:
        copy.start()
    for x in range(bx):
        copies[x].wait()
        for chunk in range(by // tall):
            rows = pl.ds(chunk * tall, tall)
            part = [pops[index, x, rows, :] for index in range(19)]
            density = part[0]
            for index in range(1, 19):
                density = density + part[index]
            inverse = 1.0 / density
            for comp in range(3):
                total = None
                for index in pairs:
                    sign = velocity_set[index][comp]
                    if sign != 0:
                        term = part[index] - part[index + 1]
                        term = term if sign > 0 else -term
                        total = term if total is None else total + term
                flow[comp, x, rows, :] = total * inverse
            flow[3, x, rows, :] = density
            flow[4, x, rows, :] = inverse


def beside(ref, field, x, step, halo, slot):
    last = ref.shape[1] - 1
    if halo is None:
        return lambda low, high: ref[field, x + step, low:high, :]
    if isinstance(x, int):
        if 0 <= x + step <= last:
            return lambda low, high: ref[field, x + step, low:high, :]
        return lambda low, high: halo[slot, low:high, :]
    inside = jnp.clip(x + step, 0, last)
    beyond = x == (0 if step < 0 else last)
    return lambda low, high: jnp.where(
        beyond, halo[slot, low:high, :], ref[field, inside, low:high, :]
    )


def differences(
    ref, field, slots, x, chunk, chunks, below, above, y_below, y_above, z_halo, lane, side
):
    slot_x, slot_y, slot_z = slots
    low, high = (chunk * tall, chunk * tall + tall)

    def load(first, stop):
        return ref[field, x, first:stop, :]

    result = [None, None, None]
    if slot_x is not None:
        after = beside(ref, field, x, 1, above, slot_x)(low, high)
        before = beside(ref, field, x, -1, below, slot_x)(low, high)
        result[0] = after - before
    if slot_y is not None:
        after = rows_of(load, chunk, chunks, -1, lambda: y_above[x, slot_y : slot_y + 1, :])
        before = rows_of(load, chunk, chunks, 1, lambda: y_below[x, slot_y : slot_y + 1, :])
        result[1] = after - before
    if slot_z is not None:
        rows, halo = (load(low, high), z_halo[x, low:high, :])
        after = columns_of(rows, halo, lane + side + slot_z, -1)
        before = columns_of(rows, halo, lane + slot_z, 1)
        result[2] = after - before
    return result


def end_place(x, bx):
    return 0 if x == 0 else 1


def plane_of(inner, outer, field, x, bx):
    if 0 < x < bx - 1:
        return inner.at[field, x - 1]
    return outer.at[field, end_place(x, bx)]


def collide_plane(x, place, pops, stretch, flow, halos, post, shift):
    by = pops.shape[2]
    chunks = by // tall
    factor = 1.0 - 0.5 / relax_time
    rate = 1.0 / relax_time
    for chunk in range(chunks):
        rows = pl.ds(chunk * tall, tall)
        terms = [[], [], []]
        for field in range(6):
            slots = [None, None, None]
            for comp in range(3):
                for axis in range(3):
                    if symmetric_slot[comp][axis] == field:
                        slots[axis] = comp
            found = differences(stretch, field, slots, x, chunk, chunks, *halos)
            for axis in range(3):
                if slots[axis] is not None:
                    terms[slots[axis]].append(found[axis])
        force = [0.5 * polymer_coeff * (part[0] + part[1] + part[2]) for part in terms]
        density, half = (flow[3, x, rows, :], 0.5 * flow[4, x, rows, :])
        moved = [flow[comp, x, rows, :] + half * force[comp] for comp in range(3)]
        for comp in range(3):
            shift[comp, place, rows, :] = moved[comp]
        squared = moved[0] * moved[0] + moved[1] * moved[1] + moved[2] * moved[2]
        work = moved[0] * force[0] + moved[1] * force[1] + moved[2] * force[2]
        weight = rate * density
        common = weight - 1.5 * weight * squared - 3.0 * factor * work
        odd = [3.0 * weight * moved[comp] + 3.0 * factor * force[comp] for comp in range(3)]
        even = [4.5 * weight * moved[comp] + 9.0 * factor * force[comp] for comp in range(3)]
        keep = 1.0 - rate
        post[0, place, rows, :] = keep * pops[0, x, rows, :] + lattice_weights[0] * common
        for index in pairs:
            both = common + along(index, moved) * along(index, even)
            differ = along(index, odd)
            scale = lattice_weights[index]
            post[index, place, rows, :] = keep * pops[index, x, rows, :] + scale * (both + differ)
            post[index + 1, place, rows, :] = keep * pops[index + 1, x, rows, :] + scale * (
                both - differ
            )


def collide_inner(
    pops,
    stretch,
    flow,
    z_rows,
    y_first,
    y_second,
    post,
    shift,
    y_below,
    y_above,
    z_halo,
):
    swapped_rows(y_first, y_second, range(3), y_below, y_above, 0)
    z_halo[...] = row_columns(z_rows[...]).reshape(z_halo.shape)
    halos = (None, None, y_below, y_above, z_halo, 0, 3)

    def plane(x, carry):
        collide_plane(x, x - 1, pops, stretch, flow, halos, post, shift)
        return carry

    lax.fori_loop(1, pops.shape[1] - 1, plane, 0)


def collide_outer(
    pops,
    stretch,
    flags,
    flow,
    x_first,
    x_second,
    y_first,
    y_second,
    z_rows,
    inner,
    post,
    shift,
    columns,
    ahead,
    behind,
    up_first,
    up_second,
    below,
    above,
    y_below,
    y_above,
    z_halo,
    gas,
):
    bx, by, bz = flags.shape
    halos = (below, above, y_below, y_above, z_halo, 0, 3)
    flip_x, flip_y = (odd("gx"), odd("gy"))
    below[...] = select(flip_x, x_first, x_second)
    above[...] = select(flip_x, x_second, x_first)
    swapped_rows(y_first, y_second, range(3), y_below, y_above, 0)
    z_halo[...] = row_columns(z_rows[...]).reshape(z_halo.shape)
    for x in (0, bx - 1):
        collide_plane(x, end_place(x, bx), pops, stretch, flow, halos, post, shift)

    tiles = []
    for x in range(bx):
        gas[x] = jnp.where(flags[x] == 0, 1.0, 0.0)
        rest = [gas.at[x]] + [flow.at[comp, x] for comp in range(3)]

        def fields(indices):
            return [plane_of(inner, post, index, x, bx) for index in indices] + rest

        swap_rows(up_first, up_second, x, bx, fields(y_up), fields(y_down), flip_y)
        tiles.append(
            packed(
                [field[:, bz - lanes : bz] for field in fields(z_up)],
                [field[:, 0:lanes] for field in fields(z_down)],
            )
        )
    columns[...] = column_rows(tiles, columns.shape[0])
    rest = up_first.shape[0] - sides * bx
    up_first[sides * bx :, :] = jnp.zeros((rest, bz), jnp.float32)
    up_second[sides * bx :, :] = jnp.zeros((rest, bz), jnp.float32)
    for slot in range(5):
        up, down = (post[x_up[slot], 1], post[x_down[slot], 0])
        ahead[slot] = jnp.where(flip_x, down, up)
        behind[slot] = jnp.where(flip_x, up, down)
    for comp in range(3):
        ahead[5 + comp] = jnp.where(flip_x, flow[comp, 0], flow[comp, bx - 1])


def restretch_plane(x, place, stretch, flow, halos, updated):
    chunks = stretch.shape[2] // tall
    for chunk in range(chunks):
        rows = pl.ds(chunk * tall, tall)
        grad = [
            differences(
                flow, comp, (comp, comp, comp), x, chunk, chunks, *halos, speed_slot, sides
            )
            for comp in range(3)
        ]
        part = [stretch[slot, x, rows, :] for slot in range(6)]
        full = [part[slot] + 1.0 if slot < 3 else part[slot] for slot in range(6)]

        def product(row, col):
            total = grad[row][0] * full[symmetric_slot[0][col]]
            for inner in (1, 2):
                total = total + grad[row][inner] * full[symmetric_slot[inner][col]]
            return total

        for slot, (row, col) in enumerate(tensor_pairs):
            old = (1.0 - 1.0 / polymer_time) * part[slot]
            if row == col:
                updated[slot, place, rows, :] = old + product(row, col)
            else:
                updated[slot, place, rows, :] = old + 0.5 * (product(row, col) + product(col, row))


def restretch_inner(
    stretch,
    flow,
    y_first,
    y_second,
    z_rows,
    new_stretch,
    mark,
    updated,
    y_below,
    y_above,
    z_halo,
    sem,
):
    bx = stretch.shape[1]
    swapped_rows(y_first, y_second, range(speed_slot, sides), y_below, y_above, 0)
    z_halo[...] = row_columns(z_rows[...]).reshape(z_halo.shape)
    halos = (None, None, y_below, y_above, z_halo)

    def plane(x, carry):
        restretch_plane(x, x - 1, stretch, flow, halos, updated)
        return carry

    lax.fori_loop(1, bx - 1, plane, 0)
    copy = pltpu.make_async_copy(updated, new_stretch.at[:, 1 : bx - 1], sem)
    copy.start()
    mark[...] = jnp.zeros(mark.shape, jnp.float32)
    copy.wait()


def restretch_outer(
    stretch,
    flow,
    x_first,
    x_second,
    y_first,
    y_second,
    z_rows,
    inner_stretch,
    inner,
    outer,
    inner_slanted,
    outer_slanted,
    late,
    new_stretch,
    fresh,
    mark,
    updated,
    below,
    above,
    y_below,
    y_above,
    z_halo,
    sems,
    store_sems,
):
    bx = stretch.shape[1]
    moves = stored(inner, outer, inner_slanted, outer_slanted, late, fresh, store_sems)
    for copy in moves:
        copy.start()
    flip_x = odd("gx")
    for comp in range(3):
        below[comp] = jnp.where(flip_x, x_first[5 + comp], x_second[comp])
        above[comp] = jnp.where(flip_x, x_second[comp], x_first[5 + comp])
    swapped_rows(y_first, y_second, range(speed_slot, sides), y_below, y_above, 0)
    z_halo[...] = row_columns(z_rows[...]).reshape(z_halo.shape)
    halos = (below, above, y_below, y_above, z_halo)
    copies = []
    for place, x in enumerate((0, bx - 1)):
        restretch_plane(x, place, stretch, flow, halos, updated)
        copies.append(
            pltpu.make_async_copy(updated.at[:, place], new_stretch.at[:, x], sems.at[place])
        )
        copies[-1].start()
    mark[...] = jnp.zeros(mark.shape, jnp.float32)
    for copy in copies + moves:
        copy.wait()


def stored(inner, outer, inner_slanted, outer_slanted, late, fresh, sems):
    bx = fresh.shape[1]
    moves = [
        (inner, fresh.at[0:first_slanted, 1 : bx - 1]),
        (inner_slanted, fresh.at[first_slanted:, 1 : bx - 1]),
    ]
    for place, x in enumerate((0, bx - 1)):
        moves.append((outer_slanted.at[:, place], fresh.at[first_slanted:, x]))
        order = (x_up, x_down)[place]
        start = 0
        for index in order + (first_slanted,):
            if index > start:
                run = slice(start, index)
                moves.append((outer.at[run, place], fresh.at[run, x]))
            if index in order:
                moves.append((late.at[order.index(index), place], fresh.at[index, x]))
            start = index + 1
    return [
        pltpu.make_async_copy(source, target, sems.at[place])
        for place, (source, target) in enumerate(moves)
    ]


up_edges = ((0, y_up.index(7)), (0, gas_slot), (1, y_down.index(9)), (1, gas_slot))
down_edges = ((0, y_up.index(10)), (0, gas_slot), (1, y_down.index(8)), (1, gas_slot))


def forward_edges(z_rows, y_first, y_second, first_out, second_out, corner, *, bx):
    halves = y_first.shape[1] // lanes
    flip_x, flip_y = (odd("gx"), odd("gy"))
    for half in range(halves):
        cut = slice(half * lanes, half * lanes + lanes)
        for place in range(4):
            found = []
            for x, edges in ((bx - 1, up_edges), (0, down_edges)):
                side, slot = edges[place]
                row = slot * bx + x
                one = y_first[row : row + 1, cut]
                two = y_second[row : row + 1, cut]
                found.append(jnp.where(flip_y, one, two) if side == 0 else jnp.where(flip_y, two, one))
            at = half * 4 + place
            first_out[at : at + 1, :] = jnp.where(flip_x, found[1], found[0])
            second_out[at : at + 1, :] = jnp.where(flip_x, found[0], found[1])
    first_out[4 * halves :, :] = z_rows[...]
    second_out[4 * halves :, :] = z_rows[...]
    corner[...] = z_rows[...]


def own_halos(flags, y_first, y_second, z_rows, gas, low_rows, high_rows, columns):
    bx, by = flags.shape[:2]
    tile = row_columns(z_rows[...])
    swapped_rows(y_first, y_second, range(speed_slot), low_rows, high_rows, 1)
    for x in range(bx):
        gas[x + 1] = jnp.where(flags[x] == 0, 1.0, 0.0)
        columns[x + 1] = tile[x * by : x * by + by, :]


def own_corners(corner_first, corner_second, low_rows, high_rows):
    bx = low_rows.shape[0] - 2
    flip = odd("gy")
    corner_below = row_columns(select(flip, corner_first, corner_second))
    corner_above = row_columns(select(flip, corner_second, corner_first))
    by = corner_below.shape[0] // bx
    for x in range(bx):
        end = x * by + by - 1
        low_rows[x + 1, edge_slot : edge_slot + 1, 0:lanes] = corner_below[end : end + 1, :]
        high_rows[x + 1, edge_slot : edge_slot + 1, 0:lanes] = corner_above[
            x * by : x * by + 1, :
        ]


def pass_on(x, chunk, indices, source, leaving_of, speed, halos, fresh, place, total, change):
    gas, low_rows, high_rows, columns = halos
    by = gas.shape[1]
    chunks = by // tall
    rows = pl.ds(chunk * tall, tall)
    rest = 1.0 - 1.5 * (speed[0] * speed[0] + speed[1] * speed[1] + speed[2] * speed[2])
    equals = {}

    def moved(load, index, slot, lane):
        step_x, step_y, step_z = velocity_set[index]
        plane = x + 1 - step_x
        edges = low_rows if step_y == 1 else high_rows
        found = rows_of(load, chunk, chunks, step_y, lambda: edges[plane, slot : slot + 1, :])
        if step_z == 0:
            return found
        halo = rows_of(
            lambda low, high: columns[plane, low:high, :],
            chunk,
            chunks,
            step_y,
            lambda: edges[plane, edge_slot : edge_slot + 1, 0:lanes],
        )
        return columns_of(found, halo, lane, step_z)

    for index in indices:
        step_x, step_y, step_z = velocity_set[index]
        first = min(index, opposite_of[index])
        if first not in equals:
            proj = along(first, speed)
            equals[first] = 2.0 * lattice_weights[first] * (rest + 4.5 * proj * proj)
        slot, lane, gas_lane = (None, None, None)
        if step_y != 0:
            slot = (y_up if step_y == 1 else y_down).index(index)
        if step_z == 1:
            lane, gas_lane = (z_up.index(index), gas_slot)
        elif step_z == -1:
            lane, gas_lane = (sides + z_down.index(index), sides + gas_slot)
        field = source(index)
        marks = gas.at[x + 1 - step_x]
        arriving = moved(lambda low, high: field[low:high, :], index, slot, lane)
        from_gas = moved(lambda low, high: marks[low:high, :], index, gas_slot, gas_lane)
        leaving = leaving_of(opposite_of[index])[rows, :]
        open_side = from_gas > 0.5
        value = jnp.where(open_side, equals[first] - leaving, arriving)
        fresh(index)[place, rows, :] = value
        total = total + value
        change = change + jnp.where(open_side, 0.0, arriving - leaving)
    return total, change


def settle(x, rows, mass, flags, code, total, change):
    read = mass[x, rows, :] + jnp.where(flags[x, rows, :] == 1, change, 0.0)
    mark = code[x, rows, :]
    liquid = mark >= 32.0
    converts = mark > 0.0
    level = jnp.where(liquid, total, 0.0)
    excess = jnp.where(converts, read - level, 0.0)
    heading = jnp.where(liquid, mark - 32.0, mark)
    return jnp.where(converts, level, read), excess, heading


slanted = tuple(index for index in range(19) if velocity_set[index][1] * velocity_set[index][2])
first_slanted = slanted[0]


def from_inside(x, bx):
    found = [index for index in range(1, 19) if 0 <= x - velocity_set[index][0] < bx]
    return [index for index in found if index not in slanted]


def from_beyond(x, bx):
    return [index for index in range(1, 19) if not 0 <= x - velocity_set[index][0] < bx]


def stream_early(
    inner_post,
    outer_post,
    inner_shift,
    outer_shift,
    flags,
    y_first,
    y_second,
    z_rows,
    inner,
    outer,
    totals,
    changes,
    gas,
    low_rows,
    high_rows,
    columns,
):
    bx, by, bz = flags.shape
    halos = (gas, low_rows, high_rows, columns)
    own_halos(flags, y_first, y_second, z_rows, *halos)

    for x in range(bx):
        inside = 0 < x < bx - 1
        place = x - 1 if inside else end_place(x, bx)
        fresh = inner if inside else outer
        for chunk in range(by // tall):
            rows = pl.ds(chunk * tall, tall)
            total = plane_of(inner_post, outer_post, 0, x, bx)[rows, :]
            fresh[0, place, rows, :] = total
            total, change = pass_on(
                x,
                chunk,
                from_inside(x, bx),
                lambda index: plane_of(
                    inner_post, outer_post, index, x - velocity_set[index][0], bx
                ),
                lambda index: plane_of(inner_post, outer_post, index, x, bx),
                [plane_of(inner_shift, outer_shift, comp, x, bx)[rows, :] for comp in range(3)],
                halos,
                lambda index: fresh.at[index],
                place,
                total,
                jnp.zeros((tall, bz), jnp.float32),
            )
            totals[x, rows, :] = total
            changes[x, rows, :] = change


def stream_slanted(
    inner_post,
    outer_post,
    inner_shift,
    outer_shift,
    mass,
    flags,
    code,
    y_first,
    y_second,
    z_rows,
    corner_first,
    corner_second,
    totals,
    changes,
    inner,
    outer,
    settled,
    excess,
    heading,
    end_totals,
    end_changes,
    gas,
    low_rows,
    high_rows,
    columns,
):
    bx, by, bz = flags.shape
    halos = (gas, low_rows, high_rows, columns)
    own_halos(flags, y_first, y_second, z_rows, *halos)
    own_corners(corner_first, corner_second, low_rows, high_rows)

    for x in range(bx):
        inside = 0 < x < bx - 1
        place = x - 1 if inside else end_place(x, bx)
        fresh = inner if inside else outer
        for chunk in range(by // tall):
            rows = pl.ds(chunk * tall, tall)
            total, change = pass_on(
                x,
                chunk,
                slanted,
                lambda index: plane_of(inner_post, outer_post, index, x, bx),
                lambda index: plane_of(inner_post, outer_post, index, x, bx),
                [plane_of(inner_shift, outer_shift, comp, x, bx)[rows, :] for comp in range(3)],
                halos,
                lambda index: fresh.at[index - first_slanted],
                place,
                totals[x, rows, :],
                changes[x, rows, :],
            )
            if inside:
                now = settle(x, rows, mass, flags, code, total, change)
                settled[place, rows, :], excess[place, rows, :], heading[place, rows, :] = now
            else:
                end_totals[place, rows, :] = total
                end_changes[place, rows, :] = change


def stream_late(
    post,
    shift,
    mass,
    flags,
    code,
    totals,
    changes,
    gas_first,
    gas_second,
    x_first,
    x_second,
    edges_first,
    edges_second,
    inner_excess,
    inner_heading,
    flow,
    after,
    late,
    v_second,
    settled,
    spread,
    line_first,
    line_second,
    out_z,
    gas,
    low_rows,
    high_rows,
    columns,
    below,
    above,
    excess,
    heading,
):
    bx, by, bz = flags.shape
    halves = bz // lanes
    flip_x = odd("gx")
    halos = (gas, low_rows, high_rows, columns)

    for comp in range(3):
        up, down = (flow[comp, bx - 1], flow[comp, 0])
        v_second[comp] = jnp.where(flip_x, up, down)
    for slot in range(5):
        below[slot] = jnp.where(flip_x, x_first[slot], x_second[slot])
        above[slot] = jnp.where(flip_x, x_second[slot], x_first[slot])
    gas[0] = jnp.where(flip_x, gas_first[3], gas_second[3])
    gas[bx + 1] = jnp.where(flip_x, gas_second[3], gas_first[3])
    edges_below = select(flip_x, edges_first, edges_second)
    edges_above = select(flip_x, edges_second, edges_first)
    for found, at, x, edges in (
        (edges_below, 0, bx - 1, up_edges),
        (edges_above, bx + 1, 0, down_edges),
    ):
        for place, (side, slot) in enumerate(edges):
            line = jnp.concatenate(
                [found[half * 4 + place : half * 4 + place + 1, :] for half in range(halves)],
                axis=1,
            )
            (low_rows, high_rows)[side][at, slot : slot + 1, :] = line
        columns[at] = row_columns(found[4 * halves :, :])[x * by : x * by + by, :]
    for place, x in enumerate((0, bx - 1)):
        halo, order = ((below, x_up), (above, x_down))[place]
        for chunk in range(by // tall):
            rows = pl.ds(chunk * tall, tall)
            total, change = pass_on(
                x,
                chunk,
                from_beyond(x, bx),
                lambda index: halo.at[order.index(index)],
                lambda index: post.at[index, place],
                [shift[comp, place, rows, :] for comp in range(3)],
                halos,
                lambda index: late.at[order.index(index)],
                place,
                totals[place, rows, :],
                changes[place, rows, :],
            )
            now = settle(x, rows, mass, flags, code, total, change)
            settled[place, rows, :], excess[x, rows, :], heading[x, rows, :] = now
    for x in range(1, bx - 1):
        excess[x] = inner_excess[x - 1]
        heading[x] = inner_heading[x - 1]

    row_at, lane_at = (iota((by, bz), 0), iota((by, bz), 1))
    line_at = iota((1, bz), 1)
    tile_lane, line_lane = (iota((by, lanes), 1), iota((1, lanes), 1))

    def rows_up(rows):
        return jnp.where(row_at == 0, 0.0, pltpu.roll(rows, 1, 0))

    def rows_down(rows):
        return jnp.where(row_at == by - 1, 0.0, pltpu.roll(rows, by - 1, 0))

    def over(rows, at, step):
        if step == 1:
            return jnp.where(at == 0, 0.0, pltpu.roll(rows, 1, 1))
        return jnp.where(at == bz - 1, 0.0, pltpu.roll(rows, bz - 1, 1))

    def summed(parts):
        total = parts[0]
        for part in parts[1:]:
            total = total + part
        return total

    tile = jnp.zeros((by, lanes), jnp.float32)
    line_up = jnp.zeros((1, lanes), jnp.float32)
    line_down = jnp.zeros((1, lanes), jnp.float32)
    flip_y = odd("gy")
    line_first[...] = jnp.zeros(line_first.shape, jnp.float32)
    line_second[...] = jnp.zeros(line_second.shape, jnp.float32)
    for target in range(bx + 2):
        groups = {}
        for index in range(1, 19):
            step_x, step_y, step_z = velocity_set[index]
            x = target - 1 - step_x
            if 0 <= x < bx:
                part = jnp.where(heading[x] == float(index), excess[x], 0.0)
                groups.setdefault((step_y, step_z), []).append(part)
        groups = {key: summed(parts) for key, parts in groups.items()}
        total = jnp.zeros((by, bz), jnp.float32)
        line = {1: jnp.zeros((1, bz), jnp.float32), -1: jnp.zeros((1, bz), jnp.float32)}
        for step_z in (0, 1, -1):
            group = jnp.zeros((by, bz), jnp.float32)
            ends = {}
            if (0, step_z) in groups:
                group = group + groups[(0, step_z)]
            if (1, step_z) in groups:
                group = group + rows_up(groups[(1, step_z)])
                ends[1] = groups[(1, step_z)][by - 1 : by, :]
            if (-1, step_z) in groups:
                group = group + rows_down(groups[(-1, step_z)])
                ends[-1] = groups[(-1, step_z)][0:1, :]
            if step_z == 0:
                total = total + group
                for side in ends:
                    line[side] = line[side] + ends[side]
                continue
            total = total + over(group, lane_at, step_z)
            for side in ends:
                line[side] = line[side] + over(ends[side], line_at, step_z)
            if step_z == 1:
                spot, cut, roll = (target, slice(bz - lanes, bz), target + 1)
            else:
                spot, cut, roll = (8 + target, slice(0, lanes), 8 + target)
            tile = jnp.where(tile_lane == spot, pltpu.roll(group[:, cut], roll, 1), tile)
            if 1 in ends:
                line_up = jnp.where(
                    line_lane == spot, pltpu.roll(ends[1][:, cut], roll, 1), line_up
                )
            if -1 in ends:
                line_down = jnp.where(
                    line_lane == spot, pltpu.roll(ends[-1][:, cut], roll, 1), line_down
                )
        spread[target] = total
        line_first[target : target + 1, :] = jnp.where(flip_y, line[-1], line[1])
        line_second[target : target + 1, :] = jnp.where(flip_y, line[1], line[-1])
    rest = jnp.zeros((lanes - by - 2, lanes), jnp.float32)
    out_z[...] = column_rows([tile, line_up, line_down, rest], 16)


def with_edges(total, target, tile, y_below, y_above):
    by, bz = total.shape
    row_at, lane_at = (iota((by, bz), 0), iota((by, bz), 1))
    total = total + jnp.where(lane_at == 0, tile[0:by, target : target + 1], 0.0)
    total = total + jnp.where(lane_at == bz - 1, tile[0:by, 8 + target : 9 + target], 0.0)
    total = total + jnp.where(row_at == 0, y_below[target : target + 1, :], 0.0)
    return total + jnp.where(row_at == by - 1, y_above[target : target + 1, :], 0.0)


def add_faces(spread, z_rows, y_first, y_second, first, second):
    last = spread.shape[0] - 1
    flip_x, flip_y = (odd("gx"), odd("gy"))
    tile = row_columns(z_rows[...])
    y_below, y_above = (select(flip_y, y_first, y_second), select(flip_y, y_second, y_first))
    up = with_edges(spread[last], last, tile, y_below, y_above)
    down = with_edges(spread[0], 0, tile, y_below, y_above)
    first[...] = jnp.where(flip_x, down, up)
    second[...] = jnp.where(flip_x, up, down)


def add_all(
    inner_settled,
    outer_settled,
    spread,
    z_rows,
    y_first,
    y_second,
    corner_first,
    corner_second,
    x_second,
    x_first,
    after,
    new_mass,
):
    bx, by, bz = new_mass.shape
    flip_x, flip_y = (odd("gx"), odd("gy"))
    tile = row_columns(z_rows[...])
    y_below, y_above = (select(flip_y, y_first, y_second), select(flip_y, y_second, y_first))
    at = iota((8, bz), 1)
    found = []
    for rows, side, corner in (
        (y_below, 0, select(flip_y, corner_first, corner_second)),
        (y_above, 1, select(flip_y, corner_second, corner_first)),
    ):
        edge = corner[:, by + side : by + side + 1]
        rows = rows + jnp.where(at == 0, edge[0:8, :], 0.0)
        found.append(rows + jnp.where(at == bz - 1, edge[8:16, :], 0.0))
    for x in range(bx):
        total = with_edges(spread[x + 1], x + 1, tile, *found)
        if x == 0:
            total = total + select(flip_x, x_first, x_second)
        if x == bx - 1:
            total = total + select(flip_x, x_second, x_first)
        if 0 < x < bx - 1:
            total = total + inner_settled[x - 1]
        else:
            total = total + outer_settled[0 if x == 0 else 1]
        new_mass[x] = total


def swapped_ahead(array, axis):
    devices = lax.axis_size(axis)
    pairing = [(i, (i + 1) % devices if i % 2 == 0 else i - 1) for i in range(devices)]
    return lax.ppermute(array, axis, pairing)


def swapped_behind(array, axis):
    devices = lax.axis_size(axis)
    pairing = [(i, (i - 1) % devices if i % 2 == 0 else (i + 1) % devices) for i in range(devices)]
    return lax.ppermute(array, axis, pairing)


def swapped(first, second, axis):
    return swapped_ahead(first, axis), swapped_behind(second, axis)


def both_ways(rows, lower):
    devices = lax.axis_size("gz")
    before = lax.ppermute(rows, "gz", [(i, (i + 1) % devices) for i in range(devices)])
    if devices == 2:
        return before
    after = lax.ppermute(rows, "gz", [(i, (i - 1) % devices) for i in range(devices)])
    return jnp.where(iota(rows.shape, 0) < lower, before, after)


remote = pl.BlockSpec(memory_space=pltpu.HBM)
anywhere = pl.BlockSpec(memory_space=pl.ANY)


def call(body, outs, specs=None, out_specs=None, scratch=(), cost=(0, 0), aliases=None):
    extra = {} if specs is None else {"in_specs": specs}
    if out_specs is not None:
        extra["out_specs"] = out_specs
    return pl.pallas_call(
        body,
        out_shape=[
            shape
            if isinstance(shape, jax.ShapeDtypeStruct)
            else jax.ShapeDtypeStruct(shape, jnp.float32)
            for shape in outs
        ],
        scratch_shapes=[
            pltpu.VMEM(shape, jnp.float32) if isinstance(shape, tuple) else shape
            for shape in scratch
        ],
        compiler_params=pltpu.CompilerParams(vmem_limit_bytes=40 * 1024 * 1024),
        input_output_aliases=aliases or {},
        cost_estimate=pl.CostEstimate(flops=cost[0], bytes_accessed=cost[1], transcendentals=0),
        **extra,
    )


def shards(populations, stretch, mass, flags, conv_source, conv_kind, conv_direction):
    bx, by, bz = flags.shape
    cells = bx * by * bz
    box, face, tile = ((bx, by, bz), (by, bz), (bx, by, lanes))

    stretch, flags, z_out, y_one, y_two, x_one, x_two = call(
        first_faces,
        [
            (6, *box),
            jax.ShapeDtypeStruct(box, jnp.int32),
            (8, bx * by),
            (4 * bx, bz),
            (4 * bx, bz),
            (4, *face),
            (4, *face),
        ],
        specs=[remote] * 2,
        scratch=[pltpu.SemaphoreType.DMA((2,))],
        cost=(10 * cells, 60 * cells),
    )(*(pltpu.with_memory_space_constraint(array, pltpu.HBM) for array in (stretch, flags)))
    first_x = swapped(x_one, x_two, "gx")
    z_first = both_ways(z_out, 3)
    y_first = swapped(y_one, y_two, "gy")

    entries = conv_source.shape[0]
    mark = (tall, lanes)
    (code,) = call(
        lambda *refs: conversions(*refs, columns=bz),
        [(bx * by, bz)],
        cost=(40 * cells, 4 * cells),
    )(*(array.reshape(1, entries) for array in (conv_source, conv_kind, conv_direction)))
    code = code.reshape(box)

    pops, flow = call(
        moments,
        [(19, *box), (5, *box)],
        specs=[remote],
        scratch=[pltpu.SemaphoreType.DMA((bx,))],
        cost=(60 * cells, 150 * cells),
    )(pltpu.with_memory_space_constraint(populations, pltpu.HBM))

    columns, rows = ((24, bx * by), (10 * bx, bz))
    sides_y = [(bx, 8, bz), (bx, 8, bz), tile]
    inside, ends = ((bx - 2, *face), (2, *face))
    inner_post, inner_shift = call(
        collide_inner,
        [(19, *inside), (3, *inside)],
        scratch=sides_y,
        cost=(150 * cells, 150 * cells),
    )(pops, stretch, flow, z_first, *y_first)
    outer_post, outer_shift, z_out, x_one, x_two, y_one, y_two = call(
        collide_outer,
        [(19, *ends), (3, *ends), columns, (8, *face), (5, *face), rows, rows],
        scratch=[(4, *face), (4, *face)] + sides_y + [box],
        cost=(150 * cells, 150 * cells),
    )(pops, stretch, flags, flow, *first_x, *y_first, z_first, inner_post)
    z_post = both_ways(z_out, sides)
    post_y = swapped(y_one, y_two, "gy")
    post_x = swapped(x_one, x_two, "gx")
    edges = (4 * (bz // lanes) + columns[0], lanes)
    x_one, x_two, corner = call(
        lambda *refs: forward_edges(*refs, bx=bx), [edges, edges, columns], cost=(4 * 10**9, 0)
    )(z_post, *post_y)
    corners = swapped(corner, corner, "gy")
    edges_x = swapped(x_one, x_two, "gx")

    rims = [(bx + 2, *face), (bx + 2, 16, bz), (bx + 2, 16, bz), (bx + 2, by, lanes)]
    posts = (inner_post, outer_post, inner_shift, outer_shift)
    inner, outer, totals, changes = call(
        stream_early,
        [(first_slanted, *inside), (first_slanted, *ends), box, box],
        scratch=rims,
        cost=(350 * cells, 200 * cells),
    )(*posts, flags, *post_y, z_post)
    (
        inner_slanted,
        outer_slanted,
        inner_settled,
        inner_excess,
        inner_heading,
        totals,
        changes,
    ) = call(
        stream_slanted,
        [(4, *inside), (4, *ends), inside, inside, inside, ends, ends],
        scratch=rims,
        cost=(100 * cells, 60 * cells),
    )(*posts, mass, flags, code, *post_y, z_post, *corners, totals, changes)
    new_stretch, inner_done = call(
        restretch_inner,
        [(6, *box), mark],
        out_specs=[remote, pl.BlockSpec()],
        scratch=[(6, *inside)] + sides_y + [pltpu.SemaphoreType.DMA],
        cost=(80 * cells, 40 * cells),
    )(stretch, flow, *post_y, z_post)
    late, v_two, outer_settled, spread, y_one, y_two, z_out = call(
        stream_late,
        [
            (5, *ends),
            (3, *face),
            ends,
            (bx + 2, *face),
            (8, bz),
            (8, bz),
            (16, bx * by),
        ],
        scratch=rims + [(5, *face), (5, *face), box, box],
        cost=(150 * cells, 100 * cells),
    )(
        outer_post,
        outer_shift,
        mass,
        flags,
        code,
        totals,
        changes,
        *first_x,
        *post_x,
        *edges_x,
        inner_excess,
        inner_heading,
        flow,
        inner_done,
    )
    z_last = both_ways(z_out, 8)
    last_y = swapped(y_one, y_two, "gy")
    last_corners = swapped(z_last, z_last, "gy")
    flow_x = (post_x[0], swapped_behind(v_two, "gx"))
    x_one, x_two = call(add_faces, [face, face], cost=(4 * 10**9, 0))(spread, z_last, *last_y)
    last_x = swapped(x_one, x_two, "gx")
    new_stretch, fresh, outer_done = call(
        restretch_outer,
        [(6, *box), (19, *box), mark],
        specs=[pl.BlockSpec()] * 7 + [remote] + [pl.BlockSpec()] * 5,
        out_specs=[remote, remote, pl.BlockSpec()],
        scratch=[(6, *ends), (3, *face), (3, *face)]
        + sides_y
        + [pltpu.SemaphoreType.DMA((2,)), pltpu.SemaphoreType.DMA((32,))],
        cost=(80 * cells, 200 * cells),
        aliases={7: 0},
    )(
        stretch,
        flow,
        *flow_x,
        *post_y,
        z_post,
        new_stretch,
        inner,
        outer,
        inner_slanted,
        outer_slanted,
        late,
    )
    (new_mass,) = call(add_all, [box])(
        inner_settled, outer_settled, spread, z_last, *last_y, *last_corners, *last_x[::-1], outer_done
    )
    return (fresh, new_stretch, new_mass)


def solution(mesh):
    return jax.shard_map(
        shards,
        mesh=mesh,
        in_specs=(
            P(None, "gx", "gy", "gz"),
            P(None, "gx", "gy", "gz"),
            P("gx", "gy", "gz"),
            P("gx", "gy", "gz"),
            P(("gx", "gy", "gz")),
            P(("gx", "gy", "gz")),
            P(("gx", "gy", "gz")),
        ),
        out_specs=(P(None, "gx", "gy", "gz"), P(None, "gx", "gy", "gz"), P("gx", "gy", "gz")),
        check_vma=False,
    )
```

```python
import jax
import jax.numpy as jnp
from jax import lax
from jax.experimental import pallas as pl
from jax.experimental.pallas import tpu as pltpu
from jax.sharding import PartitionSpec as P

velocity_set = (
    (0, 0, 0),
    (1, 0, 0),
    (-1, 0, 0),
    (0, 1, 0),
    (0, -1, 0),
    (0, 0, 1),
    (0, 0, -1),
    (1, 1, 0),
    (-1, -1, 0),
    (1, -1, 0),
    (-1, 1, 0),
    (1, 0, 1),
    (-1, 0, -1),
    (1, 0, -1),
    (-1, 0, 1),
    (0, 1, 1),
    (0, -1, -1),
    (0, 1, -1),
    (0, -1, 1),
)
opposite_of = (0, 2, 1, 4, 3, 6, 5, 8, 7, 10, 9, 12, 11, 14, 13, 16, 15, 18, 17)
lattice_weights = (1.0 / 3.0,) + (1.0 / 18.0,) * 6 + (1.0 / 36.0,) * 12
symmetric_slot = ((0, 3, 4), (3, 1, 5), (4, 5, 2))
tensor_pairs = ((0, 0), (1, 1), (2, 2), (0, 1), (0, 2), (1, 2))
relax_time = 0.8
polymer_time = 8.0
polymer_coeff = 0.05


def moving(axis, sign):
    return tuple(index for index in range(19) if velocity_set[index][axis] == sign)


x_up, x_down = (moving(0, 1), moving(0, -1))
y_up, y_down = (moving(1, 1), moving(1, -1))
z_up, z_down = (moving(2, 1), moving(2, -1))
pairs = tuple(range(1, 19, 2))
gas_slot = 5
speed_slot = 6
edge_slot = 9
sides = 9
lanes = 128
tall = 8


def iota(shape, dim):
    return lax.broadcasted_iota(jnp.int32, shape, dim)


def wide(tile, width):
    return jnp.concatenate([tile] * (width // tile.shape[1]), axis=1)


def rows_of(load, chunk, chunks, step, edge):
    low = chunk * tall
    if step == 0:
        return load(low, low + tall)
    if step == 1 and chunk > 0:
        return load(low - 1, low + tall - 1)
    if step == -1 and chunk < chunks - 1:
        return load(low + 1, low + tall + 1)
    rows = load(low, low + tall)
    at = iota(rows.shape, 0)
    if step == 1:
        return jnp.where(at == 0, edge(), pltpu.roll(rows, 1, 0))
    return jnp.where(at == tall - 1, edge(), pltpu.roll(rows, tall - 1, 0))


def columns_of(rows, halo, lane, step):
    width = rows.shape[1]
    at = iota(rows.shape, 1)
    if step == 1:
        edge = wide(pltpu.roll(halo, (lanes - lane) % lanes, 1), width)
        return jnp.where(at == 0, edge, pltpu.roll(rows, 1, 1))
    edge = wide(pltpu.roll(halo, lanes - 1 - lane, 1), width)
    return jnp.where(at == width - 1, edge, pltpu.roll(rows, width - 1, 1))


def packed(high, low):
    at = iota(high[0].shape, 1)
    tile = jnp.zeros_like(high[0])
    for slot, part in enumerate(high):
        tile = jnp.where(at == slot, pltpu.roll(part, slot + 1, 1), tile)
    for place, part in enumerate(low):
        slot = len(high) + place
        tile = jnp.where(at == slot, pltpu.roll(part, slot, 1), tile)
    return tile


def along(index, vector):
    total = None
    for comp in range(3):
        sign = velocity_set[index][comp]
        if sign != 0:
            term = vector[comp] if sign > 0 else -vector[comp]
            total = term if total is None else total + term
    return total


def conversions(source, kind, heading, code, *, columns):
    count = source.shape[1]
    value = (heading[...] + 32 * kind[...]).astype(jnp.float32)
    row, column = (source[...] // columns, source[...] % columns)
    by_row = jnp.where(iota((code.shape[0], count), 0) == row, value, 0.0).astype(jnp.bfloat16)
    by_column = jnp.where(iota((columns, count), 0) == column, 1.0, 0.0).astype(jnp.bfloat16)
    code[...] = lax.dot_general(
        by_row, by_column, (((1,), (1,)), ((), ())), preferred_element_type=jnp.float32
    )


def odd(axis):
    return lax.rem(lax.axis_index(axis), 2) == 1


def select(chosen, first, second):
    return jnp.where(chosen, first[...], second[...])


def swap_rows(first, second, x, planes, high, low, flip):
    for slot, (top, bottom) in enumerate(zip(high, low)):
        by = top.shape[0]
        up, down = (top[by - 1 : by, :], bottom[0:1, :])
        at = slot * planes + x
        first[at : at + 1, :] = jnp.where(flip, down, up)
        second[at : at + 1, :] = jnp.where(flip, up, down)


def swapped_rows(first, second, slots, low_rows, high_rows, shift):
    flip = odd("gy")
    planes = low_rows.shape[0] - 2 * shift
    for x in range(planes):
        for place, slot in enumerate(slots):
            at = slot * planes + x
            one, two = (first[at : at + 1, :], second[at : at + 1, :])
            low_rows[x + shift, place : place + 1, :] = jnp.where(flip, one, two)
            high_rows[x + shift, place : place + 1, :] = jnp.where(flip, two, one)


def column_rows(tiles, count):
    return jnp.concatenate(tiles, axis=0).T[0:count, :]


def row_columns(rows):
    rest = jnp.zeros((lanes - rows.shape[0], rows.shape[1]), jnp.float32)
    return jnp.concatenate([rows, rest], axis=0).T


def first_faces(
    stretch_in,
    flags_in,
    stretch,
    flags,
    columns,
    y_first,
    y_second,
    x_first,
    x_second,
    sems,
):
    bx, by, bz = flags.shape
    flip_x, flip_y = (odd("gx"), odd("gy"))
    copies = [
        pltpu.make_async_copy(stretch_in, stretch, sems.at[0]),
        pltpu.make_async_copy(flags_in, flags, sems.at[1]),
    ]
    for copy in copies:
        copy.start()
    for copy in copies:
        copy.wait()
    tiles = []
    for x in range(bx):
        along_y = [stretch.at[symmetric_slot[comp][1], x] for comp in range(3)]
        swap_rows(y_first, y_second, x, bx, along_y, along_y, flip_y)
        fields = [stretch.at[symmetric_slot[comp][2], x] for comp in range(3)]
        tiles.append(
            packed(
                [field[:, bz - lanes : bz] for field in fields],
                [field[:, 0:lanes] for field in fields],
            )
        )
    columns[...] = column_rows(tiles, columns.shape[0])
    rest = y_first.shape[0] - 3 * bx
    y_first[3 * bx :, :] = jnp.zeros((rest, bz), jnp.float32)
    y_second[3 * bx :, :] = jnp.zeros((rest, bz), jnp.float32)
    for out, last in ((x_first, flip_x), (x_second, jnp.logical_not(flip_x))):
        for comp in range(3):
            slot = symmetric_slot[comp][0]
            out[comp] = jnp.where(last, stretch[slot, 0], stretch[slot, bx - 1])
        out[3] = jnp.where(jnp.where(last, flags[0], flags[bx - 1]) == 0, 1.0, 0.0)


def moments(pops_in, pops, flow, sems):
    bx, by = pops.shape[1:3]
    copies = [
        pltpu.make_async_copy(pops_in.at[:, x], pops.at[:, x], sems.at[x]) for x in range(bx)
    ]
    for copy in copies:
        copy.start()
    for x in range(bx):
        copies[x].wait()
        for chunk in range(by // tall):
            rows = pl.ds(chunk * tall, tall)
            part = [pops[index, x, rows, :] for index in range(19)]
            density = part[0]
            for index in range(1, 19):
                density = density + part[index]
            inverse = 1.0 / density
            for comp in range(3):
                total = None
                for index in pairs:
                    sign = velocity_set[index][comp]
                    if sign != 0:
                        term = part[index] - part[index + 1]
                        term = term if sign > 0 else -term
                        total = term if total is None else total + term
                flow[comp, x, rows, :] = total * inverse
            flow[3, x, rows, :] = density
            flow[4, x, rows, :] = inverse


def beside(ref, field, x, step, halo, slot):
    last = ref.shape[1] - 1
    if halo is None:
        return lambda low, high: ref[field, x + step, low:high, :]
    if isinstance(x, int):
        if 0 <= x + step <= last:
            return lambda low, high: ref[field, x + step, low:high, :]
        return lambda low, high: halo[slot, low:high, :]
    inside = jnp.clip(x + step, 0, last)
    beyond = x == (0 if step < 0 else last)
    return lambda low, high: jnp.where(
        beyond, halo[slot, low:high, :], ref[field, inside, low:high, :]
    )


def differences(
    ref, field, slots, x, chunk, chunks, below, above, y_below, y_above, z_halo, lane, side
):
    slot_x, slot_y, slot_z = slots
    low, high = (chunk * tall, chunk * tall + tall)

    def load(first, stop):
        return ref[field, x, first:stop, :]

    result = [None, None, None]
    if slot_x is not None:
        after = beside(ref, field, x, 1, above, slot_x)(low, high)
        before = beside(ref, field, x, -1, below, slot_x)(low, high)
        result[0] = after - before
    if slot_y is not None:
        after = rows_of(load, chunk, chunks, -1, lambda: y_above[x, slot_y : slot_y + 1, :])
        before = rows_of(load, chunk, chunks, 1, lambda: y_below[x, slot_y : slot_y + 1, :])
        result[1] = after - before
    if slot_z is not None:
        rows, halo = (load(low, high), z_halo[x, low:high, :])
        after = columns_of(rows, halo, lane + side + slot_z, -1)
        before = columns_of(rows, halo, lane + slot_z, 1)
        result[2] = after - before
    return result


def end_place(x, bx):
    return 0 if x == 0 else 1


def plane_of(inner, outer, field, x, bx):
    if 0 < x < bx - 1:
        return inner.at[field, x - 1]
    return outer.at[field, end_place(x, bx)]


def collide_plane(x, place, pops, stretch, flow, halos, post, shift):
    by = pops.shape[2]
    chunks = by // tall
    factor = 1.0 - 0.5 / relax_time
    rate = 1.0 / relax_time
    for chunk in range(chunks):
        rows = pl.ds(chunk * tall, tall)
        terms = [[], [], []]
        for field in range(6):
            slots = [None, None, None]
            for comp in range(3):
                for axis in range(3):
                    if symmetric_slot[comp][axis] == field:
                        slots[axis] = comp
            found = differences(stretch, field, slots, x, chunk, chunks, *halos)
            for axis in range(3):
                if slots[axis] is not None:
                    terms[slots[axis]].append(found[axis])
        force = [0.5 * polymer_coeff * (part[0] + part[1] + part[2]) for part in terms]
        density, half = (flow[3, x, rows, :], 0.5 * flow[4, x, rows, :])
        moved = [flow[comp, x, rows, :] + half * force[comp] for comp in range(3)]
        for comp in range(3):
            shift[comp, place, rows, :] = moved[comp]
        squared = moved[0] * moved[0] + moved[1] * moved[1] + moved[2] * moved[2]
        work = moved[0] * force[0] + moved[1] * force[1] + moved[2] * force[2]
        weight = rate * density
        common = weight - 1.5 * weight * squared - 3.0 * factor * work
        odd = [3.0 * weight * moved[comp] + 3.0 * factor * force[comp] for comp in range(3)]
        even = [4.5 * weight * moved[comp] + 9.0 * factor * force[comp] for comp in range(3)]
        keep = 1.0 - rate
        post[0, place, rows, :] = keep * pops[0, x, rows, :] + lattice_weights[0] * common
        for index in pairs:
            both = common + along(index, moved) * along(index, even)
            differ = along(index, odd)
            scale = lattice_weights[index]
            post[index, place, rows, :] = keep * pops[index, x, rows, :] + scale * (both + differ)
            post[index + 1, place, rows, :] = keep * pops[index + 1, x, rows, :] + scale * (
                both - differ
            )


def collide_inner(
    pops,
    stretch,
    flow,
    z_rows,
    y_first,
    y_second,
    post,
    shift,
    y_below,
    y_above,
    z_halo,
):
    swapped_rows(y_first, y_second, range(3), y_below, y_above, 0)
    z_halo[...] = row_columns(z_rows[...]).reshape(z_halo.shape)
    halos = (None, None, y_below, y_above, z_halo, 0, 3)

    def plane(x, carry):
        collide_plane(x, x - 1, pops, stretch, flow, halos, post, shift)
        return carry

    lax.fori_loop(1, pops.shape[1] - 1, plane, 0)


def collide_outer(
    pops,
    stretch,
    flags,
    flow,
    x_first,
    x_second,
    y_first,
    y_second,
    z_rows,
    inner,
    post,
    shift,
    columns,
    ahead,
    behind,
    up_first,
    up_second,
    below,
    above,
    y_below,
    y_above,
    z_halo,
    gas,
):
    bx, by, bz = flags.shape
    halos = (below, above, y_below, y_above, z_halo, 0, 3)
    flip_x, flip_y = (odd("gx"), odd("gy"))
    below[...] = select(flip_x, x_first, x_second)
    above[...] = select(flip_x, x_second, x_first)
    swapped_rows(y_first, y_second, range(3), y_below, y_above, 0)
    z_halo[...] = row_columns(z_rows[...]).reshape(z_halo.shape)
    for x in (0, bx - 1):
        collide_plane(x, end_place(x, bx), pops, stretch, flow, halos, post, shift)

    tiles = []
    for x in range(bx):
        gas[x] = jnp.where(flags[x] == 0, 1.0, 0.0)
        rest = [gas.at[x]] + [flow.at[comp, x] for comp in range(3)]

        def fields(indices):
            return [plane_of(inner, post, index, x, bx) for index in indices] + rest

        swap_rows(up_first, up_second, x, bx, fields(y_up), fields(y_down), flip_y)
        tiles.append(
            packed(
                [field[:, bz - lanes : bz] for field in fields(z_up)],
                [field[:, 0:lanes] for field in fields(z_down)],
            )
        )
    columns[...] = column_rows(tiles, columns.shape[0])
    rest = up_first.shape[0] - sides * bx
    up_first[sides * bx :, :] = jnp.zeros((rest, bz), jnp.float32)
    up_second[sides * bx :, :] = jnp.zeros((rest, bz), jnp.float32)
    for slot in range(5):
        up, down = (post[x_up[slot], 1], post[x_down[slot], 0])
        ahead[slot] = jnp.where(flip_x, down, up)
        behind[slot] = jnp.where(flip_x, up, down)
    behind[5] = jnp.where(flip_x, flow[0, bx - 1], flow[0, 0])


def restretch_plane(x, place, stretch, flow, halos, updated):
    chunks = stretch.shape[2] // tall
    for chunk in range(chunks):
        rows = pl.ds(chunk * tall, tall)
        grad = [
            differences(
                flow, comp, (comp, comp, comp), x, chunk, chunks, *halos, speed_slot, sides
            )
            for comp in range(3)
        ]
        part = [stretch[slot, x, rows, :] for slot in range(6)]
        full = [part[slot] + 1.0 if slot < 3 else part[slot] for slot in range(6)]

        def product(row, col):
            total = grad[row][0] * full[symmetric_slot[0][col]]
            for inner in (1, 2):
                total = total + grad[row][inner] * full[symmetric_slot[inner][col]]
            return total

        for slot, (row, col) in enumerate(tensor_pairs):
            old = (1.0 - 1.0 / polymer_time) * part[slot]
            if row == col:
                updated[slot, place, rows, :] = old + product(row, col)
            else:
                updated[slot, place, rows, :] = old + 0.5 * (product(row, col) + product(col, row))


def restretch_inner(
    stretch,
    flow,
    y_first,
    y_second,
    z_rows,
    new_stretch,
    mark,
    updated,
    y_below,
    y_above,
    z_halo,
    sem,
):
    bx = stretch.shape[1]
    swapped_rows(y_first, y_second, range(speed_slot, sides), y_below, y_above, 0)
    z_halo[...] = row_columns(z_rows[...]).reshape(z_halo.shape)
    halos = (None, None, y_below, y_above, z_halo)

    def plane(x, carry):
        restretch_plane(x, x - 1, stretch, flow, halos, updated)
        return carry

    lax.fori_loop(1, bx - 1, plane, 0)
    copy = pltpu.make_async_copy(updated, new_stretch.at[:, 1 : bx - 1], sem)
    copy.start()
    mark[...] = jnp.zeros(mark.shape, jnp.float32)
    copy.wait()


def restretch_outer(
    stretch,
    flow,
    x_first,
    x_second,
    post_second,
    y_first,
    y_second,
    z_rows,
    inner_stretch,
    new_stretch,
    mark,
    updated,
    below,
    above,
    y_below,
    y_above,
    z_halo,
    sems,
):
    bx = stretch.shape[1]
    flip_x = odd("gx")
    for comp in range(3):
        second = post_second[5] if comp == 0 else x_second[comp - 1]
        below[comp] = jnp.where(flip_x, x_first[comp], second)
        above[comp] = jnp.where(flip_x, second, x_first[comp])
    swapped_rows(y_first, y_second, range(speed_slot, sides), y_below, y_above, 0)
    z_halo[...] = row_columns(z_rows[...]).reshape(z_halo.shape)
    halos = (below, above, y_below, y_above, z_halo)
    copies = []
    for place, x in enumerate((0, bx - 1)):
        restretch_plane(x, place, stretch, flow, halos, updated)
        copies.append(
            pltpu.make_async_copy(updated.at[:, place], new_stretch.at[:, x], sems.at[place])
        )
        copies[-1].start()
    mark[...] = jnp.zeros(mark.shape, jnp.float32)
    for copy in copies:
        copy.wait()


def store(inner, outer, inner_slanted, outer_slanted, late, fresh, sems):
    bx = fresh.shape[1]
    moves = [
        (inner, fresh.at[0:first_slanted, 1 : bx - 1]),
        (inner_slanted, fresh.at[first_slanted:, 1 : bx - 1]),
    ]
    for place, x in enumerate((0, bx - 1)):
        moves.append((outer_slanted.at[:, place], fresh.at[first_slanted:, x]))
        order = (x_up, x_down)[place]
        start = 0
        for index in order + (first_slanted,):
            if index > start:
                run = slice(start, index)
                moves.append((outer.at[run, place], fresh.at[run, x]))
            if index in order:
                moves.append((late.at[order.index(index), place], fresh.at[index, x]))
            start = index + 1
    copies = [
        pltpu.make_async_copy(source, target, sems.at[place])
        for place, (source, target) in enumerate(moves)
    ]
    for copy in copies:
        copy.start()
    for copy in copies:
        copy.wait()


up_edges = ((0, y_up.index(7)), (0, gas_slot), (1, y_down.index(9)), (1, gas_slot))
down_edges = ((0, y_up.index(10)), (0, gas_slot), (1, y_down.index(8)), (1, gas_slot))


def forward_edges(z_rows, y_first, y_second, first_out, second_out, corner, *, bx):
    halves = y_first.shape[1] // lanes
    flip_x, flip_y = (odd("gx"), odd("gy"))
    for half in range(halves):
        cut = slice(half * lanes, half * lanes + lanes)
        for place in range(4):
            found = []
            for x, edges in ((bx - 1, up_edges), (0, down_edges)):
                side, slot = edges[place]
                row = slot * bx + x
                one = y_first[row : row + 1, cut]
                two = y_second[row : row + 1, cut]
                found.append(jnp.where(flip_y, one, two) if side == 0 else jnp.where(flip_y, two, one))
            at = half * 4 + place
            first_out[at : at + 1, :] = jnp.where(flip_x, found[1], found[0])
            second_out[at : at + 1, :] = jnp.where(flip_x, found[0], found[1])
    first_out[4 * halves :, :] = z_rows[...]
    second_out[4 * halves :, :] = z_rows[...]
    corner[...] = z_rows[...]


def own_halos(flags, y_first, y_second, z_rows, gas, low_rows, high_rows, columns):
    bx, by = flags.shape[:2]
    tile = row_columns(z_rows[...])
    swapped_rows(y_first, y_second, range(speed_slot), low_rows, high_rows, 1)
    for x in range(bx):
        gas[x + 1] = jnp.where(flags[x] == 0, 1.0, 0.0)
        columns[x + 1] = tile[x * by : x * by + by, :]


def own_corners(corner_first, corner_second, low_rows, high_rows):
    bx = low_rows.shape[0] - 2
    flip = odd("gy")
    corner_below = row_columns(select(flip, corner_first, corner_second))
    corner_above = row_columns(select(flip, corner_second, corner_first))
    by = corner_below.shape[0] // bx
    for x in range(bx):
        end = x * by + by - 1
        low_rows[x + 1, edge_slot : edge_slot + 1, 0:lanes] = corner_below[end : end + 1, :]
        high_rows[x + 1, edge_slot : edge_slot + 1, 0:lanes] = corner_above[
            x * by : x * by + 1, :
        ]


def pass_on(x, chunk, indices, source, leaving_of, speed, halos, fresh, place, total, change):
    gas, low_rows, high_rows, columns = halos
    by = gas.shape[1]
    chunks = by // tall
    rows = pl.ds(chunk * tall, tall)
    rest = 1.0 - 1.5 * (speed[0] * speed[0] + speed[1] * speed[1] + speed[2] * speed[2])
    equals = {}

    def moved(load, index, slot, lane):
        step_x, step_y, step_z = velocity_set[index]
        plane = x + 1 - step_x
        edges = low_rows if step_y == 1 else high_rows
        found = rows_of(load, chunk, chunks, step_y, lambda: edges[plane, slot : slot + 1, :])
        if step_z == 0:
            return found
        halo = rows_of(
            lambda low, high: columns[plane, low:high, :],
            chunk,
            chunks,
            step_y,
            lambda: edges[plane, edge_slot : edge_slot + 1, 0:lanes],
        )
        return columns_of(found, halo, lane, step_z)

    for index in indices:
        step_x, step_y, step_z = velocity_set[index]
        first = min(index, opposite_of[index])
        if first not in equals:
            proj = along(first, speed)
            equals[first] = 2.0 * lattice_weights[first] * (rest + 4.5 * proj * proj)
        slot, lane, gas_lane = (None, None, None)
        if step_y != 0:
            slot = (y_up if step_y == 1 else y_down).index(index)
        if step_z == 1:
            lane, gas_lane = (z_up.index(index), gas_slot)
        elif step_z == -1:
            lane, gas_lane = (sides + z_down.index(index), sides + gas_slot)
        field = source(index)
        marks = gas.at[x + 1 - step_x]
        arriving = moved(lambda low, high: field[low:high, :], index, slot, lane)
        from_gas = moved(lambda low, high: marks[low:high, :], index, gas_slot, gas_lane)
        leaving = leaving_of(opposite_of[index])[rows, :]
        open_side = from_gas > 0.5
        value = jnp.where(open_side, equals[first] - leaving, arriving)
        fresh(index)[place, rows, :] = value
        total = total + value
        change = change + jnp.where(open_side, 0.0, arriving - leaving)
    return total, change


def settle(x, rows, mass, flags, code, total, change):
    read = mass[x, rows, :] + jnp.where(flags[x, rows, :] == 1, change, 0.0)
    mark = code[x, rows, :]
    liquid = mark >= 32.0
    converts = mark > 0.0
    level = jnp.where(liquid, total, 0.0)
    excess = jnp.where(converts, read - level, 0.0)
    heading = jnp.where(liquid, mark - 32.0, mark)
    return jnp.where(converts, level, read), excess, heading


slanted = tuple(index for index in range(19) if velocity_set[index][1] * velocity_set[index][2])
first_slanted = slanted[0]


def from_inside(x, bx):
    found = [index for index in range(1, 19) if 0 <= x - velocity_set[index][0] < bx]
    return [index for index in found if index not in slanted]


def from_beyond(x, bx):
    return [index for index in range(1, 19) if not 0 <= x - velocity_set[index][0] < bx]


def stream_early(
    inner_post,
    outer_post,
    inner_shift,
    outer_shift,
    flags,
    y_first,
    y_second,
    z_rows,
    inner,
    outer,
    totals,
    changes,
    gas,
    low_rows,
    high_rows,
    columns,
):
    bx, by, bz = flags.shape
    halos = (gas, low_rows, high_rows, columns)
    own_halos(flags, y_first, y_second, z_rows, *halos)

    for x in range(bx):
        inside = 0 < x < bx - 1
        place = x - 1 if inside else end_place(x, bx)
        fresh = inner if inside else outer
        for chunk in range(by // tall):
            rows = pl.ds(chunk * tall, tall)
            total = plane_of(inner_post, outer_post, 0, x, bx)[rows, :]
            fresh[0, place, rows, :] = total
            total, change = pass_on(
                x,
                chunk,
                from_inside(x, bx),
                lambda index: plane_of(
                    inner_post, outer_post, index, x - velocity_set[index][0], bx
                ),
                lambda index: plane_of(inner_post, outer_post, index, x, bx),
                [plane_of(inner_shift, outer_shift, comp, x, bx)[rows, :] for comp in range(3)],
                halos,
                lambda index: fresh.at[index],
                place,
                total,
                jnp.zeros((tall, bz), jnp.float32),
            )
            totals[x, rows, :] = total
            changes[x, rows, :] = change


def stream_slanted(
    inner_post,
    outer_post,
    inner_shift,
    outer_shift,
    mass,
    flags,
    code,
    y_first,
    y_second,
    z_rows,
    corner_first,
    corner_second,
    totals,
    changes,
    inner,
    outer,
    settled,
    excess,
    heading,
    end_totals,
    end_changes,
    gas,
    low_rows,
    high_rows,
    columns,
):
    bx, by, bz = flags.shape
    halos = (gas, low_rows, high_rows, columns)
    own_halos(flags, y_first, y_second, z_rows, *halos)
    own_corners(corner_first, corner_second, low_rows, high_rows)

    for x in range(bx):
        inside = 0 < x < bx - 1
        place = x - 1 if inside else end_place(x, bx)
        fresh = inner if inside else outer
        for chunk in range(by // tall):
            rows = pl.ds(chunk * tall, tall)
            total, change = pass_on(
                x,
                chunk,
                slanted,
                lambda index: plane_of(inner_post, outer_post, index, x, bx),
                lambda index: plane_of(inner_post, outer_post, index, x, bx),
                [plane_of(inner_shift, outer_shift, comp, x, bx)[rows, :] for comp in range(3)],
                halos,
                lambda index: fresh.at[index - first_slanted],
                place,
                totals[x, rows, :],
                changes[x, rows, :],
            )
            if inside:
                now = settle(x, rows, mass, flags, code, total, change)
                settled[place, rows, :], excess[place, rows, :], heading[place, rows, :] = now
            else:
                end_totals[place, rows, :] = total
                end_changes[place, rows, :] = change


def stream_late(
    post,
    shift,
    mass,
    flags,
    code,
    totals,
    changes,
    gas_first,
    gas_second,
    x_first,
    x_second,
    edges_first,
    edges_second,
    inner_excess,
    inner_heading,
    flow,
    after,
    late,
    v_first,
    v_second,
    settled,
    spread,
    line_first,
    line_second,
    out_z,
    gas,
    low_rows,
    high_rows,
    columns,
    below,
    above,
    excess,
    heading,
):
    bx, by, bz = flags.shape
    halves = bz // lanes
    flip_x = odd("gx")
    halos = (gas, low_rows, high_rows, columns)

    for comp in range(3):
        up, down = (flow[comp, bx - 1], flow[comp, 0])
        v_first[comp] = jnp.where(flip_x, down, up)
        if comp > 0:
            v_second[comp - 1] = jnp.where(flip_x, up, down)
    for slot in range(5):
        below[slot] = jnp.where(flip_x, x_first[slot], x_second[slot])
        above[slot] = jnp.where(flip_x, x_second[slot], x_first[slot])
    gas[0] = jnp.where(flip_x, gas_first[3], gas_second[3])
    gas[bx + 1] = jnp.where(flip_x, gas_second[3], gas_first[3])
    edges_below = select(flip_x, edges_first, edges_second)
    edges_above = select(flip_x, edges_second, edges_first)
    for found, at, x, edges in (
        (edges_below, 0, bx - 1, up_edges),
        (edges_above, bx + 1, 0, down_edges),
    ):
        for place, (side, slot) in enumerate(edges):
            line = jnp.concatenate(
                [found[half * 4 + place : half * 4 + place + 1, :] for half in range(halves)],
                axis=1,
            )
            (low_rows, high_rows)[side][at, slot : slot + 1, :] = line
        columns[at] = row_columns(found[4 * halves :, :])[x * by : x * by + by, :]
    for place, x in enumerate((0, bx - 1)):
        halo, order = ((below, x_up), (above, x_down))[place]
        for chunk in range(by // tall):
            rows = pl.ds(chunk * tall, tall)
            total, change = pass_on(
                x,
                chunk,
                from_beyond(x, bx),
                lambda index: halo.at[order.index(index)],
                lambda index: post.at[index, place],
                [shift[comp, place, rows, :] for comp in range(3)],
                halos,
                lambda index: late.at[order.index(index)],
                place,
                totals[place, rows, :],
                changes[place, rows, :],
            )
            now = settle(x, rows, mass, flags, code, total, change)
            settled[place, rows, :], excess[x, rows, :], heading[x, rows, :] = now
    for x in range(1, bx - 1):
        excess[x] = inner_excess[x - 1]
        heading[x] = inner_heading[x - 1]

    row_at, lane_at = (iota((by, bz), 0), iota((by, bz), 1))
    line_at = iota((1, bz), 1)
    tile_lane, line_lane = (iota((by, lanes), 1), iota((1, lanes), 1))

    def rows_up(rows):
        return jnp.where(row_at == 0, 0.0, pltpu.roll(rows, 1, 0))

    def rows_down(rows):
        return jnp.where(row_at == by - 1, 0.0, pltpu.roll(rows, by - 1, 0))

    def over(rows, at, step):
        if step == 1:
            return jnp.where(at == 0, 0.0, pltpu.roll(rows, 1, 1))
        return jnp.where(at == bz - 1, 0.0, pltpu.roll(rows, bz - 1, 1))

    def summed(parts):
        total = parts[0]
        for part in parts[1:]:
            total = total + part
        return total

    tile = jnp.zeros((by, lanes), jnp.float32)
    line_up = jnp.zeros((1, lanes), jnp.float32)
    line_down = jnp.zeros((1, lanes), jnp.float32)
    flip_y = odd("gy")
    line_first[...] = jnp.zeros(line_first.shape, jnp.float32)
    line_second[...] = jnp.zeros(line_second.shape, jnp.float32)
    for target in range(bx + 2):
        groups = {}
        for index in range(1, 19):
            step_x, step_y, step_z = velocity_set[index]
            x = target - 1 - step_x
            if 0 <= x < bx:
                part = jnp.where(heading[x] == float(index), excess[x], 0.0)
                groups.setdefault((step_y, step_z), []).append(part)
        groups = {key: summed(parts) for key, parts in groups.items()}
        total = jnp.zeros((by, bz), jnp.float32)
        line = {1: jnp.zeros((1, bz), jnp.float32), -1: jnp.zeros((1, bz), jnp.float32)}
        for step_z in (0, 1, -1):
            group = jnp.zeros((by, bz), jnp.float32)
            ends = {}
            if (0, step_z) in groups:
                group = group + groups[(0, step_z)]
            if (1, step_z) in groups:
                group = group + rows_up(groups[(1, step_z)])
                ends[1] = groups[(1, step_z)][by - 1 : by, :]
            if (-1, step_z) in groups:
                group = group + rows_down(groups[(-1, step_z)])
                ends[-1] = groups[(-1, step_z)][0:1, :]
            if step_z == 0:
                total = total + group
                for side in ends:
                    line[side] = line[side] + ends[side]
                continue
            total = total + over(group, lane_at, step_z)
            for side in ends:
                line[side] = line[side] + over(ends[side], line_at, step_z)
            if step_z == 1:
                spot, cut, roll = (target, slice(bz - lanes, bz), target + 1)
            else:
                spot, cut, roll = (8 + target, slice(0, lanes), 8 + target)
            tile = jnp.where(tile_lane == spot, pltpu.roll(group[:, cut], roll, 1), tile)
            if 1 in ends:
                line_up = jnp.where(
                    line_lane == spot, pltpu.roll(ends[1][:, cut], roll, 1), line_up
                )
            if -1 in ends:
                line_down = jnp.where(
                    line_lane == spot, pltpu.roll(ends[-1][:, cut], roll, 1), line_down
                )
        spread[target] = total
        line_first[target : target + 1, :] = jnp.where(flip_y, line[-1], line[1])
        line_second[target : target + 1, :] = jnp.where(flip_y, line[1], line[-1])
    rest = jnp.zeros((lanes - by - 2, lanes), jnp.float32)
    out_z[...] = column_rows([tile, line_up, line_down, rest], 16)


def with_edges(total, target, tile, y_below, y_above):
    by, bz = total.shape
    row_at, lane_at = (iota((by, bz), 0), iota((by, bz), 1))
    total = total + jnp.where(lane_at == 0, tile[0:by, target : target + 1], 0.0)
    total = total + jnp.where(lane_at == bz - 1, tile[0:by, 8 + target : 9 + target], 0.0)
    total = total + jnp.where(row_at == 0, y_below[target : target + 1, :], 0.0)
    return total + jnp.where(row_at == by - 1, y_above[target : target + 1, :], 0.0)


def add_faces(spread, z_rows, y_first, y_second, first, second):
    last = spread.shape[0] - 1
    flip_x, flip_y = (odd("gx"), odd("gy"))
    tile = row_columns(z_rows[...])
    y_below, y_above = (select(flip_y, y_first, y_second), select(flip_y, y_second, y_first))
    up = with_edges(spread[last], last, tile, y_below, y_above)
    down = with_edges(spread[0], 0, tile, y_below, y_above)
    first[...] = jnp.where(flip_x, down, up)
    second[...] = jnp.where(flip_x, up, down)


def add_all(
    inner_settled,
    outer_settled,
    spread,
    z_rows,
    y_first,
    y_second,
    corner_first,
    corner_second,
    x_second,
    x_first,
    after,
    new_mass,
):
    bx, by, bz = new_mass.shape
    flip_x, flip_y = (odd("gx"), odd("gy"))
    tile = row_columns(z_rows[...])
    y_below, y_above = (select(flip_y, y_first, y_second), select(flip_y, y_second, y_first))
    at = iota((8, bz), 1)
    found = []
    for rows, side, corner in (
        (y_below, 0, select(flip_y, corner_first, corner_second)),
        (y_above, 1, select(flip_y, corner_second, corner_first)),
    ):
        edge = corner[:, by + side : by + side + 1]
        rows = rows + jnp.where(at == 0, edge[0:8, :], 0.0)
        found.append(rows + jnp.where(at == bz - 1, edge[8:16, :], 0.0))
    for x in range(bx):
        total = with_edges(spread[x + 1], x + 1, tile, *found)
        if x == 0:
            total = total + select(flip_x, x_first, x_second)
        if x == bx - 1:
            total = total + select(flip_x, x_second, x_first)
        if 0 < x < bx - 1:
            total = total + inner_settled[x - 1]
        else:
            total = total + outer_settled[0 if x == 0 else 1]
        new_mass[x] = total


def swapped(first, second, axis):
    devices = lax.axis_size(axis)
    ahead = [(i, (i + 1) % devices if i % 2 == 0 else i - 1) for i in range(devices)]
    behind = [(i, (i - 1) % devices if i % 2 == 0 else (i + 1) % devices) for i in range(devices)]
    return lax.ppermute(first, axis, ahead), lax.ppermute(second, axis, behind)


def both_ways(rows, lower):
    devices = lax.axis_size("gz")
    before = lax.ppermute(rows, "gz", [(i, (i + 1) % devices) for i in range(devices)])
    if devices == 2:
        return before
    after = lax.ppermute(rows, "gz", [(i, (i - 1) % devices) for i in range(devices)])
    return jnp.where(iota(rows.shape, 0) < lower, before, after)


remote = pl.BlockSpec(memory_space=pltpu.HBM)
anywhere = pl.BlockSpec(memory_space=pl.ANY)


def call(body, outs, specs=None, out_specs=None, scratch=(), cost=(0, 0), aliases=None):
    extra = {} if specs is None else {"in_specs": specs}
    if out_specs is not None:
        extra["out_specs"] = out_specs
    return pl.pallas_call(
        body,
        out_shape=[
            shape
            if isinstance(shape, jax.ShapeDtypeStruct)
            else jax.ShapeDtypeStruct(shape, jnp.float32)
            for shape in outs
        ],
        scratch_shapes=[
            pltpu.VMEM(shape, jnp.float32) if isinstance(shape, tuple) else shape
            for shape in scratch
        ],
        compiler_params=pltpu.CompilerParams(vmem_limit_bytes=40 * 1024 * 1024),
        input_output_aliases=aliases or {},
        cost_estimate=pl.CostEstimate(flops=cost[0], bytes_accessed=cost[1], transcendentals=0),
        **extra,
    )


def shards(populations, stretch, mass, flags, conv_source, conv_kind, conv_direction):
    bx, by, bz = flags.shape
    cells = bx * by * bz
    box, face, tile = ((bx, by, bz), (by, bz), (bx, by, lanes))

    stretch, flags, z_out, y_one, y_two, x_one, x_two = call(
        first_faces,
        [
            (6, *box),
            jax.ShapeDtypeStruct(box, jnp.int32),
            (8, bx * by),
            (4 * bx, bz),
            (4 * bx, bz),
            (4, *face),
            (4, *face),
        ],
        specs=[remote] * 2,
        scratch=[pltpu.SemaphoreType.DMA((2,))],
        cost=(10 * cells, 60 * cells),
    )(*(pltpu.with_memory_space_constraint(array, pltpu.HBM) for array in (stretch, flags)))
    first_x = swapped(x_one, x_two, "gx")
    z_first = both_ways(z_out, 3)
    y_first = swapped(y_one, y_two, "gy")

    entries = conv_source.shape[0]
    mark = (tall, lanes)
    (code,) = call(
        lambda *refs: conversions(*refs, columns=bz),
        [(bx * by, bz)],
        cost=(40 * cells, 4 * cells),
    )(*(array.reshape(1, entries) for array in (conv_source, conv_kind, conv_direction)))
    code = code.reshape(box)

    pops, flow = call(
        moments,
        [(19, *box), (5, *box)],
        specs=[remote],
        scratch=[pltpu.SemaphoreType.DMA((bx,))],
        cost=(60 * cells, 150 * cells),
    )(pltpu.with_memory_space_constraint(populations, pltpu.HBM))

    columns, rows = ((24, bx * by), (10 * bx, bz))
    sides_y = [(bx, 8, bz), (bx, 8, bz), tile]
    inside, ends = ((bx - 2, *face), (2, *face))
    inner_post, inner_shift = call(
        collide_inner,
        [(19, *inside), (3, *inside)],
        scratch=sides_y,
        cost=(150 * cells, 150 * cells),
    )(pops, stretch, flow, z_first, *y_first)
    outer_post, outer_shift, z_out, x_one, x_two, y_one, y_two = call(
        collide_outer,
        [(19, *ends), (3, *ends), columns, (5, *face), (6, *face), rows, rows],
        scratch=[(4, *face), (4, *face)] + sides_y + [box],
        cost=(150 * cells, 150 * cells),
    )(pops, stretch, flags, flow, *first_x, *y_first, z_first, inner_post)
    z_post = both_ways(z_out, sides)
    post_y = swapped(y_one, y_two, "gy")
    post_x = swapped(x_one, x_two, "gx")
    edges = (4 * (bz // lanes) + columns[0], lanes)
    x_one, x_two, corner = call(
        lambda *refs: forward_edges(*refs, bx=bx), [edges, edges, columns], cost=(135 * 10**7, 0)
    )(z_post, *post_y)
    corners = swapped(corner, corner, "gy")
    edges_x = swapped(x_one, x_two, "gx")

    rims = [(bx + 2, *face), (bx + 2, 16, bz), (bx + 2, 16, bz), (bx + 2, by, lanes)]
    posts = (inner_post, outer_post, inner_shift, outer_shift)
    inner, outer, totals, changes = call(
        stream_early,
        [(first_slanted, *inside), (first_slanted, *ends), box, box],
        scratch=rims,
        cost=(350 * cells, 200 * cells),
    )(*posts, flags, *post_y, z_post)
    (
        inner_slanted,
        outer_slanted,
        inner_settled,
        inner_excess,
        inner_heading,
        totals,
        changes,
    ) = call(
        stream_slanted,
        [(4, *inside), (4, *ends), inside, inside, inside, ends, ends],
        scratch=rims,
        cost=(100 * cells, 60 * cells),
    )(*posts, mass, flags, code, *post_y, z_post, *corners, totals, changes)
    new_stretch, inner_done = call(
        restretch_inner,
        [(6, *box), mark],
        out_specs=[remote, pl.BlockSpec()],
        scratch=[(6, *inside)] + sides_y + [pltpu.SemaphoreType.DMA],
        cost=(80 * cells, 40 * cells),
    )(stretch, flow, *post_y, z_post)
    late, v_one, v_two, outer_settled, spread, y_one, y_two, z_out = call(
        stream_late,
        [
            (5, *ends),
            (3, *face),
            (2, *face),
            ends,
            (bx + 2, *face),
            (8, bz),
            (8, bz),
            (16, bx * by),
        ],
        scratch=rims + [(5, *face), (5, *face), box, box],
        cost=(150 * cells, 100 * cells),
    )(
        outer_post,
        outer_shift,
        mass,
        flags,
        code,
        totals,
        changes,
        *first_x,
        *post_x,
        *edges_x,
        inner_excess,
        inner_heading,
        flow,
        inner_done,
    )
    z_last = both_ways(z_out, 8)
    last_y = swapped(y_one, y_two, "gy")
    last_corners = swapped(z_last, z_last, "gy")
    flow_x = swapped(v_one, v_two, "gx")
    x_one, x_two = call(add_faces, [face, face], cost=(4 * 10**9, 0))(spread, z_last, *last_y)
    last_x = swapped(x_one, x_two, "gx")
    (fresh,) = call(
        store,
        [(19, *box)],
        out_specs=[remote],
        scratch=[pltpu.SemaphoreType.DMA((32,))],
        cost=(0, 160 * cells),
    )(inner, outer, inner_slanted, outer_slanted, late)
    new_stretch, outer_done = call(
        restretch_outer,
        [(6, *box), mark],
        specs=[pl.BlockSpec()] * 8 + [remote],
        out_specs=[remote, pl.BlockSpec()],
        scratch=[(6, *ends), (3, *face), (3, *face)]
        + sides_y
        + [pltpu.SemaphoreType.DMA((2,))],
        cost=(80 * cells, 40 * cells),
        aliases={8: 0},
    )(stretch, flow, *flow_x, post_x[1], *post_y, z_post, new_stretch)
    (new_mass,) = call(add_all, [box])(
        inner_settled, outer_settled, spread, z_last, *last_y, *last_corners, *last_x[::-1], outer_done
    )
    return (fresh, new_stretch, new_mass)


def solution(mesh):
    return jax.shard_map(
        shards,
        mesh=mesh,
        in_specs=(
            P(None, "gx", "gy", "gz"),
            P(None, "gx", "gy", "gz"),
            P("gx", "gy", "gz"),
            P("gx", "gy", "gz"),
            P(("gx", "gy", "gz")),
            P(("gx", "gy", "gz")),
            P(("gx", "gy", "gz")),
        ),
        out_specs=(P(None, "gx", "gy", "gz"), P(None, "gx", "gy", "gz"), P("gx", "gy", "gz")),
        check_vma=False,
    )
```

```python
import jax
import jax.numpy as jnp
from jax import lax
from jax.experimental import pallas as pl
from jax.experimental.pallas import tpu as pltpu
from jax.sharding import PartitionSpec as P

velocity_set = (
    (0, 0, 0),
    (1, 0, 0),
    (-1, 0, 0),
    (0, 1, 0),
    (0, -1, 0),
    (0, 0, 1),
    (0, 0, -1),
    (1, 1, 0),
    (-1, -1, 0),
    (1, -1, 0),
    (-1, 1, 0),
    (1, 0, 1),
    (-1, 0, -1),
    (1, 0, -1),
    (-1, 0, 1),
    (0, 1, 1),
    (0, -1, -1),
    (0, 1, -1),
    (0, -1, 1),
)
opposite_of = (0, 2, 1, 4, 3, 6, 5, 8, 7, 10, 9, 12, 11, 14, 13, 16, 15, 18, 17)
lattice_weights = (1.0 / 3.0,) + (1.0 / 18.0,) * 6 + (1.0 / 36.0,) * 12
symmetric_slot = ((0, 3, 4), (3, 1, 5), (4, 5, 2))
tensor_pairs = ((0, 0), (1, 1), (2, 2), (0, 1), (0, 2), (1, 2))
relax_time = 0.8
polymer_time = 8.0
polymer_coeff = 0.05


def moving(axis, sign):
    return tuple(index for index in range(19) if velocity_set[index][axis] == sign)


x_up, x_down = (moving(0, 1), moving(0, -1))
y_up, y_down = (moving(1, 1), moving(1, -1))
z_up, z_down = (moving(2, 1), moving(2, -1))
pairs = tuple(range(1, 19, 2))
gas_slot = 5
speed_slot = 6
edge_slot = 9
sides = 9
lanes = 128
tall = 8


def iota(shape, dim):
    return lax.broadcasted_iota(jnp.int32, shape, dim)


def wide(tile, width):
    return jnp.concatenate([tile] * (width // tile.shape[1]), axis=1)


def rows_of(load, chunk, chunks, step, edge):
    low = chunk * tall
    if step == 0:
        return load(low, low + tall)
    if step == 1 and chunk > 0:
        return load(low - 1, low + tall - 1)
    if step == -1 and chunk < chunks - 1:
        return load(low + 1, low + tall + 1)
    rows = load(low, low + tall)
    at = iota(rows.shape, 0)
    if step == 1:
        return jnp.where(at == 0, edge(), pltpu.roll(rows, 1, 0))
    return jnp.where(at == tall - 1, edge(), pltpu.roll(rows, tall - 1, 0))


def columns_of(rows, halo, lane, step):
    width = rows.shape[1]
    at = iota(rows.shape, 1)
    if step == 1:
        edge = wide(pltpu.roll(halo, (lanes - lane) % lanes, 1), width)
        return jnp.where(at == 0, edge, pltpu.roll(rows, 1, 1))
    edge = wide(pltpu.roll(halo, lanes - 1 - lane, 1), width)
    return jnp.where(at == width - 1, edge, pltpu.roll(rows, width - 1, 1))


def packed(high, low):
    at = iota(high[0].shape, 1)
    tile = jnp.zeros_like(high[0])
    for slot, part in enumerate(high):
        tile = jnp.where(at == slot, pltpu.roll(part, slot + 1, 1), tile)
    for place, part in enumerate(low):
        slot = len(high) + place
        tile = jnp.where(at == slot, pltpu.roll(part, slot, 1), tile)
    return tile


def along(index, vector):
    total = None
    for comp in range(3):
        sign = velocity_set[index][comp]
        if sign != 0:
            term = vector[comp] if sign > 0 else -vector[comp]
            total = term if total is None else total + term
    return total


def conversions(source, kind, heading, code, mark, *, columns):
    count = source.shape[1]
    value = (heading[...] + 32 * kind[...]).astype(jnp.float32)
    row, column = (source[...] // columns, source[...] % columns)
    by_row = jnp.where(iota((code.shape[0], count), 0) == row, value, 0.0).astype(jnp.bfloat16)
    by_column = jnp.where(iota((columns, count), 0) == column, 1.0, 0.0).astype(jnp.bfloat16)
    code[...] = lax.dot_general(
        by_row, by_column, (((1,), (1,)), ((), ())), preferred_element_type=jnp.float32
    )
    mark[...] = jnp.zeros(mark.shape, jnp.float32)


def odd(axis):
    return lax.rem(lax.axis_index(axis), 2) == 1


def select(chosen, first, second):
    return jnp.where(chosen, first[...], second[...])


def swap_rows(first, second, x, planes, high, low, flip):
    for slot, (top, bottom) in enumerate(zip(high, low)):
        by = top.shape[0]
        up, down = (top[by - 1 : by, :], bottom[0:1, :])
        at = slot * planes + x
        first[at : at + 1, :] = jnp.where(flip, down, up)
        second[at : at + 1, :] = jnp.where(flip, up, down)


def swapped_rows(first, second, slots, low_rows, high_rows, shift):
    flip = odd("gy")
    planes = low_rows.shape[0] - 2 * shift
    for x in range(planes):
        for place, slot in enumerate(slots):
            at = slot * planes + x
            one, two = (first[at : at + 1, :], second[at : at + 1, :])
            low_rows[x + shift, place : place + 1, :] = jnp.where(flip, one, two)
            high_rows[x + shift, place : place + 1, :] = jnp.where(flip, two, one)


def column_rows(tiles, count):
    return jnp.concatenate(tiles, axis=0).T[0:count, :]


def row_columns(rows):
    rest = jnp.zeros((lanes - rows.shape[0], rows.shape[1]), jnp.float32)
    return jnp.concatenate([rows, rest], axis=0).T


def first_faces(
    stretch_in,
    flags_in,
    stretch,
    flags,
    columns,
    y_first,
    y_second,
    x_first,
    x_second,
    sems,
):
    bx, by, bz = flags.shape
    flip_x, flip_y = (odd("gx"), odd("gy"))
    copies = [
        pltpu.make_async_copy(stretch_in, stretch, sems.at[0]),
        pltpu.make_async_copy(flags_in, flags, sems.at[1]),
    ]
    for copy in copies:
        copy.start()
    for copy in copies:
        copy.wait()
    tiles = []
    for x in range(bx):
        along_y = [stretch.at[symmetric_slot[comp][1], x] for comp in range(3)]
        swap_rows(y_first, y_second, x, bx, along_y, along_y, flip_y)
        fields = [stretch.at[symmetric_slot[comp][2], x] for comp in range(3)]
        tiles.append(
            packed(
                [field[:, bz - lanes : bz] for field in fields],
                [field[:, 0:lanes] for field in fields],
            )
        )
    columns[...] = column_rows(tiles, columns.shape[0])
    rest = y_first.shape[0] - 3 * bx
    y_first[3 * bx :, :] = jnp.zeros((rest, bz), jnp.float32)
    y_second[3 * bx :, :] = jnp.zeros((rest, bz), jnp.float32)
    for out, last in ((x_first, flip_x), (x_second, jnp.logical_not(flip_x))):
        for comp in range(3):
            slot = symmetric_slot[comp][0]
            out[comp] = jnp.where(last, stretch[slot, 0], stretch[slot, bx - 1])
        out[3] = jnp.where(jnp.where(last, flags[0], flags[bx - 1]) == 0, 1.0, 0.0)


def moments(pops_in, pops, flow, sems):
    bx, by = pops.shape[1:3]
    copies = [
        pltpu.make_async_copy(pops_in.at[:, x], pops.at[:, x], sems.at[x]) for x in range(bx)
    ]
    for copy in copies:
        copy.start()
    for x in range(bx):
        copies[x].wait()
        for chunk in range(by // tall):
            rows = pl.ds(chunk * tall, tall)
            part = [pops[index, x, rows, :] for index in range(19)]
            density = part[0]
            for index in range(1, 19):
                density = density + part[index]
            inverse = 1.0 / density
            for comp in range(3):
                total = None
                for index in pairs:
                    sign = velocity_set[index][comp]
                    if sign != 0:
                        term = part[index] - part[index + 1]
                        term = term if sign > 0 else -term
                        total = term if total is None else total + term
                flow[comp, x, rows, :] = total * inverse
            flow[3, x, rows, :] = density
            flow[4, x, rows, :] = inverse


def beside(ref, field, x, step, halo, slot):
    last = ref.shape[1] - 1
    if halo is None:
        return lambda low, high: ref[field, x + step, low:high, :]
    if isinstance(x, int):
        if 0 <= x + step <= last:
            return lambda low, high: ref[field, x + step, low:high, :]
        return lambda low, high: halo[slot, low:high, :]
    inside = jnp.clip(x + step, 0, last)
    beyond = x == (0 if step < 0 else last)
    return lambda low, high: jnp.where(
        beyond, halo[slot, low:high, :], ref[field, inside, low:high, :]
    )


def differences(
    ref, field, slots, x, chunk, chunks, below, above, y_below, y_above, z_halo, lane, side
):
    slot_x, slot_y, slot_z = slots
    low, high = (chunk * tall, chunk * tall + tall)

    def load(first, stop):
        return ref[field, x, first:stop, :]

    result = [None, None, None]
    if slot_x is not None:
        after = beside(ref, field, x, 1, above, slot_x)(low, high)
        before = beside(ref, field, x, -1, below, slot_x)(low, high)
        result[0] = after - before
    if slot_y is not None:
        after = rows_of(load, chunk, chunks, -1, lambda: y_above[x, slot_y : slot_y + 1, :])
        before = rows_of(load, chunk, chunks, 1, lambda: y_below[x, slot_y : slot_y + 1, :])
        result[1] = after - before
    if slot_z is not None:
        rows, halo = (load(low, high), z_halo[x, low:high, :])
        after = columns_of(rows, halo, lane + side + slot_z, -1)
        before = columns_of(rows, halo, lane + slot_z, 1)
        result[2] = after - before
    return result


def end_place(x, bx):
    return 0 if x == 0 else 1


def plane_of(inner, outer, field, x, bx):
    if 0 < x < bx - 1:
        return inner.at[field, x - 1]
    return outer.at[field, end_place(x, bx)]


def collide_plane(x, place, pops, stretch, flow, halos, post, shift):
    by = pops.shape[2]
    chunks = by // tall
    factor = 1.0 - 0.5 / relax_time
    rate = 1.0 / relax_time
    for chunk in range(chunks):
        rows = pl.ds(chunk * tall, tall)
        terms = [[], [], []]
        for field in range(6):
            slots = [None, None, None]
            for comp in range(3):
                for axis in range(3):
                    if symmetric_slot[comp][axis] == field:
                        slots[axis] = comp
            found = differences(stretch, field, slots, x, chunk, chunks, *halos)
            for axis in range(3):
                if slots[axis] is not None:
                    terms[slots[axis]].append(found[axis])
        force = [0.5 * polymer_coeff * (part[0] + part[1] + part[2]) for part in terms]
        density, half = (flow[3, x, rows, :], 0.5 * flow[4, x, rows, :])
        moved = [flow[comp, x, rows, :] + half * force[comp] for comp in range(3)]
        for comp in range(3):
            shift[comp, place, rows, :] = moved[comp]
        squared = moved[0] * moved[0] + moved[1] * moved[1] + moved[2] * moved[2]
        work = moved[0] * force[0] + moved[1] * force[1] + moved[2] * force[2]
        weight = rate * density
        common = weight - 1.5 * weight * squared - 3.0 * factor * work
        odd = [3.0 * weight * moved[comp] + 3.0 * factor * force[comp] for comp in range(3)]
        even = [4.5 * weight * moved[comp] + 9.0 * factor * force[comp] for comp in range(3)]
        keep = 1.0 - rate
        post[0, place, rows, :] = keep * pops[0, x, rows, :] + lattice_weights[0] * common
        for index in pairs:
            both = common + along(index, moved) * along(index, even)
            differ = along(index, odd)
            scale = lattice_weights[index]
            post[index, place, rows, :] = keep * pops[index, x, rows, :] + scale * (both + differ)
            post[index + 1, place, rows, :] = keep * pops[index + 1, x, rows, :] + scale * (
                both - differ
            )


def collide_inner(
    pops,
    stretch,
    flow,
    z_rows,
    y_first,
    y_second,
    post,
    shift,
    y_below,
    y_above,
    z_halo,
):
    swapped_rows(y_first, y_second, range(3), y_below, y_above, 0)
    z_halo[...] = row_columns(z_rows[...]).reshape(z_halo.shape)
    halos = (None, None, y_below, y_above, z_halo, 0, 3)

    def plane(x, carry):
        collide_plane(x, x - 1, pops, stretch, flow, halos, post, shift)
        return carry

    lax.fori_loop(1, pops.shape[1] - 1, plane, 0)


def collide_outer(
    pops,
    stretch,
    flags,
    flow,
    x_first,
    x_second,
    y_first,
    y_second,
    z_rows,
    inner,
    post,
    shift,
    columns,
    ahead,
    behind,
    up_first,
    up_second,
    below,
    above,
    y_below,
    y_above,
    z_halo,
    gas,
):
    bx, by, bz = flags.shape
    halos = (below, above, y_below, y_above, z_halo, 0, 3)
    flip_x, flip_y = (odd("gx"), odd("gy"))
    below[...] = select(flip_x, x_first, x_second)
    above[...] = select(flip_x, x_second, x_first)
    swapped_rows(y_first, y_second, range(3), y_below, y_above, 0)
    z_halo[...] = row_columns(z_rows[...]).reshape(z_halo.shape)
    for x in (0, bx - 1):
        collide_plane(x, end_place(x, bx), pops, stretch, flow, halos, post, shift)

    tiles = []
    for x in range(bx):
        gas[x] = jnp.where(flags[x] == 0, 1.0, 0.0)
        rest = [gas.at[x]] + [flow.at[comp, x] for comp in range(3)]

        def fields(indices):
            return [plane_of(inner, post, index, x, bx) for index in indices] + rest

        swap_rows(up_first, up_second, x, bx, fields(y_up), fields(y_down), flip_y)
        tiles.append(
            packed(
                [field[:, bz - lanes : bz] for field in fields(z_up)],
                [field[:, 0:lanes] for field in fields(z_down)],
            )
        )
    columns[...] = column_rows(tiles, columns.shape[0])
    rest = up_first.shape[0] - sides * bx
    up_first[sides * bx :, :] = jnp.zeros((rest, bz), jnp.float32)
    up_second[sides * bx :, :] = jnp.zeros((rest, bz), jnp.float32)
    for slot in range(5):
        up, down = (post[x_up[slot], 1], post[x_down[slot], 0])
        ahead[slot] = jnp.where(flip_x, down, up)
        behind[slot] = jnp.where(flip_x, up, down)
    for comp in range(3):
        behind[5 + comp] = jnp.where(flip_x, flow[comp, bx - 1], flow[comp, 0])


def restretch_plane(x, place, stretch, flow, halos, updated):
    chunks = stretch.shape[2] // tall
    for chunk in range(chunks):
        rows = pl.ds(chunk * tall, tall)
        grad = [
            differences(
                flow, comp, (comp, comp, comp), x, chunk, chunks, *halos, speed_slot, sides
            )
            for comp in range(3)
        ]
        part = [stretch[slot, x, rows, :] for slot in range(6)]
        full = [part[slot] + 1.0 if slot < 3 else part[slot] for slot in range(6)]

        def product(row, col):
            total = grad[row][0] * full[symmetric_slot[0][col]]
            for inner in (1, 2):
                total = total + grad[row][inner] * full[symmetric_slot[inner][col]]
            return total

        for slot, (row, col) in enumerate(tensor_pairs):
            old = (1.0 - 1.0 / polymer_time) * part[slot]
            if row == col:
                updated[slot, place, rows, :] = old + product(row, col)
            else:
                updated[slot, place, rows, :] = old + 0.5 * (product(row, col) + product(col, row))


def restretch_inner(
    stretch,
    flow,
    y_first,
    y_second,
    z_rows,
    new_stretch,
    mark,
    updated,
    y_below,
    y_above,
    z_halo,
    sem,
):
    bx = stretch.shape[1]
    swapped_rows(y_first, y_second, range(speed_slot, sides), y_below, y_above, 0)
    z_halo[...] = row_columns(z_rows[...]).reshape(z_halo.shape)
    halos = (None, None, y_below, y_above, z_halo)

    def plane(x, carry):
        restretch_plane(x, x - 1, stretch, flow, halos, updated)
        return carry

    lax.fori_loop(1, bx - 1, plane, 0)
    copy = pltpu.make_async_copy(updated, new_stretch.at[:, 1 : bx - 1], sem)
    copy.start()
    mark[...] = jnp.zeros(mark.shape, jnp.float32)
    copy.wait()


def restretch_outer(
    stretch,
    flow,
    x_first,
    x_second,
    y_first,
    y_second,
    z_rows,
    inner_stretch,
    new_stretch,
    mark,
    updated,
    below,
    above,
    y_below,
    y_above,
    z_halo,
    sems,
):
    bx = stretch.shape[1]
    flip_x = odd("gx")
    for comp in range(3):
        below[comp] = jnp.where(flip_x, x_first[comp], x_second[5 + comp])
        above[comp] = jnp.where(flip_x, x_second[5 + comp], x_first[comp])
    swapped_rows(y_first, y_second, range(speed_slot, sides), y_below, y_above, 0)
    z_halo[...] = row_columns(z_rows[...]).reshape(z_halo.shape)
    halos = (below, above, y_below, y_above, z_halo)
    copies = []
    for place, x in enumerate((0, bx - 1)):
        restretch_plane(x, place, stretch, flow, halos, updated)
        copies.append(
            pltpu.make_async_copy(updated.at[:, place], new_stretch.at[:, x], sems.at[place])
        )
        copies[-1].start()
    mark[...] = jnp.zeros(mark.shape, jnp.float32)
    for copy in copies:
        copy.wait()


def store(inner, outer, inner_slanted, outer_slanted, late, fresh, sems):
    bx = fresh.shape[1]
    moves = [
        (inner, fresh.at[0:first_slanted, 1 : bx - 1]),
        (inner_slanted, fresh.at[first_slanted:, 1 : bx - 1]),
    ]
    for place, x in enumerate((0, bx - 1)):
        moves.append((outer_slanted.at[:, place], fresh.at[first_slanted:, x]))
        order = (x_up, x_down)[place]
        start = 0
        for index in order + (first_slanted,):
            if index > start:
                run = slice(start, index)
                moves.append((outer.at[run, place], fresh.at[run, x]))
            if index in order:
                moves.append((late.at[order.index(index), place], fresh.at[index, x]))
            start = index + 1
    copies = [
        pltpu.make_async_copy(source, target, sems.at[place])
        for place, (source, target) in enumerate(moves)
    ]
    for copy in copies:
        copy.start()
    for copy in copies:
        copy.wait()


up_edges = ((0, y_up.index(7)), (0, gas_slot), (1, y_down.index(9)), (1, gas_slot))
down_edges = ((0, y_up.index(10)), (0, gas_slot), (1, y_down.index(8)), (1, gas_slot))


def forward_edges(z_rows, y_first, y_second, after, first_out, second_out, corner, *, bx):
    halves = y_first.shape[1] // lanes
    flip_x, flip_y = (odd("gx"), odd("gy"))
    for half in range(halves):
        cut = slice(half * lanes, half * lanes + lanes)
        for place in range(4):
            found = []
            for x, edges in ((bx - 1, up_edges), (0, down_edges)):
                side, slot = edges[place]
                row = slot * bx + x
                one = y_first[row : row + 1, cut]
                two = y_second[row : row + 1, cut]
                found.append(jnp.where(flip_y, one, two) if side == 0 else jnp.where(flip_y, two, one))
            at = half * 4 + place
            first_out[at : at + 1, :] = jnp.where(flip_x, found[1], found[0])
            second_out[at : at + 1, :] = jnp.where(flip_x, found[0], found[1])
    first_out[4 * halves :, :] = z_rows[...]
    second_out[4 * halves :, :] = z_rows[...]
    corner[...] = z_rows[...]


def own_halos(flags, y_first, y_second, z_rows, gas, low_rows, high_rows, columns):
    bx, by = flags.shape[:2]
    tile = row_columns(z_rows[...])
    swapped_rows(y_first, y_second, range(speed_slot), low_rows, high_rows, 1)
    for x in range(bx):
        gas[x + 1] = jnp.where(flags[x] == 0, 1.0, 0.0)
        columns[x + 1] = tile[x * by : x * by + by, :]


def own_corners(corner_first, corner_second, low_rows, high_rows):
    bx = low_rows.shape[0] - 2
    flip = odd("gy")
    corner_below = row_columns(select(flip, corner_first, corner_second))
    corner_above = row_columns(select(flip, corner_second, corner_first))
    by = corner_below.shape[0] // bx
    for x in range(bx):
        end = x * by + by - 1
        low_rows[x + 1, edge_slot : edge_slot + 1, 0:lanes] = corner_below[end : end + 1, :]
        high_rows[x + 1, edge_slot : edge_slot + 1, 0:lanes] = corner_above[
            x * by : x * by + 1, :
        ]


def pass_on(x, chunk, indices, source, leaving_of, speed, halos, fresh, place, total, change):
    gas, low_rows, high_rows, columns = halos
    by = gas.shape[1]
    chunks = by // tall
    rows = pl.ds(chunk * tall, tall)
    rest = 1.0 - 1.5 * (speed[0] * speed[0] + speed[1] * speed[1] + speed[2] * speed[2])
    equals = {}

    def moved(load, index, slot, lane):
        step_x, step_y, step_z = velocity_set[index]
        plane = x + 1 - step_x
        edges = low_rows if step_y == 1 else high_rows
        found = rows_of(load, chunk, chunks, step_y, lambda: edges[plane, slot : slot + 1, :])
        if step_z == 0:
            return found
        halo = rows_of(
            lambda low, high: columns[plane, low:high, :],
            chunk,
            chunks,
            step_y,
            lambda: edges[plane, edge_slot : edge_slot + 1, 0:lanes],
        )
        return columns_of(found, halo, lane, step_z)

    for index in indices:
        step_x, step_y, step_z = velocity_set[index]
        first = min(index, opposite_of[index])
        if first not in equals:
            proj = along(first, speed)
            equals[first] = 2.0 * lattice_weights[first] * (rest + 4.5 * proj * proj)
        slot, lane, gas_lane = (None, None, None)
        if step_y != 0:
            slot = (y_up if step_y == 1 else y_down).index(index)
        if step_z == 1:
            lane, gas_lane = (z_up.index(index), gas_slot)
        elif step_z == -1:
            lane, gas_lane = (sides + z_down.index(index), sides + gas_slot)
        field = source(index)
        marks = gas.at[x + 1 - step_x]
        arriving = moved(lambda low, high: field[low:high, :], index, slot, lane)
        from_gas = moved(lambda low, high: marks[low:high, :], index, gas_slot, gas_lane)
        leaving = leaving_of(opposite_of[index])[rows, :]
        open_side = from_gas > 0.5
        value = jnp.where(open_side, equals[first] - leaving, arriving)
        fresh(index)[place, rows, :] = value
        total = total + value
        change = change + jnp.where(open_side, 0.0, arriving - leaving)
    return total, change


def settle(x, rows, mass, flags, code, total, change):
    read = mass[x, rows, :] + jnp.where(flags[x, rows, :] == 1, change, 0.0)
    mark = code[x, rows, :]
    liquid = mark >= 32.0
    converts = mark > 0.0
    level = jnp.where(liquid, total, 0.0)
    excess = jnp.where(converts, read - level, 0.0)
    heading = jnp.where(liquid, mark - 32.0, mark)
    return jnp.where(converts, level, read), excess, heading


slanted = tuple(index for index in range(19) if velocity_set[index][1] * velocity_set[index][2])
first_slanted = slanted[0]


def from_inside(x, bx):
    found = [index for index in range(1, 19) if 0 <= x - velocity_set[index][0] < bx]
    return [index for index in found if index not in slanted]


def from_beyond(x, bx):
    return [index for index in range(1, 19) if not 0 <= x - velocity_set[index][0] < bx]


def stream_early(
    inner_post,
    outer_post,
    inner_shift,
    outer_shift,
    flags,
    y_first,
    y_second,
    z_rows,
    inner,
    outer,
    totals,
    changes,
    gas,
    low_rows,
    high_rows,
    columns,
):
    bx, by, bz = flags.shape
    halos = (gas, low_rows, high_rows, columns)
    own_halos(flags, y_first, y_second, z_rows, *halos)

    for x in range(bx):
        inside = 0 < x < bx - 1
        place = x - 1 if inside else end_place(x, bx)
        fresh = inner if inside else outer
        for chunk in range(by // tall):
            rows = pl.ds(chunk * tall, tall)
            total = plane_of(inner_post, outer_post, 0, x, bx)[rows, :]
            fresh[0, place, rows, :] = total
            total, change = pass_on(
                x,
                chunk,
                from_inside(x, bx),
                lambda index: plane_of(
                    inner_post, outer_post, index, x - velocity_set[index][0], bx
                ),
                lambda index: plane_of(inner_post, outer_post, index, x, bx),
                [plane_of(inner_shift, outer_shift, comp, x, bx)[rows, :] for comp in range(3)],
                halos,
                lambda index: fresh.at[index],
                place,
                total,
                jnp.zeros((tall, bz), jnp.float32),
            )
            totals[x, rows, :] = total
            changes[x, rows, :] = change


def stream_slanted(
    inner_post,
    outer_post,
    inner_shift,
    outer_shift,
    mass,
    flags,
    code,
    y_first,
    y_second,
    z_rows,
    corner_first,
    corner_second,
    totals,
    changes,
    inner,
    outer,
    settled,
    excess,
    heading,
    end_totals,
    end_changes,
    gas,
    low_rows,
    high_rows,
    columns,
):
    bx, by, bz = flags.shape
    halos = (gas, low_rows, high_rows, columns)
    own_halos(flags, y_first, y_second, z_rows, *halos)
    own_corners(corner_first, corner_second, low_rows, high_rows)

    for x in range(bx):
        inside = 0 < x < bx - 1
        place = x - 1 if inside else end_place(x, bx)
        fresh = inner if inside else outer
        for chunk in range(by // tall):
            rows = pl.ds(chunk * tall, tall)
            total, change = pass_on(
                x,
                chunk,
                slanted,
                lambda index: plane_of(inner_post, outer_post, index, x, bx),
                lambda index: plane_of(inner_post, outer_post, index, x, bx),
                [plane_of(inner_shift, outer_shift, comp, x, bx)[rows, :] for comp in range(3)],
                halos,
                lambda index: fresh.at[index - first_slanted],
                place,
                totals[x, rows, :],
                changes[x, rows, :],
            )
            if inside:
                now = settle(x, rows, mass, flags, code, total, change)
                settled[place, rows, :], excess[place, rows, :], heading[place, rows, :] = now
            else:
                end_totals[place, rows, :] = total
                end_changes[place, rows, :] = change


def stream_late(
    post,
    shift,
    mass,
    flags,
    code,
    totals,
    changes,
    gas_first,
    gas_second,
    x_first,
    x_second,
    edges_first,
    edges_second,
    inner_excess,
    inner_heading,
    flow,
    after,
    late,
    v_first,
    settled,
    spread,
    line_first,
    line_second,
    out_z,
    gas,
    low_rows,
    high_rows,
    columns,
    below,
    above,
    excess,
    heading,
):
    bx, by, bz = flags.shape
    halves = bz // lanes
    flip_x = odd("gx")
    halos = (gas, low_rows, high_rows, columns)

    for comp in range(3):
        up, down = (flow[comp, bx - 1], flow[comp, 0])
        v_first[comp] = jnp.where(flip_x, down, up)
    for slot in range(5):
        below[slot] = jnp.where(flip_x, x_first[slot], x_second[slot])
        above[slot] = jnp.where(flip_x, x_second[slot], x_first[slot])
    gas[0] = jnp.where(flip_x, gas_first[3], gas_second[3])
    gas[bx + 1] = jnp.where(flip_x, gas_second[3], gas_first[3])
    edges_below = select(flip_x, edges_first, edges_second)
    edges_above = select(flip_x, edges_second, edges_first)
    for found, at, x, edges in (
        (edges_below, 0, bx - 1, up_edges),
        (edges_above, bx + 1, 0, down_edges),
    ):
        for place, (side, slot) in enumerate(edges):
            line = jnp.concatenate(
                [found[half * 4 + place : half * 4 + place + 1, :] for half in range(halves)],
                axis=1,
            )
            (low_rows, high_rows)[side][at, slot : slot + 1, :] = line
        columns[at] = row_columns(found[4 * halves :, :])[x * by : x * by + by, :]
    for place, x in enumerate((0, bx - 1)):
        halo, order = ((below, x_up), (above, x_down))[place]
        for chunk in range(by // tall):
            rows = pl.ds(chunk * tall, tall)
            total, change = pass_on(
                x,
                chunk,
                from_beyond(x, bx),
                lambda index: halo.at[order.index(index)],
                lambda index: post.at[index, place],
                [shift[comp, place, rows, :] for comp in range(3)],
                halos,
                lambda index: late.at[order.index(index)],
                place,
                totals[place, rows, :],
                changes[place, rows, :],
            )
            now = settle(x, rows, mass, flags, code, total, change)
            settled[place, rows, :], excess[x, rows, :], heading[x, rows, :] = now
    for x in range(1, bx - 1):
        excess[x] = inner_excess[x - 1]
        heading[x] = inner_heading[x - 1]

    row_at, lane_at = (iota((by, bz), 0), iota((by, bz), 1))
    line_at = iota((1, bz), 1)
    tile_lane, line_lane = (iota((by, lanes), 1), iota((1, lanes), 1))

    def rows_up(rows):
        return jnp.where(row_at == 0, 0.0, pltpu.roll(rows, 1, 0))

    def rows_down(rows):
        return jnp.where(row_at == by - 1, 0.0, pltpu.roll(rows, by - 1, 0))

    def over(rows, at, step):
        if step == 1:
            return jnp.where(at == 0, 0.0, pltpu.roll(rows, 1, 1))
        return jnp.where(at == bz - 1, 0.0, pltpu.roll(rows, bz - 1, 1))

    def summed(parts):
        total = parts[0]
        for part in parts[1:]:
            total = total + part
        return total

    tile = jnp.zeros((by, lanes), jnp.float32)
    line_up = jnp.zeros((1, lanes), jnp.float32)
    line_down = jnp.zeros((1, lanes), jnp.float32)
    flip_y = odd("gy")
    line_first[...] = jnp.zeros(line_first.shape, jnp.float32)
    line_second[...] = jnp.zeros(line_second.shape, jnp.float32)
    for target in range(bx + 2):
        groups = {}
        for index in range(1, 19):
            step_x, step_y, step_z = velocity_set[index]
            x = target - 1 - step_x
            if 0 <= x < bx:
                part = jnp.where(heading[x] == float(index), excess[x], 0.0)
                groups.setdefault((step_y, step_z), []).append(part)
        groups = {key: summed(parts) for key, parts in groups.items()}
        total = jnp.zeros((by, bz), jnp.float32)
        line = {1: jnp.zeros((1, bz), jnp.float32), -1: jnp.zeros((1, bz), jnp.float32)}
        for step_z in (0, 1, -1):
            group = jnp.zeros((by, bz), jnp.float32)
            ends = {}
            if (0, step_z) in groups:
                group = group + groups[(0, step_z)]
            if (1, step_z) in groups:
                group = group + rows_up(groups[(1, step_z)])
                ends[1] = groups[(1, step_z)][by - 1 : by, :]
            if (-1, step_z) in groups:
                group = group + rows_down(groups[(-1, step_z)])
                ends[-1] = groups[(-1, step_z)][0:1, :]
            if step_z == 0:
                total = total + group
                for side in ends:
                    line[side] = line[side] + ends[side]
                continue
            total = total + over(group, lane_at, step_z)
            for side in ends:
                line[side] = line[side] + over(ends[side], line_at, step_z)
            if step_z == 1:
                spot, cut, roll = (target, slice(bz - lanes, bz), target + 1)
            else:
                spot, cut, roll = (8 + target, slice(0, lanes), 8 + target)
            tile = jnp.where(tile_lane == spot, pltpu.roll(group[:, cut], roll, 1), tile)
            if 1 in ends:
                line_up = jnp.where(
                    line_lane == spot, pltpu.roll(ends[1][:, cut], roll, 1), line_up
                )
            if -1 in ends:
                line_down = jnp.where(
                    line_lane == spot, pltpu.roll(ends[-1][:, cut], roll, 1), line_down
                )
        spread[target] = total
        line_first[target : target + 1, :] = jnp.where(flip_y, line[-1], line[1])
        line_second[target : target + 1, :] = jnp.where(flip_y, line[1], line[-1])
    rest = jnp.zeros((lanes - by - 2, lanes), jnp.float32)
    out_z[...] = column_rows([tile, line_up, line_down, rest], 16)


def with_edges(total, target, tile, y_below, y_above):
    by, bz = total.shape
    row_at, lane_at = (iota((by, bz), 0), iota((by, bz), 1))
    total = total + jnp.where(lane_at == 0, tile[0:by, target : target + 1], 0.0)
    total = total + jnp.where(lane_at == bz - 1, tile[0:by, 8 + target : 9 + target], 0.0)
    total = total + jnp.where(row_at == 0, y_below[target : target + 1, :], 0.0)
    return total + jnp.where(row_at == by - 1, y_above[target : target + 1, :], 0.0)


def add_faces(spread, z_rows, y_first, y_second, first, second):
    last = spread.shape[0] - 1
    flip_x, flip_y = (odd("gx"), odd("gy"))
    tile = row_columns(z_rows[...])
    y_below, y_above = (select(flip_y, y_first, y_second), select(flip_y, y_second, y_first))
    up = with_edges(spread[last], last, tile, y_below, y_above)
    down = with_edges(spread[0], 0, tile, y_below, y_above)
    first[...] = jnp.where(flip_x, down, up)
    second[...] = jnp.where(flip_x, up, down)


def add_all(
    inner_settled,
    outer_settled,
    spread,
    z_rows,
    y_first,
    y_second,
    corner_first,
    corner_second,
    x_second,
    x_first,
    after,
    new_mass,
):
    bx, by, bz = new_mass.shape
    flip_x, flip_y = (odd("gx"), odd("gy"))
    tile = row_columns(z_rows[...])
    y_below, y_above = (select(flip_y, y_first, y_second), select(flip_y, y_second, y_first))
    at = iota((8, bz), 1)
    found = []
    for rows, side, corner in (
        (y_below, 0, select(flip_y, corner_first, corner_second)),
        (y_above, 1, select(flip_y, corner_second, corner_first)),
    ):
        edge = corner[:, by + side : by + side + 1]
        rows = rows + jnp.where(at == 0, edge[0:8, :], 0.0)
        found.append(rows + jnp.where(at == bz - 1, edge[8:16, :], 0.0))
    for x in range(bx):
        total = with_edges(spread[x + 1], x + 1, tile, *found)
        if x == 0:
            total = total + select(flip_x, x_first, x_second)
        if x == bx - 1:
            total = total + select(flip_x, x_second, x_first)
        if 0 < x < bx - 1:
            total = total + inner_settled[x - 1]
        else:
            total = total + outer_settled[0 if x == 0 else 1]
        new_mass[x] = total


def swapped_ahead(array, axis):
    devices = lax.axis_size(axis)
    pairing = [(i, (i + 1) % devices if i % 2 == 0 else i - 1) for i in range(devices)]
    return lax.ppermute(array, axis, pairing)


def swapped_behind(array, axis):
    devices = lax.axis_size(axis)
    pairing = [(i, (i - 1) % devices if i % 2 == 0 else (i + 1) % devices) for i in range(devices)]
    return lax.ppermute(array, axis, pairing)


def swapped(first, second, axis):
    return swapped_ahead(first, axis), swapped_behind(second, axis)


def both_ways(rows, lower):
    devices = lax.axis_size("gz")
    before = lax.ppermute(rows, "gz", [(i, (i + 1) % devices) for i in range(devices)])
    if devices == 2:
        return before
    after = lax.ppermute(rows, "gz", [(i, (i - 1) % devices) for i in range(devices)])
    return jnp.where(iota(rows.shape, 0) < lower, before, after)


remote = pl.BlockSpec(memory_space=pltpu.HBM)
anywhere = pl.BlockSpec(memory_space=pl.ANY)


def call(body, outs, specs=None, out_specs=None, scratch=(), cost=(0, 0), aliases=None):
    extra = {} if specs is None else {"in_specs": specs}
    if out_specs is not None:
        extra["out_specs"] = out_specs
    return pl.pallas_call(
        body,
        out_shape=[
            shape
            if isinstance(shape, jax.ShapeDtypeStruct)
            else jax.ShapeDtypeStruct(shape, jnp.float32)
            for shape in outs
        ],
        scratch_shapes=[
            pltpu.VMEM(shape, jnp.float32) if isinstance(shape, tuple) else shape
            for shape in scratch
        ],
        compiler_params=pltpu.CompilerParams(vmem_limit_bytes=40 * 1024 * 1024),
        input_output_aliases=aliases or {},
        cost_estimate=pl.CostEstimate(flops=cost[0], bytes_accessed=cost[1], transcendentals=0),
        **extra,
    )


def shards(populations, stretch, mass, flags, conv_source, conv_kind, conv_direction):
    bx, by, bz = flags.shape
    cells = bx * by * bz
    box, face, tile = ((bx, by, bz), (by, bz), (bx, by, lanes))

    stretch, flags, z_out, y_one, y_two, x_one, x_two = call(
        first_faces,
        [
            (6, *box),
            jax.ShapeDtypeStruct(box, jnp.int32),
            (8, bx * by),
            (4 * bx, bz),
            (4 * bx, bz),
            (4, *face),
            (4, *face),
        ],
        specs=[remote] * 2,
        scratch=[pltpu.SemaphoreType.DMA((2,))],
        cost=(10 * cells, 60 * cells),
    )(*(pltpu.with_memory_space_constraint(array, pltpu.HBM) for array in (stretch, flags)))
    first_x = swapped(x_one, x_two, "gx")
    z_first = both_ways(z_out, 3)
    y_first = swapped(y_one, y_two, "gy")

    entries = conv_source.shape[0]
    mark = (tall, lanes)
    code, code_done = call(
        lambda *refs: conversions(*refs, columns=bz),
        [(bx * by, bz), mark],
        cost=(40 * cells, 4 * cells),
    )(*(array.reshape(1, entries) for array in (conv_source, conv_kind, conv_direction)))
    code = code.reshape(box)

    pops, flow = call(
        moments,
        [(19, *box), (5, *box)],
        specs=[remote],
        scratch=[pltpu.SemaphoreType.DMA((bx,))],
        cost=(60 * cells, 150 * cells),
    )(pltpu.with_memory_space_constraint(populations, pltpu.HBM))

    columns, rows = ((24, bx * by), (10 * bx, bz))
    sides_y = [(bx, 8, bz), (bx, 8, bz), tile]
    inside, ends = ((bx - 2, *face), (2, *face))
    inner_post, inner_shift = call(
        collide_inner,
        [(19, *inside), (3, *inside)],
        scratch=sides_y,
        cost=(150 * cells, 150 * cells),
    )(pops, stretch, flow, z_first, *y_first)
    outer_post, outer_shift, z_out, x_one, x_two, y_one, y_two = call(
        collide_outer,
        [(19, *ends), (3, *ends), columns, (5, *face), (8, *face), rows, rows],
        scratch=[(4, *face), (4, *face)] + sides_y + [box],
        cost=(150 * cells, 150 * cells),
    )(pops, stretch, flags, flow, *first_x, *y_first, z_first, inner_post)
    z_post = both_ways(z_out, sides)
    post_y = swapped(y_one, y_two, "gy")
    post_x = swapped(x_one, x_two, "gx")
    edges = (4 * (bz // lanes) + columns[0], lanes)
    x_one, x_two, corner = call(
        lambda *refs: forward_edges(*refs, bx=bx), [edges, edges, columns], cost=(17 * 10**8, 0)
    )(z_post, *post_y, code_done)
    corners = swapped(corner, corner, "gy")
    edges_x = swapped(x_one, x_two, "gx")

    rims = [(bx + 2, *face), (bx + 2, 16, bz), (bx + 2, 16, bz), (bx + 2, by, lanes)]
    posts = (inner_post, outer_post, inner_shift, outer_shift)
    inner, outer, totals, changes = call(
        stream_early,
        [(first_slanted, *inside), (first_slanted, *ends), box, box],
        scratch=rims,
        cost=(350 * cells, 200 * cells),
    )(*posts, flags, *post_y, z_post)
    (
        inner_slanted,
        outer_slanted,
        inner_settled,
        inner_excess,
        inner_heading,
        totals,
        changes,
    ) = call(
        stream_slanted,
        [(4, *inside), (4, *ends), inside, inside, inside, ends, ends],
        scratch=rims,
        cost=(100 * cells, 60 * cells),
    )(*posts, mass, flags, code, *post_y, z_post, *corners, totals, changes)
    new_stretch, inner_done = call(
        restretch_inner,
        [(6, *box), mark],
        out_specs=[remote, pl.BlockSpec()],
        scratch=[(6, *inside)] + sides_y + [pltpu.SemaphoreType.DMA],
        cost=(80 * cells, 40 * cells),
    )(stretch, flow, *post_y, z_post)
    late, v_one, outer_settled, spread, y_one, y_two, z_out = call(
        stream_late,
        [
            (5, *ends),
            (3, *face),
            ends,
            (bx + 2, *face),
            (8, bz),
            (8, bz),
            (16, bx * by),
        ],
        scratch=rims + [(5, *face), (5, *face), box, box],
        cost=(150 * cells, 100 * cells),
    )(
        outer_post,
        outer_shift,
        mass,
        flags,
        code,
        totals,
        changes,
        *first_x,
        *post_x,
        *edges_x,
        inner_excess,
        inner_heading,
        flow,
        inner_done,
    )
    z_last = both_ways(z_out, 8)
    last_y = swapped(y_one, y_two, "gy")
    last_corners = swapped(z_last, z_last, "gy")
    flow_x = (swapped_ahead(v_one, "gx"), post_x[1])
    x_one, x_two = call(add_faces, [face, face], cost=(4 * 10**9, 0))(spread, z_last, *last_y)
    last_x = swapped(x_one, x_two, "gx")
    (fresh,) = call(
        store,
        [(19, *box)],
        out_specs=[remote],
        scratch=[pltpu.SemaphoreType.DMA((32,))],
        cost=(0, 160 * cells),
    )(inner, outer, inner_slanted, outer_slanted, late)
    new_stretch, outer_done = call(
        restretch_outer,
        [(6, *box), mark],
        specs=[pl.BlockSpec()] * 7 + [remote],
        out_specs=[remote, pl.BlockSpec()],
        scratch=[(6, *ends), (3, *face), (3, *face)]
        + sides_y
        + [pltpu.SemaphoreType.DMA((2,))],
        cost=(80 * cells, 40 * cells),
        aliases={7: 0},
    )(stretch, flow, *flow_x, *post_y, z_post, new_stretch)
    (new_mass,) = call(add_all, [box])(
        inner_settled, outer_settled, spread, z_last, *last_y, *last_corners, *last_x[::-1], outer_done
    )
    return (fresh, new_stretch, new_mass)


def solution(mesh):
    return jax.shard_map(
        shards,
        mesh=mesh,
        in_specs=(
            P(None, "gx", "gy", "gz"),
            P(None, "gx", "gy", "gz"),
            P("gx", "gy", "gz"),
            P("gx", "gy", "gz"),
            P(("gx", "gy", "gz")),
            P(("gx", "gy", "gz")),
            P(("gx", "gy", "gz")),
        ),
        out_specs=(P(None, "gx", "gy", "gz"), P(None, "gx", "gy", "gz"), P("gx", "gy", "gz")),
        check_vma=False,
    )
```

```python
import jax
import jax.numpy as jnp
from jax import lax
from jax.experimental import pallas as pl
from jax.experimental.pallas import tpu as pltpu
from jax.sharding import PartitionSpec as P

velocity_set = (
    (0, 0, 0),
    (1, 0, 0),
    (-1, 0, 0),
    (0, 1, 0),
    (0, -1, 0),
    (0, 0, 1),
    (0, 0, -1),
    (1, 1, 0),
    (-1, -1, 0),
    (1, -1, 0),
    (-1, 1, 0),
    (1, 0, 1),
    (-1, 0, -1),
    (1, 0, -1),
    (-1, 0, 1),
    (0, 1, 1),
    (0, -1, -1),
    (0, 1, -1),
    (0, -1, 1),
)
opposite_of = (0, 2, 1, 4, 3, 6, 5, 8, 7, 10, 9, 12, 11, 14, 13, 16, 15, 18, 17)
lattice_weights = (1.0 / 3.0,) + (1.0 / 18.0,) * 6 + (1.0 / 36.0,) * 12
symmetric_slot = ((0, 3, 4), (3, 1, 5), (4, 5, 2))
tensor_pairs = ((0, 0), (1, 1), (2, 2), (0, 1), (0, 2), (1, 2))
relax_time = 0.8
polymer_time = 8.0
polymer_coeff = 0.05


def moving(axis, sign):
    return tuple(index for index in range(19) if velocity_set[index][axis] == sign)


x_up, x_down = (moving(0, 1), moving(0, -1))
y_up, y_down = (moving(1, 1), moving(1, -1))
z_up, z_down = (moving(2, 1), moving(2, -1))
pairs = tuple(range(1, 19, 2))
gas_slot = 5
speed_slot = 6
edge_slot = 9
sides = 9
lanes = 128
tall = 8


def iota(shape, dim):
    return lax.broadcasted_iota(jnp.int32, shape, dim)


def wide(tile, width):
    return jnp.concatenate([tile] * (width // tile.shape[1]), axis=1)


def rows_of(load, chunk, chunks, step, edge):
    low = chunk * tall
    if step == 0:
        return load(low, low + tall)
    if step == 1 and chunk > 0:
        return load(low - 1, low + tall - 1)
    if step == -1 and chunk < chunks - 1:
        return load(low + 1, low + tall + 1)
    rows = load(low, low + tall)
    at = iota(rows.shape, 0)
    if step == 1:
        return jnp.where(at == 0, edge(), pltpu.roll(rows, 1, 0))
    return jnp.where(at == tall - 1, edge(), pltpu.roll(rows, tall - 1, 0))


def columns_of(rows, halo, lane, step):
    width = rows.shape[1]
    at = iota(rows.shape, 1)
    if step == 1:
        edge = wide(pltpu.roll(halo, (lanes - lane) % lanes, 1), width)
        return jnp.where(at == 0, edge, pltpu.roll(rows, 1, 1))
    edge = wide(pltpu.roll(halo, lanes - 1 - lane, 1), width)
    return jnp.where(at == width - 1, edge, pltpu.roll(rows, width - 1, 1))


def packed(high, low):
    at = iota(high[0].shape, 1)
    tile = jnp.zeros_like(high[0])
    for slot, part in enumerate(high):
        tile = jnp.where(at == slot, pltpu.roll(part, slot + 1, 1), tile)
    for place, part in enumerate(low):
        slot = len(high) + place
        tile = jnp.where(at == slot, pltpu.roll(part, slot, 1), tile)
    return tile


def along(index, vector):
    total = None
    for comp in range(3):
        sign = velocity_set[index][comp]
        if sign != 0:
            term = vector[comp] if sign > 0 else -vector[comp]
            total = term if total is None else total + term
    return total


def conversions(source, kind, heading, code, mark, *, columns):
    count = source.shape[1]
    value = (heading[...] + 32 * kind[...]).astype(jnp.float32)
    row, column = (source[...] // columns, source[...] % columns)
    by_row = jnp.where(iota((code.shape[0], count), 0) == row, value, 0.0).astype(jnp.bfloat16)
    by_column = jnp.where(iota((columns, count), 0) == column, 1.0, 0.0).astype(jnp.bfloat16)
    code[...] = lax.dot_general(
        by_row, by_column, (((1,), (1,)), ((), ())), preferred_element_type=jnp.float32
    )
    mark[...] = jnp.zeros(mark.shape, jnp.float32)


def odd(axis):
    return lax.rem(lax.axis_index(axis), 2) == 1


def select(chosen, first, second):
    return jnp.where(chosen, first[...], second[...])


def swap_rows(first, second, x, planes, high, low, flip):
    for slot, (top, bottom) in enumerate(zip(high, low)):
        by = top.shape[0]
        up, down = (top[by - 1 : by, :], bottom[0:1, :])
        at = slot * planes + x
        first[at : at + 1, :] = jnp.where(flip, down, up)
        second[at : at + 1, :] = jnp.where(flip, up, down)


def swapped_rows(first, second, slots, low_rows, high_rows, shift):
    flip = odd("gy")
    planes = low_rows.shape[0] - 2 * shift
    for x in range(planes):
        for place, slot in enumerate(slots):
            at = slot * planes + x
            one, two = (first[at : at + 1, :], second[at : at + 1, :])
            low_rows[x + shift, place : place + 1, :] = jnp.where(flip, one, two)
            high_rows[x + shift, place : place + 1, :] = jnp.where(flip, two, one)


def column_rows(tiles, count):
    return jnp.concatenate(tiles, axis=0).T[0:count, :]


def row_columns(rows):
    rest = jnp.zeros((lanes - rows.shape[0], rows.shape[1]), jnp.float32)
    return jnp.concatenate([rows, rest], axis=0).T


def first_faces(
    stretch_in,
    flags_in,
    stretch,
    flags,
    columns,
    y_first,
    y_second,
    x_first,
    x_second,
    sems,
):
    bx, by, bz = flags.shape
    flip_x, flip_y = (odd("gx"), odd("gy"))
    copies = [
        pltpu.make_async_copy(stretch_in, stretch, sems.at[0]),
        pltpu.make_async_copy(flags_in, flags, sems.at[1]),
    ]
    for copy in copies:
        copy.start()
    for copy in copies:
        copy.wait()
    tiles = []
    for x in range(bx):
        along_y = [stretch.at[symmetric_slot[comp][1], x] for comp in range(3)]
        swap_rows(y_first, y_second, x, bx, along_y, along_y, flip_y)
        fields = [stretch.at[symmetric_slot[comp][2], x] for comp in range(3)]
        tiles.append(
            packed(
                [field[:, bz - lanes : bz] for field in fields],
                [field[:, 0:lanes] for field in fields],
            )
        )
    columns[...] = column_rows(tiles, columns.shape[0])
    rest = y_first.shape[0] - 3 * bx
    y_first[3 * bx :, :] = jnp.zeros((rest, bz), jnp.float32)
    y_second[3 * bx :, :] = jnp.zeros((rest, bz), jnp.float32)
    for out, last in ((x_first, flip_x), (x_second, jnp.logical_not(flip_x))):
        for comp in range(3):
            slot = symmetric_slot[comp][0]
            out[comp] = jnp.where(last, stretch[slot, 0], stretch[slot, bx - 1])
        out[3] = jnp.where(jnp.where(last, flags[0], flags[bx - 1]) == 0, 1.0, 0.0)


def moments(pops_in, pops, flow, sems):
    bx, by = pops.shape[1:3]
    copies = [
        pltpu.make_async_copy(pops_in.at[:, x], pops.at[:, x], sems.at[x]) for x in range(bx)
    ]
    for copy in copies:
        copy.start()
    for x in range(bx):
        copies[x].wait()
        for chunk in range(by // tall):
            rows = pl.ds(chunk * tall, tall)
            part = [pops[index, x, rows, :] for index in range(19)]
            density = part[0]
            for index in range(1, 19):
                density = density + part[index]
            inverse = 1.0 / density
            for comp in range(3):
                total = None
                for index in pairs:
                    sign = velocity_set[index][comp]
                    if sign != 0:
                        term = part[index] - part[index + 1]
                        term = term if sign > 0 else -term
                        total = term if total is None else total + term
                flow[comp, x, rows, :] = total * inverse
            flow[3, x, rows, :] = density
            flow[4, x, rows, :] = inverse


def beside(ref, field, x, step, halo, slot):
    last = ref.shape[1] - 1
    if halo is None:
        return lambda low, high: ref[field, x + step, low:high, :]
    if isinstance(x, int):
        if 0 <= x + step <= last:
            return lambda low, high: ref[field, x + step, low:high, :]
        return lambda low, high: halo[slot, low:high, :]
    inside = jnp.clip(x + step, 0, last)
    beyond = x == (0 if step < 0 else last)
    return lambda low, high: jnp.where(
        beyond, halo[slot, low:high, :], ref[field, inside, low:high, :]
    )


def differences(
    ref, field, slots, x, chunk, chunks, below, above, y_below, y_above, z_halo, lane, side
):
    slot_x, slot_y, slot_z = slots
    low, high = (chunk * tall, chunk * tall + tall)

    def load(first, stop):
        return ref[field, x, first:stop, :]

    result = [None, None, None]
    if slot_x is not None:
        after = beside(ref, field, x, 1, above, slot_x)(low, high)
        before = beside(ref, field, x, -1, below, slot_x)(low, high)
        result[0] = after - before
    if slot_y is not None:
        after = rows_of(load, chunk, chunks, -1, lambda: y_above[x, slot_y : slot_y + 1, :])
        before = rows_of(load, chunk, chunks, 1, lambda: y_below[x, slot_y : slot_y + 1, :])
        result[1] = after - before
    if slot_z is not None:
        rows, halo = (load(low, high), z_halo[x, low:high, :])
        after = columns_of(rows, halo, lane + side + slot_z, -1)
        before = columns_of(rows, halo, lane + slot_z, 1)
        result[2] = after - before
    return result


def end_place(x, bx):
    return 0 if x == 0 else 1


def plane_of(inner, outer, field, x, bx):
    if 0 < x < bx - 1:
        return inner.at[field, x - 1]
    return outer.at[field, end_place(x, bx)]


def collide_plane(x, place, pops, stretch, flow, halos, post, shift):
    by = pops.shape[2]
    chunks = by // tall
    factor = 1.0 - 0.5 / relax_time
    rate = 1.0 / relax_time
    for chunk in range(chunks):
        rows = pl.ds(chunk * tall, tall)
        terms = [[], [], []]
        for field in range(6):
            slots = [None, None, None]
            for comp in range(3):
                for axis in range(3):
                    if symmetric_slot[comp][axis] == field:
                        slots[axis] = comp
            found = differences(stretch, field, slots, x, chunk, chunks, *halos)
            for axis in range(3):
                if slots[axis] is not None:
                    terms[slots[axis]].append(found[axis])
        force = [0.5 * polymer_coeff * (part[0] + part[1] + part[2]) for part in terms]
        density, half = (flow[3, x, rows, :], 0.5 * flow[4, x, rows, :])
        moved = [flow[comp, x, rows, :] + half * force[comp] for comp in range(3)]
        for comp in range(3):
            shift[comp, place, rows, :] = moved[comp]
        squared = moved[0] * moved[0] + moved[1] * moved[1] + moved[2] * moved[2]
        work = moved[0] * force[0] + moved[1] * force[1] + moved[2] * force[2]
        weight = rate * density
        common = weight - 1.5 * weight * squared - 3.0 * factor * work
        odd = [3.0 * weight * moved[comp] + 3.0 * factor * force[comp] for comp in range(3)]
        even = [4.5 * weight * moved[comp] + 9.0 * factor * force[comp] for comp in range(3)]
        keep = 1.0 - rate
        post[0, place, rows, :] = keep * pops[0, x, rows, :] + lattice_weights[0] * common
        for index in pairs:
            both = common + along(index, moved) * along(index, even)
            differ = along(index, odd)
            scale = lattice_weights[index]
            post[index, place, rows, :] = keep * pops[index, x, rows, :] + scale * (both + differ)
            post[index + 1, place, rows, :] = keep * pops[index + 1, x, rows, :] + scale * (
                both - differ
            )


def collide_inner(
    pops,
    stretch,
    flow,
    z_rows,
    y_first,
    y_second,
    post,
    shift,
    y_below,
    y_above,
    z_halo,
):
    swapped_rows(y_first, y_second, range(3), y_below, y_above, 0)
    z_halo[...] = row_columns(z_rows[...]).reshape(z_halo.shape)
    halos = (None, None, y_below, y_above, z_halo, 0, 3)

    def plane(x, carry):
        collide_plane(x, x - 1, pops, stretch, flow, halos, post, shift)
        return carry

    lax.fori_loop(1, pops.shape[1] - 1, plane, 0)


def collide_outer(
    pops,
    stretch,
    flags,
    flow,
    x_first,
    x_second,
    y_first,
    y_second,
    z_rows,
    inner,
    post,
    shift,
    columns,
    ahead,
    behind,
    up_first,
    up_second,
    below,
    above,
    y_below,
    y_above,
    z_halo,
    gas,
):
    bx, by, bz = flags.shape
    halos = (below, above, y_below, y_above, z_halo, 0, 3)
    flip_x, flip_y = (odd("gx"), odd("gy"))
    below[...] = select(flip_x, x_first, x_second)
    above[...] = select(flip_x, x_second, x_first)
    swapped_rows(y_first, y_second, range(3), y_below, y_above, 0)
    z_halo[...] = row_columns(z_rows[...]).reshape(z_halo.shape)
    for x in (0, bx - 1):
        collide_plane(x, end_place(x, bx), pops, stretch, flow, halos, post, shift)

    tiles = []
    for x in range(bx):
        gas[x] = jnp.where(flags[x] == 0, 1.0, 0.0)
        rest = [gas.at[x]] + [flow.at[comp, x] for comp in range(3)]

        def fields(indices):
            return [plane_of(inner, post, index, x, bx) for index in indices] + rest

        swap_rows(up_first, up_second, x, bx, fields(y_up), fields(y_down), flip_y)
        tiles.append(
            packed(
                [field[:, bz - lanes : bz] for field in fields(z_up)],
                [field[:, 0:lanes] for field in fields(z_down)],
            )
        )
    columns[...] = column_rows(tiles, columns.shape[0])
    rest = up_first.shape[0] - sides * bx
    up_first[sides * bx :, :] = jnp.zeros((rest, bz), jnp.float32)
    up_second[sides * bx :, :] = jnp.zeros((rest, bz), jnp.float32)
    for slot in range(5):
        up, down = (post[x_up[slot], 1], post[x_down[slot], 0])
        ahead[slot] = jnp.where(flip_x, down, up)
        behind[slot] = jnp.where(flip_x, up, down)
    for comp in range(3):
        behind[5 + comp] = jnp.where(flip_x, flow[comp, bx - 1], flow[comp, 0])


def restretch_plane(x, place, stretch, flow, halos, updated):
    chunks = stretch.shape[2] // tall
    for chunk in range(chunks):
        rows = pl.ds(chunk * tall, tall)
        grad = [
            differences(
                flow, comp, (comp, comp, comp), x, chunk, chunks, *halos, speed_slot, sides
            )
            for comp in range(3)
        ]
        part = [stretch[slot, x, rows, :] for slot in range(6)]
        full = [part[slot] + 1.0 if slot < 3 else part[slot] for slot in range(6)]

        def product(row, col):
            total = grad[row][0] * full[symmetric_slot[0][col]]
            for inner in (1, 2):
                total = total + grad[row][inner] * full[symmetric_slot[inner][col]]
            return total

        for slot, (row, col) in enumerate(tensor_pairs):
            old = (1.0 - 1.0 / polymer_time) * part[slot]
            if row == col:
                updated[slot, place, rows, :] = old + product(row, col)
            else:
                updated[slot, place, rows, :] = old + 0.5 * (product(row, col) + product(col, row))


def restretch_inner(
    stretch,
    flow,
    y_first,
    y_second,
    z_rows,
    new_stretch,
    mark,
    updated,
    y_below,
    y_above,
    z_halo,
    sem,
):
    bx = stretch.shape[1]
    swapped_rows(y_first, y_second, range(speed_slot, sides), y_below, y_above, 0)
    z_halo[...] = row_columns(z_rows[...]).reshape(z_halo.shape)
    halos = (None, None, y_below, y_above, z_halo)

    def plane(x, carry):
        restretch_plane(x, x - 1, stretch, flow, halos, updated)
        return carry

    lax.fori_loop(1, bx - 1, plane, 0)
    copy = pltpu.make_async_copy(updated, new_stretch.at[:, 1 : bx - 1], sem)
    copy.start()
    mark[...] = jnp.zeros(mark.shape, jnp.float32)
    copy.wait()


def restretch_outer(
    stretch,
    flow,
    x_first,
    x_second,
    y_first,
    y_second,
    z_rows,
    inner_stretch,
    inner,
    outer,
    inner_slanted,
    outer_slanted,
    late,
    new_stretch,
    fresh,
    mark,
    updated,
    below,
    above,
    y_below,
    y_above,
    z_halo,
    sems,
    store_sems,
):
    bx = stretch.shape[1]
    moves = stored(inner, outer, inner_slanted, outer_slanted, late, fresh, store_sems)
    for copy in moves:
        copy.start()
    flip_x = odd("gx")
    for comp in range(3):
        below[comp] = jnp.where(flip_x, x_first[comp], x_second[5 + comp])
        above[comp] = jnp.where(flip_x, x_second[5 + comp], x_first[comp])
    swapped_rows(y_first, y_second, range(speed_slot, sides), y_below, y_above, 0)
    z_halo[...] = row_columns(z_rows[...]).reshape(z_halo.shape)
    halos = (below, above, y_below, y_above, z_halo)
    copies = []
    for place, x in enumerate((0, bx - 1)):
        restretch_plane(x, place, stretch, flow, halos, updated)
        copies.append(
            pltpu.make_async_copy(updated.at[:, place], new_stretch.at[:, x], sems.at[place])
        )
        copies[-1].start()
    mark[...] = jnp.zeros(mark.shape, jnp.float32)
    for copy in copies + moves:
        copy.wait()


def stored(inner, outer, inner_slanted, outer_slanted, late, fresh, sems):
    bx = fresh.shape[1]
    moves = [
        (inner, fresh.at[0:first_slanted, 1 : bx - 1]),
        (inner_slanted, fresh.at[first_slanted:, 1 : bx - 1]),
    ]
    for place, x in enumerate((0, bx - 1)):
        moves.append((outer_slanted.at[:, place], fresh.at[first_slanted:, x]))
        order = (x_up, x_down)[place]
        start = 0
        for index in order + (first_slanted,):
            if index > start:
                run = slice(start, index)
                moves.append((outer.at[run, place], fresh.at[run, x]))
            if index in order:
                moves.append((late.at[order.index(index), place], fresh.at[index, x]))
            start = index + 1
    return [
        pltpu.make_async_copy(source, target, sems.at[place])
        for place, (source, target) in enumerate(moves)
    ]


up_edges = ((0, y_up.index(7)), (0, gas_slot), (1, y_down.index(9)), (1, gas_slot))
down_edges = ((0, y_up.index(10)), (0, gas_slot), (1, y_down.index(8)), (1, gas_slot))


def forward_edges(z_rows, y_first, y_second, after, first_out, second_out, corner, *, bx):
    halves = y_first.shape[1] // lanes
    flip_x, flip_y = (odd("gx"), odd("gy"))
    for half in range(halves):
        cut = slice(half * lanes, half * lanes + lanes)
        for place in range(4):
            found = []
            for x, edges in ((bx - 1, up_edges), (0, down_edges)):
                side, slot = edges[place]
                row = slot * bx + x
                one = y_first[row : row + 1, cut]
                two = y_second[row : row + 1, cut]
                found.append(jnp.where(flip_y, one, two) if side == 0 else jnp.where(flip_y, two, one))
            at = half * 4 + place
            first_out[at : at + 1, :] = jnp.where(flip_x, found[1], found[0])
            second_out[at : at + 1, :] = jnp.where(flip_x, found[0], found[1])
    first_out[4 * halves :, :] = z_rows[...]
    second_out[4 * halves :, :] = z_rows[...]
    corner[...] = z_rows[...]


def own_halos(flags, y_first, y_second, z_rows, gas, low_rows, high_rows, columns):
    bx, by = flags.shape[:2]
    tile = row_columns(z_rows[...])
    swapped_rows(y_first, y_second, range(speed_slot), low_rows, high_rows, 1)
    for x in range(bx):
        gas[x + 1] = jnp.where(flags[x] == 0, 1.0, 0.0)
        columns[x + 1] = tile[x * by : x * by + by, :]


def own_corners(corner_first, corner_second, low_rows, high_rows):
    bx = low_rows.shape[0] - 2
    flip = odd("gy")
    corner_below = row_columns(select(flip, corner_first, corner_second))
    corner_above = row_columns(select(flip, corner_second, corner_first))
    by = corner_below.shape[0] // bx
    for x in range(bx):
        end = x * by + by - 1
        low_rows[x + 1, edge_slot : edge_slot + 1, 0:lanes] = corner_below[end : end + 1, :]
        high_rows[x + 1, edge_slot : edge_slot + 1, 0:lanes] = corner_above[
            x * by : x * by + 1, :
        ]


def pass_on(x, chunk, indices, source, leaving_of, speed, halos, fresh, place, total, change):
    gas, low_rows, high_rows, columns = halos
    by = gas.shape[1]
    chunks = by // tall
    rows = pl.ds(chunk * tall, tall)
    rest = 1.0 - 1.5 * (speed[0] * speed[0] + speed[1] * speed[1] + speed[2] * speed[2])
    equals = {}

    def moved(load, index, slot, lane):
        step_x, step_y, step_z = velocity_set[index]
        plane = x + 1 - step_x
        edges = low_rows if step_y == 1 else high_rows
        found = rows_of(load, chunk, chunks, step_y, lambda: edges[plane, slot : slot + 1, :])
        if step_z == 0:
            return found
        halo = rows_of(
            lambda low, high: columns[plane, low:high, :],
            chunk,
            chunks,
            step_y,
            lambda: edges[plane, edge_slot : edge_slot + 1, 0:lanes],
        )
        return columns_of(found, halo, lane, step_z)

    for index in indices:
        step_x, step_y, step_z = velocity_set[index]
        first = min(index, opposite_of[index])
        if first not in equals:
            proj = along(first, speed)
            equals[first] = 2.0 * lattice_weights[first] * (rest + 4.5 * proj * proj)
        slot, lane, gas_lane = (None, None, None)
        if step_y != 0:
            slot = (y_up if step_y == 1 else y_down).index(index)
        if step_z == 1:
            lane, gas_lane = (z_up.index(index), gas_slot)
        elif step_z == -1:
            lane, gas_lane = (sides + z_down.index(index), sides + gas_slot)
        field = source(index)
        marks = gas.at[x + 1 - step_x]
        arriving = moved(lambda low, high: field[low:high, :], index, slot, lane)
        from_gas = moved(lambda low, high: marks[low:high, :], index, gas_slot, gas_lane)
        leaving = leaving_of(opposite_of[index])[rows, :]
        open_side = from_gas > 0.5
        value = jnp.where(open_side, equals[first] - leaving, arriving)
        fresh(index)[place, rows, :] = value
        total = total + value
        change = change + jnp.where(open_side, 0.0, arriving - leaving)
    return total, change


def settle(x, rows, mass, flags, code, total, change):
    read = mass[x, rows, :] + jnp.where(flags[x, rows, :] == 1, change, 0.0)
    mark = code[x, rows, :]
    liquid = mark >= 32.0
    converts = mark > 0.0
    level = jnp.where(liquid, total, 0.0)
    excess = jnp.where(converts, read - level, 0.0)
    heading = jnp.where(liquid, mark - 32.0, mark)
    return jnp.where(converts, level, read), excess, heading


slanted = tuple(index for index in range(19) if velocity_set[index][1] * velocity_set[index][2])
first_slanted = slanted[0]


def from_inside(x, bx):
    found = [index for index in range(1, 19) if 0 <= x - velocity_set[index][0] < bx]
    return [index for index in found if index not in slanted]


def from_beyond(x, bx):
    return [index for index in range(1, 19) if not 0 <= x - velocity_set[index][0] < bx]


def stream_early(
    inner_post,
    outer_post,
    inner_shift,
    outer_shift,
    flags,
    y_first,
    y_second,
    z_rows,
    inner,
    outer,
    totals,
    changes,
    gas,
    low_rows,
    high_rows,
    columns,
):
    bx, by, bz = flags.shape
    halos = (gas, low_rows, high_rows, columns)
    own_halos(flags, y_first, y_second, z_rows, *halos)

    for x in range(bx):
        inside = 0 < x < bx - 1
        place = x - 1 if inside else end_place(x, bx)
        fresh = inner if inside else outer
        for chunk in range(by // tall):
            rows = pl.ds(chunk * tall, tall)
            total = plane_of(inner_post, outer_post, 0, x, bx)[rows, :]
            fresh[0, place, rows, :] = total
            total, change = pass_on(
                x,
                chunk,
                from_inside(x, bx),
                lambda index: plane_of(
                    inner_post, outer_post, index, x - velocity_set[index][0], bx
                ),
                lambda index: plane_of(inner_post, outer_post, index, x, bx),
                [plane_of(inner_shift, outer_shift, comp, x, bx)[rows, :] for comp in range(3)],
                halos,
                lambda index: fresh.at[index],
                place,
                total,
                jnp.zeros((tall, bz), jnp.float32),
            )
            totals[x, rows, :] = total
            changes[x, rows, :] = change


def stream_slanted(
    inner_post,
    outer_post,
    inner_shift,
    outer_shift,
    mass,
    flags,
    code,
    y_first,
    y_second,
    z_rows,
    corner_first,
    corner_second,
    totals,
    changes,
    inner,
    outer,
    settled,
    excess,
    heading,
    end_totals,
    end_changes,
    gas,
    low_rows,
    high_rows,
    columns,
):
    bx, by, bz = flags.shape
    halos = (gas, low_rows, high_rows, columns)
    own_halos(flags, y_first, y_second, z_rows, *halos)
    own_corners(corner_first, corner_second, low_rows, high_rows)

    for x in range(bx):
        inside = 0 < x < bx - 1
        place = x - 1 if inside else end_place(x, bx)
        fresh = inner if inside else outer
        for chunk in range(by // tall):
            rows = pl.ds(chunk * tall, tall)
            total, change = pass_on(
                x,
                chunk,
                slanted,
                lambda index: plane_of(inner_post, outer_post, index, x, bx),
                lambda index: plane_of(inner_post, outer_post, index, x, bx),
                [plane_of(inner_shift, outer_shift, comp, x, bx)[rows, :] for comp in range(3)],
                halos,
                lambda index: fresh.at[index - first_slanted],
                place,
                totals[x, rows, :],
                changes[x, rows, :],
            )
            if inside:
                now = settle(x, rows, mass, flags, code, total, change)
                settled[place, rows, :], excess[place, rows, :], heading[place, rows, :] = now
            else:
                end_totals[place, rows, :] = total
                end_changes[place, rows, :] = change


def stream_late(
    post,
    shift,
    mass,
    flags,
    code,
    totals,
    changes,
    gas_first,
    gas_second,
    x_first,
    x_second,
    edges_first,
    edges_second,
    inner_excess,
    inner_heading,
    flow,
    after,
    late,
    v_first,
    settled,
    spread,
    line_first,
    line_second,
    out_z,
    gas,
    low_rows,
    high_rows,
    columns,
    below,
    above,
    excess,
    heading,
):
    bx, by, bz = flags.shape
    halves = bz // lanes
    flip_x = odd("gx")
    halos = (gas, low_rows, high_rows, columns)

    for comp in range(3):
        up, down = (flow[comp, bx - 1], flow[comp, 0])
        v_first[comp] = jnp.where(flip_x, down, up)
    for slot in range(5):
        below[slot] = jnp.where(flip_x, x_first[slot], x_second[slot])
        above[slot] = jnp.where(flip_x, x_second[slot], x_first[slot])
    gas[0] = jnp.where(flip_x, gas_first[3], gas_second[3])
    gas[bx + 1] = jnp.where(flip_x, gas_second[3], gas_first[3])
    edges_below = select(flip_x, edges_first, edges_second)
    edges_above = select(flip_x, edges_second, edges_first)
    for found, at, x, edges in (
        (edges_below, 0, bx - 1, up_edges),
        (edges_above, bx + 1, 0, down_edges),
    ):
        for place, (side, slot) in enumerate(edges):
            line = jnp.concatenate(
                [found[half * 4 + place : half * 4 + place + 1, :] for half in range(halves)],
                axis=1,
            )
            (low_rows, high_rows)[side][at, slot : slot + 1, :] = line
        columns[at] = row_columns(found[4 * halves :, :])[x * by : x * by + by, :]
    for place, x in enumerate((0, bx - 1)):
        halo, order = ((below, x_up), (above, x_down))[place]
        for chunk in range(by // tall):
            rows = pl.ds(chunk * tall, tall)
            total, change = pass_on(
                x,
                chunk,
                from_beyond(x, bx),
                lambda index: halo.at[order.index(index)],
                lambda index: post.at[index, place],
                [shift[comp, place, rows, :] for comp in range(3)],
                halos,
                lambda index: late.at[order.index(index)],
                place,
                totals[place, rows, :],
                changes[place, rows, :],
            )
            now = settle(x, rows, mass, flags, code, total, change)
            settled[place, rows, :], excess[x, rows, :], heading[x, rows, :] = now
    for x in range(1, bx - 1):
        excess[x] = inner_excess[x - 1]
        heading[x] = inner_heading[x - 1]

    row_at, lane_at = (iota((by, bz), 0), iota((by, bz), 1))
    line_at = iota((1, bz), 1)
    tile_lane, line_lane = (iota((by, lanes), 1), iota((1, lanes), 1))

    def rows_up(rows):
        return jnp.where(row_at == 0, 0.0, pltpu.roll(rows, 1, 0))

    def rows_down(rows):
        return jnp.where(row_at == by - 1, 0.0, pltpu.roll(rows, by - 1, 0))

    def over(rows, at, step):
        if step == 1:
            return jnp.where(at == 0, 0.0, pltpu.roll(rows, 1, 1))
        return jnp.where(at == bz - 1, 0.0, pltpu.roll(rows, bz - 1, 1))

    def summed(parts):
        total = parts[0]
        for part in parts[1:]:
            total = total + part
        return total

    tile = jnp.zeros((by, lanes), jnp.float32)
    line_up = jnp.zeros((1, lanes), jnp.float32)
    line_down = jnp.zeros((1, lanes), jnp.float32)
    flip_y = odd("gy")
    line_first[...] = jnp.zeros(line_first.shape, jnp.float32)
    line_second[...] = jnp.zeros(line_second.shape, jnp.float32)
    for target in range(bx + 2):
        groups = {}
        for index in range(1, 19):
            step_x, step_y, step_z = velocity_set[index]
            x = target - 1 - step_x
            if 0 <= x < bx:
                part = jnp.where(heading[x] == float(index), excess[x], 0.0)
                groups.setdefault((step_y, step_z), []).append(part)
        groups = {key: summed(parts) for key, parts in groups.items()}
        total = jnp.zeros((by, bz), jnp.float32)
        line = {1: jnp.zeros((1, bz), jnp.float32), -1: jnp.zeros((1, bz), jnp.float32)}
        for step_z in (0, 1, -1):
            group = jnp.zeros((by, bz), jnp.float32)
            ends = {}
            if (0, step_z) in groups:
                group = group + groups[(0, step_z)]
            if (1, step_z) in groups:
                group = group + rows_up(groups[(1, step_z)])
                ends[1] = groups[(1, step_z)][by - 1 : by, :]
            if (-1, step_z) in groups:
                group = group + rows_down(groups[(-1, step_z)])
                ends[-1] = groups[(-1, step_z)][0:1, :]
            if step_z == 0:
                total = total + group
                for side in ends:
                    line[side] = line[side] + ends[side]
                continue
            total = total + over(group, lane_at, step_z)
            for side in ends:
                line[side] = line[side] + over(ends[side], line_at, step_z)
            if step_z == 1:
                spot, cut, roll = (target, slice(bz - lanes, bz), target + 1)
            else:
                spot, cut, roll = (8 + target, slice(0, lanes), 8 + target)
            tile = jnp.where(tile_lane == spot, pltpu.roll(group[:, cut], roll, 1), tile)
            if 1 in ends:
                line_up = jnp.where(
                    line_lane == spot, pltpu.roll(ends[1][:, cut], roll, 1), line_up
                )
            if -1 in ends:
                line_down = jnp.where(
                    line_lane == spot, pltpu.roll(ends[-1][:, cut], roll, 1), line_down
                )
        spread[target] = total
        line_first[target : target + 1, :] = jnp.where(flip_y, line[-1], line[1])
        line_second[target : target + 1, :] = jnp.where(flip_y, line[1], line[-1])
    rest = jnp.zeros((lanes - by - 2, lanes), jnp.float32)
    out_z[...] = column_rows([tile, line_up, line_down, rest], 16)


def with_edges(total, target, tile, y_below, y_above):
    by, bz = total.shape
    row_at, lane_at = (iota((by, bz), 0), iota((by, bz), 1))
    total = total + jnp.where(lane_at == 0, tile[0:by, target : target + 1], 0.0)
    total = total + jnp.where(lane_at == bz - 1, tile[0:by, 8 + target : 9 + target], 0.0)
    total = total + jnp.where(row_at == 0, y_below[target : target + 1, :], 0.0)
    return total + jnp.where(row_at == by - 1, y_above[target : target + 1, :], 0.0)


def add_faces(spread, z_rows, y_first, y_second, first, second):
    last = spread.shape[0] - 1
    flip_x, flip_y = (odd("gx"), odd("gy"))
    tile = row_columns(z_rows[...])
    y_below, y_above = (select(flip_y, y_first, y_second), select(flip_y, y_second, y_first))
    up = with_edges(spread[last], last, tile, y_below, y_above)
    down = with_edges(spread[0], 0, tile, y_below, y_above)
    first[...] = jnp.where(flip_x, down, up)
    second[...] = jnp.where(flip_x, up, down)


def add_all(
    inner_settled,
    outer_settled,
    spread,
    z_rows,
    y_first,
    y_second,
    corner_first,
    corner_second,
    x_second,
    x_first,
    after,
    new_mass,
):
    bx, by, bz = new_mass.shape
    flip_x, flip_y = (odd("gx"), odd("gy"))
    tile = row_columns(z_rows[...])
    y_below, y_above = (select(flip_y, y_first, y_second), select(flip_y, y_second, y_first))
    at = iota((8, bz), 1)
    found = []
    for rows, side, corner in (
        (y_below, 0, select(flip_y, corner_first, corner_second)),
        (y_above, 1, select(flip_y, corner_second, corner_first)),
    ):
        edge = corner[:, by + side : by + side + 1]
        rows = rows + jnp.where(at == 0, edge[0:8, :], 0.0)
        found.append(rows + jnp.where(at == bz - 1, edge[8:16, :], 0.0))
    for x in range(bx):
        total = with_edges(spread[x + 1], x + 1, tile, *found)
        if x == 0:
            total = total + select(flip_x, x_first, x_second)
        if x == bx - 1:
            total = total + select(flip_x, x_second, x_first)
        if 0 < x < bx - 1:
            total = total + inner_settled[x - 1]
        else:
            total = total + outer_settled[0 if x == 0 else 1]
        new_mass[x] = total


def swapped_ahead(array, axis):
    devices = lax.axis_size(axis)
    pairing = [(i, (i + 1) % devices if i % 2 == 0 else i - 1) for i in range(devices)]
    return lax.ppermute(array, axis, pairing)


def swapped_behind(array, axis):
    devices = lax.axis_size(axis)
    pairing = [(i, (i - 1) % devices if i % 2 == 0 else (i + 1) % devices) for i in range(devices)]
    return lax.ppermute(array, axis, pairing)


def swapped(first, second, axis):
    return swapped_ahead(first, axis), swapped_behind(second, axis)


def both_ways(rows, lower):
    devices = lax.axis_size("gz")
    before = lax.ppermute(rows, "gz", [(i, (i + 1) % devices) for i in range(devices)])
    if devices == 2:
        return before
    after = lax.ppermute(rows, "gz", [(i, (i - 1) % devices) for i in range(devices)])
    return jnp.where(iota(rows.shape, 0) < lower, before, after)


remote = pl.BlockSpec(memory_space=pltpu.HBM)
anywhere = pl.BlockSpec(memory_space=pl.ANY)


def call(body, outs, specs=None, out_specs=None, scratch=(), cost=(0, 0), aliases=None):
    extra = {} if specs is None else {"in_specs": specs}
    if out_specs is not None:
        extra["out_specs"] = out_specs
    return pl.pallas_call(
        body,
        out_shape=[
            shape
            if isinstance(shape, jax.ShapeDtypeStruct)
            else jax.ShapeDtypeStruct(shape, jnp.float32)
            for shape in outs
        ],
        scratch_shapes=[
            pltpu.VMEM(shape, jnp.float32) if isinstance(shape, tuple) else shape
            for shape in scratch
        ],
        compiler_params=pltpu.CompilerParams(vmem_limit_bytes=40 * 1024 * 1024),
        input_output_aliases=aliases or {},
        cost_estimate=pl.CostEstimate(flops=cost[0], bytes_accessed=cost[1], transcendentals=0),
        **extra,
    )


def shards(populations, stretch, mass, flags, conv_source, conv_kind, conv_direction):
    bx, by, bz = flags.shape
    cells = bx * by * bz
    box, face, tile = ((bx, by, bz), (by, bz), (bx, by, lanes))

    stretch, flags, z_out, y_one, y_two, x_one, x_two = call(
        first_faces,
        [
            (6, *box),
            jax.ShapeDtypeStruct(box, jnp.int32),
            (8, bx * by),
            (4 * bx, bz),
            (4 * bx, bz),
            (4, *face),
            (4, *face),
        ],
        specs=[remote] * 2,
        scratch=[pltpu.SemaphoreType.DMA((2,))],
        cost=(10 * cells, 60 * cells),
    )(*(pltpu.with_memory_space_constraint(array, pltpu.HBM) for array in (stretch, flags)))
    first_x = swapped(x_one, x_two, "gx")
    z_first = both_ways(z_out, 3)
    y_first = swapped(y_one, y_two, "gy")

    entries = conv_source.shape[0]
    mark = (tall, lanes)
    code, code_done = call(
        lambda *refs: conversions(*refs, columns=bz),
        [(bx * by, bz), mark],
        cost=(40 * cells, 4 * cells),
    )(*(array.reshape(1, entries) for array in (conv_source, conv_kind, conv_direction)))
    code = code.reshape(box)

    pops, flow = call(
        moments,
        [(19, *box), (5, *box)],
        specs=[remote],
        scratch=[pltpu.SemaphoreType.DMA((bx,))],
        cost=(60 * cells, 150 * cells),
    )(pltpu.with_memory_space_constraint(populations, pltpu.HBM))

    columns, rows = ((24, bx * by), (10 * bx, bz))
    sides_y = [(bx, 8, bz), (bx, 8, bz), tile]
    inside, ends = ((bx - 2, *face), (2, *face))
    inner_post, inner_shift = call(
        collide_inner,
        [(19, *inside), (3, *inside)],
        scratch=sides_y,
        cost=(150 * cells, 150 * cells),
    )(pops, stretch, flow, z_first, *y_first)
    outer_post, outer_shift, z_out, x_one, x_two, y_one, y_two = call(
        collide_outer,
        [(19, *ends), (3, *ends), columns, (5, *face), (8, *face), rows, rows],
        scratch=[(4, *face), (4, *face)] + sides_y + [box],
        cost=(150 * cells, 150 * cells),
    )(pops, stretch, flags, flow, *first_x, *y_first, z_first, inner_post)
    z_post = both_ways(z_out, sides)
    post_y = swapped(y_one, y_two, "gy")
    post_x = swapped(x_one, x_two, "gx")
    edges = (4 * (bz // lanes) + columns[0], lanes)
    x_one, x_two, corner = call(
        lambda *refs: forward_edges(*refs, bx=bx), [edges, edges, columns], cost=(17 * 10**8, 0)
    )(z_post, *post_y, code_done)
    corners = swapped(corner, corner, "gy")
    edges_x = swapped(x_one, x_two, "gx")

    rims = [(bx + 2, *face), (bx + 2, 16, bz), (bx + 2, 16, bz), (bx + 2, by, lanes)]
    posts = (inner_post, outer_post, inner_shift, outer_shift)
    inner, outer, totals, changes = call(
        stream_early,
        [(first_slanted, *inside), (first_slanted, *ends), box, box],
        scratch=rims,
        cost=(350 * cells, 200 * cells),
    )(*posts, flags, *post_y, z_post)
    (
        inner_slanted,
        outer_slanted,
        inner_settled,
        inner_excess,
        inner_heading,
        totals,
        changes,
    ) = call(
        stream_slanted,
        [(4, *inside), (4, *ends), inside, inside, inside, ends, ends],
        scratch=rims,
        cost=(100 * cells, 60 * cells),
    )(*posts, mass, flags, code, *post_y, z_post, *corners, totals, changes)
    new_stretch, inner_done = call(
        restretch_inner,
        [(6, *box), mark],
        out_specs=[remote, pl.BlockSpec()],
        scratch=[(6, *inside)] + sides_y + [pltpu.SemaphoreType.DMA],
        cost=(80 * cells, 40 * cells),
    )(stretch, flow, *post_y, z_post)
    late, v_one, outer_settled, spread, y_one, y_two, z_out = call(
        stream_late,
        [
            (5, *ends),
            (3, *face),
            ends,
            (bx + 2, *face),
            (8, bz),
            (8, bz),
            (16, bx * by),
        ],
        scratch=rims + [(5, *face), (5, *face), box, box],
        cost=(150 * cells, 100 * cells),
    )(
        outer_post,
        outer_shift,
        mass,
        flags,
        code,
        totals,
        changes,
        *first_x,
        *post_x,
        *edges_x,
        inner_excess,
        inner_heading,
        flow,
        inner_done,
    )
    z_last = both_ways(z_out, 8)
    last_y = swapped(y_one, y_two, "gy")
    last_corners = swapped(z_last, z_last, "gy")
    flow_x = (swapped_ahead(v_one, "gx"), post_x[1])
    x_one, x_two = call(add_faces, [face, face], cost=(4 * 10**9, 0))(spread, z_last, *last_y)
    last_x = swapped(x_one, x_two, "gx")
    new_stretch, fresh, outer_done = call(
        restretch_outer,
        [(6, *box), (19, *box), mark],
        specs=[pl.BlockSpec()] * 7 + [remote] + [pl.BlockSpec()] * 5,
        out_specs=[remote, remote, pl.BlockSpec()],
        scratch=[(6, *ends), (3, *face), (3, *face)]
        + sides_y
        + [pltpu.SemaphoreType.DMA((2,)), pltpu.SemaphoreType.DMA((32,))],
        cost=(80 * cells, 200 * cells),
        aliases={7: 0},
    )(
        stretch,
        flow,
        *flow_x,
        *post_y,
        z_post,
        new_stretch,
        inner,
        outer,
        inner_slanted,
        outer_slanted,
        late,
    )
    (new_mass,) = call(add_all, [box])(
        inner_settled, outer_settled, spread, z_last, *last_y, *last_corners, *last_x[::-1], outer_done
    )
    return (fresh, new_stretch, new_mass)


def solution(mesh):
    return jax.shard_map(
        shards,
        mesh=mesh,
        in_specs=(
            P(None, "gx", "gy", "gz"),
            P(None, "gx", "gy", "gz"),
            P("gx", "gy", "gz"),
            P("gx", "gy", "gz"),
            P(("gx", "gy", "gz")),
            P(("gx", "gy", "gz")),
            P(("gx", "gy", "gz")),
        ),
        out_specs=(P(None, "gx", "gy", "gz"), P(None, "gx", "gy", "gz"), P("gx", "gy", "gz")),
        check_vma=False,
    )
```

```python
import jax
import jax.numpy as jnp
from jax import lax
from jax.experimental import pallas as pl
from jax.experimental.pallas import tpu as pltpu
from jax.sharding import PartitionSpec as P

velocity_set = (
    (0, 0, 0),
    (1, 0, 0),
    (-1, 0, 0),
    (0, 1, 0),
    (0, -1, 0),
    (0, 0, 1),
    (0, 0, -1),
    (1, 1, 0),
    (-1, -1, 0),
    (1, -1, 0),
    (-1, 1, 0),
    (1, 0, 1),
    (-1, 0, -1),
    (1, 0, -1),
    (-1, 0, 1),
    (0, 1, 1),
    (0, -1, -1),
    (0, 1, -1),
    (0, -1, 1),
)
opposite_of = (0, 2, 1, 4, 3, 6, 5, 8, 7, 10, 9, 12, 11, 14, 13, 16, 15, 18, 17)
lattice_weights = (1.0 / 3.0,) + (1.0 / 18.0,) * 6 + (1.0 / 36.0,) * 12
symmetric_slot = ((0, 3, 4), (3, 1, 5), (4, 5, 2))
tensor_pairs = ((0, 0), (1, 1), (2, 2), (0, 1), (0, 2), (1, 2))
relax_time = 0.8
polymer_time = 8.0
polymer_coeff = 0.05


def moving(axis, sign):
    return tuple(index for index in range(19) if velocity_set[index][axis] == sign)


x_up, x_down = (moving(0, 1), moving(0, -1))
y_up, y_down = (moving(1, 1), moving(1, -1))
z_up, z_down = (moving(2, 1), moving(2, -1))
pairs = tuple(range(1, 19, 2))
gas_slot = 5
speed_slot = 6
edge_slot = 9
sides = 9
lanes = 128
tall = 8


def iota(shape, dim):
    return lax.broadcasted_iota(jnp.int32, shape, dim)


def wide(tile, width):
    return jnp.concatenate([tile] * (width // tile.shape[1]), axis=1)


def rows_of(load, chunk, chunks, step, edge):
    low = chunk * tall
    if step == 0:
        return load(low, low + tall)
    if step == 1 and chunk > 0:
        return load(low - 1, low + tall - 1)
    if step == -1 and chunk < chunks - 1:
        return load(low + 1, low + tall + 1)
    rows = load(low, low + tall)
    at = iota(rows.shape, 0)
    if step == 1:
        return jnp.where(at == 0, edge(), pltpu.roll(rows, 1, 0))
    return jnp.where(at == tall - 1, edge(), pltpu.roll(rows, tall - 1, 0))


def columns_of(rows, halo, lane, step):
    width = rows.shape[1]
    at = iota(rows.shape, 1)
    if step == 1:
        edge = wide(pltpu.roll(halo, (lanes - lane) % lanes, 1), width)
        return jnp.where(at == 0, edge, pltpu.roll(rows, 1, 1))
    edge = wide(pltpu.roll(halo, lanes - 1 - lane, 1), width)
    return jnp.where(at == width - 1, edge, pltpu.roll(rows, width - 1, 1))


def packed(high, low):
    at = iota(high[0].shape, 1)
    tile = jnp.zeros_like(high[0])
    for slot, part in enumerate(high):
        tile = jnp.where(at == slot, pltpu.roll(part, slot + 1, 1), tile)
    for place, part in enumerate(low):
        slot = len(high) + place
        tile = jnp.where(at == slot, pltpu.roll(part, slot, 1), tile)
    return tile


def along(index, vector):
    total = None
    for comp in range(3):
        sign = velocity_set[index][comp]
        if sign != 0:
            term = vector[comp] if sign > 0 else -vector[comp]
            total = term if total is None else total + term
    return total


def conversions(source, kind, heading, code, mark, *, columns):
    count = source.shape[1]
    value = (heading[...] + 32 * kind[...]).astype(jnp.float32)
    row, column = (source[...] // columns, source[...] % columns)
    by_row = jnp.where(iota((code.shape[0], count), 0) == row, value, 0.0).astype(jnp.bfloat16)
    by_column = jnp.where(iota((columns, count), 0) == column, 1.0, 0.0).astype(jnp.bfloat16)
    code[...] = lax.dot_general(
        by_row, by_column, (((1,), (1,)), ((), ())), preferred_element_type=jnp.float32
    )
    mark[...] = jnp.zeros(mark.shape, jnp.float32)


def odd(axis):
    return lax.rem(lax.axis_index(axis), 2) == 1


def select(chosen, first, second):
    return jnp.where(chosen, first[...], second[...])


def swap_rows(first, second, x, planes, high, low, flip):
    for slot, (top, bottom) in enumerate(zip(high, low)):
        by = top.shape[0]
        up, down = (top[by - 1 : by, :], bottom[0:1, :])
        at = slot * planes + x
        first[at : at + 1, :] = jnp.where(flip, down, up)
        second[at : at + 1, :] = jnp.where(flip, up, down)


def swapped_rows(first, second, slots, low_rows, high_rows, shift):
    flip = odd("gy")
    planes = low_rows.shape[0] - 2 * shift
    for x in range(planes):
        for place, slot in enumerate(slots):
            at = slot * planes + x
            one, two = (first[at : at + 1, :], second[at : at + 1, :])
            low_rows[x + shift, place : place + 1, :] = jnp.where(flip, one, two)
            high_rows[x + shift, place : place + 1, :] = jnp.where(flip, two, one)


def column_rows(tiles, count):
    return jnp.concatenate(tiles, axis=0).T[0:count, :]


def row_columns(rows):
    rest = jnp.zeros((lanes - rows.shape[0], rows.shape[1]), jnp.float32)
    return jnp.concatenate([rows, rest], axis=0).T


def first_faces(
    stretch_in,
    flags_in,
    stretch,
    flags,
    columns,
    y_first,
    y_second,
    x_first,
    x_second,
    sems,
):
    bx, by, bz = flags.shape
    flip_x, flip_y = (odd("gx"), odd("gy"))
    copies = [
        pltpu.make_async_copy(stretch_in, stretch, sems.at[0]),
        pltpu.make_async_copy(flags_in, flags, sems.at[1]),
    ]
    for copy in copies:
        copy.start()
    for copy in copies:
        copy.wait()
    tiles = []
    for x in range(bx):
        along_y = [stretch.at[symmetric_slot[comp][1], x] for comp in range(3)]
        swap_rows(y_first, y_second, x, bx, along_y, along_y, flip_y)
        fields = [stretch.at[symmetric_slot[comp][2], x] for comp in range(3)]
        tiles.append(
            packed(
                [field[:, bz - lanes : bz] for field in fields],
                [field[:, 0:lanes] for field in fields],
            )
        )
    columns[...] = column_rows(tiles, columns.shape[0])
    rest = y_first.shape[0] - 3 * bx
    y_first[3 * bx :, :] = jnp.zeros((rest, bz), jnp.float32)
    y_second[3 * bx :, :] = jnp.zeros((rest, bz), jnp.float32)
    for out, last in ((x_first, flip_x), (x_second, jnp.logical_not(flip_x))):
        for comp in range(3):
            slot = symmetric_slot[comp][0]
            out[comp] = jnp.where(last, stretch[slot, 0], stretch[slot, bx - 1])
        out[3] = jnp.where(jnp.where(last, flags[0], flags[bx - 1]) == 0, 1.0, 0.0)


def moments(pops_in, pops, flow, sems):
    bx, by = pops.shape[1:3]
    copies = [
        pltpu.make_async_copy(pops_in.at[:, x], pops.at[:, x], sems.at[x]) for x in range(bx)
    ]
    for copy in copies:
        copy.start()
    for x in range(bx):
        copies[x].wait()
        for chunk in range(by // tall):
            rows = pl.ds(chunk * tall, tall)
            part = [pops[index, x, rows, :] for index in range(19)]
            density = part[0]
            for index in range(1, 19):
                density = density + part[index]
            inverse = 1.0 / density
            for comp in range(3):
                total = None
                for index in pairs:
                    sign = velocity_set[index][comp]
                    if sign != 0:
                        term = part[index] - part[index + 1]
                        term = term if sign > 0 else -term
                        total = term if total is None else total + term
                flow[comp, x, rows, :] = total * inverse
            flow[3, x, rows, :] = density
            flow[4, x, rows, :] = inverse


def beside(ref, field, x, step, halo, slot):
    last = ref.shape[1] - 1
    if halo is None:
        return lambda low, high: ref[field, x + step, low:high, :]
    if isinstance(x, int):
        if 0 <= x + step <= last:
            return lambda low, high: ref[field, x + step, low:high, :]
        return lambda low, high: halo[slot, low:high, :]
    inside = jnp.clip(x + step, 0, last)
    beyond = x == (0 if step < 0 else last)
    return lambda low, high: jnp.where(
        beyond, halo[slot, low:high, :], ref[field, inside, low:high, :]
    )


def differences(
    ref, field, slots, x, chunk, chunks, below, above, y_below, y_above, z_halo, lane, side
):
    slot_x, slot_y, slot_z = slots
    low, high = (chunk * tall, chunk * tall + tall)

    def load(first, stop):
        return ref[field, x, first:stop, :]

    result = [None, None, None]
    if slot_x is not None:
        after = beside(ref, field, x, 1, above, slot_x)(low, high)
        before = beside(ref, field, x, -1, below, slot_x)(low, high)
        result[0] = after - before
    if slot_y is not None:
        after = rows_of(load, chunk, chunks, -1, lambda: y_above[x, slot_y : slot_y + 1, :])
        before = rows_of(load, chunk, chunks, 1, lambda: y_below[x, slot_y : slot_y + 1, :])
        result[1] = after - before
    if slot_z is not None:
        rows, halo = (load(low, high), z_halo[x, low:high, :])
        after = columns_of(rows, halo, lane + side + slot_z, -1)
        before = columns_of(rows, halo, lane + slot_z, 1)
        result[2] = after - before
    return result


def end_place(x, bx):
    return 0 if x == 0 else 1


def plane_of(inner, outer, field, x, bx):
    if 0 < x < bx - 1:
        return inner.at[field, x - 1]
    return outer.at[field, end_place(x, bx)]


def collide_plane(x, place, pops, stretch, flow, halos, post, shift):
    by = pops.shape[2]
    chunks = by // tall
    factor = 1.0 - 0.5 / relax_time
    rate = 1.0 / relax_time
    for chunk in range(chunks):
        rows = pl.ds(chunk * tall, tall)
        terms = [[], [], []]
        for field in range(6):
            slots = [None, None, None]
            for comp in range(3):
                for axis in range(3):
                    if symmetric_slot[comp][axis] == field:
                        slots[axis] = comp
            found = differences(stretch, field, slots, x, chunk, chunks, *halos)
            for axis in range(3):
                if slots[axis] is not None:
                    terms[slots[axis]].append(found[axis])
        force = [0.5 * polymer_coeff * (part[0] + part[1] + part[2]) for part in terms]
        density, half = (flow[3, x, rows, :], 0.5 * flow[4, x, rows, :])
        moved = [flow[comp, x, rows, :] + half * force[comp] for comp in range(3)]
        for comp in range(3):
            shift[comp, place, rows, :] = moved[comp]
        squared = moved[0] * moved[0] + moved[1] * moved[1] + moved[2] * moved[2]
        work = moved[0] * force[0] + moved[1] * force[1] + moved[2] * force[2]
        weight = rate * density
        common = weight - 1.5 * weight * squared - 3.0 * factor * work
        odd = [3.0 * weight * moved[comp] + 3.0 * factor * force[comp] for comp in range(3)]
        even = [4.5 * weight * moved[comp] + 9.0 * factor * force[comp] for comp in range(3)]
        keep = 1.0 - rate
        post[0, place, rows, :] = keep * pops[0, x, rows, :] + lattice_weights[0] * common
        for index in pairs:
            both = common + along(index, moved) * along(index, even)
            differ = along(index, odd)
            scale = lattice_weights[index]
            post[index, place, rows, :] = keep * pops[index, x, rows, :] + scale * (both + differ)
            post[index + 1, place, rows, :] = keep * pops[index + 1, x, rows, :] + scale * (
                both - differ
            )


def collide_inner(
    pops,
    stretch,
    flow,
    z_rows,
    y_first,
    y_second,
    post,
    shift,
    y_below,
    y_above,
    z_halo,
):
    swapped_rows(y_first, y_second, range(3), y_below, y_above, 0)
    z_halo[...] = row_columns(z_rows[...]).reshape(z_halo.shape)
    halos = (None, None, y_below, y_above, z_halo, 0, 3)

    def plane(x, carry):
        collide_plane(x, x - 1, pops, stretch, flow, halos, post, shift)
        return carry

    lax.fori_loop(1, pops.shape[1] - 1, plane, 0)


def collide_outer(
    pops,
    stretch,
    flags,
    flow,
    x_first,
    x_second,
    y_first,
    y_second,
    z_rows,
    inner,
    post,
    shift,
    columns,
    ahead,
    behind,
    up_first,
    up_second,
    below,
    above,
    y_below,
    y_above,
    z_halo,
    gas,
):
    bx, by, bz = flags.shape
    halos = (below, above, y_below, y_above, z_halo, 0, 3)
    flip_x, flip_y = (odd("gx"), odd("gy"))
    below[...] = select(flip_x, x_first, x_second)
    above[...] = select(flip_x, x_second, x_first)
    swapped_rows(y_first, y_second, range(3), y_below, y_above, 0)
    z_halo[...] = row_columns(z_rows[...]).reshape(z_halo.shape)
    for x in (0, bx - 1):
        collide_plane(x, end_place(x, bx), pops, stretch, flow, halos, post, shift)

    tiles = []
    for x in range(bx):
        gas[x] = jnp.where(flags[x] == 0, 1.0, 0.0)
        rest = [gas.at[x]] + [flow.at[comp, x] for comp in range(3)]

        def fields(indices):
            return [plane_of(inner, post, index, x, bx) for index in indices] + rest

        swap_rows(up_first, up_second, x, bx, fields(y_up), fields(y_down), flip_y)
        tiles.append(
            packed(
                [field[:, bz - lanes : bz] for field in fields(z_up)],
                [field[:, 0:lanes] for field in fields(z_down)],
            )
        )
    columns[...] = column_rows(tiles, columns.shape[0])
    rest = up_first.shape[0] - sides * bx
    up_first[sides * bx :, :] = jnp.zeros((rest, bz), jnp.float32)
    up_second[sides * bx :, :] = jnp.zeros((rest, bz), jnp.float32)
    for slot in range(5):
        up, down = (post[x_up[slot], 1], post[x_down[slot], 0])
        ahead[slot] = jnp.where(flip_x, down, up)
        behind[slot] = jnp.where(flip_x, up, down)
    for comp in range(3):
        behind[5 + comp] = jnp.where(flip_x, flow[comp, bx - 1], flow[comp, 0])


def restretch_plane(x, place, stretch, flow, halos, updated):
    chunks = stretch.shape[2] // tall
    for chunk in range(chunks):
        rows = pl.ds(chunk * tall, tall)
        grad = [
            differences(
                flow, comp, (comp, comp, comp), x, chunk, chunks, *halos, speed_slot, sides
            )
            for comp in range(3)
        ]
        part = [stretch[slot, x, rows, :] for slot in range(6)]
        full = [part[slot] + 1.0 if slot < 3 else part[slot] for slot in range(6)]

        def product(row, col):
            total = grad[row][0] * full[symmetric_slot[0][col]]
            for inner in (1, 2):
                total = total + grad[row][inner] * full[symmetric_slot[inner][col]]
            return total

        for slot, (row, col) in enumerate(tensor_pairs):
            old = (1.0 - 1.0 / polymer_time) * part[slot]
            if row == col:
                updated[slot, place, rows, :] = old + product(row, col)
            else:
                updated[slot, place, rows, :] = old + 0.5 * (product(row, col) + product(col, row))


def restretch_inner(
    stretch,
    flow,
    y_first,
    y_second,
    z_rows,
    new_stretch,
    mark,
    updated,
    y_below,
    y_above,
    z_halo,
    sem,
):
    bx = stretch.shape[1]
    swapped_rows(y_first, y_second, range(speed_slot, sides), y_below, y_above, 0)
    z_halo[...] = row_columns(z_rows[...]).reshape(z_halo.shape)
    halos = (None, None, y_below, y_above, z_halo)

    def plane(x, carry):
        restretch_plane(x, x - 1, stretch, flow, halos, updated)
        return carry

    lax.fori_loop(1, bx - 1, plane, 0)
    copy = pltpu.make_async_copy(updated, new_stretch.at[:, 1 : bx - 1], sem)
    copy.start()
    mark[...] = jnp.zeros(mark.shape, jnp.float32)
    copy.wait()


def restretch_outer(
    stretch,
    flow,
    x_first,
    x_second,
    y_first,
    y_second,
    z_rows,
    inner_stretch,
    outer,
    outer_slanted,
    late,
    inner_fresh,
    new_stretch,
    fresh,
    mark,
    updated,
    below,
    above,
    y_below,
    y_above,
    z_halo,
    sems,
    store_sems,
):
    bx = stretch.shape[1]
    moves = stored(outer, outer_slanted, late, fresh, store_sems)
    for copy in moves:
        copy.start()
    flip_x = odd("gx")
    for comp in range(3):
        below[comp] = jnp.where(flip_x, x_first[comp], x_second[5 + comp])
        above[comp] = jnp.where(flip_x, x_second[5 + comp], x_first[comp])
    swapped_rows(y_first, y_second, range(speed_slot, sides), y_below, y_above, 0)
    z_halo[...] = row_columns(z_rows[...]).reshape(z_halo.shape)
    halos = (below, above, y_below, y_above, z_halo)
    copies = []
    for place, x in enumerate((0, bx - 1)):
        restretch_plane(x, place, stretch, flow, halos, updated)
        copies.append(
            pltpu.make_async_copy(updated.at[:, place], new_stretch.at[:, x], sems.at[place])
        )
        copies[-1].start()
    mark[...] = jnp.zeros(mark.shape, jnp.float32)
    for copy in copies + moves:
        copy.wait()


def stored(outer, outer_slanted, late, fresh, sems):
    bx = fresh.shape[1]
    moves = []
    for place, x in enumerate((0, bx - 1)):
        moves.append((outer_slanted.at[:, place], fresh.at[first_slanted:, x]))
        order = (x_up, x_down)[place]
        start = 0
        for index in order + (first_slanted,):
            if index > start:
                run = slice(start, index)
                moves.append((outer.at[run, place], fresh.at[run, x]))
            if index in order:
                moves.append((late.at[order.index(index), place], fresh.at[index, x]))
            start = index + 1
    return [
        pltpu.make_async_copy(source, target, sems.at[place])
        for place, (source, target) in enumerate(moves)
    ]


def store_inner(inner, inner_slanted, after, fresh, mark, sems):
    bx = fresh.shape[1]
    copies = [
        pltpu.make_async_copy(
            inner, fresh.at[0:first_slanted, 1 : bx - 1], sems.at[0]
        ),
        pltpu.make_async_copy(
            inner_slanted, fresh.at[first_slanted:, 1 : bx - 1], sems.at[1]
        ),
    ]
    for copy in copies:
        copy.start()
    mark[...] = jnp.zeros(mark.shape, jnp.float32)
    for copy in copies:
        copy.wait()


up_edges = ((0, y_up.index(7)), (0, gas_slot), (1, y_down.index(9)), (1, gas_slot))
down_edges = ((0, y_up.index(10)), (0, gas_slot), (1, y_down.index(8)), (1, gas_slot))


def forward_edges(z_rows, y_first, y_second, after, first_out, second_out, corner, *, bx):
    halves = y_first.shape[1] // lanes
    flip_x, flip_y = (odd("gx"), odd("gy"))
    for half in range(halves):
        cut = slice(half * lanes, half * lanes + lanes)
        for place in range(4):
            found = []
            for x, edges in ((bx - 1, up_edges), (0, down_edges)):
                side, slot = edges[place]
                row = slot * bx + x
                one = y_first[row : row + 1, cut]
                two = y_second[row : row + 1, cut]
                found.append(jnp.where(flip_y, one, two) if side == 0 else jnp.where(flip_y, two, one))
            at = half * 4 + place
            first_out[at : at + 1, :] = jnp.where(flip_x, found[1], found[0])
            second_out[at : at + 1, :] = jnp.where(flip_x, found[0], found[1])
    first_out[4 * halves :, :] = z_rows[...]
    second_out[4 * halves :, :] = z_rows[...]
    corner[...] = z_rows[...]


def own_halos(flags, y_first, y_second, z_rows, gas, low_rows, high_rows, columns):
    bx, by = flags.shape[:2]
    tile = row_columns(z_rows[...])
    swapped_rows(y_first, y_second, range(speed_slot), low_rows, high_rows, 1)
    for x in range(bx):
        gas[x + 1] = jnp.where(flags[x] == 0, 1.0, 0.0)
        columns[x + 1] = tile[x * by : x * by + by, :]


def own_corners(corner_first, corner_second, low_rows, high_rows):
    bx = low_rows.shape[0] - 2
    flip = odd("gy")
    corner_below = row_columns(select(flip, corner_first, corner_second))
    corner_above = row_columns(select(flip, corner_second, corner_first))
    by = corner_below.shape[0] // bx
    for x in range(bx):
        end = x * by + by - 1
        low_rows[x + 1, edge_slot : edge_slot + 1, 0:lanes] = corner_below[end : end + 1, :]
        high_rows[x + 1, edge_slot : edge_slot + 1, 0:lanes] = corner_above[
            x * by : x * by + 1, :
        ]


def pass_on(x, chunk, indices, source, leaving_of, speed, halos, fresh, place, total, change):
    gas, low_rows, high_rows, columns = halos
    by = gas.shape[1]
    chunks = by // tall
    rows = pl.ds(chunk * tall, tall)
    rest = 1.0 - 1.5 * (speed[0] * speed[0] + speed[1] * speed[1] + speed[2] * speed[2])
    equals = {}

    def moved(load, index, slot, lane):
        step_x, step_y, step_z = velocity_set[index]
        plane = x + 1 - step_x
        edges = low_rows if step_y == 1 else high_rows
        found = rows_of(load, chunk, chunks, step_y, lambda: edges[plane, slot : slot + 1, :])
        if step_z == 0:
            return found
        halo = rows_of(
            lambda low, high: columns[plane, low:high, :],
            chunk,
            chunks,
            step_y,
            lambda: edges[plane, edge_slot : edge_slot + 1, 0:lanes],
        )
        return columns_of(found, halo, lane, step_z)

    for index in indices:
        step_x, step_y, step_z = velocity_set[index]
        first = min(index, opposite_of[index])
        if first not in equals:
            proj = along(first, speed)
            equals[first] = 2.0 * lattice_weights[first] * (rest + 4.5 * proj * proj)
        slot, lane, gas_lane = (None, None, None)
        if step_y != 0:
            slot = (y_up if step_y == 1 else y_down).index(index)
        if step_z == 1:
            lane, gas_lane = (z_up.index(index), gas_slot)
        elif step_z == -1:
            lane, gas_lane = (sides + z_down.index(index), sides + gas_slot)
        field = source(index)
        marks = gas.at[x + 1 - step_x]
        arriving = moved(lambda low, high: field[low:high, :], index, slot, lane)
        from_gas = moved(lambda low, high: marks[low:high, :], index, gas_slot, gas_lane)
        leaving = leaving_of(opposite_of[index])[rows, :]
        open_side = from_gas > 0.5
        value = jnp.where(open_side, equals[first] - leaving, arriving)
        fresh(index)[place, rows, :] = value
        total = total + value
        change = change + jnp.where(open_side, 0.0, arriving - leaving)
    return total, change


def settle(x, rows, mass, flags, code, total, change):
    read = mass[x, rows, :] + jnp.where(flags[x, rows, :] == 1, change, 0.0)
    mark = code[x, rows, :]
    liquid = mark >= 32.0
    converts = mark > 0.0
    level = jnp.where(liquid, total, 0.0)
    excess = jnp.where(converts, read - level, 0.0)
    heading = jnp.where(liquid, mark - 32.0, mark)
    return jnp.where(converts, level, read), excess, heading


slanted = tuple(index for index in range(19) if velocity_set[index][1] * velocity_set[index][2])
first_slanted = slanted[0]


def from_inside(x, bx):
    found = [index for index in range(1, 19) if 0 <= x - velocity_set[index][0] < bx]
    return [index for index in found if index not in slanted]


def from_beyond(x, bx):
    return [index for index in range(1, 19) if not 0 <= x - velocity_set[index][0] < bx]


def stream_early(
    inner_post,
    outer_post,
    inner_shift,
    outer_shift,
    flags,
    y_first,
    y_second,
    z_rows,
    inner,
    outer,
    totals,
    changes,
    gas,
    low_rows,
    high_rows,
    columns,
):
    bx, by, bz = flags.shape
    halos = (gas, low_rows, high_rows, columns)
    own_halos(flags, y_first, y_second, z_rows, *halos)

    for x in range(bx):
        inside = 0 < x < bx - 1
        place = x - 1 if inside else end_place(x, bx)
        fresh = inner if inside else outer
        for chunk in range(by // tall):
            rows = pl.ds(chunk * tall, tall)
            total = plane_of(inner_post, outer_post, 0, x, bx)[rows, :]
            fresh[0, place, rows, :] = total
            total, change = pass_on(
                x,
                chunk,
                from_inside(x, bx),
                lambda index: plane_of(
                    inner_post, outer_post, index, x - velocity_set[index][0], bx
                ),
                lambda index: plane_of(inner_post, outer_post, index, x, bx),
                [plane_of(inner_shift, outer_shift, comp, x, bx)[rows, :] for comp in range(3)],
                halos,
                lambda index: fresh.at[index],
                place,
                total,
                jnp.zeros((tall, bz), jnp.float32),
            )
            totals[x, rows, :] = total
            changes[x, rows, :] = change


def stream_slanted(
    inner_post,
    outer_post,
    inner_shift,
    outer_shift,
    mass,
    flags,
    code,
    y_first,
    y_second,
    z_rows,
    corner_first,
    corner_second,
    totals,
    changes,
    inner,
    outer,
    settled,
    excess,
    heading,
    end_totals,
    end_changes,
    gas,
    low_rows,
    high_rows,
    columns,
):
    bx, by, bz = flags.shape
    halos = (gas, low_rows, high_rows, columns)
    own_halos(flags, y_first, y_second, z_rows, *halos)
    own_corners(corner_first, corner_second, low_rows, high_rows)

    for x in range(bx):
        inside = 0 < x < bx - 1
        place = x - 1 if inside else end_place(x, bx)
        fresh = inner if inside else outer
        for chunk in range(by // tall):
            rows = pl.ds(chunk * tall, tall)
            total, change = pass_on(
                x,
                chunk,
                slanted,
                lambda index: plane_of(inner_post, outer_post, index, x, bx),
                lambda index: plane_of(inner_post, outer_post, index, x, bx),
                [plane_of(inner_shift, outer_shift, comp, x, bx)[rows, :] for comp in range(3)],
                halos,
                lambda index: fresh.at[index - first_slanted],
                place,
                totals[x, rows, :],
                changes[x, rows, :],
            )
            if inside:
                now = settle(x, rows, mass, flags, code, total, change)
                settled[place, rows, :], excess[place, rows, :], heading[place, rows, :] = now
            else:
                end_totals[place, rows, :] = total
                end_changes[place, rows, :] = change


def stream_late(
    post,
    shift,
    mass,
    flags,
    code,
    totals,
    changes,
    gas_first,
    gas_second,
    x_first,
    x_second,
    edges_first,
    edges_second,
    inner_excess,
    inner_heading,
    flow,
    after,
    late,
    v_first,
    settled,
    spread,
    line_first,
    line_second,
    out_z,
    gas,
    low_rows,
    high_rows,
    columns,
    below,
    above,
    excess,
    heading,
):
    bx, by, bz = flags.shape
    halves = bz // lanes
    flip_x = odd("gx")
    halos = (gas, low_rows, high_rows, columns)

    for comp in range(3):
        up, down = (flow[comp, bx - 1], flow[comp, 0])
        v_first[comp] = jnp.where(flip_x, down, up)
    for slot in range(5):
        below[slot] = jnp.where(flip_x, x_first[slot], x_second[slot])
        above[slot] = jnp.where(flip_x, x_second[slot], x_first[slot])
    gas[0] = jnp.where(flip_x, gas_first[3], gas_second[3])
    gas[bx + 1] = jnp.where(flip_x, gas_second[3], gas_first[3])
    edges_below = select(flip_x, edges_first, edges_second)
    edges_above = select(flip_x, edges_second, edges_first)
    for found, at, x, edges in (
        (edges_below, 0, bx - 1, up_edges),
        (edges_above, bx + 1, 0, down_edges),
    ):
        for place, (side, slot) in enumerate(edges):
            line = jnp.concatenate(
                [found[half * 4 + place : half * 4 + place + 1, :] for half in range(halves)],
                axis=1,
            )
            (low_rows, high_rows)[side][at, slot : slot + 1, :] = line
        columns[at] = row_columns(found[4 * halves :, :])[x * by : x * by + by, :]
    for place, x in enumerate((0, bx - 1)):
        halo, order = ((below, x_up), (above, x_down))[place]
        for chunk in range(by // tall):
            rows = pl.ds(chunk * tall, tall)
            total, change = pass_on(
                x,
                chunk,
                from_beyond(x, bx),
                lambda index: halo.at[order.index(index)],
                lambda index: post.at[index, place],
                [shift[comp, place, rows, :] for comp in range(3)],
                halos,
                lambda index: late.at[order.index(index)],
                place,
                totals[place, rows, :],
                changes[place, rows, :],
            )
            now = settle(x, rows, mass, flags, code, total, change)
            settled[place, rows, :], excess[x, rows, :], heading[x, rows, :] = now
    for x in range(1, bx - 1):
        excess[x] = inner_excess[x - 1]
        heading[x] = inner_heading[x - 1]

    row_at, lane_at = (iota((by, bz), 0), iota((by, bz), 1))
    line_at = iota((1, bz), 1)
    tile_lane, line_lane = (iota((by, lanes), 1), iota((1, lanes), 1))

    def rows_up(rows):
        return jnp.where(row_at == 0, 0.0, pltpu.roll(rows, 1, 0))

    def rows_down(rows):
        return jnp.where(row_at == by - 1, 0.0, pltpu.roll(rows, by - 1, 0))

    def over(rows, at, step):
        if step == 1:
            return jnp.where(at == 0, 0.0, pltpu.roll(rows, 1, 1))
        return jnp.where(at == bz - 1, 0.0, pltpu.roll(rows, bz - 1, 1))

    def summed(parts):
        total = parts[0]
        for part in parts[1:]:
            total = total + part
        return total

    tile = jnp.zeros((by, lanes), jnp.float32)
    line_up = jnp.zeros((1, lanes), jnp.float32)
    line_down = jnp.zeros((1, lanes), jnp.float32)
    flip_y = odd("gy")
    line_first[...] = jnp.zeros(line_first.shape, jnp.float32)
    line_second[...] = jnp.zeros(line_second.shape, jnp.float32)
    for target in range(bx + 2):
        groups = {}
        for index in range(1, 19):
            step_x, step_y, step_z = velocity_set[index]
            x = target - 1 - step_x
            if 0 <= x < bx:
                part = jnp.where(heading[x] == float(index), excess[x], 0.0)
                groups.setdefault((step_y, step_z), []).append(part)
        groups = {key: summed(parts) for key, parts in groups.items()}
        total = jnp.zeros((by, bz), jnp.float32)
        line = {1: jnp.zeros((1, bz), jnp.float32), -1: jnp.zeros((1, bz), jnp.float32)}
        for step_z in (0, 1, -1):
            group = jnp.zeros((by, bz), jnp.float32)
            ends = {}
            if (0, step_z) in groups:
                group = group + groups[(0, step_z)]
            if (1, step_z) in groups:
                group = group + rows_up(groups[(1, step_z)])
                ends[1] = groups[(1, step_z)][by - 1 : by, :]
            if (-1, step_z) in groups:
                group = group + rows_down(groups[(-1, step_z)])
                ends[-1] = groups[(-1, step_z)][0:1, :]
            if step_z == 0:
                total = total + group
                for side in ends:
                    line[side] = line[side] + ends[side]
                continue
            total = total + over(group, lane_at, step_z)
            for side in ends:
                line[side] = line[side] + over(ends[side], line_at, step_z)
            if step_z == 1:
                spot, cut, roll = (target, slice(bz - lanes, bz), target + 1)
            else:
                spot, cut, roll = (8 + target, slice(0, lanes), 8 + target)
            tile = jnp.where(tile_lane == spot, pltpu.roll(group[:, cut], roll, 1), tile)
            if 1 in ends:
                line_up = jnp.where(
                    line_lane == spot, pltpu.roll(ends[1][:, cut], roll, 1), line_up
                )
            if -1 in ends:
                line_down = jnp.where(
                    line_lane == spot, pltpu.roll(ends[-1][:, cut], roll, 1), line_down
                )
        spread[target] = total
        line_first[target : target + 1, :] = jnp.where(flip_y, line[-1], line[1])
        line_second[target : target + 1, :] = jnp.where(flip_y, line[1], line[-1])
    rest = jnp.zeros((lanes - by - 2, lanes), jnp.float32)
    out_z[...] = column_rows([tile, line_up, line_down, rest], 16)


def with_edges(total, target, tile, y_below, y_above):
    by, bz = total.shape
    row_at, lane_at = (iota((by, bz), 0), iota((by, bz), 1))
    total = total + jnp.where(lane_at == 0, tile[0:by, target : target + 1], 0.0)
    total = total + jnp.where(lane_at == bz - 1, tile[0:by, 8 + target : 9 + target], 0.0)
    total = total + jnp.where(row_at == 0, y_below[target : target + 1, :], 0.0)
    return total + jnp.where(row_at == by - 1, y_above[target : target + 1, :], 0.0)


def add_faces(spread, z_rows, y_first, y_second, after, first, second):
    last = spread.shape[0] - 1
    flip_x, flip_y = (odd("gx"), odd("gy"))
    tile = row_columns(z_rows[...])
    y_below, y_above = (select(flip_y, y_first, y_second), select(flip_y, y_second, y_first))
    up = with_edges(spread[last], last, tile, y_below, y_above)
    down = with_edges(spread[0], 0, tile, y_below, y_above)
    first[...] = jnp.where(flip_x, down, up)
    second[...] = jnp.where(flip_x, up, down)


def add_all(
    inner_settled,
    outer_settled,
    spread,
    z_rows,
    y_first,
    y_second,
    corner_first,
    corner_second,
    x_second,
    x_first,
    after,
    new_mass,
):
    bx, by, bz = new_mass.shape
    flip_x, flip_y = (odd("gx"), odd("gy"))
    tile = row_columns(z_rows[...])
    y_below, y_above = (select(flip_y, y_first, y_second), select(flip_y, y_second, y_first))
    at = iota((8, bz), 1)
    found = []
    for rows, side, corner in (
        (y_below, 0, select(flip_y, corner_first, corner_second)),
        (y_above, 1, select(flip_y, corner_second, corner_first)),
    ):
        edge = corner[:, by + side : by + side + 1]
        rows = rows + jnp.where(at == 0, edge[0:8, :], 0.0)
        found.append(rows + jnp.where(at == bz - 1, edge[8:16, :], 0.0))
    for x in range(bx):
        total = with_edges(spread[x + 1], x + 1, tile, *found)
        if x == 0:
            total = total + select(flip_x, x_first, x_second)
        if x == bx - 1:
            total = total + select(flip_x, x_second, x_first)
        if 0 < x < bx - 1:
            total = total + inner_settled[x - 1]
        else:
            total = total + outer_settled[0 if x == 0 else 1]
        new_mass[x] = total


def swapped_ahead(array, axis):
    devices = lax.axis_size(axis)
    pairing = [(i, (i + 1) % devices if i % 2 == 0 else i - 1) for i in range(devices)]
    return lax.ppermute(array, axis, pairing)


def swapped_behind(array, axis):
    devices = lax.axis_size(axis)
    pairing = [(i, (i - 1) % devices if i % 2 == 0 else (i + 1) % devices) for i in range(devices)]
    return lax.ppermute(array, axis, pairing)


def swapped(first, second, axis):
    return swapped_ahead(first, axis), swapped_behind(second, axis)


def both_ways(rows, lower):
    devices = lax.axis_size("gz")
    before = lax.ppermute(rows, "gz", [(i, (i + 1) % devices) for i in range(devices)])
    if devices == 2:
        return before
    after = lax.ppermute(rows, "gz", [(i, (i - 1) % devices) for i in range(devices)])
    return jnp.where(iota(rows.shape, 0) < lower, before, after)


remote = pl.BlockSpec(memory_space=pltpu.HBM)
anywhere = pl.BlockSpec(memory_space=pl.ANY)


def call(body, outs, specs=None, out_specs=None, scratch=(), cost=(0, 0), aliases=None):
    extra = {} if specs is None else {"in_specs": specs}
    if out_specs is not None:
        extra["out_specs"] = out_specs
    return pl.pallas_call(
        body,
        out_shape=[
            shape
            if isinstance(shape, jax.ShapeDtypeStruct)
            else jax.ShapeDtypeStruct(shape, jnp.float32)
            for shape in outs
        ],
        scratch_shapes=[
            pltpu.VMEM(shape, jnp.float32) if isinstance(shape, tuple) else shape
            for shape in scratch
        ],
        compiler_params=pltpu.CompilerParams(vmem_limit_bytes=40 * 1024 * 1024),
        input_output_aliases=aliases or {},
        cost_estimate=pl.CostEstimate(flops=cost[0], bytes_accessed=cost[1], transcendentals=0),
        **extra,
    )


def shards(populations, stretch, mass, flags, conv_source, conv_kind, conv_direction):
    bx, by, bz = flags.shape
    cells = bx * by * bz
    box, face, tile = ((bx, by, bz), (by, bz), (bx, by, lanes))

    stretch, flags, z_out, y_one, y_two, x_one, x_two = call(
        first_faces,
        [
            (6, *box),
            jax.ShapeDtypeStruct(box, jnp.int32),
            (8, bx * by),
            (4 * bx, bz),
            (4 * bx, bz),
            (4, *face),
            (4, *face),
        ],
        specs=[remote] * 2,
        scratch=[pltpu.SemaphoreType.DMA((2,))],
        cost=(10 * cells, 60 * cells),
    )(*(pltpu.with_memory_space_constraint(array, pltpu.HBM) for array in (stretch, flags)))
    first_x = swapped(x_one, x_two, "gx")
    z_first = both_ways(z_out, 3)
    y_first = swapped(y_one, y_two, "gy")

    entries = conv_source.shape[0]
    mark = (tall, lanes)
    code, code_done = call(
        lambda *refs: conversions(*refs, columns=bz),
        [(bx * by, bz), mark],
        cost=(40 * cells, 4 * cells),
    )(*(array.reshape(1, entries) for array in (conv_source, conv_kind, conv_direction)))
    code = code.reshape(box)

    pops, flow = call(
        moments,
        [(19, *box), (5, *box)],
        specs=[remote],
        scratch=[pltpu.SemaphoreType.DMA((bx,))],
        cost=(60 * cells, 150 * cells),
    )(pltpu.with_memory_space_constraint(populations, pltpu.HBM))

    columns, rows = ((24, bx * by), (10 * bx, bz))
    sides_y = [(bx, 8, bz), (bx, 8, bz), tile]
    inside, ends = ((bx - 2, *face), (2, *face))
    inner_post, inner_shift = call(
        collide_inner,
        [(19, *inside), (3, *inside)],
        scratch=sides_y,
        cost=(150 * cells, 150 * cells),
    )(pops, stretch, flow, z_first, *y_first)
    outer_post, outer_shift, z_out, x_one, x_two, y_one, y_two = call(
        collide_outer,
        [(19, *ends), (3, *ends), columns, (5, *face), (8, *face), rows, rows],
        scratch=[(4, *face), (4, *face)] + sides_y + [box],
        cost=(150 * cells, 150 * cells),
    )(pops, stretch, flags, flow, *first_x, *y_first, z_first, inner_post)
    z_post = both_ways(z_out, sides)
    post_y = swapped(y_one, y_two, "gy")
    post_x = swapped(x_one, x_two, "gx")
    edges = (4 * (bz // lanes) + columns[0], lanes)
    x_one, x_two, corner = call(
        lambda *refs: forward_edges(*refs, bx=bx), [edges, edges, columns], cost=(17 * 10**8, 0)
    )(z_post, *post_y, code_done)
    corners = swapped(corner, corner, "gy")
    edges_x = swapped(x_one, x_two, "gx")

    rims = [(bx + 2, *face), (bx + 2, 16, bz), (bx + 2, 16, bz), (bx + 2, by, lanes)]
    posts = (inner_post, outer_post, inner_shift, outer_shift)
    inner, outer, totals, changes = call(
        stream_early,
        [(first_slanted, *inside), (first_slanted, *ends), box, box],
        scratch=rims,
        cost=(350 * cells, 200 * cells),
    )(*posts, flags, *post_y, z_post)
    (
        inner_slanted,
        outer_slanted,
        inner_settled,
        inner_excess,
        inner_heading,
        totals,
        changes,
    ) = call(
        stream_slanted,
        [(4, *inside), (4, *ends), inside, inside, inside, ends, ends],
        scratch=rims,
        cost=(100 * cells, 60 * cells),
    )(*posts, mass, flags, code, *post_y, z_post, *corners, totals, changes)
    new_stretch, inner_done = call(
        restretch_inner,
        [(6, *box), mark],
        out_specs=[remote, pl.BlockSpec()],
        scratch=[(6, *inside)] + sides_y + [pltpu.SemaphoreType.DMA],
        cost=(80 * cells, 40 * cells),
    )(stretch, flow, *post_y, z_post)
    late, v_one, outer_settled, spread, y_one, y_two, z_out = call(
        stream_late,
        [
            (5, *ends),
            (3, *face),
            ends,
            (bx + 2, *face),
            (8, bz),
            (8, bz),
            (16, bx * by),
        ],
        scratch=rims + [(5, *face), (5, *face), box, box],
        cost=(150 * cells, 100 * cells),
    )(
        outer_post,
        outer_shift,
        mass,
        flags,
        code,
        totals,
        changes,
        *first_x,
        *post_x,
        *edges_x,
        inner_excess,
        inner_heading,
        flow,
        inner_done,
    )
    z_last = both_ways(z_out, 8)
    last_y = swapped(y_one, y_two, "gy")
    last_corners = swapped(z_last, z_last, "gy")
    flow_x = (swapped_ahead(v_one, "gx"), post_x[1])
    fresh, inner_stored = call(
        store_inner,
        [(19, *box), mark],
        specs=[pl.BlockSpec()] * 2 + [anywhere],
        out_specs=[remote, pl.BlockSpec()],
        scratch=[pltpu.SemaphoreType.DMA((2,))],
        cost=(0, 80 * cells),
    )(inner, inner_slanted, late)
    x_one, x_two = call(add_faces, [face, face], cost=(4 * 10**9, 0))(
        spread, z_last, *last_y, inner_stored
    )
    last_x = swapped(x_one, x_two, "gx")
    new_stretch, fresh, outer_done = call(
        restretch_outer,
        [(6, *box), (19, *box), mark],
        specs=[pl.BlockSpec()] * 7 + [remote] + [pl.BlockSpec()] * 3 + [remote],
        out_specs=[remote, remote, pl.BlockSpec()],
        scratch=[(6, *ends), (3, *face), (3, *face)]
        + sides_y
        + [pltpu.SemaphoreType.DMA((2,)), pltpu.SemaphoreType.DMA((32,))],
        cost=(80 * cells, 200 * cells),
        aliases={7: 0, 11: 1},
    )(
        stretch,
        flow,
        *flow_x,
        *post_y,
        z_post,
        new_stretch,
        outer,
        outer_slanted,
        late,
        fresh,
    )
    (new_mass,) = call(add_all, [box])(
        inner_settled, outer_settled, spread, z_last, *last_y, *last_corners, *last_x[::-1], outer_done
    )
    return (fresh, new_stretch, new_mass)


def solution(mesh):
    return jax.shard_map(
        shards,
        mesh=mesh,
        in_specs=(
            P(None, "gx", "gy", "gz"),
            P(None, "gx", "gy", "gz"),
            P("gx", "gy", "gz"),
            P("gx", "gy", "gz"),
            P(("gx", "gy", "gz")),
            P(("gx", "gy", "gz")),
            P(("gx", "gy", "gz")),
        ),
        out_specs=(P(None, "gx", "gy", "gz"), P(None, "gx", "gy", "gz"), P("gx", "gy", "gz")),
        check_vma=False,
    )
```

```python
import jax
import jax.numpy as jnp
from jax import lax
from jax.experimental import pallas as pl
from jax.experimental.pallas import tpu as pltpu
from jax.sharding import PartitionSpec as P

velocity_set = (
    (0, 0, 0),
    (1, 0, 0),
    (-1, 0, 0),
    (0, 1, 0),
    (0, -1, 0),
    (0, 0, 1),
    (0, 0, -1),
    (1, 1, 0),
    (-1, -1, 0),
    (1, -1, 0),
    (-1, 1, 0),
    (1, 0, 1),
    (-1, 0, -1),
    (1, 0, -1),
    (-1, 0, 1),
    (0, 1, 1),
    (0, -1, -1),
    (0, 1, -1),
    (0, -1, 1),
)
opposite_of = (0, 2, 1, 4, 3, 6, 5, 8, 7, 10, 9, 12, 11, 14, 13, 16, 15, 18, 17)
lattice_weights = (1.0 / 3.0,) + (1.0 / 18.0,) * 6 + (1.0 / 36.0,) * 12
symmetric_slot = ((0, 3, 4), (3, 1, 5), (4, 5, 2))
tensor_pairs = ((0, 0), (1, 1), (2, 2), (0, 1), (0, 2), (1, 2))
relax_time = 0.8
polymer_time = 8.0
polymer_coeff = 0.05


def moving(axis, sign):
    return tuple(index for index in range(19) if velocity_set[index][axis] == sign)


x_up, x_down = (moving(0, 1), moving(0, -1))
y_up, y_down = (moving(1, 1), moving(1, -1))
z_up, z_down = (moving(2, 1), moving(2, -1))
pairs = tuple(range(1, 19, 2))
gas_slot = 5
speed_slot = 6
edge_slot = 9
sides = 9
lanes = 128
tall = 8


def iota(shape, dim):
    return lax.broadcasted_iota(jnp.int32, shape, dim)


def wide(tile, width):
    return jnp.concatenate([tile] * (width // tile.shape[1]), axis=1)


def rows_of(load, chunk, chunks, step, edge):
    low = chunk * tall
    if step == 0:
        return load(low, low + tall)
    if step == 1 and chunk > 0:
        return load(low - 1, low + tall - 1)
    if step == -1 and chunk < chunks - 1:
        return load(low + 1, low + tall + 1)
    rows = load(low, low + tall)
    at = iota(rows.shape, 0)
    if step == 1:
        return jnp.where(at == 0, edge(), pltpu.roll(rows, 1, 0))
    return jnp.where(at == tall - 1, edge(), pltpu.roll(rows, tall - 1, 0))


def columns_of(rows, halo, lane, step):
    width = rows.shape[1]
    at = iota(rows.shape, 1)
    if step == 1:
        edge = wide(pltpu.roll(halo, (lanes - lane) % lanes, 1), width)
        return jnp.where(at == 0, edge, pltpu.roll(rows, 1, 1))
    edge = wide(pltpu.roll(halo, lanes - 1 - lane, 1), width)
    return jnp.where(at == width - 1, edge, pltpu.roll(rows, width - 1, 1))


def packed(high, low):
    at = iota(high[0].shape, 1)
    tile = jnp.zeros_like(high[0])
    for slot, part in enumerate(high):
        tile = jnp.where(at == slot, pltpu.roll(part, slot + 1, 1), tile)
    for place, part in enumerate(low):
        slot = len(high) + place
        tile = jnp.where(at == slot, pltpu.roll(part, slot, 1), tile)
    return tile


def along(index, vector):
    total = None
    for comp in range(3):
        sign = velocity_set[index][comp]
        if sign != 0:
            term = vector[comp] if sign > 0 else -vector[comp]
            total = term if total is None else total + term
    return total


def conversions(source, kind, heading, code, mark, *, columns):
    count = source.shape[1]
    value = (heading[...] + 32 * kind[...]).astype(jnp.float32)
    row, column = (source[...] // columns, source[...] % columns)
    by_row = jnp.where(iota((code.shape[0], count), 0) == row, value, 0.0).astype(jnp.bfloat16)
    by_column = jnp.where(iota((columns, count), 0) == column, 1.0, 0.0).astype(jnp.bfloat16)
    code[...] = lax.dot_general(
        by_row, by_column, (((1,), (1,)), ((), ())), preferred_element_type=jnp.float32
    )
    mark[...] = jnp.zeros(mark.shape, jnp.float32)


def odd(axis):
    return lax.rem(lax.axis_index(axis), 2) == 1


def select(chosen, first, second):
    return jnp.where(chosen, first[...], second[...])


def swap_rows(first, second, x, planes, high, low, flip):
    for slot, (top, bottom) in enumerate(zip(high, low)):
        by = top.shape[0]
        up, down = (top[by - 1 : by, :], bottom[0:1, :])
        at = slot * planes + x
        first[at : at + 1, :] = jnp.where(flip, down, up)
        second[at : at + 1, :] = jnp.where(flip, up, down)


def swapped_rows(first, second, slots, low_rows, high_rows, shift):
    flip = odd("gy")
    planes = low_rows.shape[0] - 2 * shift
    for x in range(planes):
        for place, slot in enumerate(slots):
            at = slot * planes + x
            one, two = (first[at : at + 1, :], second[at : at + 1, :])
            low_rows[x + shift, place : place + 1, :] = jnp.where(flip, one, two)
            high_rows[x + shift, place : place + 1, :] = jnp.where(flip, two, one)


def column_rows(tiles, count):
    return jnp.concatenate(tiles, axis=0).T[0:count, :]


def row_columns(rows):
    rest = jnp.zeros((lanes - rows.shape[0], rows.shape[1]), jnp.float32)
    return jnp.concatenate([rows, rest], axis=0).T


def first_faces(
    stretch_in,
    flags_in,
    stretch,
    flags,
    columns,
    y_first,
    y_second,
    x_first,
    x_second,
    sems,
):
    bx, by, bz = flags.shape
    flip_x, flip_y = (odd("gx"), odd("gy"))
    copies = [
        pltpu.make_async_copy(stretch_in, stretch, sems.at[0]),
        pltpu.make_async_copy(flags_in, flags, sems.at[1]),
    ]
    for copy in copies:
        copy.start()
    for copy in copies:
        copy.wait()
    tiles = []
    for x in range(bx):
        along_y = [stretch.at[symmetric_slot[comp][1], x] for comp in range(3)]
        swap_rows(y_first, y_second, x, bx, along_y, along_y, flip_y)
        fields = [stretch.at[symmetric_slot[comp][2], x] for comp in range(3)]
        tiles.append(
            packed(
                [field[:, bz - lanes : bz] for field in fields],
                [field[:, 0:lanes] for field in fields],
            )
        )
    columns[...] = column_rows(tiles, columns.shape[0])
    rest = y_first.shape[0] - 3 * bx
    y_first[3 * bx :, :] = jnp.zeros((rest, bz), jnp.float32)
    y_second[3 * bx :, :] = jnp.zeros((rest, bz), jnp.float32)
    for out, last in ((x_first, flip_x), (x_second, jnp.logical_not(flip_x))):
        for comp in range(3):
            slot = symmetric_slot[comp][0]
            out[comp] = jnp.where(last, stretch[slot, 0], stretch[slot, bx - 1])
        out[3] = jnp.where(jnp.where(last, flags[0], flags[bx - 1]) == 0, 1.0, 0.0)


def moments(pops_in, pops, flow, sems):
    bx, by = pops.shape[1:3]
    copies = [
        pltpu.make_async_copy(pops_in.at[:, x], pops.at[:, x], sems.at[x]) for x in range(bx)
    ]
    for copy in copies:
        copy.start()
    for x in range(bx):
        copies[x].wait()
        for chunk in range(by // tall):
            rows = pl.ds(chunk * tall, tall)
            part = [pops[index, x, rows, :] for index in range(19)]
            density = part[0]
            for index in range(1, 19):
                density = density + part[index]
            inverse = 1.0 / density
            for comp in range(3):
                total = None
                for index in pairs:
                    sign = velocity_set[index][comp]
                    if sign != 0:
                        term = part[index] - part[index + 1]
                        term = term if sign > 0 else -term
                        total = term if total is None else total + term
                flow[comp, x, rows, :] = total * inverse
            flow[3, x, rows, :] = density
            flow[4, x, rows, :] = inverse


def beside(ref, field, x, step, halo, slot):
    last = ref.shape[1] - 1
    if halo is None:
        return lambda low, high: ref[field, x + step, low:high, :]
    if isinstance(x, int):
        if 0 <= x + step <= last:
            return lambda low, high: ref[field, x + step, low:high, :]
        return lambda low, high: halo[slot, low:high, :]
    inside = jnp.clip(x + step, 0, last)
    beyond = x == (0 if step < 0 else last)
    return lambda low, high: jnp.where(
        beyond, halo[slot, low:high, :], ref[field, inside, low:high, :]
    )


def differences(
    ref, field, slots, x, chunk, chunks, below, above, y_below, y_above, z_halo, lane, side
):
    slot_x, slot_y, slot_z = slots
    low, high = (chunk * tall, chunk * tall + tall)

    def load(first, stop):
        return ref[field, x, first:stop, :]

    result = [None, None, None]
    if slot_x is not None:
        after = beside(ref, field, x, 1, above, slot_x)(low, high)
        before = beside(ref, field, x, -1, below, slot_x)(low, high)
        result[0] = after - before
    if slot_y is not None:
        after = rows_of(load, chunk, chunks, -1, lambda: y_above[x, slot_y : slot_y + 1, :])
        before = rows_of(load, chunk, chunks, 1, lambda: y_below[x, slot_y : slot_y + 1, :])
        result[1] = after - before
    if slot_z is not None:
        rows, halo = (load(low, high), z_halo[x, low:high, :])
        after = columns_of(rows, halo, lane + side + slot_z, -1)
        before = columns_of(rows, halo, lane + slot_z, 1)
        result[2] = after - before
    return result


def end_place(x, bx):
    return 0 if x == 0 else 1


def plane_of(inner, outer, field, x, bx):
    if 0 < x < bx - 1:
        return inner.at[field, x - 1]
    return outer.at[field, end_place(x, bx)]


def collide_plane(x, place, pops, stretch, flow, halos, post, shift):
    by = pops.shape[2]
    chunks = by // tall
    factor = 1.0 - 0.5 / relax_time
    rate = 1.0 / relax_time
    for chunk in range(chunks):
        rows = pl.ds(chunk * tall, tall)
        terms = [[], [], []]
        for field in range(6):
            slots = [None, None, None]
            for comp in range(3):
                for axis in range(3):
                    if symmetric_slot[comp][axis] == field:
                        slots[axis] = comp
            found = differences(stretch, field, slots, x, chunk, chunks, *halos)
            for axis in range(3):
                if slots[axis] is not None:
                    terms[slots[axis]].append(found[axis])
        force = [0.5 * polymer_coeff * (part[0] + part[1] + part[2]) for part in terms]
        density, half = (flow[3, x, rows, :], 0.5 * flow[4, x, rows, :])
        moved = [flow[comp, x, rows, :] + half * force[comp] for comp in range(3)]
        for comp in range(3):
            shift[comp, place, rows, :] = moved[comp]
        squared = moved[0] * moved[0] + moved[1] * moved[1] + moved[2] * moved[2]
        work = moved[0] * force[0] + moved[1] * force[1] + moved[2] * force[2]
        weight = rate * density
        common = weight - 1.5 * weight * squared - 3.0 * factor * work
        odd = [3.0 * weight * moved[comp] + 3.0 * factor * force[comp] for comp in range(3)]
        even = [4.5 * weight * moved[comp] + 9.0 * factor * force[comp] for comp in range(3)]
        keep = 1.0 - rate
        post[0, place, rows, :] = keep * pops[0, x, rows, :] + lattice_weights[0] * common
        for index in pairs:
            both = common + along(index, moved) * along(index, even)
            differ = along(index, odd)
            scale = lattice_weights[index]
            post[index, place, rows, :] = keep * pops[index, x, rows, :] + scale * (both + differ)
            post[index + 1, place, rows, :] = keep * pops[index + 1, x, rows, :] + scale * (
                both - differ
            )


def collide_inner(
    pops,
    stretch,
    flow,
    z_rows,
    y_first,
    y_second,
    post,
    shift,
    y_below,
    y_above,
    z_halo,
):
    swapped_rows(y_first, y_second, range(3), y_below, y_above, 0)
    z_halo[...] = row_columns(z_rows[...]).reshape(z_halo.shape)
    halos = (None, None, y_below, y_above, z_halo, 0, 3)

    def plane(x, carry):
        collide_plane(x, x - 1, pops, stretch, flow, halos, post, shift)
        return carry

    lax.fori_loop(1, pops.shape[1] - 1, plane, 0)


def collide_outer(
    pops,
    stretch,
    flags,
    flow,
    x_first,
    x_second,
    y_first,
    y_second,
    z_rows,
    inner,
    post,
    shift,
    columns,
    ahead,
    behind,
    up_first,
    up_second,
    below,
    above,
    y_below,
    y_above,
    z_halo,
    gas,
):
    bx, by, bz = flags.shape
    halos = (below, above, y_below, y_above, z_halo, 0, 3)
    flip_x, flip_y = (odd("gx"), odd("gy"))
    below[...] = select(flip_x, x_first, x_second)
    above[...] = select(flip_x, x_second, x_first)
    swapped_rows(y_first, y_second, range(3), y_below, y_above, 0)
    z_halo[...] = row_columns(z_rows[...]).reshape(z_halo.shape)
    for x in (0, bx - 1):
        collide_plane(x, end_place(x, bx), pops, stretch, flow, halos, post, shift)

    tiles = []
    for x in range(bx):
        gas[x] = jnp.where(flags[x] == 0, 1.0, 0.0)
        rest = [gas.at[x]] + [flow.at[comp, x] for comp in range(3)]

        def fields(indices):
            return [plane_of(inner, post, index, x, bx) for index in indices] + rest

        swap_rows(up_first, up_second, x, bx, fields(y_up), fields(y_down), flip_y)
        tiles.append(
            packed(
                [field[:, bz - lanes : bz] for field in fields(z_up)],
                [field[:, 0:lanes] for field in fields(z_down)],
            )
        )
    columns[...] = column_rows(tiles, columns.shape[0])
    rest = up_first.shape[0] - sides * bx
    up_first[sides * bx :, :] = jnp.zeros((rest, bz), jnp.float32)
    up_second[sides * bx :, :] = jnp.zeros((rest, bz), jnp.float32)
    for slot in range(5):
        up, down = (post[x_up[slot], 1], post[x_down[slot], 0])
        ahead[slot] = jnp.where(flip_x, down, up)
        behind[slot] = jnp.where(flip_x, up, down)
    for comp in range(3):
        behind[5 + comp] = jnp.where(flip_x, flow[comp, bx - 1], flow[comp, 0])


def restretch_plane(x, place, stretch, flow, halos, updated):
    chunks = stretch.shape[2] // tall
    for chunk in range(chunks):
        rows = pl.ds(chunk * tall, tall)
        grad = [
            differences(
                flow, comp, (comp, comp, comp), x, chunk, chunks, *halos, speed_slot, sides
            )
            for comp in range(3)
        ]
        part = [stretch[slot, x, rows, :] for slot in range(6)]
        full = [part[slot] + 1.0 if slot < 3 else part[slot] for slot in range(6)]

        def product(row, col):
            total = grad[row][0] * full[symmetric_slot[0][col]]
            for inner in (1, 2):
                total = total + grad[row][inner] * full[symmetric_slot[inner][col]]
            return total

        for slot, (row, col) in enumerate(tensor_pairs):
            old = (1.0 - 1.0 / polymer_time) * part[slot]
            if row == col:
                updated[slot, place, rows, :] = old + product(row, col)
            else:
                updated[slot, place, rows, :] = old + 0.5 * (product(row, col) + product(col, row))


def restretch_inner(
    stretch,
    flow,
    y_first,
    y_second,
    z_rows,
    new_stretch,
    mark,
    updated,
    y_below,
    y_above,
    z_halo,
    sem,
):
    bx = stretch.shape[1]
    swapped_rows(y_first, y_second, range(speed_slot, sides), y_below, y_above, 0)
    z_halo[...] = row_columns(z_rows[...]).reshape(z_halo.shape)
    halos = (None, None, y_below, y_above, z_halo)

    def plane(x, carry):
        restretch_plane(x, x - 1, stretch, flow, halos, updated)
        return carry

    lax.fori_loop(1, bx - 1, plane, 0)
    copy = pltpu.make_async_copy(updated, new_stretch.at[:, 1 : bx - 1], sem)
    copy.start()
    mark[...] = jnp.zeros(mark.shape, jnp.float32)
    copy.wait()


def restretch_outer(
    stretch,
    flow,
    x_first,
    x_second,
    y_first,
    y_second,
    z_rows,
    inner_stretch,
    outer,
    inner_slanted,
    outer_slanted,
    late,
    inner_fresh,
    new_stretch,
    fresh,
    mark,
    updated,
    below,
    above,
    y_below,
    y_above,
    z_halo,
    sems,
    store_sems,
):
    bx = stretch.shape[1]
    moves = stored(outer, inner_slanted, outer_slanted, late, fresh, store_sems)
    for copy in moves:
        copy.start()
    flip_x = odd("gx")
    for comp in range(3):
        below[comp] = jnp.where(flip_x, x_first[comp], x_second[5 + comp])
        above[comp] = jnp.where(flip_x, x_second[5 + comp], x_first[comp])
    swapped_rows(y_first, y_second, range(speed_slot, sides), y_below, y_above, 0)
    z_halo[...] = row_columns(z_rows[...]).reshape(z_halo.shape)
    halos = (below, above, y_below, y_above, z_halo)
    copies = []
    for place, x in enumerate((0, bx - 1)):
        restretch_plane(x, place, stretch, flow, halos, updated)
        copies.append(
            pltpu.make_async_copy(updated.at[:, place], new_stretch.at[:, x], sems.at[place])
        )
        copies[-1].start()
    mark[...] = jnp.zeros(mark.shape, jnp.float32)
    for copy in copies + moves:
        copy.wait()


def stored(outer, inner_slanted, outer_slanted, late, fresh, sems):
    bx = fresh.shape[1]
    moves = [(inner_slanted, fresh.at[first_slanted:, 1 : bx - 1])]
    for place, x in enumerate((0, bx - 1)):
        moves.append((outer_slanted.at[:, place], fresh.at[first_slanted:, x]))
        order = (x_up, x_down)[place]
        start = 0
        for index in order + (first_slanted,):
            if index > start:
                run = slice(start, index)
                moves.append((outer.at[run, place], fresh.at[run, x]))
            if index in order:
                moves.append((late.at[order.index(index), place], fresh.at[index, x]))
            start = index + 1
    return [
        pltpu.make_async_copy(source, target, sems.at[place])
        for place, (source, target) in enumerate(moves)
    ]


def store_inner(inner, fresh, mark, sem):
    copy = pltpu.make_async_copy(inner, fresh.at[0:first_slanted, 1 : fresh.shape[1] - 1], sem)
    copy.start()
    mark[...] = jnp.zeros(mark.shape, jnp.float32)
    copy.wait()


up_edges = ((0, y_up.index(7)), (0, gas_slot), (1, y_down.index(9)), (1, gas_slot))
down_edges = ((0, y_up.index(10)), (0, gas_slot), (1, y_down.index(8)), (1, gas_slot))


def forward_edges(z_rows, y_first, y_second, after, first_out, second_out, corner, *, bx):
    halves = y_first.shape[1] // lanes
    flip_x, flip_y = (odd("gx"), odd("gy"))
    for half in range(halves):
        cut = slice(half * lanes, half * lanes + lanes)
        for place in range(4):
            found = []
            for x, edges in ((bx - 1, up_edges), (0, down_edges)):
                side, slot = edges[place]
                row = slot * bx + x
                one = y_first[row : row + 1, cut]
                two = y_second[row : row + 1, cut]
                found.append(jnp.where(flip_y, one, two) if side == 0 else jnp.where(flip_y, two, one))
            at = half * 4 + place
            first_out[at : at + 1, :] = jnp.where(flip_x, found[1], found[0])
            second_out[at : at + 1, :] = jnp.where(flip_x, found[0], found[1])
    first_out[4 * halves :, :] = z_rows[...]
    second_out[4 * halves :, :] = z_rows[...]
    corner[...] = z_rows[...]


def own_halos(flags, y_first, y_second, z_rows, gas, low_rows, high_rows, columns):
    bx, by = flags.shape[:2]
    tile = row_columns(z_rows[...])
    swapped_rows(y_first, y_second, range(speed_slot), low_rows, high_rows, 1)
    for x in range(bx):
        gas[x + 1] = jnp.where(flags[x] == 0, 1.0, 0.0)
        columns[x + 1] = tile[x * by : x * by + by, :]


def own_corners(corner_first, corner_second, low_rows, high_rows):
    bx = low_rows.shape[0] - 2
    flip = odd("gy")
    corner_below = row_columns(select(flip, corner_first, corner_second))
    corner_above = row_columns(select(flip, corner_second, corner_first))
    by = corner_below.shape[0] // bx
    for x in range(bx):
        end = x * by + by - 1
        low_rows[x + 1, edge_slot : edge_slot + 1, 0:lanes] = corner_below[end : end + 1, :]
        high_rows[x + 1, edge_slot : edge_slot + 1, 0:lanes] = corner_above[
            x * by : x * by + 1, :
        ]


def pass_on(x, chunk, indices, source, leaving_of, speed, halos, fresh, place, total, change):
    gas, low_rows, high_rows, columns = halos
    by = gas.shape[1]
    chunks = by // tall
    rows = pl.ds(chunk * tall, tall)
    rest = 1.0 - 1.5 * (speed[0] * speed[0] + speed[1] * speed[1] + speed[2] * speed[2])
    equals = {}

    def moved(load, index, slot, lane):
        step_x, step_y, step_z = velocity_set[index]
        plane = x + 1 - step_x
        edges = low_rows if step_y == 1 else high_rows
        found = rows_of(load, chunk, chunks, step_y, lambda: edges[plane, slot : slot + 1, :])
        if step_z == 0:
            return found
        halo = rows_of(
            lambda low, high: columns[plane, low:high, :],
            chunk,
            chunks,
            step_y,
            lambda: edges[plane, edge_slot : edge_slot + 1, 0:lanes],
        )
        return columns_of(found, halo, lane, step_z)

    for index in indices:
        step_x, step_y, step_z = velocity_set[index]
        first = min(index, opposite_of[index])
        if first not in equals:
            proj = along(first, speed)
            equals[first] = 2.0 * lattice_weights[first] * (rest + 4.5 * proj * proj)
        slot, lane, gas_lane = (None, None, None)
        if step_y != 0:
            slot = (y_up if step_y == 1 else y_down).index(index)
        if step_z == 1:
            lane, gas_lane = (z_up.index(index), gas_slot)
        elif step_z == -1:
            lane, gas_lane = (sides + z_down.index(index), sides + gas_slot)
        field = source(index)
        marks = gas.at[x + 1 - step_x]
        arriving = moved(lambda low, high: field[low:high, :], index, slot, lane)
        from_gas = moved(lambda low, high: marks[low:high, :], index, gas_slot, gas_lane)
        leaving = leaving_of(opposite_of[index])[rows, :]
        open_side = from_gas > 0.5
        value = jnp.where(open_side, equals[first] - leaving, arriving)
        fresh(index)[place, rows, :] = value
        total = total + value
        change = change + jnp.where(open_side, 0.0, arriving - leaving)
    return total, change


def settle(x, rows, mass, flags, code, total, change):
    read = mass[x, rows, :] + jnp.where(flags[x, rows, :] == 1, change, 0.0)
    mark = code[x, rows, :]
    liquid = mark >= 32.0
    converts = mark > 0.0
    level = jnp.where(liquid, total, 0.0)
    excess = jnp.where(converts, read - level, 0.0)
    heading = jnp.where(liquid, mark - 32.0, mark)
    return jnp.where(converts, level, read), excess, heading


slanted = tuple(index for index in range(19) if velocity_set[index][1] * velocity_set[index][2])
first_slanted = slanted[0]


def from_inside(x, bx):
    found = [index for index in range(1, 19) if 0 <= x - velocity_set[index][0] < bx]
    return [index for index in found if index not in slanted]


def from_beyond(x, bx):
    return [index for index in range(1, 19) if not 0 <= x - velocity_set[index][0] < bx]


def stream_early(
    inner_post,
    outer_post,
    inner_shift,
    outer_shift,
    flags,
    y_first,
    y_second,
    z_rows,
    inner,
    outer,
    totals,
    changes,
    gas,
    low_rows,
    high_rows,
    columns,
):
    bx, by, bz = flags.shape
    halos = (gas, low_rows, high_rows, columns)
    own_halos(flags, y_first, y_second, z_rows, *halos)

    for x in range(bx):
        inside = 0 < x < bx - 1
        place = x - 1 if inside else end_place(x, bx)
        fresh = inner if inside else outer
        for chunk in range(by // tall):
            rows = pl.ds(chunk * tall, tall)
            total = plane_of(inner_post, outer_post, 0, x, bx)[rows, :]
            fresh[0, place, rows, :] = total
            total, change = pass_on(
                x,
                chunk,
                from_inside(x, bx),
                lambda index: plane_of(
                    inner_post, outer_post, index, x - velocity_set[index][0], bx
                ),
                lambda index: plane_of(inner_post, outer_post, index, x, bx),
                [plane_of(inner_shift, outer_shift, comp, x, bx)[rows, :] for comp in range(3)],
                halos,
                lambda index: fresh.at[index],
                place,
                total,
                jnp.zeros((tall, bz), jnp.float32),
            )
            totals[x, rows, :] = total
            changes[x, rows, :] = change


def stream_slanted(
    inner_post,
    outer_post,
    inner_shift,
    outer_shift,
    mass,
    flags,
    code,
    y_first,
    y_second,
    z_rows,
    corner_first,
    corner_second,
    totals,
    changes,
    after,
    inner,
    outer,
    settled,
    excess,
    heading,
    end_totals,
    end_changes,
    gas,
    low_rows,
    high_rows,
    columns,
):
    bx, by, bz = flags.shape
    halos = (gas, low_rows, high_rows, columns)
    own_halos(flags, y_first, y_second, z_rows, *halos)
    own_corners(corner_first, corner_second, low_rows, high_rows)

    for x in range(bx):
        inside = 0 < x < bx - 1
        place = x - 1 if inside else end_place(x, bx)
        fresh = inner if inside else outer
        for chunk in range(by // tall):
            rows = pl.ds(chunk * tall, tall)
            total, change = pass_on(
                x,
                chunk,
                slanted,
                lambda index: plane_of(inner_post, outer_post, index, x, bx),
                lambda index: plane_of(inner_post, outer_post, index, x, bx),
                [plane_of(inner_shift, outer_shift, comp, x, bx)[rows, :] for comp in range(3)],
                halos,
                lambda index: fresh.at[index - first_slanted],
                place,
                totals[x, rows, :],
                changes[x, rows, :],
            )
            if inside:
                now = settle(x, rows, mass, flags, code, total, change)
                settled[place, rows, :], excess[place, rows, :], heading[place, rows, :] = now
            else:
                end_totals[place, rows, :] = total
                end_changes[place, rows, :] = change


def stream_late(
    post,
    shift,
    mass,
    flags,
    code,
    totals,
    changes,
    gas_first,
    gas_second,
    x_first,
    x_second,
    edges_first,
    edges_second,
    inner_excess,
    inner_heading,
    flow,
    after,
    late,
    v_first,
    settled,
    spread,
    line_first,
    line_second,
    out_z,
    gas,
    low_rows,
    high_rows,
    columns,
    below,
    above,
    excess,
    heading,
):
    bx, by, bz = flags.shape
    halves = bz // lanes
    flip_x = odd("gx")
    halos = (gas, low_rows, high_rows, columns)

    for comp in range(3):
        up, down = (flow[comp, bx - 1], flow[comp, 0])
        v_first[comp] = jnp.where(flip_x, down, up)
    for slot in range(5):
        below[slot] = jnp.where(flip_x, x_first[slot], x_second[slot])
        above[slot] = jnp.where(flip_x, x_second[slot], x_first[slot])
    gas[0] = jnp.where(flip_x, gas_first[3], gas_second[3])
    gas[bx + 1] = jnp.where(flip_x, gas_second[3], gas_first[3])
    edges_below = select(flip_x, edges_first, edges_second)
    edges_above = select(flip_x, edges_second, edges_first)
    for found, at, x, edges in (
        (edges_below, 0, bx - 1, up_edges),
        (edges_above, bx + 1, 0, down_edges),
    ):
        for place, (side, slot) in enumerate(edges):
            line = jnp.concatenate(
                [found[half * 4 + place : half * 4 + place + 1, :] for half in range(halves)],
                axis=1,
            )
            (low_rows, high_rows)[side][at, slot : slot + 1, :] = line
        columns[at] = row_columns(found[4 * halves :, :])[x * by : x * by + by, :]
    for place, x in enumerate((0, bx - 1)):
        halo, order = ((below, x_up), (above, x_down))[place]
        for chunk in range(by // tall):
            rows = pl.ds(chunk * tall, tall)
            total, change = pass_on(
                x,
                chunk,
                from_beyond(x, bx),
                lambda index: halo.at[order.index(index)],
                lambda index: post.at[index, place],
                [shift[comp, place, rows, :] for comp in range(3)],
                halos,
                lambda index: late.at[order.index(index)],
                place,
                totals[place, rows, :],
                changes[place, rows, :],
            )
            now = settle(x, rows, mass, flags, code, total, change)
            settled[place, rows, :], excess[x, rows, :], heading[x, rows, :] = now
    for x in range(1, bx - 1):
        excess[x] = inner_excess[x - 1]
        heading[x] = inner_heading[x - 1]

    row_at, lane_at = (iota((by, bz), 0), iota((by, bz), 1))
    line_at = iota((1, bz), 1)
    tile_lane, line_lane = (iota((by, lanes), 1), iota((1, lanes), 1))

    def rows_up(rows):
        return jnp.where(row_at == 0, 0.0, pltpu.roll(rows, 1, 0))

    def rows_down(rows):
        return jnp.where(row_at == by - 1, 0.0, pltpu.roll(rows, by - 1, 0))

    def over(rows, at, step):
        if step == 1:
            return jnp.where(at == 0, 0.0, pltpu.roll(rows, 1, 1))
        return jnp.where(at == bz - 1, 0.0, pltpu.roll(rows, bz - 1, 1))

    def summed(parts):
        total = parts[0]
        for part in parts[1:]:
            total = total + part
        return total

    tile = jnp.zeros((by, lanes), jnp.float32)
    line_up = jnp.zeros((1, lanes), jnp.float32)
    line_down = jnp.zeros((1, lanes), jnp.float32)
    flip_y = odd("gy")
    line_first[...] = jnp.zeros(line_first.shape, jnp.float32)
    line_second[...] = jnp.zeros(line_second.shape, jnp.float32)
    for target in range(bx + 2):
        groups = {}
        for index in range(1, 19):
            step_x, step_y, step_z = velocity_set[index]
            x = target - 1 - step_x
            if 0 <= x < bx:
                part = jnp.where(heading[x] == float(index), excess[x], 0.0)
                groups.setdefault((step_y, step_z), []).append(part)
        groups = {key: summed(parts) for key, parts in groups.items()}
        total = jnp.zeros((by, bz), jnp.float32)
        line = {1: jnp.zeros((1, bz), jnp.float32), -1: jnp.zeros((1, bz), jnp.float32)}
        for step_z in (0, 1, -1):
            group = jnp.zeros((by, bz), jnp.float32)
            ends = {}
            if (0, step_z) in groups:
                group = group + groups[(0, step_z)]
            if (1, step_z) in groups:
                group = group + rows_up(groups[(1, step_z)])
                ends[1] = groups[(1, step_z)][by - 1 : by, :]
            if (-1, step_z) in groups:
                group = group + rows_down(groups[(-1, step_z)])
                ends[-1] = groups[(-1, step_z)][0:1, :]
            if step_z == 0:
                total = total + group
                for side in ends:
                    line[side] = line[side] + ends[side]
                continue
            total = total + over(group, lane_at, step_z)
            for side in ends:
                line[side] = line[side] + over(ends[side], line_at, step_z)
            if step_z == 1:
                spot, cut, roll = (target, slice(bz - lanes, bz), target + 1)
            else:
                spot, cut, roll = (8 + target, slice(0, lanes), 8 + target)
            tile = jnp.where(tile_lane == spot, pltpu.roll(group[:, cut], roll, 1), tile)
            if 1 in ends:
                line_up = jnp.where(
                    line_lane == spot, pltpu.roll(ends[1][:, cut], roll, 1), line_up
                )
            if -1 in ends:
                line_down = jnp.where(
                    line_lane == spot, pltpu.roll(ends[-1][:, cut], roll, 1), line_down
                )
        spread[target] = total
        line_first[target : target + 1, :] = jnp.where(flip_y, line[-1], line[1])
        line_second[target : target + 1, :] = jnp.where(flip_y, line[1], line[-1])
    rest = jnp.zeros((lanes - by - 2, lanes), jnp.float32)
    out_z[...] = column_rows([tile, line_up, line_down, rest], 16)


def with_edges(total, target, tile, y_below, y_above):
    by, bz = total.shape
    row_at, lane_at = (iota((by, bz), 0), iota((by, bz), 1))
    total = total + jnp.where(lane_at == 0, tile[0:by, target : target + 1], 0.0)
    total = total + jnp.where(lane_at == bz - 1, tile[0:by, 8 + target : 9 + target], 0.0)
    total = total + jnp.where(row_at == 0, y_below[target : target + 1, :], 0.0)
    return total + jnp.where(row_at == by - 1, y_above[target : target + 1, :], 0.0)


def add_faces(spread, z_rows, y_first, y_second, first, second):
    last = spread.shape[0] - 1
    flip_x, flip_y = (odd("gx"), odd("gy"))
    tile = row_columns(z_rows[...])
    y_below, y_above = (select(flip_y, y_first, y_second), select(flip_y, y_second, y_first))
    up = with_edges(spread[last], last, tile, y_below, y_above)
    down = with_edges(spread[0], 0, tile, y_below, y_above)
    first[...] = jnp.where(flip_x, down, up)
    second[...] = jnp.where(flip_x, up, down)


def add_all(
    inner_settled,
    outer_settled,
    spread,
    z_rows,
    y_first,
    y_second,
    corner_first,
    corner_second,
    x_second,
    x_first,
    after,
    new_mass,
):
    bx, by, bz = new_mass.shape
    flip_x, flip_y = (odd("gx"), odd("gy"))
    tile = row_columns(z_rows[...])
    y_below, y_above = (select(flip_y, y_first, y_second), select(flip_y, y_second, y_first))
    at = iota((8, bz), 1)
    found = []
    for rows, side, corner in (
        (y_below, 0, select(flip_y, corner_first, corner_second)),
        (y_above, 1, select(flip_y, corner_second, corner_first)),
    ):
        edge = corner[:, by + side : by + side + 1]
        rows = rows + jnp.where(at == 0, edge[0:8, :], 0.0)
        found.append(rows + jnp.where(at == bz - 1, edge[8:16, :], 0.0))
    for x in range(bx):
        total = with_edges(spread[x + 1], x + 1, tile, *found)
        if x == 0:
            total = total + select(flip_x, x_first, x_second)
        if x == bx - 1:
            total = total + select(flip_x, x_second, x_first)
        if 0 < x < bx - 1:
            total = total + inner_settled[x - 1]
        else:
            total = total + outer_settled[0 if x == 0 else 1]
        new_mass[x] = total


def swapped_ahead(array, axis):
    devices = lax.axis_size(axis)
    pairing = [(i, (i + 1) % devices if i % 2 == 0 else i - 1) for i in range(devices)]
    return lax.ppermute(array, axis, pairing)


def swapped_behind(array, axis):
    devices = lax.axis_size(axis)
    pairing = [(i, (i - 1) % devices if i % 2 == 0 else (i + 1) % devices) for i in range(devices)]
    return lax.ppermute(array, axis, pairing)


def swapped(first, second, axis):
    return swapped_ahead(first, axis), swapped_behind(second, axis)


def both_ways(rows, lower):
    devices = lax.axis_size("gz")
    before = lax.ppermute(rows, "gz", [(i, (i + 1) % devices) for i in range(devices)])
    if devices == 2:
        return before
    after = lax.ppermute(rows, "gz", [(i, (i - 1) % devices) for i in range(devices)])
    return jnp.where(iota(rows.shape, 0) < lower, before, after)


remote = pl.BlockSpec(memory_space=pltpu.HBM)
anywhere = pl.BlockSpec(memory_space=pl.ANY)


def call(body, outs, specs=None, out_specs=None, scratch=(), cost=(0, 0), aliases=None):
    extra = {} if specs is None else {"in_specs": specs}
    if out_specs is not None:
        extra["out_specs"] = out_specs
    return pl.pallas_call(
        body,
        out_shape=[
            shape
            if isinstance(shape, jax.ShapeDtypeStruct)
            else jax.ShapeDtypeStruct(shape, jnp.float32)
            for shape in outs
        ],
        scratch_shapes=[
            pltpu.VMEM(shape, jnp.float32) if isinstance(shape, tuple) else shape
            for shape in scratch
        ],
        compiler_params=pltpu.CompilerParams(vmem_limit_bytes=40 * 1024 * 1024),
        input_output_aliases=aliases or {},
        cost_estimate=pl.CostEstimate(flops=cost[0], bytes_accessed=cost[1], transcendentals=0),
        **extra,
    )


def shards(populations, stretch, mass, flags, conv_source, conv_kind, conv_direction):
    bx, by, bz = flags.shape
    cells = bx * by * bz
    box, face, tile = ((bx, by, bz), (by, bz), (bx, by, lanes))

    stretch, flags, z_out, y_one, y_two, x_one, x_two = call(
        first_faces,
        [
            (6, *box),
            jax.ShapeDtypeStruct(box, jnp.int32),
            (8, bx * by),
            (4 * bx, bz),
            (4 * bx, bz),
            (4, *face),
            (4, *face),
        ],
        specs=[remote] * 2,
        scratch=[pltpu.SemaphoreType.DMA((2,))],
        cost=(10 * cells, 60 * cells),
    )(*(pltpu.with_memory_space_constraint(array, pltpu.HBM) for array in (stretch, flags)))
    first_x = swapped(x_one, x_two, "gx")
    z_first = both_ways(z_out, 3)
    y_first = swapped(y_one, y_two, "gy")

    entries = conv_source.shape[0]
    mark = (tall, lanes)
    code, code_done = call(
        lambda *refs: conversions(*refs, columns=bz),
        [(bx * by, bz), mark],
        cost=(40 * cells, 4 * cells),
    )(*(array.reshape(1, entries) for array in (conv_source, conv_kind, conv_direction)))
    code = code.reshape(box)

    pops, flow = call(
        moments,
        [(19, *box), (5, *box)],
        specs=[remote],
        scratch=[pltpu.SemaphoreType.DMA((bx,))],
        cost=(60 * cells, 150 * cells),
    )(pltpu.with_memory_space_constraint(populations, pltpu.HBM))

    columns, rows = ((24, bx * by), (10 * bx, bz))
    sides_y = [(bx, 8, bz), (bx, 8, bz), tile]
    inside, ends = ((bx - 2, *face), (2, *face))
    inner_post, inner_shift = call(
        collide_inner,
        [(19, *inside), (3, *inside)],
        scratch=sides_y,
        cost=(150 * cells, 150 * cells),
    )(pops, stretch, flow, z_first, *y_first)
    outer_post, outer_shift, z_out, x_one, x_two, y_one, y_two = call(
        collide_outer,
        [(19, *ends), (3, *ends), columns, (5, *face), (8, *face), rows, rows],
        scratch=[(4, *face), (4, *face)] + sides_y + [box],
        cost=(150 * cells, 150 * cells),
    )(pops, stretch, flags, flow, *first_x, *y_first, z_first, inner_post)
    z_post = both_ways(z_out, sides)
    post_y = swapped(y_one, y_two, "gy")
    post_x = swapped(x_one, x_two, "gx")
    edges = (4 * (bz // lanes) + columns[0], lanes)
    x_one, x_two, corner = call(
        lambda *refs: forward_edges(*refs, bx=bx), [edges, edges, columns], cost=(17 * 10**8, 0)
    )(z_post, *post_y, code_done)
    corners = swapped(corner, corner, "gy")
    edges_x = swapped(x_one, x_two, "gx")

    rims = [(bx + 2, *face), (bx + 2, 16, bz), (bx + 2, 16, bz), (bx + 2, by, lanes)]
    posts = (inner_post, outer_post, inner_shift, outer_shift)
    inner, outer, totals, changes = call(
        stream_early,
        [(first_slanted, *inside), (first_slanted, *ends), box, box],
        scratch=rims,
        cost=(350 * cells, 200 * cells),
    )(*posts, flags, *post_y, z_post)
    fresh, inner_stored = call(
        store_inner,
        [(19, *box), mark],
        out_specs=[remote, pl.BlockSpec()],
        scratch=[pltpu.SemaphoreType.DMA],
        cost=(0, 60 * cells),
    )(inner)
    (
        inner_slanted,
        outer_slanted,
        inner_settled,
        inner_excess,
        inner_heading,
        totals,
        changes,
    ) = call(
        stream_slanted,
        [(4, *inside), (4, *ends), inside, inside, inside, ends, ends],
        scratch=rims,
        cost=(100 * cells, 60 * cells),
    )(*posts, mass, flags, code, *post_y, z_post, *corners, totals, changes, inner_stored)
    new_stretch, inner_done = call(
        restretch_inner,
        [(6, *box), mark],
        out_specs=[remote, pl.BlockSpec()],
        scratch=[(6, *inside)] + sides_y + [pltpu.SemaphoreType.DMA],
        cost=(80 * cells, 40 * cells),
    )(stretch, flow, *post_y, z_post)
    late, v_one, outer_settled, spread, y_one, y_two, z_out = call(
        stream_late,
        [
            (5, *ends),
            (3, *face),
            ends,
            (bx + 2, *face),
            (8, bz),
            (8, bz),
            (16, bx * by),
        ],
        scratch=rims + [(5, *face), (5, *face), box, box],
        cost=(150 * cells, 100 * cells),
    )(
        outer_post,
        outer_shift,
        mass,
        flags,
        code,
        totals,
        changes,
        *first_x,
        *post_x,
        *edges_x,
        inner_excess,
        inner_heading,
        flow,
        inner_done,
    )
    z_last = both_ways(z_out, 8)
    last_y = swapped(y_one, y_two, "gy")
    last_corners = swapped(z_last, z_last, "gy")
    flow_x = (swapped_ahead(v_one, "gx"), post_x[1])
    x_one, x_two = call(add_faces, [face, face], cost=(4 * 10**9, 0))(
        spread, z_last, *last_y
    )
    last_x = swapped(x_one, x_two, "gx")
    new_stretch, fresh, outer_done = call(
        restretch_outer,
        [(6, *box), (19, *box), mark],
        specs=[pl.BlockSpec()] * 7 + [remote] + [pl.BlockSpec()] * 4 + [remote],
        out_specs=[remote, remote, pl.BlockSpec()],
        scratch=[(6, *ends), (3, *face), (3, *face)]
        + sides_y
        + [pltpu.SemaphoreType.DMA((2,)), pltpu.SemaphoreType.DMA((32,))],
        cost=(80 * cells, 200 * cells),
        aliases={7: 0, 12: 1},
    )(
        stretch,
        flow,
        *flow_x,
        *post_y,
        z_post,
        new_stretch,
        outer,
        inner_slanted,
        outer_slanted,
        late,
        fresh,
    )
    (new_mass,) = call(add_all, [box])(
        inner_settled, outer_settled, spread, z_last, *last_y, *last_corners, *last_x[::-1], outer_done
    )
    return (fresh, new_stretch, new_mass)


def solution(mesh):
    return jax.shard_map(
        shards,
        mesh=mesh,
        in_specs=(
            P(None, "gx", "gy", "gz"),
            P(None, "gx", "gy", "gz"),
            P("gx", "gy", "gz"),
            P("gx", "gy", "gz"),
            P(("gx", "gy", "gz")),
            P(("gx", "gy", "gz")),
            P(("gx", "gy", "gz")),
        ),
        out_specs=(P(None, "gx", "gy", "gz"), P(None, "gx", "gy", "gz"), P("gx", "gy", "gz")),
        check_vma=False,
    )
```
